32 devices in a mesh: section: 4 (over z), dp: 8 (over y, x, core).
Axes of the slice: x: 2, y: 2, z: 4, core: 2. Of those that a mesh axis runs over, the one named last changes fastest.
Arguments:
- clip_inputs: bfloat16 [16, 1280, 768], P('dp'), may hold values from -6 to 6
- out_grad: bfloat16 [16, 1280, 768], P('dp'), may hold values from -6 to 6
- clip_class: int32 [16], P('dp'), may hold values from 0 to 1, as said below
- w_front: bfloat16 [4, 768, 3072], P('section')
- w_back: bfloat16 [4, 1536, 768], P('section'), may hold values from -0.109375 to 0.109375
- norm_gain: float32 [4, 768], P('section'), may hold values from 0.25 to 1.75
- norm_shift: float32 [4, 768], P('section'), may hold values from -3 to 3
- bias_query_value: float32 [2, 1536], replicated, may hold values from -3 to 3
- bias_attn_out: float32 [2, 768], replicated, may hold values from -3 to 3
- bias_up: float32 [2, 3072], replicated, may hold values from -3 to 3
- bias_down: float32 [2, 768], replicated, may hold values from -3 to 3
Outputs:
- activations: bfloat16 [4, 16, 1280, 768], P('section', 'dp')
- input_grads: float32 [4, 16, 1280, 768], P('section', 'dp')
- grad_front: float32 [4, 768, 3072], P('section')
- grad_back: float32 [4, 1536, 768], P('section')
- grad_gain: float32 [4, 768], P('section')
- grad_shift: float32 [4, 768], P('section')
- grad_query_value: float32 [2, 1536], replicated
- grad_attn_out: float32 [2, 768], replicated
- grad_up: float32 [2, 3072], replicated
- grad_down: float32 [2, 768], replicated
The draws below stay inside these ranges and needn't reach their ends.
Inputs may be any that keep to these rules, and one draw needn't show every extreme that they name: `clip_class`: 1 marks a clip of 1214 tokens, 0 one of 514; the first clip is long and the second short.
All inputs are finite; a program needn't handle non-finite values.
Results may differ from the reference program's by a relative error of at most 0.014.
Values may be sent and summed in bfloat16 or wider, within the bound.
A program may use at most 320 MiB of HBM per device.

```python
import jax
import jax.numpy as jnp
from jax import lax

D = 768
HEADS = 12
FF = 3072
LONG = 1214
SHORT = 514
LPAD = 1280
CLIPS = 16
LAYERS = 2
N_SECTION = 4


def draw_w_front(key, part):
    key = jax.random.fold_in(key, 11)
    basic_draw = jax.random.truncated_normal(key, -3.0, 3.0, (N_SECTION, D, FF), jnp.float32)
    section_ids = lax.broadcasted_iota(jnp.int32, (N_SECTION, D, FF), 0)
    columns = lax.broadcasted_iota(jnp.int32, (N_SECTION, D, FF), 2)
    booster = jnp.where((section_ids % 2 == 0) & (columns >= 3 * D), 16.0, 1.0)
    return (basic_draw * booster * D ** (-0.5)).astype(jnp.bfloat16)


def draw_clip_class(key, part):
    key = jax.random.fold_in(key, 23)
    picks = jax.random.randint(key, (CLIPS,), 0, 2, jnp.int32)
    return picks.at[0].set(1).at[1].set(0)


def steps_of(key, extent, pieces, smallest, top_value):
    factor_of = 1.0
    for position, blocks in pieces:
        draws = jax.random.uniform(jax.random.fold_in(jax.random.fold_in(key, 6), position), (blocks,), jnp.float32, smallest / len(pieces), top_value / len(pieces))
        factor_of = factor_of * jnp.repeat(jnp.exp(draws), extent[position] // blocks).reshape((-1,) + (1,) * (len(extent) - 1 - position))
    return factor_of


def gaussian(own_key, shape, width, reach, shards=(), kind=jnp.bfloat16):
    values = jax.random.normal(own_key, shape, jnp.float32) * width
    if len(shards) > 0:
        values = steps_of(own_key, shape, shards, -0.22, 0.18) * values
    return jnp.clip(values, min=-reach, max=reach).astype(kind)


def setup_inputs(seed: int = 0) -> dict:
    streams_of = jax.random.split(jax.random.key(seed), 12)
    clip_inputs = gaussian(streams_of[0], (CLIPS, LPAD, D), 1.0, 6.0, ((0, 8),))
    out_grad = gaussian(streams_of[1], (CLIPS, LPAD, D), 1.0, 6.0, ((0, 8),))
    clip_class = draw_clip_class(jax.random.fold_in(streams_of[11], 71), 0)
    w_front = draw_w_front(jax.random.fold_in(streams_of[11], 71), 0)
    w_back = gaussian(streams_of[4], (N_SECTION, FF // 2, D), FF ** -0.5, 0.109375, ((0, 4),))
    norm_gain = jnp.clip(1.0 + 0.15 * jax.random.normal(streams_of[5], (N_SECTION, D), jnp.float32), 0.25, 1.75)
    norm_shift = gaussian(streams_of[6], (N_SECTION, D), 0.5, 3.0, ((0, 4),), jnp.float32)
    bias_query_value = gaussian(streams_of[7], (LAYERS, 2 * D), 0.5, 3.0, (), jnp.float32)
    bias_attn_out = gaussian(streams_of[8], (LAYERS, D), 0.5, 3.0, (), jnp.float32)
    bias_up = gaussian(streams_of[9], (LAYERS, FF), 0.5, 3.0, (), jnp.float32)
    bias_down = gaussian(streams_of[10], (LAYERS, D), 0.5, 3.0, (), jnp.float32)
    return {"clip_inputs": clip_inputs, "out_grad": out_grad, "clip_class": clip_class, "w_front": w_front, "w_back": w_back, "norm_gain": norm_gain, "norm_shift": norm_shift, "bias_query_value": bias_query_value, "bias_attn_out": bias_attn_out, "bias_up": bias_up, "bias_down": bias_down}


EPS = 1e-06
HIGH = lax.Precision.HIGHEST

@jax.custom_vjp
def low(v):
    return lax.optimization_barrier(v.astype(jnp.bfloat16)).astype(jnp.float32)

@jax.custom_vjp
def low_back(v):
    return v

def low_keep(v):
    return (low(v), None)

def low_pass(kept, grad):
    return (grad,)

def back_keep(v):
    return (v, None)

def back_low(kept, grad):
    return (low(grad),)
low.defvjp(low_keep, low_pass)
low_back.defvjp(back_keep, back_low)

def layer_norm(hidden_in, scales, offset):
    average = lax.optimization_barrier(jnp.mean(hidden_in, axis=-1, keepdims=True))
    centred = hidden_in - average
    spread = lax.optimization_barrier(jnp.mean(centred * centred, axis=-1, keepdims=True))
    return centred * lax.rsqrt(spread + EPS) * scales + offset

def attention_layer(hidden_in, row_mask, weight_in, scales, offset, bias_pair, bias_out):
    padded = hidden_in.shape[0]
    model_width = hidden_in.shape[1]
    head_dim = model_width // HEADS
    normed = low(layer_norm(hidden_in, scales, offset))
    full_bias = jnp.concatenate([bias_pair[:model_width], jnp.zeros((model_width,), jnp.float32), bias_pair[model_width:]])
    qkv = low_back(low(jnp.dot(normed, weight_in[:, :3 * model_width], precision=HIGH) + full_bias))
    query_heads = qkv[:, :model_width].reshape(padded, HEADS, head_dim)
    key_heads = qkv[:, model_width:2 * model_width].reshape(padded, HEADS, head_dim)
    value_heads = qkv[:, 2 * model_width:].reshape(padded, HEADS, head_dim)
    scores = low_back(jnp.einsum('qhd,khd->hqk', query_heads, key_heads, precision=HIGH) * head_dim ** (-0.5))
    scores = jnp.where(row_mask[None, None, :] > 0, scores, -1e+30)
    powered = jnp.exp(scores - lax.optimization_barrier(jnp.max(scores, axis=-1, keepdims=True)))
    attn_probs = low(powered / lax.optimization_barrier(jnp.sum(powered, axis=-1, keepdims=True)))
    attended = jnp.einsum('hqk,khd->qhd', attn_probs, value_heads, precision=HIGH).reshape(padded, model_width)
    attended = low_back(low(attended))
    branch = jnp.dot(attended, weight_in[:, 3 * model_width:].T, precision=HIGH) + bias_out
    return row_mask[:, None] * (hidden_in + branch)

def mlp_layer(hidden_in, row_mask, weight_up, weight_down, scales, offset, bias_in, bias_out):
    normed = low(layer_norm(hidden_in, scales, offset))
    pre_act = low_back(jnp.dot(normed, weight_up, precision=HIGH) + bias_in)
    activated = low(jax.nn.gelu(pre_act, approximate=False))
    branch = jnp.dot(activated, weight_down, precision=HIGH) + bias_out
    return row_mask[:, None] * (hidden_in + branch)

def section_chain(params, clip_in, probes, row_mask):
    w_front, w_back, norm_gain, norm_shift, bias_qv, bias_attn, bias_in, bias_out = params
    hidden_in = clip_in * row_mask[:, None] + probes[0]
    outputs = []
    for section_id in range(N_SECTION):
        if section_id > 0:
            hidden_in = low_back(hidden_in) + probes[section_id]
        layer_id = section_id // 2
        if section_id % 2 == 0:
            leaving = attention_layer(hidden_in, row_mask, w_front[section_id], norm_gain[section_id], norm_shift[section_id], bias_qv[layer_id], bias_attn[layer_id])
        else:
            weight_down = jnp.concatenate([w_back[section_id - 1], w_back[section_id]], axis=0)
            leaving = mlp_layer(hidden_in, row_mask, w_front[section_id], weight_down, norm_gain[section_id], norm_shift[section_id], bias_in[layer_id], bias_out[layer_id])
        hidden_in = low(leaving)
        outputs.append(hidden_in)
    return jnp.stack(outputs)

def reference(clip_inputs, out_grad, clip_class, w_front, w_back, norm_gain, norm_shift, bias_query_value, bias_attn_out, bias_up, bias_down):
    params = tuple((argument.astype(jnp.float32) for argument in (w_front, w_back, norm_gain, norm_shift, bias_query_value, bias_attn_out, bias_up, bias_down)))
    lengths = SHORT + (LONG - SHORT) * clip_class
    positions = jnp.arange(LPAD, dtype=jnp.int32)

    def per_clip(totals, clip_item):
        clip_in, clip_grad, length = clip_item
        row_mask = (positions < length).astype(jnp.float32)
        probes = jnp.zeros((N_SECTION, LPAD, D), jnp.float32)

        def chain(weights, probe_set):
            return section_chain(weights, clip_in.astype(jnp.float32), probe_set, row_mask)
        outputs, backward = jax.vjp(chain, params, probes)
        cotangent = jnp.zeros_like(outputs).at[N_SECTION - 1].set(clip_grad.astype(jnp.float32))
        grad_params, grad_probes = backward(cotangent)
        totals = jax.tree.map(jnp.add, totals, grad_params)
        return (totals, (outputs.astype(jnp.bfloat16), grad_probes))
    start = jax.tree.map(jnp.zeros_like, params)
    totals, (stacked_acts, stacked_grads) = lax.scan(per_clip, start, (clip_inputs, out_grad, lengths))
    activations = jnp.swapaxes(stacked_acts, 0, 1)
    input_grads = jnp.swapaxes(stacked_grads, 0, 1)
    return (activations, input_grads, totals[0], totals[1], totals[2], totals[3], totals[4], totals[5], totals[6], totals[7])
```

```python
import functools
import math

import jax
import jax.numpy as jnp
from jax import lax
from jax.experimental import pallas as pl
from jax.experimental.pallas import tpu as pltpu
from jax.sharding import PartitionSpec as P

HEADS = 12
LONG = 1214
SHORT = 514
EPS = 1e-06
HEAD_DIM = 64
PAIR = 2 * HEAD_DIM
MASKED = -1e30
F32 = jnp.float32
BF16 = jnp.bfloat16
KERNEL_VMEM = 56 * 2**20


def mm(left, right):
    return jnp.dot(left, right, preferred_element_type=F32)


def contract_rows(left, right):
    return lax.dot_general(left, right, (((0,), (0,)), ((), ())), preferred_element_type=F32)


def contract_cols(left, right):
    return lax.dot_general(left, right, (((1,), (1,)), ((), ())), preferred_element_type=F32)


def lane_ids(shape):
    return lax.broadcasted_iota(jnp.int32, shape, len(shape) - 1)


def three_parts(value):
    high = value.astype(BF16).astype(F32)
    rest = value - high
    middle = rest.astype(BF16).astype(F32)
    return high, middle, rest - middle


def extend_keys(keys_out, values_out, blocks, bias_ref, head):
    aux = HEAD_DIM * (1 - head)
    row = 0
    for key_ref, value_ref in blocks:
        rows = key_ref.shape[0]
        span = slice(row, row + rows)
        lanes = lane_ids((rows, PAIR))
        inside = (lanes // HEAD_DIM) == head
        ones = jnp.where((lanes > aux) & (lanes <= aux + 3), 1.0, 0.0)
        extra = jnp.where(lanes == aux, bias_ref[span, :], ones)
        keys_out[span, :] = jnp.where(inside, key_ref[...].astype(F32), extra).astype(BF16)
        ones = jnp.where((lanes >= aux) & (lanes < aux + 3), 1.0, 0.0)
        values_out[span, :] = jnp.where(inside, value_ref[...].astype(F32), ones).astype(BF16)
        row += rows


def attention_forward_body(
    chunk, query_ref, key_own, value_own, key_far, value_far, bias_ref,
    out_ref, extended_ref, keys, values,
):
    rows = query_ref.shape[0]
    for head in (0, 1):
        extend_keys(
            keys.at[head], values.at[head], ((key_own, value_own), (key_far, value_far)), bias_ref, head
        )
    lanes = lane_ids((chunk, PAIR))
    for start in range(0, rows, chunk):
        span = slice(start, start + chunk)
        outs = []
        for head in (0, 1):
            aux = HEAD_DIM * (1 - head)
            inside = (lanes // HEAD_DIM) == head
            query = query_ref[span, :].astype(F32)
            extended = jnp.where(inside, query, jnp.where(lanes == aux, 1.0, 0.0))
            scores = contract_cols(extended.astype(BF16), keys[head])
            top = jnp.max(scores, axis=1, keepdims=True)
            powered = jnp.exp(scores - top).astype(BF16)
            summed = mm(powered, values[head])
            total = summed[:, aux : aux + 1]
            outs.append(summed / total)
            high, middle, low = three_parts(-(top + jnp.log(total)))
            extended = jnp.where(lanes == aux + 1, high, extended)
            extended = jnp.where(lanes == aux + 2, middle, extended)
            extended = jnp.where(lanes == aux + 3, low, extended)
            extended_ref[head, span, :] = extended.astype(BF16)
        out_ref[span, :] = jnp.where(lanes < HEAD_DIM, outs[0], outs[1])


def attention_forward(qkv, kv_far, key_bias):
    rows, width = qkv.shape[0], qkv.shape[1] // 3
    pairs = width // PAIR

    def block(base):
        return pl.BlockSpec((rows, PAIR), lambda p: (0, base + p))

    return pl.pallas_call(
        functools.partial(attention_forward_body, rows // 2),
        grid=(pairs,),
        in_specs=[
            block(0), block(pairs), block(2 * pairs), block(0), block(pairs),
            pl.BlockSpec((2 * rows, 1), lambda p: (0, 0)),
        ],
        out_specs=[block(0), pl.BlockSpec((2, rows, PAIR), lambda p: (p, 0, 0))],
        out_shape=[
            jax.ShapeDtypeStruct((rows, width), F32),
            jax.ShapeDtypeStruct((2 * pairs, rows, PAIR), BF16),
        ],
        scratch_shapes=[pltpu.VMEM((2, 2 * rows, PAIR), BF16)] * 2,
        compiler_params=pltpu.CompilerParams(vmem_limit_bytes=KERNEL_VMEM),
        cost_estimate=pl.CostEstimate(
            flops=16 * rows * rows * 2 * width * 2, bytes_accessed=12 * rows * width,
            transcendentals=2 * rows * rows * 2 * pairs,
        ),
        name="attention_forward",
    )(qkv, qkv, qkv, kv_far, kv_far, key_bias)


def attention_backward_body(
    chunks, extended_ref, key_own, value_own, key_far, value_far, bias_ref, grad_ref, out_ref,
    grad_query, grad_key_own, grad_value_own, grad_key_far, grad_value_far,
    keys, values, key_sums, value_sums,
):
    rows = extended_ref.shape[1]
    for head in (0, 1):
        extend_keys(
            keys.at[head], values.at[head], ((key_own, value_own), (key_far, value_far)), bias_ref, head
        )
    for start, size in chunks:
        span = slice(start, start + size)
        lanes = lane_ids((size, PAIR))
        parts = []
        for head in (0, 1):
            aux = HEAD_DIM * (1 - head)
            inside = (lanes // HEAD_DIM) == head
            query = extended_ref[head, span, :]
            grad = jnp.where(inside, grad_ref[span, :].astype(F32), 0.0)
            dots = jnp.sum(grad * out_ref[span, :], axis=1, keepdims=True)
            high, middle, low = three_parts(-dots)
            grad = jnp.where(lanes == aux, high, grad)
            grad = jnp.where(lanes == aux + 1, middle, grad)
            grad = jnp.where(lanes == aux + 2, low, grad)
            probs = jnp.exp(contract_cols(query, keys[head]))
            shifted = contract_cols(grad.astype(BF16), values[head])
            grad_scores = (probs * shifted).astype(BF16)
            parts.append(mm(grad_scores, keys[head]) * HEAD_DIM**-0.5)
            to_values = mm(grad.T.astype(BF16), probs.astype(BF16)).T
            to_keys = mm(query.astype(F32).T.astype(BF16), grad_scores).T
            if start == 0:
                key_sums[head] = to_keys
                value_sums[head] = to_values
            else:
                key_sums[head] += to_keys
                value_sums[head] += to_values
        grad_query[span, :] = jnp.where(lanes < HEAD_DIM, parts[0], parts[1]).astype(BF16)
    lanes = lane_ids((rows, PAIR))
    for part, (to_key, to_value) in enumerate(
        ((grad_key_own, grad_value_own), (grad_key_far, grad_value_far))
    ):
        span = slice(part * rows, (part + 1) * rows)
        first = lanes < HEAD_DIM
        to_key[...] = jnp.where(first, key_sums[0, span, :], key_sums[1, span, :]).astype(BF16)
        to_value[...] = jnp.where(first, value_sums[0, span, :], value_sums[1, span, :]).astype(BF16)


def attention_backward(extended, qkv, kv_far, key_bias, grad, out):
    rows, width = out.shape
    pairs = width // PAIR

    def block(base):
        return pl.BlockSpec((rows, PAIR), lambda p: (0, base + p))

    shape = jax.ShapeDtypeStruct((rows, width), BF16)
    return pl.pallas_call(
        functools.partial(attention_backward_body, ((0, rows),)),
        grid=(pairs,),
        in_specs=[
            pl.BlockSpec((2, rows, PAIR), lambda p: (p, 0, 0)),
            block(pairs), block(2 * pairs), block(0), block(pairs),
            pl.BlockSpec((2 * rows, 1), lambda p: (0, 0)),
            block(0), block(0),
        ],
        out_specs=[block(0)] * 5,
        out_shape=[shape] * 5,
        scratch_shapes=[pltpu.VMEM((2, 2 * rows, PAIR), BF16)] * 2
        + [pltpu.VMEM((2, 2 * rows, PAIR), F32)] * 2,
        compiler_params=pltpu.CompilerParams(vmem_limit_bytes=KERNEL_VMEM),
        cost_estimate=pl.CostEstimate(
            flops=40 * rows * rows * 2 * width * 2, bytes_accessed=24 * rows * width,
            transcendentals=2 * rows * rows * 2 * pairs,
        ),
        name="attention_backward",
    )(extended, qkv, qkv, kv_far, kv_far, key_bias, grad, out)


def norm_parts(hidden):
    average = jnp.mean(hidden, axis=-1, keepdims=True)
    centred = hidden - average
    inverse = lax.rsqrt(jnp.mean(centred * centred, axis=-1, keepdims=True) + EPS)
    return centred * inverse, inverse


def norm_backward(hidden, grad_normed, gain):
    unit, inverse = norm_parts(hidden)
    scaled = grad_normed * gain
    first = jnp.mean(scaled, axis=-1, keepdims=True)
    second = jnp.mean(scaled * unit, axis=-1, keepdims=True)
    grad_hidden = inverse * (scaled - first - unit * second)
    return grad_hidden, jnp.sum(grad_normed * unit, axis=0), jnp.sum(grad_normed, axis=0)


def gelu_and_slope(pre):
    size = jnp.abs(pre) * (0.5**0.5)
    density = jnp.exp(-0.5 * pre * pre)
    t = 1.0 / (1.0 + 0.3275911 * size)
    series = t * (0.254829592 + t * (-0.284496736 + t * (1.421413741 + t * (-1.453152027 + t * 1.061405429))))
    tail = 0.5 * series * density
    below = jnp.where(pre < 0, tail, 1.0 - tail)
    return pre * below, below + pre * density * (1.0 / math.sqrt(2.0 * math.pi))


def swap(block, bit):
    count = lax.axis_size("dp")
    return lax.ppermute(block, "dp", [(i, i ^ bit) for i in range(count)])


def spread_over_sections(piece, source, section):
    result = piece
    for step, last in ((1, lax.axis_size("section") - 1), (-1, 0)):
        carried = piece
        for at in range(source, last, step):
            carried = lax.ppermute(carried, "section", [(at, at + step)])
            result = jnp.where(section == at + step, carried, result)
    return result


def rows_from(array, start, size):
    return lax.dynamic_slice_in_dim(array, start, size, 0)


def gather_rows(weight, source, place):
    rows = weight.shape[0]
    half, part = rows // 2, rows // 4
    mine = rows_from(weight, place.core * half + place.parity * part, part)
    mine = spread_over_sections(mine, source, place.section)
    from_x = swap(mine[: part // 2], place.x_bit)
    from_y = swap(mine[part // 2 :], place.y_bit)
    near = jnp.concatenate([from_x, from_y], axis=0)
    first = jnp.where(place.parity == 0, mine, near)
    second = jnp.where(place.parity == 0, near, mine)
    own = jnp.concatenate([first, second], axis=0)
    other = swap(own, 1)
    return jnp.concatenate(
        [jnp.where(place.core == 0, own, other), jnp.where(place.core == 0, other, own)], axis=0
    )


def add(a, b):
    return (a.astype(F32) + b.astype(F32)).astype(BF16)


def scatter_rows(grad, place):
    half = grad.shape[0] // 2
    kept = rows_from(grad, place.core * half, half)
    given = rows_from(grad, (1 - place.core) * half, half)
    kept = add(kept, swap(given, 1))
    columns = kept.shape[1] // 2
    lanes = []
    for lane, bits in enumerate((place.bits, place.bits[::-1])):
        block = kept[:, lane * columns : (lane + 1) * columns]
        for bit in bits:
            size = block.shape[0] // 2
            high = (place.dp // bit) % 2
            given = rows_from(block, (1 - high) * size, size)
            block = add(rows_from(block, high * size, size), swap(given, bit))
        lanes.append(block)
    return jnp.stack(lanes)


def to_section(block, target, section):
    count = lax.axis_size("section")
    total = jnp.where(section == target, block.astype(F32), 0.0)
    for source in range(count):
        if source != target:
            total = total + lax.ppermute(block, "section", [(source, target)]).astype(F32)
    return total


def gather_scattered(lanes, place):
    out = []
    for lane, bits in enumerate((place.bits, place.bits[::-1])):
        block = lanes[lane]
        for bit in bits[::-1]:
            high = (place.dp // bit) % 2
            far = swap(block, bit)
            block = jnp.concatenate(
                [jnp.where(high == 0, block, far), jnp.where(high == 0, far, block)], axis=0
            )
        out.append(block)
    own = jnp.concatenate(out, axis=1)
    far = swap(own, 1)
    return jnp.concatenate(
        [jnp.where(place.core == 0, own, far), jnp.where(place.core == 0, far, own)], axis=0
    ).astype(F32)


def deliver(block, target):
    sections, count = lax.axis_size("section"), lax.axis_size("dp")
    pieces = []
    for slot in (0, 1):
        for core in (0, 1):
            route = [
                (z * count + d, target * count + (d - core + z // 2))
                for z in range(slot, sections, 2)
                for d in range(core, count, 2)
            ]
            pieces.append(lax.ppermute(block, ("section", "dp"), route))
    return pieces


class Place:
    def __init__(self):
        self.section = lax.axis_index("section")
        self.dp = lax.axis_index("dp")
        count = lax.axis_size("dp")
        self.core = self.dp % 2
        self.bits = [1 << i for i in range(1, count.bit_length() - 1)]
        self.x_bit, self.y_bit = self.bits[0], self.bits[-1]
        self.parity = ((self.dp // self.x_bit) + (self.dp // self.y_bit)) % 2


def per_device(
    clip_inputs, out_grad, clip_class, w_front, w_back, norm_gain, norm_shift,
    bias_query_value, bias_attn_out, bias_up, bias_down,
):
    place = Place()
    sections = lax.axis_size("section")
    padded, width = clip_inputs.shape[1:]
    rows = -(-LONG // 32) * 16
    core, section = place.core, place.section

    owner, slot = section // 2, section % 2
    mine = jnp.stack([lax.dynamic_index_in_dim(a, slot, 0, False) for a in (clip_inputs, out_grad)])
    far = swap(lax.dynamic_slice_in_dim(mine, (1 - core) * rows, rows, 1), 1)
    near = lax.dynamic_slice_in_dim(mine, core * rows, rows, 1)
    clip_pair = jnp.where(core == owner, near, far)
    own_class = lax.dynamic_index_in_dim(clip_class, slot, 0, False).astype(F32)
    own_class = jnp.broadcast_to(own_class, (8, 128))
    clip_kind = jnp.where(core == owner, own_class, swap(own_class, 1))[0, 0]
    length = SHORT + (LONG - SHORT) * clip_kind
    positions = jnp.arange(rows, dtype=jnp.int32)
    own_rows = (positions + core * rows).astype(F32) < length
    far_rows = (positions + (1 - core) * rows).astype(F32) < length
    row_mask = own_rows.astype(F32)[:, None]
    key_bias = jnp.where(jnp.concatenate([own_rows, far_rows]), 0.0, MASKED)[:, None]

    gains = lax.all_gather(norm_gain[0], "section")
    shifts = lax.all_gather(norm_shift[0], "section")
    fronts = [gather_rows(w_front[0], s, place) for s in range(sections)]
    downs = [
        jnp.concatenate([gather_rows(w_back[0], s - 1, place), gather_rows(w_back[0], s, place)], axis=0)
        if s % 2
        else None
        for s in range(sections)
    ]

    hidden = (clip_pair[0].astype(F32) * row_mask).astype(BF16)
    saved, delivered = [], []
    for s in range(sections):
        layer = s // 2
        entering = hidden.astype(F32)
        unit, _ = norm_parts(entering)
        normed = (unit * gains[s] + shifts[s]).astype(BF16)
        if s % 2 == 0:
            pair = bias_query_value[layer]
            bias = jnp.concatenate([pair[:width], jnp.zeros((width,), F32), pair[width:]])
            scale = jnp.where(jnp.arange(3 * width) < width, HEAD_DIM**-0.5, 1.0)
            qkv = ((mm(normed, fronts[s][:, : 3 * width]) + bias).astype(BF16) * scale).astype(BF16)
            kv_far = swap(qkv[:, width:], 1)
            attended, extended = attention_forward(qkv, kv_far, key_bias)
            attended_b = attended.astype(BF16)
            branch = contract_cols(attended_b, fronts[s][:, 3 * width :]) + bias_attn_out[layer]
            saved.append((hidden, normed, qkv, kv_far, attended, attended_b, extended))
        else:
            pre = mm(normed, fronts[s]) + bias_up[layer]
            act, slope = gelu_and_slope(pre)
            act, slope = act.astype(BF16), slope.astype(BF16)
            branch = mm(act, downs[s]) + bias_down[layer]
            saved.append((hidden, normed, act, slope))
        hidden = (row_mask * (entering + branch)).astype(BF16)
        delivered.append(deliver(hidden, s))

    incoming = clip_pair[1]
    sent_grads = [None] * sections
    front_total = jnp.zeros((), F32)
    back_total = jnp.zeros((), F32)
    grad_gain, grad_shift = [None] * sections, [None] * sections
    grad_pairs, grad_outs, grad_ups, grad_downs = [], [], [], []
    for s in reversed(range(sections)):
        grad_rows = row_mask * incoming.astype(F32)
        grad_b = grad_rows.astype(BF16)
        front = fronts[s]
        if s % 2 == 0:
            entered, normed, qkv, kv_far, attended, attended_b, extended = saved[s]
            grad_attended = mm(grad_b, front[:, 3 * width :]).astype(BF16)
            to_query, to_key, to_value, key_far, value_far = attention_backward(
                extended, qkv, kv_far, key_bias, grad_attended, attended
            )
            back = swap(jnp.stack([key_far, value_far]), 1)
            grad_qkv = jnp.concatenate([to_query, add(to_key, back[0]), add(to_value, back[1])], axis=1)
            sums = jnp.sum(grad_qkv.astype(F32), axis=0)
            grad_pairs.insert(0, jnp.concatenate([sums[:width], sums[2 * width :]]))
            grad_outs.insert(0, jnp.sum(grad_rows, axis=0))
            grad_front = jnp.concatenate(
                [contract_rows(normed, grad_qkv).astype(BF16), contract_rows(grad_b, attended_b).astype(BF16)],
                axis=1,
            )
            grad_normed = contract_cols(grad_qkv, front[:, : 3 * width])
        else:
            entered, normed, act, slope = saved[s]
            grad_act = contract_cols(grad_b, downs[s])
            grad_pre = (grad_act * slope.astype(F32)).astype(BF16)
            grad_down = contract_rows(act, grad_b).astype(BF16)
            grad_front = contract_rows(normed, grad_pre).astype(BF16)
            grad_ups.insert(0, jnp.sum(grad_pre.astype(F32), axis=0))
            grad_downs.insert(0, jnp.sum(grad_rows, axis=0))
            grad_normed = contract_cols(grad_pre, front)
            half = grad_down.shape[0] // 2
            for target, piece in ((s - 1, grad_down[:half]), (s, grad_down[half:])):
                back_total = back_total + to_section(scatter_rows(piece, place), target, section)
        front_total = front_total + to_section(scatter_rows(grad_front, place), s, section)
        grad_hidden, grad_gain[s], grad_shift[s] = norm_backward(entered.astype(F32), grad_normed, gains[s])
        incoming = (grad_rows + grad_hidden).astype(BF16)
        sent_grads[s] = deliver(incoming, s)

    def assemble(pieces, kind):
        clips = []
        for slot_id in (0, 1):
            halves = []
            for half in (0, 1):
                choice = pieces[0][2 * slot_id + half]
                for s in range(1, sections):
                    choice = jnp.where(section == s, pieces[s][2 * slot_id + half], choice)
                halves.append(choice.astype(kind))
            halves.append(jnp.zeros((padded - 2 * rows, width), kind))
            clips.append(jnp.concatenate(halves, axis=0))
        return jnp.stack(clips)[None]

    small = lax.psum(
        jnp.concatenate(
            [v.reshape(-1) for v in grad_gain + grad_shift + grad_pairs + grad_outs + grad_ups + grad_downs]
        ),
        ("section", "dp"),
    )
    parts, place_at = [], 0
    layers, hidden_units = bias_up.shape
    for count, size in (
        (sections, width), (sections, width), (layers, 2 * width), (layers, width),
        (layers, hidden_units), (layers, width),
    ):
        parts.append(small[place_at : place_at + count * size].reshape(count, size))
        place_at += count * size
    return (
        assemble(delivered, BF16),
        assemble(sent_grads, F32),
        gather_scattered(front_total.astype(BF16), place)[None],
        gather_scattered(back_total.astype(BF16), place)[None],
        lax.dynamic_slice_in_dim(parts[0], section, 1, 0),
        lax.dynamic_slice_in_dim(parts[1], section, 1, 0),
        *parts[2:],
    )


def solution(mesh):
    placed = (
        P("dp", None, None), P("dp", None, None), P("dp"),
        P("section", None, None), P("section", None, None), P("section", None), P("section", None),
        P(), P(), P(), P(),
    )
    return jax.shard_map(
        per_device,
        mesh=mesh,
        in_specs=placed,
        out_specs=(
            P("section", "dp", None, None), P("section", "dp", None, None),
            P("section", None, None), P("section", None, None), P("section", None), P("section", None),
            P(), P(), P(), P(),
        ),
        check_vma=False,
    )
```

```python
import functools
import math

import jax
import jax.numpy as jnp
from jax import lax
from jax.experimental import pallas as pl
from jax.experimental.pallas import tpu as pltpu
from jax.sharding import PartitionSpec as P

HEADS = 12
LONG = 1214
SHORT = 514
EPS = 1e-06
HEAD_DIM = 64
PAIR = 2 * HEAD_DIM
MASKED = -1e30
F32 = jnp.float32
BF16 = jnp.bfloat16
KERNEL_VMEM = 56 * 2**20


def mm(left, right):
    return jnp.dot(left, right, preferred_element_type=F32)


def contract_rows(left, right):
    return lax.dot_general(left, right, (((0,), (0,)), ((), ())), preferred_element_type=F32)


def contract_cols(left, right):
    return lax.dot_general(left, right, (((1,), (1,)), ((), ())), preferred_element_type=F32)


def lane_ids(shape):
    return lax.broadcasted_iota(jnp.int32, shape, len(shape) - 1)


def three_parts(value):
    high = value.astype(BF16).astype(F32)
    rest = value - high
    middle = rest.astype(BF16).astype(F32)
    return high, middle, rest - middle


def extend_keys(keys_out, values_out, blocks, bias_ref, head):
    aux = HEAD_DIM * (1 - head)
    row = 0
    for key_ref, value_ref in blocks:
        rows = key_ref.shape[0]
        span = slice(row, row + rows)
        lanes = lane_ids((rows, PAIR))
        inside = (lanes // HEAD_DIM) == head
        ones = jnp.where((lanes > aux) & (lanes <= aux + 3), 1.0, 0.0)
        extra = jnp.where(lanes == aux, bias_ref[span, :], ones)
        keys_out[span, :] = jnp.where(inside, key_ref[...].astype(F32), extra).astype(BF16)
        ones = jnp.where((lanes >= aux) & (lanes < aux + 3), 1.0, 0.0)
        values_out[span, :] = jnp.where(inside, value_ref[...].astype(F32), ones).astype(BF16)
        row += rows


def attention_forward_body(
    chunk, query_ref, key_own, value_own, key_far, value_far, bias_ref,
    out_ref, extended_ref, keys, values,
):
    rows = query_ref.shape[0]
    for head in (0, 1):
        extend_keys(
            keys.at[head], values.at[head], ((key_own, value_own), (key_far, value_far)), bias_ref, head
        )
    lanes = lane_ids((chunk, PAIR))
    for start in range(0, rows, chunk):
        span = slice(start, start + chunk)
        outs = []
        for head in (0, 1):
            aux = HEAD_DIM * (1 - head)
            inside = (lanes // HEAD_DIM) == head
            query = query_ref[span, :].astype(F32)
            extended = jnp.where(inside, query, jnp.where(lanes == aux, 1.0, 0.0))
            scores = contract_cols(extended.astype(BF16), keys[head])
            top = jnp.max(scores, axis=1, keepdims=True)
            powered = jnp.exp(scores - top).astype(BF16)
            summed = mm(powered, values[head])
            total = summed[:, aux : aux + 1]
            outs.append(summed / total)
            high, middle, low = three_parts(-(top + jnp.log(total)))
            extended = jnp.where(lanes == aux + 1, high, extended)
            extended = jnp.where(lanes == aux + 2, middle, extended)
            extended = jnp.where(lanes == aux + 3, low, extended)
            extended_ref[head, span, :] = extended.astype(BF16)
        out_ref[span, :] = jnp.where(lanes < HEAD_DIM, outs[0], outs[1])


def attention_forward(qkv, kv_far, key_bias):
    rows, width = qkv.shape[0], qkv.shape[1] // 3
    pairs = width // PAIR

    def block(base):
        return pl.BlockSpec((rows, PAIR), lambda p: (0, base + p))

    return pl.pallas_call(
        functools.partial(attention_forward_body, rows // 2),
        grid=(pairs,),
        in_specs=[
            block(0), block(pairs), block(2 * pairs), block(0), block(pairs),
            pl.BlockSpec((2 * rows, 1), lambda p: (0, 0)),
        ],
        out_specs=[block(0), pl.BlockSpec((2, rows, PAIR), lambda p: (p, 0, 0))],
        out_shape=[
            jax.ShapeDtypeStruct((rows, width), F32),
            jax.ShapeDtypeStruct((2 * pairs, rows, PAIR), BF16),
        ],
        scratch_shapes=[pltpu.VMEM((2, 2 * rows, PAIR), BF16)] * 2,
        compiler_params=pltpu.CompilerParams(vmem_limit_bytes=KERNEL_VMEM),
        cost_estimate=pl.CostEstimate(
            flops=16 * rows * rows * 2 * width * 2, bytes_accessed=12 * rows * width,
            transcendentals=2 * rows * rows * 2 * pairs,
        ),
        name="attention_forward",
    )(qkv, qkv, qkv, kv_far, kv_far, key_bias)


def attention_backward_body(
    chunks, extended_ref, key_own, value_own, key_far, value_far, bias_ref, grad_ref, out_ref,
    grad_query, grad_key_own, grad_value_own, grad_key_far, grad_value_far,
    keys, values, key_sums, value_sums,
):
    rows = extended_ref.shape[1]
    for head in (0, 1):
        extend_keys(
            keys.at[head], values.at[head], ((key_own, value_own), (key_far, value_far)), bias_ref, head
        )
    for start, size in chunks:
        span = slice(start, start + size)
        lanes = lane_ids((size, PAIR))
        parts = []
        for head in (0, 1):
            aux = HEAD_DIM * (1 - head)
            inside = (lanes // HEAD_DIM) == head
            query = extended_ref[head, span, :]
            grad = jnp.where(inside, grad_ref[span, :].astype(F32), 0.0)
            dots = jnp.sum(grad * out_ref[span, :], axis=1, keepdims=True)
            high, middle, low = three_parts(-dots)
            grad = jnp.where(lanes == aux, high, grad)
            grad = jnp.where(lanes == aux + 1, middle, grad)
            grad = jnp.where(lanes == aux + 2, low, grad)
            probs = jnp.exp(contract_cols(query, keys[head]))
            shifted = contract_cols(grad.astype(BF16), values[head])
            grad_scores = (probs * shifted).astype(BF16)
            parts.append(mm(grad_scores, keys[head]) * HEAD_DIM**-0.5)
            to_values = mm(grad.T.astype(BF16), probs.astype(BF16)).T
            to_keys = mm(query.astype(F32).T.astype(BF16), grad_scores).T
            if start == 0:
                key_sums[head] = to_keys
                value_sums[head] = to_values
            else:
                key_sums[head] += to_keys
                value_sums[head] += to_values
        grad_query[span, :] = jnp.where(lanes < HEAD_DIM, parts[0], parts[1]).astype(BF16)
    lanes = lane_ids((rows, PAIR))
    for part, (to_key, to_value) in enumerate(
        ((grad_key_own, grad_value_own), (grad_key_far, grad_value_far))
    ):
        span = slice(part * rows, (part + 1) * rows)
        first = lanes < HEAD_DIM
        to_key[...] = jnp.where(first, key_sums[0, span, :], key_sums[1, span, :]).astype(BF16)
        to_value[...] = jnp.where(first, value_sums[0, span, :], value_sums[1, span, :]).astype(BF16)


def attention_backward(extended, qkv, kv_far, key_bias, grad, out):
    rows, width = out.shape
    pairs = width // PAIR

    def block(base):
        return pl.BlockSpec((rows, PAIR), lambda p: (0, base + p))

    shape = jax.ShapeDtypeStruct((rows, width), BF16)
    return pl.pallas_call(
        functools.partial(attention_backward_body, ((0, rows),)),
        grid=(pairs,),
        in_specs=[
            pl.BlockSpec((2, rows, PAIR), lambda p: (p, 0, 0)),
            block(pairs), block(2 * pairs), block(0), block(pairs),
            pl.BlockSpec((2 * rows, 1), lambda p: (0, 0)),
            block(0), block(0),
        ],
        out_specs=[block(0)] * 5,
        out_shape=[shape] * 5,
        scratch_shapes=[pltpu.VMEM((2, 2 * rows, PAIR), BF16)] * 2
        + [pltpu.VMEM((2, 2 * rows, PAIR), F32)] * 2,
        compiler_params=pltpu.CompilerParams(vmem_limit_bytes=KERNEL_VMEM),
        cost_estimate=pl.CostEstimate(
            flops=40 * rows * rows * 2 * width * 2, bytes_accessed=24 * rows * width,
            transcendentals=2 * rows * rows * 2 * pairs,
        ),
        name="attention_backward",
    )(extended, qkv, qkv, kv_far, kv_far, key_bias, grad, out)


def norm_parts(hidden):
    average = jnp.mean(hidden, axis=-1, keepdims=True)
    centred = hidden - average
    inverse = lax.rsqrt(jnp.mean(centred * centred, axis=-1, keepdims=True) + EPS)
    return centred * inverse, inverse


def norm_backward(hidden, grad_normed, gain):
    unit, inverse = norm_parts(hidden)
    scaled = grad_normed * gain
    first = jnp.mean(scaled, axis=-1, keepdims=True)
    second = jnp.mean(scaled * unit, axis=-1, keepdims=True)
    grad_hidden = inverse * (scaled - first - unit * second)
    return grad_hidden, jnp.sum(grad_normed * unit, axis=0), jnp.sum(grad_normed, axis=0)


def gelu_and_slope(pre):
    size = jnp.abs(pre) * (0.5**0.5)
    density = jnp.exp(-0.5 * pre * pre)
    t = 1.0 / (1.0 + 0.3275911 * size)
    series = t * (0.254829592 + t * (-0.284496736 + t * (1.421413741 + t * (-1.453152027 + t * 1.061405429))))
    tail = 0.5 * series * density
    below = jnp.where(pre < 0, tail, 1.0 - tail)
    return pre * below, below + pre * density * (1.0 / math.sqrt(2.0 * math.pi))


def swap(block, bit):
    count = lax.axis_size("dp")
    return lax.ppermute(block, "dp", [(i, i ^ bit) for i in range(count)])


def add(a, b):
    return (a.astype(F32) + b.astype(F32)).astype(BF16)


class Spot:
    def __init__(self):
        self.z, self.sections = lax.axis_index("section"), lax.axis_size("section")
        self.d, self.count = lax.axis_index("dp"), lax.axis_size("dp")
        self.x_bit, self.y_bit = 2, 2 * math.isqrt(self.count // 2)
        self.core = self.d % 2
        self.xb, self.yb = (self.d // self.x_bit) % 2, (self.d // self.y_bit) % 2
        self.c, self.c_x = self.yb * 2 + self.xb, self.yb * 2 + 1 - self.xb
        self.c_y, self.c_d = (1 - self.yb) * 2 + self.xb, (1 - self.yb) * 2 + 1 - self.xb
        self.mate, self.x, self.y = (self.flipped(b) for b in (1, self.x_bit, self.y_bit))
        self.above, self.below = {"section": self.z + 1}, {"section": self.z - 1}
        self.spare_bits = [
            1 << i for i in range(self.count.bit_length() - 1) if 1 << i not in (1, self.x_bit, self.y_bit)
        ]

    def flipped(self, bit):
        return {"dp": self.d + bit * (1 - 2 * ((self.d // bit) % 2))}

    def greet(self):
        barrier = pltpu.get_barrier_semaphore()
        devices = [self.x, self.y]
        for step in range(self.sections):
            for core in (0, 1):
                if step or core:
                    devices.append({
                        "section": (self.z + step) % self.sections,
                        "dp": self.d - self.core + (self.core + core) % 2,
                    })
        for device in devices:
            pl.semaphore_signal(barrier, inc=1, device_id=device, device_id_type=pl.DeviceIdType.MESH)
        pl.semaphore_wait(barrier, len(devices))


def remote(src, dst, send, recv, device):
    return pltpu.make_async_remote_copy(
        src_ref=src, dst_ref=dst, send_sem=send, recv_sem=recv,
        device_id=device, device_id_type=pl.DeviceIdType.MESH,
    )


class PlaneGather:
    SENDS, RECEIVES = 9, 9

    def __init__(self, spot, dst, send, recv):
        self.spot, self.dst, self.send, self.recv = spot, dst, send, recv

    def blocks(self, core, chip, half=None):
        at = core * 8 + chip * 2
        return pl.ds(at, 2) if half is None else pl.ds(at + half, 1)

    def copies(self, own=None):
        s, k = self.spot, self.spot.core
        plan = {
            "x": (self.blocks(k, s.c), s.x), "y": (self.blocks(k, s.c), s.y),
            "m": (self.blocks(k, s.c), s.mate),
            "xy": (self.blocks(k, s.c_x, 0), s.y), "yx": (self.blocks(k, s.c_y, 1), s.x),
            "mx": (self.blocks(k, s.c_x), s.mate), "my": (self.blocks(k, s.c_y), s.mate),
            "md0": (self.blocks(k, s.c_d, 0), s.mate), "md1": (self.blocks(k, s.c_d, 1), s.mate),
        }
        out = {}
        for index, (name, (rows, device)) in enumerate(plan.items()):
            src = own if own is not None and name in ("x", "y", "m") else self.dst.at[rows]
            out[name] = remote(src, self.dst.at[rows], self.send.at[index], self.recv.at[index], device)
        return out

    def arrivals(self):
        s, k = self.spot, self.spot.core
        plan = {
            "x": self.blocks(k, s.c_x), "y": self.blocks(k, s.c_y), "m": self.blocks(1 - k, s.c),
            "xy": self.blocks(k, s.c_d, 0), "yx": self.blocks(k, s.c_d, 1),
            "mx": self.blocks(1 - k, s.c_x), "my": self.blocks(1 - k, s.c_y),
            "md0": self.blocks(1 - k, s.c_d, 0), "md1": self.blocks(1 - k, s.c_d, 1),
        }
        return {
            name: remote(self.dst.at[rows], self.dst.at[rows], self.send.at[i], self.recv.at[i], s.mate)
            for i, (name, rows) in enumerate(plan.items())
        }

    def begin(self, own):
        copies = self.copies(own)
        for name in ("x", "y", "m"):
            copies[name].start()

    def second(self):
        copies, arrivals = self.copies(), self.arrivals()
        arrivals["x"].wait_recv()
        copies["xy"].start()
        copies["mx"].start()
        arrivals["y"].wait_recv()
        copies["yx"].start()
        copies["my"].start()

    def third(self):
        copies, arrivals = self.copies(), self.arrivals()
        for name, after in (("xy", "md0"), ("yx", "md1")):
            arrivals[name].wait_recv()
            copies[after].start()

    def finish(self):
        copies, arrivals = self.copies(), self.arrivals()
        for name in copies:
            copies[name].wait_send()
        for name in ("m", "mx", "my", "md0", "md1"):
            arrivals[name].wait_recv()


class WeightGather(PlaneGather):
    def __init__(self, spot, src, dst, source, send, recv):
        super().__init__(spot, dst, send, recv)
        self.src, self.source = src, source
        self.own = self.blocks(spot.core, spot.c)

    def along(self, src):
        s = self.spot
        return (
            remote(src.at[self.own], self.dst.at[self.own], self.send.at[9], self.recv.at[9], s.above),
            remote(src.at[self.own], self.dst.at[self.own], self.send.at[10], self.recv.at[9], s.below),
            pltpu.make_async_copy(src.at[self.own], self.dst.at[self.own], self.send.at[11]),
        )

    def open(self):
        z, source = self.spot.z, self.source
        up, down, stay = self.along(self.src)
        @pl.when(z == source)
        def _():
            if source + 1 < self.spot.sections:
                up.start()
            if source:
                down.start()
            stay.start()
            self.begin(self.src.at[self.own])

    def first(self):
        z, source, last = self.spot.z, self.source, self.spot.sections - 1
        up, down, _ = self.along(self.dst)
        @pl.when(z != source)
        def _():
            up.wait_recv()
            if source < last - 1:
                pl.when((z > source) & (z < last))(up.start)
            if source > 1:
                pl.when((z < source) & (z > 0))(down.start)
            self.begin(self.dst.at[self.own])

    def finish(self):
        z, source, last = self.spot.z, self.source, self.spot.sections - 1
        up, down, stay = self.along(self.src)
        if source < last:
            pl.when((z >= source) & (z < last))(up.wait_send)
        if source:
            pl.when((z <= source) & (z > 0))(down.wait_send)
        pl.when(z == source)(stay.wait)
        super().finish()


def gather_weights_body(front, back, norms, *refs):
    fronts, downs, norm_all = refs[:4], refs[4:6], refs[6]
    send, recv, norm_send, norm_recv = refs[7:]
    spot = Spot()
    spot.greet()
    norm_copies = [
        remote(
            norms, norm_all.at[spot.z], norm_send.at[step], norm_recv.at[step],
            {"section": (spot.z + step) % spot.sections},
        )
        for step in range(1, spot.sections)
    ]
    kept = pltpu.make_async_copy(norms, norm_all.at[spot.z], norm_send.at[0])
    for copy in norm_copies + [kept]:
        copy.start()
    jobs = []
    for layer in range(2):
        low, high = downs[layer].at[pl.ds(0, 16)], downs[layer].at[pl.ds(16, 16)]
        jobs += [(front, fronts[2 * layer], 2 * layer), (front, fronts[2 * layer + 1], 2 * layer + 1)]
        jobs += [(back, low, 2 * layer), (back, high, 2 * layer + 1)]
    gathers = [WeightGather(spot, a, b, s, send.at[i], recv.at[i]) for i, (a, b, s) in enumerate(jobs)]
    for gather in gathers:
        gather.open()
    for i in range(len(gathers) + 2):
        if i < len(gathers):
            gathers[i].first()
        if 0 <= i - 1 < len(gathers):
            gathers[i - 1].second()
        if i >= 2:
            gathers[i - 2].third()
    for gather in gathers:
        gather.finish()
    kept.wait()
    for step, copy in enumerate(norm_copies, 1):
        copy.wait_send()
        block = norm_all.at[(spot.z + spot.sections - step) % spot.sections]
        remote(block, block, norm_send.at[step], norm_recv.at[step], spot.mate).wait_recv()


def gather_weights(front, back, norms):
    sections = lax.axis_size("section")
    blocks = lambda a, n: (n, a.shape[0] // 16, a.shape[1])
    front_b, back_b = front.reshape(blocks(front, 16)), back.reshape(blocks(back, 16))
    full = jax.ShapeDtypeStruct(front_b.shape, BF16)
    down = jax.ShapeDtypeStruct((32,) + back_b.shape[1:], BF16)
    hbm = pl.BlockSpec(memory_space=pl.ANY)
    out = pl.pallas_call(
        gather_weights_body,
        in_specs=[hbm] * 3, out_specs=[hbm] * 7,
        out_shape=[full] * 4 + [down] * 2 + [jax.ShapeDtypeStruct((sections,) + norms.shape, F32)],
        scratch_shapes=[
            pltpu.SemaphoreType.DMA((8, 12)), pltpu.SemaphoreType.DMA((8, 10)),
            pltpu.SemaphoreType.DMA((sections,)), pltpu.SemaphoreType.DMA((sections,)),
        ],
        compiler_params=pltpu.CompilerParams(collective_id=0, has_side_effects=True),
        name="gather_weights",
    )(front_b, back_b, norms)
    fronts = [a.reshape(front.shape) for a in out[:4]]
    downs = [a.reshape(2 * back.shape[0], back.shape[1]) for a in out[4:6]]
    return fronts, downs, out[6]


class Deliver:
    def __init__(self, spot, src, dst, target, send, recv, core_rows):
        self.spot, self.src, self.dst, self.target, self.send, self.recv = spot, src, dst, target, send, recv
        self.rows = core_rows
        self.owner, self.slot = spot.z // 2, spot.z % 2
        self.home = (spot.z == target) & (spot.core == self.owner)

    def place(self, slot, core):
        return self.dst.at[slot, pl.ds(pl.multiple_of(core * self.rows, 16), self.rows)]

    def copies(self):
        s, spot = self, self.spot
        spot_at = s.place(s.slot, spot.core)
        away = remote(
            s.src, spot_at, s.send.at[0], s.recv.at[s.slot * 2 + spot.core],
            {"section": s.target, "dp": spot.d - spot.core + s.owner},
        )
        return away, pltpu.make_async_copy(s.src, spot_at, s.send.at[1])

    def start(self):
        away, stay = self.copies()
        pl.when(self.home)(stay.start)
        pl.when(jnp.logical_not(self.home))(away.start)

    def finish(self):
        away, stay = self.copies()
        pl.when(self.home)(stay.wait)
        pl.when(jnp.logical_not(self.home))(away.wait_send)
        spot = self.spot
        for slot in (0, 1):
            for core in (0, 1):
                here = (spot.core * 2 + slot == spot.z) & (spot.core == core)
                block = self.place(slot, core)
                landing = remote(block, block, self.send.at[0], self.recv.at[slot * 2 + core], spot.mate)
                pl.when((spot.z == self.target) & jnp.logical_not(here))(landing.wait_recv)


def add_into(target, *others):
    blocks, rows, _ = target.shape
    def step(i, carry):
        b, r = i // (rows // 16), pl.ds(pl.multiple_of((i % (rows // 16)) * 16, 16), 16)
        total = target[b, r, :].astype(F32)
        for other in others:
            total = total + other[b, r, :].astype(F32)
        target[b, r, :] = total.astype(BF16)
        return carry
    lax.fori_loop(0, blocks * (rows // 16), step, 0)


class ScatterSum:
    SEMS = 9

    def __init__(self, spot, src, target, bufs, send, recv):
        self.spot, self.src, self.target, self.send, self.recv = spot, src, target, send, recv
        self.half, self.from_mate, self.in_x, self.in_y, self.in_yx, self.in_xy, self.from_z = bufs

    @staticmethod
    def scratch(block_rows, columns):
        return [
            pltpu.VMEM((n, block_rows, columns), BF16) for n in (8, 8, 2, 2, 1, 1, 4)
        ]

    def mate_copies(self):
        s, spot = self, self.spot
        return (
            pltpu.make_async_copy(s.src.at[pl.ds(spot.core * 8, 8)], s.half, s.send.at[0]),
            remote(s.src.at[pl.ds((1 - spot.core) * 8, 8)], s.from_mate, s.send.at[1], s.recv.at[1], spot.mate),
        )

    def start(self):
        for copy in self.mate_copies():
            copy.start()

    def block(self, chip, half):
        return self.half.at[pl.ds(chip * 2 + half, 1)]

    def first_copies(self):
        s, spot = self, self.spot
        first, second = pl.ds(0, 1), pl.ds(1, 1)
        return (
            remote(s.block(spot.c_x, 0), s.in_x.at[first], s.send.at[2], s.recv.at[2], spot.x),
            remote(s.block(spot.c_d, 0), s.in_x.at[second], s.send.at[3], s.recv.at[3], spot.x),
            remote(s.block(spot.c_y, 1), s.in_y.at[first], s.send.at[4], s.recv.at[4], spot.y),
            remote(s.block(spot.c_d, 1), s.in_y.at[second], s.send.at[5], s.recv.at[5], spot.y),
        )

    def second_copies(self):
        s, spot = self, self.spot
        return (
            remote(s.block(spot.c_y, 0), s.in_xy, s.send.at[6], s.recv.at[6], spot.y),
            remote(s.block(spot.c_x, 1), s.in_yx, s.send.at[7], s.recv.at[7], spot.x),
        )

    def first(self):
        for copy in self.mate_copies():
            copy.wait()
        add_into(self.half, self.from_mate)
        for copy in self.first_copies():
            copy.start()

    def second(self):
        s, spot = self, self.spot
        for copy in self.first_copies():
            copy.wait_recv()
        first, other = pl.ds(0, 1), pl.ds(1, 1)
        add_into(s.block(spot.c_y, 0), s.in_x.at[other])
        add_into(s.block(spot.c_x, 1), s.in_y.at[other])
        for copy in self.second_copies():
            copy.start()
        add_into(s.block(spot.c, 0), s.in_x.at[first])
        add_into(s.block(spot.c, 1), s.in_y.at[first])

    def third(self):
        s, spot = self, self.spot
        for copy in self.second_copies():
            copy.wait_recv()
        add_into(s.block(spot.c, 0), s.in_xy)
        add_into(s.block(spot.c, 1), s.in_yx)

    def own(self):
        return self.half.at[pl.ds(self.spot.c * 2, 2)]

    def along(self):
        s, spot = self, self.spot
        down = remote(s.own(), s.from_z.at[pl.ds(0, 2)], s.send.at[8], s.recv.at[8], spot.below)
        up = remote(s.own(), s.from_z.at[pl.ds(2, 2)], s.send.at[8], s.recv.at[0], spot.above)
        return up, down

    def pass_on(self, z):
        up, down = self.along()
        last = self.spot.sections - 1

        @pl.when(self.spot.z == z)
        def _():
            if z >= self.target and z < last:
                down.wait_recv()
                add_into(self.own(), self.from_z.at[pl.ds(0, 2)])
            if z <= self.target and z > 0:
                up.wait_recv()
                add_into(self.own(), self.from_z.at[pl.ds(2, 2)])
            if z > self.target:
                down.start()
            if z < self.target:
                up.start()

    def fourth(self):
        for z in range(self.spot.sections):
            self.pass_on(z)

    def finish(self):
        for copy in self.first_copies() + self.second_copies():
            copy.wait_send()
        up, down = self.along()
        pl.when(self.spot.z != self.target)(up.wait_send)


def collect_body(rows, n_small, *refs):
    sections = lax.axis_size("section")
    take = lambda n: tuple(refs_list.pop(0) for _ in range(n))
    refs_list = list(refs)
    acts, grads, fronts, backs, (small,) = take(sections), take(sections), take(sections), take(sections), take(1)
    acts_out, grads_out, front_out, back_out, small_out = take(5)
    zeros, sums, arriving = take(3)
    front_bufs = [take(7) for _ in range(sections)]
    back_bufs = [take(7) for _ in range(sections)]
    send, recv, dsend, drecv, asend, arecv, ssend, srecv, psem = take(9)
    spot = Spot()
    spot.greet()
    scatters = {}
    for s in range(sections):
        scatters["front", s] = ScatterSum(spot, fronts[s], s, front_bufs[s], send.at[s], recv.at[s])
        scatters["back", s] = ScatterSum(spot, backs[s], s, back_bufs[s], send.at[sections + s], recv.at[sections + s])
    order = []
    for s in reversed(range(sections)):
        order.append(scatters["front", s])
        if s % 2:
            order += [scatters["back", s - 1], scatters["back", s]]
    delivers = [Deliver(spot, a, acts_out, s, dsend.at[s], drecv.at[s], rows) for s, a in enumerate(acts)]
    delivers += [
        Deliver(spot, a, grads_out, s, dsend.at[sections + s], drecv.at[sections + s], rows)
        for s, a in enumerate(grads)
    ]
    for scatter in order:
        scatter.start()
    for deliver in delivers:
        deliver.start()
    zeros[...] = jnp.zeros_like(zeros)
    pad = acts_out.shape[1] - 2 * rows
    pads = [
        pltpu.make_async_copy(zeros, acts_out.at[slot, pl.ds(2 * rows, pad)], psem.at[slot]) for slot in (0, 1)
    ]
    for copy in pads:
        copy.start()
    sums[0] = small[...]
    partners = [spot.mate, spot.x, spot.y] + [
        {"section": spot.z + bit * (1 - 2 * ((spot.z // bit) % 2))}
        for bit in (1 << i for i in range((sections - 1).bit_length()))
    ]

    def small_step(i):
        copy = remote(sums.at[i], arriving.at[i], ssend.at[i], srecv.at[i], partners[i])
        copy.start()
        copy.wait()
        sums[i + 1] = sums[i] + arriving[i]

    count = len(order)
    for i in range(count + 3):
        if i < count:
            order[i].first()
        if 0 <= i - 1 < count:
            order[i - 1].second()
        if 0 <= i - 2 < count:
            order[i - 2].third()
        if 0 <= i - 3 < count:
            order[i - 3].fourth()
        if i < len(partners):
            small_step(i)
    small_out[...] = sums[len(partners)]
    gathers = [
        PlaneGather(spot, out, asend.at[i], arecv.at[i]) for i, out in enumerate((front_out, back_out))
    ]
    stays = []
    for i, (gather, kind) in enumerate(zip(gathers, ("front", "back"))):
        for s in range(sections):
            own = scatters[kind, s].own()
            stay = pltpu.make_async_copy(own, gather.dst.at[gather.blocks(spot.core, spot.c)], psem.at[2 + i])

            @pl.when(spot.z == s)
            def _(gather=gather, own=own, stay=stay):
                stay.start()
                gather.begin(own)
        stays.append(stay)
    for gather in gathers:
        gather.second()
    for gather in gathers:
        gather.third()
    for gather in gathers:
        gather.finish()
    for copy in stays + pads:
        copy.wait()
    for deliver in delivers:
        deliver.finish()
    for scatter in order:
        scatter.finish()


def collect(acts, grads, fronts, backs, small, padded):
    sections = lax.axis_size("section")
    rows, width = acts[0].shape
    blocked = lambda a: a.reshape(16, a.shape[0] // 16, a.shape[1])
    fronts, backs = [blocked(a) for a in fronts], [blocked(a) for a in backs]
    hbm, vmem = pl.BlockSpec(memory_space=pl.ANY), pl.BlockSpec(memory_space=pltpu.VMEM)
    steps = 3 + (sections - 1).bit_length()
    sems = pltpu.SemaphoreType.DMA
    out = pl.pallas_call(
        functools.partial(collect_body, rows, small.shape[0]),
        in_specs=[hbm] * (4 * sections) + [vmem],
        out_specs=[hbm] * 4 + [vmem],
        out_shape=[
            jax.ShapeDtypeStruct((2, padded, width), BF16), jax.ShapeDtypeStruct((2, 2 * rows, width), BF16),
            jax.ShapeDtypeStruct(fronts[0].shape, BF16), jax.ShapeDtypeStruct(backs[0].shape, BF16),
            jax.ShapeDtypeStruct(small.shape, F32),
        ],
        scratch_shapes=[
            pltpu.VMEM((padded - 2 * rows, width), BF16),
            pltpu.VMEM((steps + 1,) + small.shape, F32), pltpu.VMEM((steps,) + small.shape, F32),
        ]
        + ScatterSum.scratch(*fronts[0].shape[1:]) * sections
        + ScatterSum.scratch(*backs[0].shape[1:]) * sections
        + [
            sems((2 * sections, 9)), sems((2 * sections, 9)), sems((2 * sections, 2)), sems((2 * sections, 4)),
            sems((2, 9)), sems((2, 9)), sems((steps,)), sems((steps,)), sems((4,)),
        ],
        compiler_params=pltpu.CompilerParams(
            collective_id=1, has_side_effects=True, vmem_limit_bytes=62 * 2**20
        ),
        name="collect",
    )(*acts, *grads, *fronts, *backs, small)
    return out[0], out[1], out[2].reshape(-1, fronts[0].shape[2]), out[3].reshape(-1, backs[0].shape[2]), out[4]


def per_device(
    clip_inputs, out_grad, clip_class, w_front, w_back, norm_gain, norm_shift,
    bias_query_value, bias_attn_out, bias_up, bias_down,
):
    spot = Spot()
    sections = lax.axis_size("section")
    padded, width = clip_inputs.shape[1:]
    rows = -(-LONG // 32) * 16
    core, section = spot.core, spot.z

    owner, slot = section // 2, section % 2
    mine = jnp.stack([lax.dynamic_index_in_dim(a, slot, 0, False) for a in (clip_inputs, out_grad)])
    far = swap(lax.dynamic_slice_in_dim(mine, (1 - core) * rows, rows, 1), 1)
    near = lax.dynamic_slice_in_dim(mine, core * rows, rows, 1)
    clip_pair = jnp.where(core == owner, near, far)
    own_class = lax.dynamic_index_in_dim(clip_class, slot, 0, False).astype(F32)
    own_class = jnp.broadcast_to(own_class, (8, 128))
    clip_kind = jnp.where(core == owner, own_class, swap(own_class, 1))[0, 0]
    length = SHORT + (LONG - SHORT) * clip_kind
    positions = jnp.arange(rows, dtype=jnp.int32)
    own_rows = (positions + core * rows).astype(F32) < length
    far_rows = (positions + (1 - core) * rows).astype(F32) < length
    row_mask = own_rows.astype(F32)[:, None]
    key_bias = jnp.where(jnp.concatenate([own_rows, far_rows]), 0.0, MASKED)[:, None]

    norms = jnp.concatenate([norm_gain, norm_shift, jnp.zeros((6, width), F32)], axis=0)
    fronts, downs, norm_all = gather_weights(w_front[0], w_back[0], norms)
    gains, shifts = norm_all[:, 0], norm_all[:, 1]

    hidden = (clip_pair[0].astype(F32) * row_mask).astype(BF16)
    saved, delivered = [], []
    for s in range(sections):
        layer = s // 2
        entering = hidden.astype(F32)
        unit, _ = norm_parts(entering)
        normed = (unit * gains[s] + shifts[s]).astype(BF16)
        if s % 2 == 0:
            pair = bias_query_value[layer]
            bias = jnp.concatenate([pair[:width], jnp.zeros((width,), F32), pair[width:]])
            scale = jnp.where(jnp.arange(3 * width) < width, HEAD_DIM**-0.5, 1.0)
            qkv = ((mm(normed, fronts[s][:, : 3 * width]) + bias).astype(BF16) * scale).astype(BF16)
            kv_far = swap(qkv[:, width:], 1)
            attended, extended = attention_forward(qkv, kv_far, key_bias)
            attended_b = attended.astype(BF16)
            branch = contract_cols(attended_b, fronts[s][:, 3 * width :]) + bias_attn_out[layer]
            saved.append((hidden, normed, qkv, kv_far, attended, attended_b, extended))
        else:
            pre = mm(normed, fronts[s]) + bias_up[layer]
            act, slope = gelu_and_slope(pre)
            act, slope = act.astype(BF16), slope.astype(BF16)
            branch = mm(act, downs[layer]) + bias_down[layer]
            saved.append((hidden, normed, act, slope))
        hidden = (row_mask * (entering + branch)).astype(BF16)
        delivered.append(hidden)

    incoming = clip_pair[1]
    sent_grads = [None] * sections
    grad_fronts, grad_backs = [None] * sections, [None] * sections
    grad_gain, grad_shift = [None] * sections, [None] * sections
    grad_pairs, grad_outs, grad_ups, grad_downs = [], [], [], []
    for s in reversed(range(sections)):
        grad_rows = row_mask * incoming.astype(F32)
        grad_b = grad_rows.astype(BF16)
        front = fronts[s]
        if s % 2 == 0:
            entered, normed, qkv, kv_far, attended, attended_b, extended = saved[s]
            grad_attended = mm(grad_b, front[:, 3 * width :]).astype(BF16)
            to_query, to_key, to_value, key_far, value_far = attention_backward(
                extended, qkv, kv_far, key_bias, grad_attended, attended
            )
            back = swap(jnp.stack([key_far, value_far]), 1)
            grad_qkv = jnp.concatenate([to_query, add(to_key, back[0]), add(to_value, back[1])], axis=1)
            sums = jnp.sum(grad_qkv.astype(F32), axis=0)
            grad_pairs.insert(0, jnp.concatenate([sums[:width], sums[2 * width :]]))
            grad_outs.insert(0, jnp.sum(grad_rows, axis=0))
            grad_fronts[s] = jnp.concatenate(
                [contract_rows(normed, grad_qkv).astype(BF16), contract_rows(grad_b, attended_b).astype(BF16)],
                axis=1,
            )
            grad_normed = contract_cols(grad_qkv, front[:, : 3 * width])
        else:
            entered, normed, act, slope = saved[s]
            grad_act = contract_cols(grad_b, downs[s // 2])
            grad_pre = (grad_act * slope.astype(F32)).astype(BF16)
            grad_down = contract_rows(act, grad_b).astype(BF16)
            grad_fronts[s] = contract_rows(normed, grad_pre).astype(BF16)
            grad_ups.insert(0, jnp.sum(grad_pre.astype(F32), axis=0))
            grad_downs.insert(0, jnp.sum(grad_rows, axis=0))
            grad_normed = contract_cols(grad_pre, front)
            half = grad_down.shape[0] // 2
            grad_backs[s - 1], grad_backs[s] = grad_down[:half], grad_down[half:]
        grad_hidden, grad_gain[s], grad_shift[s] = norm_backward(entered.astype(F32), grad_normed, gains[s])
        incoming = (grad_rows + grad_hidden).astype(BF16)
        sent_grads[s] = incoming

    small = jnp.concatenate(
        [v.reshape(-1) for v in grad_gain + grad_shift + grad_pairs + grad_outs + grad_ups + grad_downs]
    )
    acts_out, grads_out, front_out, back_out, small = collect(
        delivered, sent_grads, grad_fronts, grad_backs, small.reshape(-1, 128), padded
    )
    small = small.reshape(-1)
    for bit in spot.spare_bits:
        small = small + swap(small, bit)
        front_out, back_out = add(front_out, swap(front_out, bit)), add(back_out, swap(back_out, bit))
    grads_out = jnp.pad(grads_out.astype(F32), ((0, 0), (0, padded - 2 * rows), (0, 0)))
    parts, place_at = [], 0
    layers, hidden_units = bias_up.shape
    for count, size in (
        (sections, width), (sections, width), (layers, 2 * width), (layers, width),
        (layers, hidden_units), (layers, width),
    ):
        parts.append(small[place_at : place_at + count * size].reshape(count, size))
        place_at += count * size
    return (
        acts_out[None],
        grads_out[None],
        front_out.astype(F32)[None],
        back_out.astype(F32)[None],
        lax.dynamic_slice_in_dim(parts[0], section, 1, 0),
        lax.dynamic_slice_in_dim(parts[1], section, 1, 0),
        *parts[2:],
    )


def solution(mesh):
    placed = (
        P("dp", None, None), P("dp", None, None), P("dp"),
        P("section", None, None), P("section", None, None), P("section", None), P("section", None),
        P(), P(), P(), P(),
    )
    return jax.shard_map(
        per_device,
        mesh=mesh,
        in_specs=placed,
        out_specs=(
            P("section", "dp", None, None), P("section", "dp", None, None),
            P("section", None, None), P("section", None, None), P("section", None), P("section", None),
            P(), P(), P(), P(),
        ),
        check_vma=False,
    )
```

```python
import functools
import math

import jax
import jax.numpy as jnp
from jax import lax
from jax.experimental import pallas as pl
from jax.experimental.pallas import tpu as pltpu
from jax.sharding import PartitionSpec as P

HEADS = 12
LONG = 1214
SHORT = 514
EPS = 1e-06
HEAD_DIM = 64
PAIR = 2 * HEAD_DIM
MASKED = -1e30
F32 = jnp.float32
BF16 = jnp.bfloat16
KERNEL_VMEM = 56 * 2**20


def mm(left, right):
    return jnp.dot(left, right, preferred_element_type=F32)


def contract_rows(left, right):
    return lax.dot_general(left, right, (((0,), (0,)), ((), ())), preferred_element_type=F32)


def contract_cols(left, right):
    return lax.dot_general(left, right, (((1,), (1,)), ((), ())), preferred_element_type=F32)


def swap(block, bit):
    count = lax.axis_size("dp")
    return lax.ppermute(block, "dp", [(i, i ^ bit) for i in range(count)])


def add(a, b):
    return (a.astype(F32) + b.astype(F32)).astype(BF16)


class Spot:
    def __init__(self):
        self.z, self.sections = lax.axis_index("section"), lax.axis_size("section")
        self.d, self.count = lax.axis_index("dp"), lax.axis_size("dp")
        self.x_bit, self.y_bit = 2, 2 * math.isqrt(self.count // 2)
        self.core = self.d % 2
        self.xb, self.yb = (self.d // self.x_bit) % 2, (self.d // self.y_bit) % 2
        self.c, self.c_x = self.yb * 2 + self.xb, self.yb * 2 + 1 - self.xb
        self.c_y, self.c_d = (1 - self.yb) * 2 + self.xb, (1 - self.yb) * 2 + 1 - self.xb
        self.mate, self.x, self.y = (self.flipped(b) for b in (1, self.x_bit, self.y_bit))
        self.above, self.below = {"section": self.z + 1}, {"section": self.z - 1}
        self.spare_bits = [
            1 << i for i in range(self.count.bit_length() - 1) if 1 << i not in (1, self.x_bit, self.y_bit)
        ]

    def flipped(self, bit):
        return {"dp": self.d + bit * (1 - 2 * ((self.d // bit) % 2))}

    def greet_mate(self):
        barrier = pltpu.get_barrier_semaphore()
        pl.semaphore_signal(barrier, inc=1, device_id=self.mate, device_id_type=pl.DeviceIdType.MESH)
        pl.semaphore_wait(barrier, 1)

    def greet(self):
        barrier = pltpu.get_barrier_semaphore()
        devices = [self.x, self.y]
        for step in range(self.sections):
            for core in (0, 1):
                if step or core:
                    devices.append({
                        "section": (self.z + step) % self.sections,
                        "dp": self.d - self.core + (self.core + core) % 2,
                    })
        for device in devices:
            pl.semaphore_signal(barrier, inc=1, device_id=device, device_id_type=pl.DeviceIdType.MESH)
        pl.semaphore_wait(barrier, len(devices))


def remote(src, dst, send, recv, device):
    return pltpu.make_async_remote_copy(
        src_ref=src, dst_ref=dst, send_sem=send, recv_sem=recv,
        device_id=device, device_id_type=pl.DeviceIdType.MESH,
    )


class PlaneGather:
    SENDS, RECEIVES = 9, 9

    def __init__(self, spot, dst, send, recv):
        self.spot, self.dst, self.send, self.recv = spot, dst, send, recv

    def blocks(self, core, chip, half=None):
        at = core * 8 + chip * 2
        return pl.ds(at, 2) if half is None else pl.ds(at + half, 1)

    def copies(self, own=None):
        s, k = self.spot, self.spot.core
        plan = {
            "x": (self.blocks(k, s.c), s.x), "y": (self.blocks(k, s.c), s.y),
            "m": (self.blocks(k, s.c), s.mate),
            "xy": (self.blocks(k, s.c_x, 0), s.y), "yx": (self.blocks(k, s.c_y, 1), s.x),
            "mx": (self.blocks(k, s.c_x), s.mate), "my": (self.blocks(k, s.c_y), s.mate),
            "md0": (self.blocks(k, s.c_d, 0), s.mate), "md1": (self.blocks(k, s.c_d, 1), s.mate),
        }
        out = {}
        for index, (name, (rows, device)) in enumerate(plan.items()):
            src = own if own is not None and name in ("x", "y", "m") else self.dst.at[rows]
            out[name] = remote(src, self.dst.at[rows], self.send.at[index], self.recv.at[index], device)
        return out

    def arrivals(self):
        s, k = self.spot, self.spot.core
        plan = {
            "x": self.blocks(k, s.c_x), "y": self.blocks(k, s.c_y), "m": self.blocks(1 - k, s.c),
            "xy": self.blocks(k, s.c_d, 0), "yx": self.blocks(k, s.c_d, 1),
            "mx": self.blocks(1 - k, s.c_x), "my": self.blocks(1 - k, s.c_y),
            "md0": self.blocks(1 - k, s.c_d, 0), "md1": self.blocks(1 - k, s.c_d, 1),
        }
        return {
            name: remote(self.dst.at[rows], self.dst.at[rows], self.send.at[i], self.recv.at[i], s.mate)
            for i, (name, rows) in enumerate(plan.items())
        }

    def begin(self, own):
        copies = self.copies(own)
        for name in ("x", "y", "m"):
            copies[name].start()

    def second(self):
        copies, arrivals = self.copies(), self.arrivals()
        arrivals["x"].wait_recv()
        copies["xy"].start()
        copies["mx"].start()
        arrivals["y"].wait_recv()
        copies["yx"].start()
        copies["my"].start()

    def third(self):
        copies, arrivals = self.copies(), self.arrivals()
        for name, after in (("xy", "md0"), ("yx", "md1")):
            arrivals[name].wait_recv()
            copies[after].start()

    def finish(self):
        copies, arrivals = self.copies(), self.arrivals()
        for name in copies:
            copies[name].wait_send()
        for name in ("m", "mx", "my", "md0", "md1"):
            arrivals[name].wait_recv()


class WeightGather(PlaneGather):
    def __init__(self, spot, src, dst, source, send, recv):
        super().__init__(spot, dst, send, recv)
        self.src, self.source = src, source
        self.own = self.blocks(spot.core, spot.c)

    def along(self, src):
        s = self.spot
        return (
            remote(src.at[self.own], self.dst.at[self.own], self.send.at[9], self.recv.at[9], s.above),
            remote(src.at[self.own], self.dst.at[self.own], self.send.at[10], self.recv.at[9], s.below),
            pltpu.make_async_copy(src.at[self.own], self.dst.at[self.own], self.send.at[11]),
        )

    def open(self):
        z, source = self.spot.z, self.source
        up, down, stay = self.along(self.src)
        @pl.when(z == source)
        def _():
            if source + 1 < self.spot.sections:
                up.start()
            if source:
                down.start()
            stay.start()
            self.begin(self.src.at[self.own])

    def first(self):
        z, source, last = self.spot.z, self.source, self.spot.sections - 1
        up, down, _ = self.along(self.dst)
        @pl.when(z != source)
        def _():
            up.wait_recv()
            if source < last - 1:
                pl.when((z > source) & (z < last))(up.start)
            if source > 1:
                pl.when((z < source) & (z > 0))(down.start)
            self.begin(self.dst.at[self.own])

    def finish(self):
        z, source, last = self.spot.z, self.source, self.spot.sections - 1
        up, down, stay = self.along(self.src)
        if source < last:
            pl.when((z >= source) & (z < last))(up.wait_send)
        if source:
            pl.when((z <= source) & (z > 0))(down.wait_send)
        pl.when(z == source)(stay.wait)
        super().finish()


def gather_weights_body(front, back, norms, *refs):
    fronts, downs, norm_all = refs[:4], refs[4:6], refs[6]
    send, recv, norm_send, norm_recv = refs[7:]
    spot = Spot()
    spot.greet()
    norm_copies = [
        remote(
            norms, norm_all.at[spot.z], norm_send.at[step], norm_recv.at[step],
            {"section": (spot.z + step) % spot.sections},
        )
        for step in range(1, spot.sections)
    ]
    kept = pltpu.make_async_copy(norms, norm_all.at[spot.z], norm_send.at[0])
    for copy in norm_copies + [kept]:
        copy.start()
    jobs = []
    for layer in range(2):
        low, high = downs[layer].at[pl.ds(0, 16)], downs[layer].at[pl.ds(16, 16)]
        jobs += [(front, fronts[2 * layer], 2 * layer), (front, fronts[2 * layer + 1], 2 * layer + 1)]
        jobs += [(back, low, 2 * layer), (back, high, 2 * layer + 1)]
    gathers = [WeightGather(spot, a, b, s, send.at[i], recv.at[i]) for i, (a, b, s) in enumerate(jobs)]
    for gather in gathers:
        gather.open()
    for i in range(len(gathers) + 2):
        if i < len(gathers):
            gathers[i].first()
        if 0 <= i - 1 < len(gathers):
            gathers[i - 1].second()
        if i >= 2:
            gathers[i - 2].third()
    for gather in gathers:
        gather.finish()
    kept.wait()
    for step, copy in enumerate(norm_copies, 1):
        copy.wait_send()
        block = norm_all.at[(spot.z + spot.sections - step) % spot.sections]
        remote(block, block, norm_send.at[step], norm_recv.at[step], spot.mate).wait_recv()


def gather_weights(front, back, norms):
    sections = lax.axis_size("section")
    blocks = lambda a, n: (n, a.shape[0] // 16, a.shape[1])
    front_b, back_b = front.reshape(blocks(front, 16)), back.reshape(blocks(back, 16))
    full = jax.ShapeDtypeStruct(front_b.shape, BF16)
    down = jax.ShapeDtypeStruct((32,) + back_b.shape[1:], BF16)
    hbm = pl.BlockSpec(memory_space=pl.ANY)
    out = pl.pallas_call(
        gather_weights_body,
        in_specs=[hbm] * 3, out_specs=[hbm] * 7,
        out_shape=[full] * 4 + [down] * 2 + [jax.ShapeDtypeStruct((sections,) + norms.shape, F32)],
        scratch_shapes=[
            pltpu.SemaphoreType.DMA((8, 12)), pltpu.SemaphoreType.DMA((8, 10)),
            pltpu.SemaphoreType.DMA((sections,)), pltpu.SemaphoreType.DMA((sections,)),
        ],
        compiler_params=pltpu.CompilerParams(collective_id=0, has_side_effects=True),
        name="gather_weights",
    )(front_b, back_b, norms)
    fronts = [a.reshape(front.shape) for a in out[:4]]
    downs = [a.reshape(2 * back.shape[0], back.shape[1]) for a in out[4:6]]
    return fronts, downs, out[6]


class Deliver:
    def __init__(self, spot, src, dst, target, send, recv, core_rows):
        self.spot, self.src, self.dst, self.target, self.send, self.recv = spot, src, dst, target, send, recv
        self.rows = core_rows
        self.owner, self.slot = spot.z // 2, spot.z % 2
        self.home = (spot.z == target) & (spot.core == self.owner)

    def place(self, slot, core):
        return self.dst.at[slot, pl.ds(pl.multiple_of(core * self.rows, 16), self.rows)]

    def copies(self):
        s, spot = self, self.spot
        spot_at = s.place(s.slot, spot.core)
        away = remote(
            s.src, spot_at, s.send.at[0], s.recv.at[s.slot * 2 + spot.core],
            {"section": s.target, "dp": spot.d - spot.core + s.owner},
        )
        return away, pltpu.make_async_copy(s.src, spot_at, s.send.at[1])

    def start(self):
        away, stay = self.copies()
        pl.when(self.home)(stay.start)
        pl.when(jnp.logical_not(self.home))(away.start)

    def finish(self):
        away, stay = self.copies()
        pl.when(self.home)(stay.wait)
        pl.when(jnp.logical_not(self.home))(away.wait_send)
        spot = self.spot
        for slot in (0, 1):
            for core in (0, 1):
                here = (spot.core * 2 + slot == spot.z) & (spot.core == core)
                block = self.place(slot, core)
                landing = remote(block, block, self.send.at[0], self.recv.at[slot * 2 + core], spot.mate)
                pl.when((spot.z == self.target) & jnp.logical_not(here))(landing.wait_recv)


def add_into(target, *others):
    blocks, rows, _ = target.shape
    def step(i, carry):
        b, r = i // (rows // 16), pl.ds(pl.multiple_of((i % (rows // 16)) * 16, 16), 16)
        total = target[b, r, :].astype(F32)
        for other in others:
            total = total + other[b, r, :].astype(F32)
        target[b, r, :] = total.astype(BF16)
        return carry
    lax.fori_loop(0, blocks * (rows // 16), step, 0)


class ScatterSum:
    SEMS = 9

    def __init__(self, spot, src, target, bufs, send, recv):
        self.spot, self.src, self.target, self.send, self.recv = spot, src, target, send, recv
        self.half, self.from_mate, self.in_x, self.in_y, self.in_yx, self.in_xy, self.from_z = bufs

    @staticmethod
    def scratch(block_rows, columns):
        return [
            pltpu.VMEM((n, block_rows, columns), BF16) for n in (8, 8, 2, 2, 1, 1, 4)
        ]

    def mate_copies(self):
        s, spot = self, self.spot
        return (
            pltpu.make_async_copy(s.src.at[pl.ds(spot.core * 8, 8)], s.half, s.send.at[0]),
            remote(s.src.at[pl.ds((1 - spot.core) * 8, 8)], s.from_mate, s.send.at[1], s.recv.at[1], spot.mate),
        )

    def start(self):
        for copy in self.mate_copies():
            copy.start()

    def block(self, chip, half):
        return self.half.at[pl.ds(chip * 2 + half, 1)]

    def first_copies(self):
        s, spot = self, self.spot
        first, second = pl.ds(0, 1), pl.ds(1, 1)
        return (
            remote(s.block(spot.c_x, 0), s.in_x.at[first], s.send.at[2], s.recv.at[2], spot.x),
            remote(s.block(spot.c_d, 0), s.in_x.at[second], s.send.at[3], s.recv.at[3], spot.x),
            remote(s.block(spot.c_y, 1), s.in_y.at[first], s.send.at[4], s.recv.at[4], spot.y),
            remote(s.block(spot.c_d, 1), s.in_y.at[second], s.send.at[5], s.recv.at[5], spot.y),
        )

    def second_copies(self):
        s, spot = self, self.spot
        return (
            remote(s.block(spot.c_y, 0), s.in_xy, s.send.at[6], s.recv.at[6], spot.y),
            remote(s.block(spot.c_x, 1), s.in_yx, s.send.at[7], s.recv.at[7], spot.x),
        )

    def first(self):
        for copy in self.mate_copies():
            copy.wait()
        add_into(self.half, self.from_mate)
        for copy in self.first_copies():
            copy.start()

    def second(self):
        s, spot = self, self.spot
        for copy in self.first_copies():
            copy.wait_recv()
        first, other = pl.ds(0, 1), pl.ds(1, 1)
        add_into(s.block(spot.c_y, 0), s.in_x.at[other])
        add_into(s.block(spot.c_x, 1), s.in_y.at[other])
        for copy in self.second_copies():
            copy.start()
        add_into(s.block(spot.c, 0), s.in_x.at[first])
        add_into(s.block(spot.c, 1), s.in_y.at[first])

    def third(self):
        s, spot = self, self.spot
        for copy in self.second_copies():
            copy.wait_recv()
        add_into(s.block(spot.c, 0), s.in_xy)
        add_into(s.block(spot.c, 1), s.in_yx)

    def own(self):
        return self.half.at[pl.ds(self.spot.c * 2, 2)]

    def along(self):
        s, spot = self, self.spot
        down = remote(s.own(), s.from_z.at[pl.ds(0, 2)], s.send.at[8], s.recv.at[8], spot.below)
        up = remote(s.own(), s.from_z.at[pl.ds(2, 2)], s.send.at[8], s.recv.at[0], spot.above)
        return up, down

    def pass_on(self, z):
        up, down = self.along()
        last = self.spot.sections - 1

        @pl.when(self.spot.z == z)
        def _():
            if z >= self.target and z < last:
                down.wait_recv()
                add_into(self.own(), self.from_z.at[pl.ds(0, 2)])
            if z <= self.target and z > 0:
                up.wait_recv()
                add_into(self.own(), self.from_z.at[pl.ds(2, 2)])
            if z > self.target:
                down.start()
            if z < self.target:
                up.start()

    def fourth(self):
        for z in range(self.spot.sections):
            self.pass_on(z)

    def finish(self):
        for copy in self.first_copies() + self.second_copies():
            copy.wait_send()
        up, down = self.along()
        pl.when(self.spot.z != self.target)(up.wait_send)


def collect_body(rows, n_small, *refs):
    sections = lax.axis_size("section")
    take = lambda n: tuple(refs_list.pop(0) for _ in range(n))
    refs_list = list(refs)
    acts, grads, fronts, downs, (small,) = take(sections), take(sections), take(sections), take(sections // 2), take(1)
    backs = [downs[s // 2].at[pl.ds(16 * (s % 2), 16)] for s in range(sections)]
    acts_out, grads_out, front_out, back_out, small_out = take(5)
    zeros, sums, arriving = take(3)
    front_bufs = [take(7) for _ in range(sections)]
    back_bufs = [take(7) for _ in range(sections)]
    send, recv, dsend, drecv, asend, arecv, ssend, srecv, psem = take(9)
    spot = Spot()
    spot.greet()
    scatters = {}
    for s in range(sections):
        scatters["front", s] = ScatterSum(spot, fronts[s], s, front_bufs[s], send.at[s], recv.at[s])
        scatters["back", s] = ScatterSum(spot, backs[s], s, back_bufs[s], send.at[sections + s], recv.at[sections + s])
    order = []
    for s in reversed(range(sections)):
        order.append(scatters["front", s])
        if s % 2:
            order += [scatters["back", s - 1], scatters["back", s]]
    delivers = [Deliver(spot, a, acts_out, s, dsend.at[s], drecv.at[s], rows) for s, a in enumerate(acts)]
    delivers += [
        Deliver(spot, a, grads_out, s, dsend.at[sections + s], drecv.at[sections + s], rows)
        for s, a in enumerate(grads)
    ]
    for scatter in order:
        scatter.start()
    for deliver in delivers:
        deliver.start()
    zeros[...] = jnp.zeros_like(zeros)
    pad = acts_out.shape[1] - 2 * rows
    pads = [
        pltpu.make_async_copy(zeros, acts_out.at[slot, pl.ds(2 * rows, pad)], psem.at[slot]) for slot in (0, 1)
    ]
    for copy in pads:
        copy.start()
    sums[0] = small[...]
    partners = [spot.mate, spot.x, spot.y] + [
        {"section": spot.z + bit * (1 - 2 * ((spot.z // bit) % 2))}
        for bit in (1 << i for i in range((sections - 1).bit_length()))
    ]

    def small_step(i):
        copy = remote(sums.at[i], arriving.at[i], ssend.at[i], srecv.at[i], partners[i])
        copy.start()
        copy.wait()
        sums[i + 1] = sums[i] + arriving[i]

    count = len(order)
    for i in range(count + 3):
        if i < count:
            order[i].first()
        if 0 <= i - 1 < count:
            order[i - 1].second()
        if 0 <= i - 2 < count:
            order[i - 2].third()
        if 0 <= i - 3 < count:
            order[i - 3].fourth()
        if i < len(partners):
            small_step(i)
    small_out[...] = sums[len(partners)]
    gathers = [
        PlaneGather(spot, out, asend.at[i], arecv.at[i]) for i, out in enumerate((front_out, back_out))
    ]
    stays = []
    for i, (gather, kind) in enumerate(zip(gathers, ("front", "back"))):
        for s in range(sections):
            own = scatters[kind, s].own()
            stay = pltpu.make_async_copy(own, gather.dst.at[gather.blocks(spot.core, spot.c)], psem.at[2 + i])

            @pl.when(spot.z == s)
            def _(gather=gather, own=own, stay=stay):
                stay.start()
                gather.begin(own)
        stays.append(stay)
    for gather in gathers:
        gather.second()
    for gather in gathers:
        gather.third()
    for gather in gathers:
        gather.finish()
    for copy in stays + pads:
        copy.wait()
    for deliver in delivers:
        deliver.finish()
    for scatter in order:
        scatter.finish()


def collect(acts, grads, fronts, downs, small, padded):
    sections = lax.axis_size("section")
    rows, width = acts[0].shape
    back_shape = (16,) + downs[0].shape[1:]
    hbm, vmem = pl.BlockSpec(memory_space=pl.ANY), pl.BlockSpec(memory_space=pltpu.VMEM)
    steps = 3 + (sections - 1).bit_length()
    sems = pltpu.SemaphoreType.DMA
    out = pl.pallas_call(
        functools.partial(collect_body, rows, small.shape[0]),
        in_specs=[hbm] * (3 * sections + sections // 2) + [vmem],
        out_specs=[hbm] * 4 + [vmem],
        out_shape=[
            jax.ShapeDtypeStruct((2, padded, width), BF16), jax.ShapeDtypeStruct((2, 2 * rows, width), BF16),
            jax.ShapeDtypeStruct(fronts[0].shape, BF16), jax.ShapeDtypeStruct(back_shape, BF16),
            jax.ShapeDtypeStruct(small.shape, F32),
        ],
        scratch_shapes=[
            pltpu.VMEM((padded - 2 * rows, width), BF16),
            pltpu.VMEM((steps + 1,) + small.shape, F32), pltpu.VMEM((steps,) + small.shape, F32),
        ]
        + ScatterSum.scratch(*fronts[0].shape[1:]) * sections
        + ScatterSum.scratch(*back_shape[1:]) * sections
        + [
            sems((2 * sections, 9)), sems((2 * sections, 9)), sems((2 * sections, 2)), sems((2 * sections, 4)),
            sems((2, 9)), sems((2, 9)), sems((steps,)), sems((steps,)), sems((4,)),
        ],
        compiler_params=pltpu.CompilerParams(
            collective_id=1, has_side_effects=True, vmem_limit_bytes=62 * 2**20
        ),
        name="collect",
    )(*acts, *grads, *fronts, *downs, small)
    return out[0], out[1], out[2].reshape(-1, fronts[0].shape[2]), out[3].reshape(-1, back_shape[2]), out[4]


def norm_rows(hidden):
    average = jnp.mean(hidden, axis=-1, keepdims=True)
    centred = hidden - average
    inverse = lax.rsqrt(jnp.mean(centred * centred, axis=-1, keepdims=True) + EPS)
    return centred * inverse, inverse


def norm_backward(hidden, grad_normed, gain):
    unit, inverse = norm_rows(hidden)
    scaled = grad_normed * gain
    first = jnp.mean(scaled, axis=-1, keepdims=True)
    second = jnp.mean(scaled * unit, axis=-1, keepdims=True)
    return (
        inverse * (scaled - first - unit * second),
        jnp.sum(grad_normed * unit, axis=0, keepdims=True),
        jnp.sum(grad_normed, axis=0, keepdims=True),
    )


def gelu_and_slope(pre):
    density = jnp.exp(-0.5 * pre * pre)
    t = 1.0 / (1.0 + (0.3275911 * 0.5**0.5) * jnp.abs(pre))
    series = t * (0.127414796 + t * (-0.142248368 + t * (0.7107068705 + t * (-0.7265760135 + t * 0.5307027145))))
    tail = series * density
    below = jnp.where(pre < 0, tail, 1.0 - tail)
    return pre * below, below + pre * density * (1.0 / math.sqrt(2.0 * math.pi))


def pairs_of(block):
    return [block[:, p * PAIR : (p + 1) * PAIR] for p in range(block.shape[1] // PAIR)]


def joined(ref, lead=()):
    return jnp.concatenate([ref[lead + (p,)] for p in range(ref.shape[len(lead)])], axis=1)


def whole(shape):
    return pl.BlockSpec(shape, lambda i: (0,) * len(shape))


def swap_with_mate(spot, src, dst, send, recv):
    return remote(src, dst, send, recv, spot.mate)


def ff_forward_body(
    hidden_ref, mask_ref, gain_ref, shift_ref, up_ref, bias_up_ref, down_ref, bias_down_ref,
    act_ref, slope_ref, normed_out, out_ref, normed, total,
):
    step, last = pl.program_id(0), pl.num_programs(0) - 1

    @pl.when(step == 0)
    def _():
        unit, _ = norm_rows(hidden_ref[...].astype(F32))
        normed[...] = (unit * gain_ref[...] + shift_ref[...]).astype(BF16)
        normed_out[...] = normed[...]

    rows = normed.shape[0]
    for span in (slice(0, rows // 2), slice(rows // 2, rows)):
        pre = mm(normed[span, :], up_ref[...]) + bias_up_ref[...]
        act, slope = gelu_and_slope(pre)
        act_ref[span, :] = act.astype(BF16)
        slope_ref[span, :] = slope.astype(BF16)
        part = mm(act.astype(BF16), down_ref[...])
        total[span, :] = jnp.where(step == 0, part, total[span, :] + part)

    @pl.when(step == last)
    def _():
        hidden = hidden_ref[...].astype(F32)
        out_ref[...] = (mask_ref[...] * (hidden + total[...] + bias_down_ref[...])).astype(BF16)


def ff_forward(hidden, mask, gain, shift, up, bias_up, down, bias_down):
    rows, width = hidden.shape
    units = up.shape[1]
    size = width
    columns = pl.BlockSpec((rows, size), lambda i: (0, i))
    return pl.pallas_call(
        ff_forward_body,
        grid=(units // size,),
        in_specs=[
            whole((rows, width)), whole((rows, 1)), whole((1, width)), whole((1, width)),
            pl.BlockSpec((width, size), lambda i: (0, i)), pl.BlockSpec((1, size), lambda i: (0, i)),
            pl.BlockSpec((size, width), lambda i: (i, 0)), whole((1, width)),
        ],
        out_specs=[columns, columns, whole((rows, width)), whole((rows, width))],
        out_shape=[
            jax.ShapeDtypeStruct((rows, units), BF16), jax.ShapeDtypeStruct((rows, units), BF16),
            jax.ShapeDtypeStruct((rows, width), BF16), jax.ShapeDtypeStruct((rows, width), BF16),
        ],
        scratch_shapes=[pltpu.VMEM((rows, width), BF16), pltpu.VMEM((rows, width), F32)],
        compiler_params=pltpu.CompilerParams(vmem_limit_bytes=KERNEL_VMEM),
        name="ff_forward",
    )(hidden, mask, gain, shift, up, bias_up, down, bias_down)


def ff_backward_body(
    incoming_ref, mask_ref, hidden_ref, normed_ref, act_ref, slope_ref, up_ref, down_ref, gain_ref,
    up_grad, down_grad, out_ref, gain_grad, shift_grad, up_bias_grad, down_bias_grad,
    grad, normed_t, total,
):
    step, last = pl.program_id(0), pl.num_programs(0) - 1

    @pl.when(step == 0)
    def _():
        grad_rows = mask_ref[...] * incoming_ref[...].astype(F32)
        grad[...] = grad_rows.astype(BF16)
        down_bias_grad[...] = jnp.sum(grad_rows, axis=0, keepdims=True)
        normed_t[...] = normed_ref[...].astype(F32).T.astype(BF16)

    grad_pre = (contract_cols(grad[...], down_ref[...]) * slope_ref[...].astype(F32)).astype(BF16)
    down_grad[...] = contract_rows(act_ref[...], grad[...]).astype(BF16).reshape(down_grad.shape)
    up_bias_grad[...] = jnp.sum(grad_pre.astype(F32), axis=0, keepdims=True)
    up_grad[...] = mm(normed_t[...], grad_pre).astype(BF16).reshape(up_grad.shape)
    part = contract_cols(grad_pre, up_ref[...])
    total[...] = jnp.where(step == 0, part, total[...] + part)

    @pl.when(step == last)
    def _():
        grad_hidden, gain_grad[...], shift_grad[...] = norm_backward(
            hidden_ref[...].astype(F32), total[...], gain_ref[...]
        )
        out_ref[...] = (grad[...].astype(F32) + grad_hidden).astype(BF16)


def ff_backward(incoming, mask, hidden, normed, act, slope, up, down, gain):
    rows, width = hidden.shape
    units, size = up.shape[1], width
    columns = pl.BlockSpec((rows, size), lambda i: (0, i))
    vector = jax.ShapeDtypeStruct((1, width), F32)
    return pl.pallas_call(
        ff_backward_body,
        grid=(units // size,),
        in_specs=[
            whole((rows, width)), whole((rows, 1)), whole((rows, width)), whole((rows, width)), columns, columns,
            pl.BlockSpec((width, size), lambda i: (0, i)), pl.BlockSpec((size, width), lambda i: (i, 0)),
            whole((1, width)),
        ],
        out_specs=[
            pl.BlockSpec((16, width // 16, size), lambda i: (0, 0, i)),
            pl.BlockSpec((size * 32 // units, units // 32, width), lambda i: (i, 0, 0)),
            whole((rows, width)), whole((1, width)), whole((1, width)),
            pl.BlockSpec((1, size), lambda i: (0, i)), whole((1, width)),
        ],
        out_shape=[
            jax.ShapeDtypeStruct((16, width // 16, units), BF16), jax.ShapeDtypeStruct((32, units // 32, width), BF16),
            jax.ShapeDtypeStruct((rows, width), BF16), vector, vector,
            jax.ShapeDtypeStruct((1, units), F32), vector,
        ],
        scratch_shapes=[
            pltpu.VMEM((rows, width), BF16), pltpu.VMEM((width, rows), BF16), pltpu.VMEM((rows, width), F32),
        ],
        compiler_params=pltpu.CompilerParams(vmem_limit_bytes=KERNEL_VMEM),
        name="ff_backward",
    )(incoming, mask, hidden, normed, act, slope, up, down, gain)


def lane_ids(shape):
    return lax.broadcasted_iota(jnp.int32, shape, len(shape) - 1)


def three_parts(value):
    high = value.astype(BF16).astype(F32)
    rest = value - high
    middle = rest.astype(BF16).astype(F32)
    return high, middle, rest - middle


def extend_keys(keys_out, values_out, blocks, bias_ref, head):
    aux = HEAD_DIM * (1 - head)
    row = 0
    for key, value in blocks:
        rows = key.shape[0]
        span = slice(row, row + rows)
        lanes = lane_ids((rows, PAIR))
        inside = (lanes // HEAD_DIM) == head
        ones = jnp.where((lanes > aux) & (lanes <= aux + 3), 1.0, 0.0)
        extra = jnp.where(lanes == aux, bias_ref[span, :], ones)
        keys_out[span, :] = jnp.where(inside, key.astype(F32), extra).astype(BF16)
        ones = jnp.where((lanes >= aux) & (lanes < aux + 3), 1.0, 0.0)
        values_out[span, :] = jnp.where(inside, value.astype(F32), ones).astype(BF16)
        row += rows


def pair_forward(query_of, keys, values, rows, chunk, save):
    lanes = lane_ids((chunk, PAIR))
    units = [(start, head) for start in range(0, rows, chunk) for head in (0, 1)]

    def extended(start, head):
        aux = HEAD_DIM * (1 - head)
        inside = (lanes // HEAD_DIM) == head
        query = query_of(slice(start, start + chunk)).astype(F32)
        return jnp.where(inside, query, jnp.where(lanes == aux, 1.0, 0.0))

    def scores(start, head):
        return contract_cols(extended(start, head).astype(BF16), keys[head])

    ahead = [scores(*unit) for unit in units[:2]]
    for index, (start, head) in enumerate(units):
        now = ahead.pop(0)
        if index + 2 < len(units):
            ahead.append(scores(*units[index + 2]))
        aux = HEAD_DIM * (1 - head)
        top = jnp.max(now, axis=1, keepdims=True)
        summed = mm(jnp.exp(now - top).astype(BF16), values[head])
        total = summed[:, aux : aux + 1]
        query = extended(start, head)
        for lane, part in enumerate(three_parts(-(top + jnp.log(total))), aux + 1):
            query = jnp.where(lanes == lane, part, query)
        save(head, slice(start, start + chunk), query.astype(BF16), summed / total)


def attention_forward_body(
    hidden_ref, mask_ref, gain_ref, shift_ref, weight_ref, bias_ref, key_bias_ref, out_bias_ref,
    normed_out, key_out, value_out, key_far_out, value_far_out, extended_out, attended_out, out_ref,
    normed, own, far, attended, keys, values, send, recv,
):
    step, last = pl.program_id(0), pl.num_programs(0) - 1
    rows, width = normed.shape
    pairs = width // PAIR
    spot = Spot()

    def swaps():
        return [swap_with_mate(spot, own.at[j], far.at[j], send.at[j], recv.at[j]) for j in (0, 1)]

    @pl.when(step == 0)
    def _():
        spot.greet_mate()
        unit, _ = norm_rows(hidden_ref[...].astype(F32))
        normed[...] = (unit * gain_ref[...] + shift_ref[...]).astype(BF16)
        normed_out[...] = normed[...]

    for j, scale in ((0, 1.0), (1, 1.0), (2, HEAD_DIM**-0.5)):
        @pl.when(step == j)
        def _(j=j, scale=scale):
            block = (mm(normed[...], weight_ref[...]) + bias_ref[...]).astype(BF16)
            if scale != 1.0:
                block = (block.astype(F32) * scale).astype(BF16)
            for p, part in enumerate(pairs_of(block)):
                own[j, p] = part
            if j < 2:
                swaps()[j].start()
            else:
                for copy in swaps():
                    copy.wait()

    @pl.when((step >= 3) & (step < 3 + pairs))
    def _():
        p = step - 3
        for head in (0, 1):
            extend_keys(
                keys.at[head], values.at[head], [(own[0, p], own[1, p]), (far[0, p], far[1, p])],
                key_bias_ref, head,
            )
        for j, out in enumerate((key_out, value_out)):
            out[0] = own[j, p]
        for j, out in enumerate((key_far_out, value_far_out)):
            out[0] = far[j, p]
        lanes = lane_ids((rows // 2, PAIR))
        firsts = {}

        def save(head, span, query, out):
            extended_out[head, span, :] = query
            if head == 0:
                firsts[span.start] = out
            else:
                both = jnp.where(lanes < HEAD_DIM, firsts[span.start], out)
                attended_out[0, span, :] = both
                attended[p, span, :] = both.astype(BF16)

        pair_forward(lambda span: own[2, p, span, :], keys, values, rows, rows // 2, save)

    @pl.when(step == last)
    def _():
        branch = contract_cols(joined(attended), weight_ref[...]) + out_bias_ref[...]
        out_ref[...] = (mask_ref[...] * (hidden_ref[...].astype(F32) + branch)).astype(BF16)


def attention_forward(hidden, mask, gain, shift, weight, bias, key_bias, out_bias, collective_id):
    rows, width = hidden.shape
    pairs = width // PAIR
    pair = lambda i: jnp.clip(i - 3, 0, pairs - 1)
    part = lambda i: jnp.where(i < 3, (i + 1) % 3, 3)
    block = pl.BlockSpec((1, rows, PAIR), lambda i: (pair(i), 0, 0))
    saved = jax.ShapeDtypeStruct((pairs, rows, PAIR), BF16)
    full = jax.ShapeDtypeStruct((rows, width), BF16)
    return pl.pallas_call(
        attention_forward_body,
        grid=(pairs + 4,),
        in_specs=[
            whole((rows, width)), whole((rows, 1)), whole((1, width)), whole((1, width)),
            pl.BlockSpec((width, width), lambda i: (0, part(i))),
            pl.BlockSpec((1, width), lambda i: (0, jnp.minimum(part(i), 2))),
            whole((2 * rows, 1)), whole((1, width)),
        ],
        out_specs=[whole((rows, width))] + [block] * 4
        + [pl.BlockSpec((2, rows, PAIR), lambda i: (pair(i), 0, 0)), block, whole((rows, width))],
        out_shape=[full] + [saved] * 4 + [
            jax.ShapeDtypeStruct((2 * pairs, rows, PAIR), BF16),
            jax.ShapeDtypeStruct((pairs, rows, PAIR), F32), full,
        ],
        scratch_shapes=[
            pltpu.VMEM((rows, width), BF16), pltpu.VMEM((3, pairs, rows, PAIR), BF16),
            pltpu.VMEM((2, pairs, rows, PAIR), BF16), pltpu.VMEM((pairs, rows, PAIR), BF16),
            pltpu.VMEM((2, 2 * rows, PAIR), BF16), pltpu.VMEM((2, 2 * rows, PAIR), BF16),
            pltpu.SemaphoreType.DMA((2,)), pltpu.SemaphoreType.DMA((2,)),
        ],
        compiler_params=pltpu.CompilerParams(
            vmem_limit_bytes=KERNEL_VMEM, collective_id=collective_id, has_side_effects=True
        ),
        name="attention_forward",
    )(hidden, mask, gain, shift, weight, bias, key_bias, out_bias)


def pair_backward(query_of, grad_of, out_of, keys, values, key_sums, value_sums, rows, save):
    lanes = lane_ids((rows, PAIR))
    parts = []
    for head in (0, 1):
        aux = HEAD_DIM * (1 - head)
        inside = (lanes // HEAD_DIM) == head
        query = query_of(head)
        grad = jnp.where(inside, grad_of().astype(F32), 0.0)
        dots = jnp.sum(grad * out_of(), axis=1, keepdims=True)
        for lane, part in enumerate(three_parts(-dots), aux):
            grad = jnp.where(lanes == lane, part, grad)
        probs = jnp.exp(contract_cols(query, keys[head]))
        shifted = contract_cols(grad.astype(BF16), values[head])
        grad_scores = (probs * shifted).astype(BF16)
        parts.append(mm(grad_scores, keys[head]) * HEAD_DIM**-0.5)
        value_sums[head] = mm(grad.T.astype(BF16), probs.astype(BF16)).T
        key_sums[head] = mm(query.astype(F32).T.astype(BF16), grad_scores).T
    save(jnp.where(lanes < HEAD_DIM, parts[0], parts[1]).astype(BF16))


def attention_backward_body(
    incoming_ref, mask_ref, hidden_ref, normed_ref, key_ref, value_ref, key_far_ref, value_far_ref,
    extended_ref, attended_ref, weight_ref, gain_ref, key_bias_ref,
    weight_grad, out_ref, gain_grad, shift_grad, query_bias_grad, value_bias_grad, out_bias_grad,
    grad, grad_out, attended, normed_t, total, grads, sent, arrived, keys, values, key_sums, value_sums,
    send, recv,
):
    step, last = pl.program_id(0), pl.num_programs(0) - 1
    rows, width = grad.shape
    pairs = width // PAIR
    spot = Spot()

    def swap_of(p):
        return swap_with_mate(spot, sent.at[p], arrived.at[p], send.at[p], recv.at[p])

    @pl.when(step == 0)
    def _():
        spot.greet_mate()
        grad_rows = mask_ref[...] * incoming_ref[...].astype(F32)
        grad[...] = grad_rows.astype(BF16)
        out_bias_grad[...] = jnp.sum(grad_rows, axis=0, keepdims=True)
        for p, part in enumerate(pairs_of(mm(grad[...], weight_ref[...]).astype(BF16))):
            grad_out[p] = part

    @pl.when(step < pairs)
    def _():
        p = step
        for head in (0, 1):
            extend_keys(
                keys.at[head], values.at[head],
                [(key_ref[0], value_ref[0]), (key_far_ref[0], value_far_ref[0])], key_bias_ref, head,
            )
        attended[p] = attended_ref[0].astype(BF16)

        def save(value):
            grads[0, p] = value

        pair_backward(
            lambda head: extended_ref[head], lambda: grad_out[p], lambda: attended_ref[0],
            keys, values, key_sums, value_sums, rows, save,
        )
        first = lane_ids((rows, PAIR)) < HEAD_DIM
        for j, sums in enumerate((key_sums, value_sums)):
            grads[1 + j, p] = jnp.where(first, sums[0, :rows, :], sums[1, :rows, :]).astype(BF16)
            sent[p, j] = jnp.where(first, sums[0, rows:, :], sums[1, rows:, :]).astype(BF16)
        swap_of(p).start()

    @pl.when(step == pairs)
    def _():
        normed_t[...] = normed_ref[...].astype(F32).T.astype(BF16)
        for p in range(pairs):
            swap_of(p).wait()
            for j in (0, 1):
                grads[1 + j, p] = (grads[1 + j, p].astype(F32) + arrived[p, j].astype(F32)).astype(BF16)

    @pl.when((step >= pairs) & (step < last))
    def _():
        j = step - pairs
        part = joined(grads, (j,))
        sums = jnp.sum(part.astype(F32), axis=0, keepdims=True)

        @pl.when(j == 0)
        def _():
            query_bias_grad[...] = sums

        @pl.when(j == 2)
        def _():
            value_bias_grad[...] = sums

        weight_grad[...] = mm(normed_t[...], part).astype(BF16).reshape(weight_grad.shape)
        product = contract_cols(part, weight_ref[...])
        total[...] = jnp.where(j == 0, product, total[...] + product)

    @pl.when(step == last)
    def _():
        weight_grad[...] = contract_rows(grad[...], joined(attended)).astype(BF16).reshape(weight_grad.shape)
        grad_hidden, gain_grad[...], shift_grad[...] = norm_backward(
            hidden_ref[...].astype(F32), total[...], gain_ref[...]
        )
        out_ref[...] = (grad[...].astype(F32) + grad_hidden).astype(BF16)


def attention_backward(
    incoming, mask, hidden, normed, key, value, key_far, value_far, extended, attended, weight, gain, key_bias,
    collective_id,
):
    rows, width = hidden.shape
    pairs = width // PAIR
    pair = lambda i: jnp.minimum(i, pairs - 1)
    block = pl.BlockSpec((1, rows, PAIR), lambda i: (pair(i), 0, 0))
    vector = jax.ShapeDtypeStruct((1, width), F32)
    return pl.pallas_call(
        attention_backward_body,
        grid=(pairs + 4,),
        in_specs=[whole((rows, width)), whole((rows, 1)), whole((rows, width)), whole((rows, width))]
        + [block] * 4
        + [
            pl.BlockSpec((2, rows, PAIR), lambda i: (pair(i), 0, 0)), block,
            pl.BlockSpec((width, width), lambda i: (0, jnp.where(i < pairs, 3, jnp.minimum(i - pairs, 2)))),
            whole((1, width)), whole((2 * rows, 1)),
        ],
        out_specs=[
            pl.BlockSpec((16, width // 16, width), lambda i: (0, 0, jnp.maximum(i - pairs, 0))),
            whole((rows, width)),
        ] + [whole((1, width))] * 5,
        out_shape=[
            jax.ShapeDtypeStruct((16, width // 16, 4 * width), BF16), jax.ShapeDtypeStruct((rows, width), BF16),
        ] + [vector] * 5,
        scratch_shapes=[
            pltpu.VMEM((rows, width), BF16), pltpu.VMEM((pairs, rows, PAIR), BF16),
            pltpu.VMEM((pairs, rows, PAIR), BF16), pltpu.VMEM((width, rows), BF16),
            pltpu.VMEM((rows, width), F32), pltpu.VMEM((3, pairs, rows, PAIR), BF16),
            pltpu.VMEM((pairs, 2, rows, PAIR), BF16), pltpu.VMEM((pairs, 2, rows, PAIR), BF16),
            pltpu.VMEM((2, 2 * rows, PAIR), BF16), pltpu.VMEM((2, 2 * rows, PAIR), BF16),
            pltpu.VMEM((2, 2 * rows, PAIR), F32), pltpu.VMEM((2, 2 * rows, PAIR), F32),
            pltpu.SemaphoreType.DMA((pairs,)), pltpu.SemaphoreType.DMA((pairs,)),
        ],
        compiler_params=pltpu.CompilerParams(
            vmem_limit_bytes=KERNEL_VMEM, collective_id=collective_id, has_side_effects=True
        ),
        name="attention_backward",
    )(
        incoming, mask, hidden, normed, key, value, key_far, value_far, extended, attended, weight, gain, key_bias
    )


def per_device(
    clip_inputs, out_grad, clip_class, w_front, w_back, norm_gain, norm_shift,
    bias_query_value, bias_attn_out, bias_up, bias_down,
):
    spot = Spot()
    sections = lax.axis_size("section")
    padded, width = clip_inputs.shape[1:]
    rows = -(-LONG // 32) * 16
    core, section = spot.core, spot.z

    owner, slot = section // 2, section % 2
    mine = jnp.stack([lax.dynamic_index_in_dim(a, slot, 0, False) for a in (clip_inputs, out_grad)])
    far = swap(lax.dynamic_slice_in_dim(mine, (1 - core) * rows, rows, 1), 1)
    near = lax.dynamic_slice_in_dim(mine, core * rows, rows, 1)
    clip_pair = jnp.where(core == owner, near, far)
    own_class = lax.dynamic_index_in_dim(clip_class, slot, 0, False).astype(F32)
    own_class = jnp.broadcast_to(own_class, (8, 128))
    clip_kind = jnp.where(core == owner, own_class, swap(own_class, 1))[0, 0]
    length = SHORT + (LONG - SHORT) * clip_kind
    positions = jnp.arange(rows, dtype=jnp.int32)
    own_rows = (positions + core * rows).astype(F32) < length
    far_rows = (positions + (1 - core) * rows).astype(F32) < length
    row_mask = own_rows.astype(F32)[:, None]
    key_bias = jnp.where(jnp.concatenate([own_rows, far_rows]), 0.0, MASKED)[:, None]

    norms = jnp.concatenate([norm_gain, norm_shift, jnp.zeros((6, width), F32)], axis=0)
    fronts, downs, norm_all = gather_weights(w_front[0], w_back[0], norms)
    gains, shifts = norm_all[:, 0], norm_all[:, 1]

    hidden = (clip_pair[0].astype(F32) * row_mask).astype(BF16)
    row = lambda a: a.reshape(1, -1)
    saved, delivered = [], []
    for s in range(sections):
        layer = s // 2
        gain, shift = row(gains[s]), row(shifts[s])
        if s % 2 == 0:
            pair = bias_query_value[layer]
            bias = jnp.concatenate([pair[:width], jnp.zeros((width,), F32), pair[width:]])
            *kept, leaving = attention_forward(
                hidden, row_mask, gain, shift, fronts[s], row(bias), key_bias, row(bias_attn_out[layer]), 2 + s
            )
        else:
            *kept, leaving = ff_forward(
                hidden, row_mask, gain, shift, fronts[s], row(bias_up[layer]), downs[layer], row(bias_down[layer])
            )
        saved.append((hidden, *kept))
        hidden = leaving
        delivered.append(leaving)

    incoming = clip_pair[1]
    sent_grads, grad_fronts, grad_downs = [None] * sections, [None] * sections, [None] * 2
    grad_gain, grad_shift = [None] * sections, [None] * sections
    query_sums, value_sums, out_sums, up_sums, down_sums = ([None] * 2 for _ in range(5))
    for s in reversed(range(sections)):
        layer, gain = s // 2, row(gains[s])
        if s % 2 == 0:
            entered, normed, key, value, key_far, value_far, extended, attended = saved[s]
            (
                grad_fronts[s], incoming, grad_gain[s], grad_shift[s],
                query_sums[layer], value_sums[layer], out_sums[layer],
            ) = attention_backward(
                incoming, row_mask, entered, normed, key, value, key_far, value_far, extended, attended,
                fronts[s], gain, key_bias, 3 + s,
            )
        else:
            entered, act, slope, normed = saved[s]
            (
                grad_fronts[s], grad_downs[layer], incoming, grad_gain[s], grad_shift[s],
                up_sums[layer], down_sums[layer],
            ) = ff_backward(incoming, row_mask, entered, normed, act, slope, fronts[s], downs[layer], gain)
        sent_grads[s] = incoming

    pair_sums = [jnp.concatenate([q, v], axis=1) for q, v in zip(query_sums, value_sums)]
    small = jnp.concatenate(
        [v.reshape(-1) for v in grad_gain + grad_shift + pair_sums + out_sums + up_sums + down_sums]
    )
    acts_out, grads_out, front_out, back_out, small = collect(
        delivered, sent_grads, grad_fronts, grad_downs, small.reshape(-1, 128), padded
    )
    small = small.reshape(-1)
    for bit in spot.spare_bits:
        small = small + swap(small, bit)
        front_out, back_out = add(front_out, swap(front_out, bit)), add(back_out, swap(back_out, bit))
    grads_out = jnp.pad(grads_out.astype(F32), ((0, 0), (0, padded - 2 * rows), (0, 0)))
    parts, place_at = [], 0
    layers, hidden_units = bias_up.shape
    for count, size in (
        (sections, width), (sections, width), (layers, 2 * width), (layers, width),
        (layers, hidden_units), (layers, width),
    ):
        parts.append(small[place_at : place_at + count * size].reshape(count, size))
        place_at += count * size
    return (
        acts_out[None],
        grads_out[None],
        front_out.astype(F32)[None],
        back_out.astype(F32)[None],
        lax.dynamic_slice_in_dim(parts[0], section, 1, 0),
        lax.dynamic_slice_in_dim(parts[1], section, 1, 0),
        *parts[2:],
    )


def solution(mesh):
    placed = (
        P("dp", None, None), P("dp", None, None), P("dp"),
        P("section", None, None), P("section", None, None), P("section", None), P("section", None),
        P(), P(), P(), P(),
    )
    return jax.shard_map(
        per_device,
        mesh=mesh,
        in_specs=placed,
        out_specs=(
            P("section", "dp", None, None), P("section", "dp", None, None),
            P("section", None, None), P("section", None, None), P("section", None), P("section", None),
            P(), P(), P(), P(),
        ),
        check_vma=False,
    )
```

```python
import functools
import math

import jax
import jax.numpy as jnp
from jax import lax
from jax.experimental import pallas as pl
from jax.experimental.pallas import tpu as pltpu
from jax.sharding import PartitionSpec as P

HEADS = 12
LONG = 1214
SHORT = 514
EPS = 1e-06
HEAD_DIM = 64
PAIR = 2 * HEAD_DIM
MASKED = -1e30
F32 = jnp.float32
BF16 = jnp.bfloat16
KERNEL_VMEM = 56 * 2**20


def mm(left, right):
    return jnp.dot(left, right, preferred_element_type=F32)


def contract_rows(left, right):
    return lax.dot_general(left, right, (((0,), (0,)), ((), ())), preferred_element_type=F32)


def contract_cols(left, right):
    return lax.dot_general(left, right, (((1,), (1,)), ((), ())), preferred_element_type=F32)


def swap(block, bit):
    count = lax.axis_size("dp")
    return lax.ppermute(block, "dp", [(i, i ^ bit) for i in range(count)])


def add(a, b):
    return (a.astype(F32) + b.astype(F32)).astype(BF16)


class Spot:
    def __init__(self):
        self.z, self.sections = lax.axis_index("section"), lax.axis_size("section")
        self.d, self.count = lax.axis_index("dp"), lax.axis_size("dp")
        self.x_bit, self.y_bit = 2, 2 * math.isqrt(self.count // 2)
        self.core = self.d % 2
        self.xb, self.yb = (self.d // self.x_bit) % 2, (self.d // self.y_bit) % 2
        self.c, self.c_x = self.yb * 2 + self.xb, self.yb * 2 + 1 - self.xb
        self.c_y, self.c_d = (1 - self.yb) * 2 + self.xb, (1 - self.yb) * 2 + 1 - self.xb
        self.mate, self.x, self.y = (self.flipped(b) for b in (1, self.x_bit, self.y_bit))
        self.above, self.below = {"section": self.z + 1}, {"section": self.z - 1}
        self.spare_bits = [
            1 << i for i in range(self.count.bit_length() - 1) if 1 << i not in (1, self.x_bit, self.y_bit)
        ]

    def flipped(self, bit):
        return {"dp": self.d + bit * (1 - 2 * ((self.d // bit) % 2))}

    def greet_mate(self):
        barrier = pltpu.get_barrier_semaphore()
        pl.semaphore_signal(barrier, inc=1, device_id=self.mate, device_id_type=pl.DeviceIdType.MESH)
        pl.semaphore_wait(barrier, 1)

    def greet(self):
        barrier = pltpu.get_barrier_semaphore()
        devices = [self.x, self.y]
        for step in range(self.sections):
            for core in (0, 1):
                if step or core:
                    devices.append({
                        "section": (self.z + step) % self.sections,
                        "dp": self.d - self.core + (self.core + core) % 2,
                    })
        for device in devices:
            pl.semaphore_signal(barrier, inc=1, device_id=device, device_id_type=pl.DeviceIdType.MESH)
        pl.semaphore_wait(barrier, len(devices))


def remote(src, dst, send, recv, device):
    return pltpu.make_async_remote_copy(
        src_ref=src, dst_ref=dst, send_sem=send, recv_sem=recv,
        device_id=device, device_id_type=pl.DeviceIdType.MESH,
    )


class PlaneGather:
    SENDS, RECEIVES = 9, 9

    def __init__(self, spot, dst, send, recv):
        self.spot, self.dst, self.send, self.recv = spot, dst, send, recv

    def blocks(self, core, chip, half=None):
        at = core * 8 + chip * 2
        return pl.ds(at, 2) if half is None else pl.ds(at + half, 1)

    def copies(self, own=None):
        s, k = self.spot, self.spot.core
        plan = {
            "x": (self.blocks(k, s.c), s.x), "y": (self.blocks(k, s.c), s.y),
            "m": (self.blocks(k, s.c), s.mate),
            "xy": (self.blocks(k, s.c_x, 0), s.y), "yx": (self.blocks(k, s.c_y, 1), s.x),
            "mx": (self.blocks(k, s.c_x), s.mate), "my": (self.blocks(k, s.c_y), s.mate),
            "md0": (self.blocks(k, s.c_d, 0), s.mate), "md1": (self.blocks(k, s.c_d, 1), s.mate),
        }
        out = {}
        for index, (name, (rows, device)) in enumerate(plan.items()):
            src = own if own is not None and name in ("x", "y", "m") else self.dst.at[rows]
            out[name] = remote(src, self.dst.at[rows], self.send.at[index], self.recv.at[index], device)
        return out

    def arrivals(self):
        s, k = self.spot, self.spot.core
        plan = {
            "x": self.blocks(k, s.c_x), "y": self.blocks(k, s.c_y), "m": self.blocks(1 - k, s.c),
            "xy": self.blocks(k, s.c_d, 0), "yx": self.blocks(k, s.c_d, 1),
            "mx": self.blocks(1 - k, s.c_x), "my": self.blocks(1 - k, s.c_y),
            "md0": self.blocks(1 - k, s.c_d, 0), "md1": self.blocks(1 - k, s.c_d, 1),
        }
        return {
            name: remote(self.dst.at[rows], self.dst.at[rows], self.send.at[i], self.recv.at[i], s.mate)
            for i, (name, rows) in enumerate(plan.items())
        }

    def begin(self, own):
        copies = self.copies(own)
        for name in ("x", "y", "m"):
            copies[name].start()

    def second(self):
        copies, arrivals = self.copies(), self.arrivals()
        arrivals["x"].wait_recv()
        copies["xy"].start()
        copies["mx"].start()
        arrivals["y"].wait_recv()
        copies["yx"].start()
        copies["my"].start()

    def third(self):
        copies, arrivals = self.copies(), self.arrivals()
        for name, after in (("xy", "md0"), ("yx", "md1")):
            arrivals[name].wait_recv()
            copies[after].start()

    def finish(self):
        copies, arrivals = self.copies(), self.arrivals()
        for name in copies:
            copies[name].wait_send()
        for name in ("m", "mx", "my", "md0", "md1"):
            arrivals[name].wait_recv()


class SpreadHop:
    def __init__(self, spot, own, source, hop, send, recv, ways="both"):
        self.spot, self.own, self.send, self.recv = spot, own, send, recv
        self.up_from = source + hop - 1 if source + hop < spot.sections and ways != "down" else None
        self.down_from = source - hop + 1 if source - hop >= 0 and ways != "up" else None

    def copies(self):
        s, spot = self, self.spot
        return (
            remote(s.own, s.own, s.send.at[0], s.recv, spot.above),
            remote(s.own, s.own, s.send.at[1], s.recv, spot.below),
        )

    def start(self, upwards=True, downwards=True):
        up, down = self.copies()
        if upwards and self.up_from is not None:
            pl.when(self.spot.z == self.up_from)(up.start)
        if downwards and self.down_from is not None:
            pl.when(self.spot.z == self.down_from)(down.start)

    def arrive(self):
        up, _ = self.copies()
        if self.up_from is not None:
            pl.when(self.spot.z == self.up_from + 1)(up.wait_recv)
        if self.down_from is not None:
            pl.when(self.spot.z == self.down_from - 1)(up.wait_recv)

    def leave(self):
        up, down = self.copies()
        if self.up_from is not None:
            pl.when(self.spot.z == self.up_from)(up.wait_send)
        if self.down_from is not None:
            pl.when(self.spot.z == self.down_from)(down.wait_send)

    def finish(self):
        self.arrive()
        self.leave()


def hops_from(source, sections):
    return max(source, sections - 1 - source)


COLUMN_CHUNKS = 4
BEGUN = (
    ("front", 1, 2, "both"), ("back", 0, 1, "both"), ("back", 1, 1, "both"), ("front", 2, 1, "down"),
    ("front", 3, 1, "both"), ("back", 2, 1, "both"), ("back", 3, 1, "both"),
)


def first_weights_body(*refs):
    refs_list = list(refs)
    take = lambda n: [refs_list.pop(0) for _ in range(n)]
    own_in, norms, _ = take(1)[0], take(1)[0], take(len(BEGUN))
    front, norm_all, owns = take(1)[0], take(1)[0], take(len(BEGUN))
    own, own_sem, norm_send, norm_recv, zsend, zrecv, psend, precv, stay_sem, bsend, brecv = take(11)
    spot = Spot()
    load = pltpu.make_async_copy(own_in, own, own_sem)
    load.start()
    load.wait()
    spot.greet()
    size = own.shape[2] // COLUMN_CHUNKS
    hops, gathers, stays = [], [], []
    for j in range(COLUMN_CHUNKS):
        at = pl.ds((j + 1) % COLUMN_CHUNKS * size, size)
        piece = own.at[:, :, at]
        hops.append([SpreadHop(spot, piece, 0, hop, zsend.at[j, hop - 1], zrecv.at[j, hop - 1]) for hop in (1, 2, 3)])
        gathers.append(PlaneGather(spot, front.at[:, :, at], psend.at[j], precv.at[j]))
        stays.append(
            pltpu.make_async_copy(piece, gathers[j].dst.at[gathers[j].blocks(spot.core, spot.c)], stay_sem.at[j])
        )
        hops[j][0].start()
        if j == 0:
            norm_copies = [
                remote(
                    norms, norm_all.at[spot.z], norm_send.at[step], norm_recv.at[step],
                    {"section": (spot.z + step) % spot.sections},
                )
                for step in range(1, spot.sections)
            ]
            norm_copies.append(pltpu.make_async_copy(norms, norm_all.at[spot.z], norm_send.at[0]))
            for copy in norm_copies:
                copy.start()
    begun, count = [], 0
    for held, (_, source, made, ways) in zip(owns, BEGUN):
        begun.append([
            SpreadHop(
                spot, held, source, hop + 1, bsend.at[count + hop], brecv.at[count + hop], "both" if hop else ways
            )
            for hop in range(made)
        ])
        count += made
    for chain in begun:
        chain[0].start(upwards=False)
    begun[5][0].start(downwards=False)
    for j in range(COLUMN_CHUNKS):
        for hop in range(3):
            hops[j][hop].arrive()
            if hop < 2:
                hops[j][hop + 1].start()
        gathers[j].begin(own.at[:, :, pl.ds((j + 1) % COLUMN_CHUNKS * size, size)])
        stays[j].start()
    for chain in begun[:5] + begun[6:]:
        chain[0].start(downwards=False)
    for j in range(COLUMN_CHUNKS):
        gathers[j].second()
    begun[0][0].arrive()
    begun[0][1].start()
    for gather in gathers:
        gather.third()
    for chain in begun[1:]:
        chain[0].arrive()
    begun[0][1].arrive()
    for chain in begun:
        for hop in chain:
            hop.leave()
    for j in range(COLUMN_CHUNKS):
        for hop in hops[j]:
            hop.leave()
        gathers[j].finish()
        stays[j].wait()
    norm_copies[-1].wait()
    for step, copy in enumerate(norm_copies[:-1], 1):
        copy.wait_send()
        block = norm_all.at[(spot.z + spot.sections - step) % spot.sections]
        remote(block, block, norm_send.at[step], norm_recv.at[step], spot.mate).wait_recv()


def first_weights(front, back, norms):
    sections = lax.axis_size("section")
    spot = Spot()
    at = spot.core * 8 + spot.c * 2
    owns = {}
    for kind, weight in (("front", front), ("back", back)):
        blocks = weight.reshape(16, weight.shape[0] // 16, weight.shape[1])
        owns[kind] = lax.dynamic_slice_in_dim(blocks, at, 2, 0)
    hbm = hbm_spec()
    sems = pltpu.SemaphoreType.DMA
    begun = [owns[kind] for kind, _, _, _ in BEGUN]
    made = sum(hops for _, _, hops, _ in BEGUN)
    shape = lambda a: jax.ShapeDtypeStruct(a.shape, a.dtype)
    full = jax.ShapeDtypeStruct((16,) + owns["front"].shape[1:], BF16)
    out = pl.pallas_call(
        first_weights_body,
        in_specs=[hbm] * (2 + len(begun)), out_specs=[hbm] * (2 + len(begun)),
        out_shape=[full, jax.ShapeDtypeStruct((sections,) + norms.shape, F32)] + [shape(a) for a in begun],
        scratch_shapes=[
            pltpu.VMEM(owns["front"].shape, BF16), sems, sems((sections,)), sems((sections,)),
            sems((COLUMN_CHUNKS, 3, 2)), sems((COLUMN_CHUNKS, 3)), sems((COLUMN_CHUNKS, 9)), sems((COLUMN_CHUNKS, 9)),
            sems((COLUMN_CHUNKS,)), sems((made, 2)), sems((made,)),
        ],
        input_output_aliases={2 + i: 2 + i for i in range(len(begun))},
        compiler_params=pltpu.CompilerParams(collective_id=0, has_side_effects=True),
        name="first_weights",
    )(owns["front"], norms, *begun)
    return out[0], out[1], {(kind, source): held for (kind, source, _, _), held in zip(BEGUN, out[2:])}


class Deliver:
    def __init__(self, spot, src, dst, target, send, recv, start=0, size=None):
        self.spot, self.src, self.dst, self.target, self.send, self.recv = spot, src, dst, target, send, recv
        self.rows, self.start_row = src.shape[0], start
        self.size = size or src.shape[0]
        self.owner, self.slot = spot.z // 2, spot.z % 2
        self.home = (spot.z == target) & (spot.core == self.owner)

    def place(self, slot, core):
        at = pl.multiple_of(core * self.rows + self.start_row, 16)
        return self.dst.at[slot, pl.ds(at, self.size)]

    def copies(self):
        s, spot = self, self.spot
        spot_at, src = s.place(s.slot, spot.core), s.src.at[pl.ds(s.start_row, s.size)]
        away = remote(
            src, spot_at, s.send.at[0], s.recv.at[s.slot * 2 + spot.core],
            {"section": s.target, "dp": spot.d - spot.core + s.owner},
        )
        return away, pltpu.make_async_copy(src, spot_at, s.send.at[1])

    def start(self):
        away, stay = self.copies()
        pl.when(self.home)(stay.start)
        pl.when(jnp.logical_not(self.home))(away.start)

    def finish(self):
        away, stay = self.copies()
        pl.when(self.home)(stay.wait)
        pl.when(jnp.logical_not(self.home))(away.wait_send)
        spot = self.spot
        for slot in (0, 1):
            for core in (0, 1):
                here = (spot.core * 2 + slot == spot.z) & (spot.core == core)
                block = self.place(slot, core)
                landing = remote(block, block, self.send.at[0], self.recv.at[slot * 2 + core], spot.mate)
                pl.when((spot.z == self.target) & jnp.logical_not(here))(landing.wait_recv)


class Guest:
    def __init__(self, inputs=(), outputs=(), scratch=(), aliases=(), plan=None):
        self.inputs, self.outputs, self.scratch = list(inputs), list(outputs), list(scratch)
        self.aliases, self.plan = list(aliases), plan


def hbm_spec():
    return pl.BlockSpec(memory_space=pl.ANY)


def vmem_spec():
    return pl.BlockSpec(memory_space=pltpu.VMEM)


def hosted(body, grid, operands, results, scratch, guests, collective_id, name, vmem=KERNEL_VMEM):
    guest_in = [pair for g in guests for pair in g.inputs]
    guest_out = [pair for g in guests for pair in g.outputs]
    guest_scratch = [s for g in guests for s in g.scratch]
    aliases, at_in, at_out = {}, len(operands), len(results)
    for g in guests:
        for i, o in g.aliases:
            aliases[at_in + i] = at_out + o
        at_in, at_out = at_in + len(g.inputs), at_out + len(g.outputs)

    def kernel(*refs):
        refs = list(refs)
        take = lambda n: [refs.pop(0) for _ in range(n)]
        ins, gins = take(len(operands)), take(len(guest_in))
        outs, gouts = take(len(results)), take(len(guest_out))
        held, gheld = take(len(scratch)), take(len(guest_scratch))
        spot, step = Spot(), pl.program_id(0)
        pl.when(step == 0)(spot.greet)
        hooks = {}
        for g in guests:
            parts = [[r.pop(0) for _ in range(n)] for r, n in (
                (gins, len(g.inputs)), (gouts, len(g.outputs)), (gheld, len(g.scratch))
            )]
            for at, actions in g.plan(spot, *parts).items():
                hooks.setdefault(at, []).extend(actions)

        def run(actions):
            for action in actions:
                action()

        for at in sorted(k for k in hooks if k != "end"):
            pl.when(step == at)(functools.partial(run, hooks[at]))
        body(spot, *ins, *outs, *held)
        if "end" in hooks:
            pl.when(step == grid - 1)(functools.partial(run, hooks["end"]))

    out = pl.pallas_call(
        kernel,
        grid=(grid,),
        in_specs=[s for _, s in operands + guest_in],
        out_specs=[s for _, s in results + guest_out],
        out_shape=[s for s, _ in results + guest_out],
        scratch_shapes=list(scratch) + guest_scratch,
        input_output_aliases=aliases,
        compiler_params=pltpu.CompilerParams(
            vmem_limit_bytes=vmem, collective_id=collective_id, has_side_effects=True
        ),
        name=name,
    )(*[a for a, _ in operands + guest_in])
    own, rest, per_guest = out[: len(results)], list(out[len(results) :]), []
    for g in guests:
        per_guest.append([rest.pop(0) for _ in g.outputs])
    return own, per_guest


def deliver_guest(pieces, home, steps):
    sems = pltpu.SemaphoreType.DMA
    count = len(pieces)

    def plan(spot, ins, outs, held):
        send, recv = held
        hooks = {}
        for i, (_, target, first, size) in enumerate(pieces):
            blocks = size // 16
            for step in range(steps):
                low, high = blocks * step // steps, blocks * (step + 1) // steps
                if high > low:
                    part = Deliver(
                        spot, ins[i], outs[0], target, send.at[i], recv.at[i], first + 16 * low, 16 * (high - low)
                    )
                    hooks.setdefault(step, []).append(part.start)
            every = Deliver(spot, ins[i], outs[0], target, send.at[i], recv.at[i], first, size)
            hooks.setdefault("end", []).append(every.finish)
        return hooks

    return Guest(
        [(piece[0], hbm_spec()) for piece in pieces] + [(home, hbm_spec())],
        [(jax.ShapeDtypeStruct(home.shape, home.dtype), hbm_spec())],
        [sems((count, 2)), sems((count, 4))],
        [(count, 0)], plan,
    )


def plane_gather_guest(parts, shapes, stages):
    sems = pltpu.SemaphoreType.DMA

    def plan(spot, ins, outs, held):
        send, recv, stay_sem = held
        hooks = {}
        for i, (_, result, first) in enumerate(parts):
            job = PlaneGather(spot, outs[result].at[pl.ds(first, 16)], send.at[i], recv.at[i])
            stay = pltpu.make_async_copy(ins[i], job.dst.at[job.blocks(spot.core, spot.c)], stay_sem.at[i])
            actions = (functools.partial(job.begin, ins[i]), job.second, job.third)
            for at, action in zip(stages[i], actions):
                hooks.setdefault(at, []).append(action)
            hooks.setdefault(stages[i][0], []).append(stay.start)
            hooks.setdefault("end", []).extend([job.finish, stay.wait])
        return hooks

    return Guest(
        [(a, vmem_spec()) for a, _, _ in parts],
        [(jax.ShapeDtypeStruct(shape, BF16), hbm_spec()) for shape in shapes],
        [sems((len(parts), 9)), sems((len(parts), 9)), sems((len(parts),))],
        (), plan,
    )


def spread_gather_guest(jobs, shape):
    sems = pltpu.SemaphoreType.DMA
    made = sum(len(job[2]) for job in jobs)

    def plan(spot, ins, outs, held):
        hsend, hrecv, send, recv, stay_sem = held
        hooks, count = {}, 0
        for i, (_, source, hop_steps, stages, first) in enumerate(jobs):
            own, before = outs[i], None
            for back, at in enumerate(hop_steps):
                hop = SpreadHop(
                    spot, own, source, hops_from(source, spot.sections) - len(hop_steps) + 1 + back,
                    hsend.at[count], hrecv.at[count],
                )
                count += 1
                if before is not None:
                    hooks.setdefault(at, []).append(before.arrive)
                hooks.setdefault(at, []).append(hop.start)
                hooks.setdefault("end", []).append(hop.leave)
                before = hop
            job = PlaneGather(spot, outs[-1].at[pl.ds(first, 16)], send.at[i], recv.at[i])
            stay = pltpu.make_async_copy(own, job.dst.at[job.blocks(spot.core, spot.c)], stay_sem.at[i])
            hooks.setdefault(stages[0], []).extend([before.arrive, functools.partial(job.begin, own), stay.start])
            hooks.setdefault(stages[1], []).append(job.second)
            hooks.setdefault(stages[2], []).append(job.third)
            hooks.setdefault("end", []).extend([job.finish, stay.wait])
        return hooks

    return Guest(
        [(job[0], hbm_spec()) for job in jobs],
        [(jax.ShapeDtypeStruct(job[0].shape, BF16), hbm_spec()) for job in jobs]
        + [(jax.ShapeDtypeStruct(shape, BF16), hbm_spec())],
        [sems((made, 2)), sems((made,)), sems((len(jobs), 9)), sems((len(jobs), 9)), sems((len(jobs),))],
        [(i, i) for i in range(len(jobs))], plan,
    )


def spread_hop_guest(arrays, jobs, start=0):
    sems = pltpu.SemaphoreType.DMA

    def plan(spot, ins, outs, held):
        send, recv = held
        hops = [
            SpreadHop(spot, outs[i], source, hop, send.at[n], recv.at[n], ways)
            for n, (i, source, hop, ways) in enumerate(jobs)
        ]
        return {start: [h.start for h in hops], "end": [h.finish for h in hops]}

    return Guest(
        [(a, hbm_spec()) for a in arrays],
        [(jax.ShapeDtypeStruct(a.shape, a.dtype), hbm_spec()) for a in arrays],
        [sems((len(jobs), 2)), sems((len(jobs),))],
        [(i, i) for i in range(len(arrays))], plan,
    )


def plane_sum_guest(jobs, stages):
    sems = pltpu.SemaphoreType.DMA
    shapes = [(a.shape[1], a.shape[2]) for a, _ in jobs]
    arrays = []
    for a, _ in jobs:
        if not any(a is b for b in arrays):
            arrays.append(a)
    index = [next(i for i, b in enumerate(arrays) if b is a) for a, _ in jobs]

    def plan(spot, ins, outs, held):
        send, recv = held[-2:]
        hooks = {}
        for i, (_, first) in enumerate(jobs):
            src = ins[index[i]].at[pl.ds(first, 16)]
            job = PlaneSum(spot, src, held[6 * i : 6 * i + 6], send.at[i], recv.at[i])
            actions = (job.start, job.first, job.second, functools.partial(job.third, outs[i]))
            for at, action in zip(stages[i], actions):
                hooks.setdefault(at, []).append(action)
            hooks.setdefault("end", []).append(job.finish)
        return hooks

    return Guest(
        [(a, hbm_spec()) for a in arrays],
        [(jax.ShapeDtypeStruct((2,) + s, BF16), vmem_spec()) for s in shapes],
        [b for s in shapes for b in PlaneSum.scratch(*s)] + [sems((len(jobs), 8)), sems((len(jobs), 8))],
        (), plan,
    )


def section_hop_guest(jobs, start=0):
    sems = pltpu.SemaphoreType.DMA

    def plan(spot, ins, outs, held):
        send, recv = held[-2:]
        hops = [
            SectionHop(spot, ins[i], outs[i], held[i], target, hop, send.at[i], recv.at[i])
            for i, (_, target, hop) in enumerate(jobs)
        ]
        return {start: [h.start for h in hops], "end": [h.finish for h in hops]}

    return Guest(
        [(a, vmem_spec()) for a, _, _ in jobs],
        [(jax.ShapeDtypeStruct(a.shape, BF16), vmem_spec()) for a, _, _ in jobs],
        [pltpu.VMEM((2 * a.shape[0],) + a.shape[1:], BF16) for a, _, _ in jobs]
        + [sems((len(jobs),)), sems((len(jobs), 2))],
        (), plan,
    )


def add_into(target, *others):
    def step(b, carry):
        total = target[b].astype(F32)
        for other in others:
            total = total + other[b].astype(F32)
        target[b] = total.astype(BF16)
        return carry

    lax.fori_loop(0, target.shape[0], step, 0)


class PlaneSum:
    def __init__(self, spot, src, bufs, send, recv):
        self.spot, self.src, self.send, self.recv = spot, src, send, recv
        self.half, self.from_mate, self.in_x, self.in_y, self.in_yx, self.in_xy = bufs

    @staticmethod
    def scratch(block_rows, columns):
        return [pltpu.VMEM((n, block_rows, columns), BF16) for n in (8, 8, 2, 2, 1, 1)]

    def mate_copies(self):
        s, spot = self, self.spot
        return (
            pltpu.make_async_copy(s.src.at[pl.ds(spot.core * 8, 8)], s.half, s.send.at[0]),
            remote(s.src.at[pl.ds((1 - spot.core) * 8, 8)], s.from_mate, s.send.at[1], s.recv.at[1], spot.mate),
        )

    def start(self):
        for copy in self.mate_copies():
            copy.start()

    def block(self, chip, half):
        return self.half.at[pl.ds(chip * 2 + half, 1)]

    def first_copies(self):
        s, spot = self, self.spot
        first, second = pl.ds(0, 1), pl.ds(1, 1)
        return (
            remote(s.block(spot.c_x, 0), s.in_x.at[first], s.send.at[2], s.recv.at[2], spot.x),
            remote(s.block(spot.c_d, 0), s.in_x.at[second], s.send.at[3], s.recv.at[3], spot.x),
            remote(s.block(spot.c_y, 1), s.in_y.at[first], s.send.at[4], s.recv.at[4], spot.y),
            remote(s.block(spot.c_d, 1), s.in_y.at[second], s.send.at[5], s.recv.at[5], spot.y),
        )

    def second_copies(self):
        s, spot = self, self.spot
        return (
            remote(s.block(spot.c_y, 0), s.in_xy, s.send.at[6], s.recv.at[6], spot.y),
            remote(s.block(spot.c_x, 1), s.in_yx, s.send.at[7], s.recv.at[7], spot.x),
        )

    def first(self):
        for copy in self.mate_copies():
            copy.wait()
        add_into(self.half, self.from_mate)
        for copy in self.first_copies():
            copy.start()

    def second(self):
        s, spot = self, self.spot
        for copy in self.first_copies():
            copy.wait_recv()
        first, other = pl.ds(0, 1), pl.ds(1, 1)
        add_into(s.block(spot.c_y, 0), s.in_x.at[other])
        add_into(s.block(spot.c_x, 1), s.in_y.at[other])
        for copy in self.second_copies():
            copy.start()

    def third(self, out):
        s, spot = self, self.spot
        for copy in self.second_copies():
            copy.wait_recv()
        first = pl.ds(0, 1)
        add_into(s.block(spot.c, 0), s.in_x.at[first], s.in_xy)
        add_into(s.block(spot.c, 1), s.in_y.at[first], s.in_yx)
        out[...] = s.half[pl.ds(spot.c * 2, 2)]

    def finish(self):
        for copy in self.first_copies() + self.second_copies():
            copy.wait_send()


class SectionHop:
    def __init__(self, spot, src, total, bufs, target, hop, send, recv):
        self.spot, self.src, self.total, self.bufs, self.send, self.recv = spot, src, total, bufs, send, recv
        last = spot.sections - 1
        self.below = hop - 1 if hop <= target else None
        self.above = last - hop + 1 if last - hop >= target else None

    def copies(self):
        s, spot, n = self, self.spot, self.src.shape[0]
        up = remote(s.src, s.bufs.at[pl.ds(n, n)], s.send, s.recv.at[1], spot.above)
        down = remote(s.src, s.bufs.at[pl.ds(0, n)], s.send, s.recv.at[0], spot.below)
        return up, down

    def start(self):
        up, down = self.copies()
        if self.below is not None:
            pl.when(self.spot.z == self.below)(up.start)
        if self.above is not None:
            pl.when(self.spot.z == self.above)(down.start)
        self.total[...] = self.src[...]

    def finish(self):
        up, down = self.copies()
        n = self.src.shape[0]
        if self.below is not None:
            pl.when(self.spot.z == self.below)(up.wait_send)

            @pl.when(self.spot.z == self.below + 1)
            def _():
                up.wait_recv()
                add_into(self.total, self.bufs.at[pl.ds(n, n)])
        if self.above is not None:
            pl.when(self.spot.z == self.above)(down.wait_send)

            @pl.when(self.spot.z == self.above - 1)
            def _():
                down.wait_recv()
                add_into(self.total, self.bufs.at[pl.ds(0, n)])


LEFT = (("front", 3, 2), ("back", 3, 2), ("front", 2, 1), ("back", 2, 2), ("front", 1, 0), ("back", 0, 0), ("back", 1, 0))


def collect_body(*refs):
    sections = lax.axis_size("section")
    refs_list = list(refs)
    take = lambda n: [refs_list.pop(0) for _ in range(n)]
    last, second, first_front = take(3)
    parts = take(len(LEFT))
    small, _ = take(2)
    home, front_out, back_out, small_out = take(4)
    plane_bufs, own, (sums, arriving) = take(6), take(1)[0], take(2)
    psend, precv, dsend, drecv, asend, arecv, ssend, srecv, stay_sem, zsend, zrecv = take(11)
    hop_refs = refs_list
    spot = Spot()
    spot.greet()
    delivers = [
        Deliver(spot, piece, home, target, dsend.at[target // 2], drecv.at[target // 2], *rows)
        for piece, target, rows in ((last, 0, ()), (second, 2, (192, second.shape[0] - 192)))
    ]
    plane = PlaneSum(spot, first_front, plane_bufs, psend, precv)
    count = 0

    def chain(src, target, done):
        nonlocal count
        hops = []
        for hop in range(done + 1, max(target, sections - 1 - target) + 1):
            total, bufs = hop_refs.pop(0), hop_refs.pop(0)
            hops.append(SectionHop(spot, src, total, bufs, target, hop, zsend.at[count], zrecv.at[count]))
            src, count = total, count + 1
        return hops, src

    chains = [chain(part, target, done) for part, (_, target, done) in zip(parts, LEFT)]
    first_chains = [chain(own.at[pl.ds(i, 1)], 0, 0) for i in (0, 1)]

    def turn(which, i):
        for hops, _ in which:
            if 0 < i <= len(hops):
                hops[i - 1].finish()
        for hops, _ in which:
            if i < len(hops):
                hops[i].start()

    plane.start()
    turn(chains, 0)
    sums[0] = small[...]
    partners = [spot.mate, spot.x, spot.y] + [
        {"section": spot.z + bit * (1 - 2 * ((spot.z // bit) % 2))}
        for bit in (1 << i for i in range((sections - 1).bit_length()))
    ]

    def small_step(i):
        copy = remote(sums.at[i], arriving.at[i], ssend.at[i], srecv.at[i], partners[i])
        copy.start()
        copy.wait()
        sums[i + 1] = sums[i] + arriving[i]

    small_step(0)
    plane.first()
    for deliver in delivers:
        deliver.start()
    turn(chains, 1)
    for i in range(1, len(partners)):
        small_step(i)
    small_out[...] = sums[len(partners)]
    plane.second()
    turn(chains, 2)
    plane.third(own)
    turn(first_chains[:1], 0)
    turn(first_chains[1:], 0)
    turn(chains, 3)
    gathers = [
        PlaneGather(spot, out, asend.at[i], arecv.at[i]) for i, out in enumerate((front_out, back_out))
    ]
    ends = {(kind, target): end for (kind, target, _), (_, end) in zip(LEFT, chains)}
    stays = []

    def begin(i, kind):
        gather = gathers[i]
        for z in range(sections):
            blocks = gather.blocks(spot.core, spot.c)
            if kind == "front" and z == 0:
                pieces = [
                    (end, gather.dst.at[gather.blocks(spot.core, spot.c, half)], stay_sem.at[half])
                    for half, (_, end) in enumerate(first_chains)
                ]
            else:
                pieces = [(ends[kind, z], gather.dst.at[blocks], stay_sem.at[2 + i])]
            copies = [pltpu.make_async_copy(*piece) for piece in pieces]

            @pl.when(spot.z == z)
            def _(gather=gather, copies=copies):
                for copy in copies:
                    copy.start()
                for copy in copies:
                    copy.wait()
                gather.begin(gather.dst.at[gather.blocks(spot.core, spot.c)])

    begin(1, "back")
    turn(first_chains[:1], 1)
    turn(first_chains[1:], 1)
    gathers[1].second()
    turn(first_chains[:1], 2)
    turn(first_chains[1:], 2)
    gathers[1].third()
    turn(first_chains[:1], 3)
    turn(first_chains[1:], 3)
    begin(0, "front")
    gathers[0].second()
    gathers[0].third()
    for gather in gathers:
        gather.finish()
    for deliver in delivers:
        deliver.finish()
    plane.finish()


def collect(last, second, home, first_front, parts, small):
    sections = lax.axis_size("section")
    hbm, vmem = hbm_spec(), vmem_spec()
    steps = 3 + (sections - 1).bit_length()
    sems = pltpu.SemaphoreType.DMA
    front_shape = first_front.shape
    back_shape = (16,) + parts[1].shape[1:]
    hop_scratch, hops = [], 0
    jobs = [(p.shape, target, done) for p, (_, target, done) in zip(parts, LEFT)]
    for shape, target, done in jobs + [((1,) + front_shape[1:], 0, 0)] * 2:
        for _ in range(done, max(target, sections - 1 - target)):
            hop_scratch += [pltpu.VMEM(shape, BF16), pltpu.VMEM((2 * shape[0],) + shape[1:], BF16)]
            hops += 1
    return pl.pallas_call(
        collect_body,
        in_specs=[hbm] * 3 + [vmem] * (len(parts) + 1) + [hbm],
        out_specs=[hbm] * 3 + [vmem],
        out_shape=[
            jax.ShapeDtypeStruct(home.shape, BF16), jax.ShapeDtypeStruct(front_shape, BF16),
            jax.ShapeDtypeStruct(back_shape, BF16), jax.ShapeDtypeStruct(small.shape, F32),
        ],
        scratch_shapes=PlaneSum.scratch(*front_shape[1:])
        + [
            pltpu.VMEM((2,) + front_shape[1:], BF16),
            pltpu.VMEM((steps + 1,) + small.shape, F32), pltpu.VMEM((steps,) + small.shape, F32),
            sems((8,)), sems((8,)), sems((2, 2)), sems((2, 4)),
            sems((2, 9)), sems((2, 9)), sems((steps,)), sems((steps,)), sems((4,)),
            sems((hops,)), sems((hops, 2)),
        ]
        + hop_scratch,
        input_output_aliases={4 + len(parts): 0},
        compiler_params=pltpu.CompilerParams(
            collective_id=1, has_side_effects=True, vmem_limit_bytes=KERNEL_VMEM
        ),
        name="collect",
    )(last, second, first_front, *parts, small, home)


def norm_rows(hidden):
    average = jnp.mean(hidden, axis=-1, keepdims=True)
    centred = hidden - average
    inverse = lax.rsqrt(jnp.mean(centred * centred, axis=-1, keepdims=True) + EPS)
    return centred * inverse, inverse


def norm_backward(hidden, grad_normed, gain):
    unit, inverse = norm_rows(hidden)
    scaled = grad_normed * gain
    first = jnp.mean(scaled, axis=-1, keepdims=True)
    second = jnp.mean(scaled * unit, axis=-1, keepdims=True)
    return (
        inverse * (scaled - first - unit * second),
        jnp.sum(grad_normed * unit, axis=0, keepdims=True),
        jnp.sum(grad_normed, axis=0, keepdims=True),
    )


def gelu_and_slope(pre):
    density = jnp.exp(-0.5 * pre * pre)
    t = 1.0 / (1.0 + (0.3275911 * 0.5**0.5) * jnp.abs(pre))
    series = t * (0.127414796 + t * (-0.142248368 + t * (0.7107068705 + t * (-0.7265760135 + t * 0.5307027145))))
    tail = series * density
    below = jnp.where(pre < 0, tail, 1.0 - tail)
    return pre * below, below + pre * density * (1.0 / math.sqrt(2.0 * math.pi))


def pairs_of(block):
    return [block[:, p * PAIR : (p + 1) * PAIR] for p in range(block.shape[1] // PAIR)]


def joined(ref, lead=()):
    return jnp.concatenate([ref[lead + (p,)] for p in range(ref.shape[len(lead)])], axis=1)


def whole(shape):
    return pl.BlockSpec(shape, lambda i: (0,) * len(shape))


def swap_with_mate(spot, src, dst, send, recv):
    return remote(src, dst, send, recv, spot.mate)


def ff_forward_body(
    spot, hidden_ref, mask_ref, gain_ref, shift_ref, up_ref, bias_up_ref, down_ref, bias_down_ref,
    act_ref, slope_ref, normed_out, out_ref, normed, total,
):
    step, last = pl.program_id(0), pl.num_programs(0) - 1

    @pl.when(step == 0)
    def _():
        unit, _ = norm_rows(hidden_ref[...].astype(F32))
        normed[...] = (unit * gain_ref[...] + shift_ref[...]).astype(BF16)
        normed_out[...] = normed[...]

    rows = normed.shape[0]
    for span in (slice(0, rows // 2), slice(rows // 2, rows)):
        pre = mm(normed[span, :], up_ref[...]) + bias_up_ref[...]
        act, slope = gelu_and_slope(pre)
        act_ref[span, :] = act.astype(BF16)
        slope_ref[span, :] = slope.astype(BF16)
        part = mm(act.astype(BF16), down_ref[...])
        total[span, :] = jnp.where(step == 0, part, total[span, :] + part)

    @pl.when(step == last)
    def _():
        hidden = hidden_ref[...].astype(F32)
        out_ref[...] = (mask_ref[...] * (hidden + total[...] + bias_down_ref[...])).astype(BF16)


def ff_forward(hidden, mask, gain, shift, up, bias_up, down, bias_down, guests, collective_id):
    rows, width = hidden.shape
    units = up.shape[1]
    size = width
    columns = pl.BlockSpec((rows, size), lambda i: (0, i))
    in_specs = ([
            whole((rows, width)), whole((rows, 1)), whole((1, width)), whole((1, width)),
            pl.BlockSpec((width, size), lambda i: (0, i)), pl.BlockSpec((1, size), lambda i: (0, i)),
            pl.BlockSpec((size, width), lambda i: (i, 0)), whole((1, width)),
        ])
    out_specs = ([columns, columns, whole((rows, width)), whole((rows, width))])
    out_shape = ([
            jax.ShapeDtypeStruct((rows, units), BF16), jax.ShapeDtypeStruct((rows, units), BF16),
            jax.ShapeDtypeStruct((rows, width), BF16), jax.ShapeDtypeStruct((rows, width), BF16),
        ])
    scratch = ([pltpu.VMEM((rows, width), BF16), pltpu.VMEM((rows, width), F32)])
    return hosted(
        ff_forward_body, units // size, list(zip((hidden, mask, gain, shift, up, bias_up, down, bias_down), in_specs)), list(zip(out_shape, out_specs)), scratch,
        guests, collective_id, "ff_forward",
    )


def ff_backward_body(
    spot, incoming_ref, mask_ref, hidden_ref, normed_ref, act_ref, slope_ref, up_ref, down_ref, gain_ref,
    up_grad, down_grad, out_ref, gain_grad, shift_grad, up_bias_grad, down_bias_grad,
    grad, normed_t, total,
):
    step, last = pl.program_id(0), pl.num_programs(0) - 1

    @pl.when(step == 0)
    def _():
        grad_rows = mask_ref[...] * incoming_ref[...].astype(F32)
        grad[...] = grad_rows.astype(BF16)
        down_bias_grad[...] = jnp.sum(grad_rows, axis=0, keepdims=True)
        normed_t[...] = normed_ref[...].astype(F32).T.astype(BF16)

    grad_pre = (contract_cols(grad[...], down_ref[...]) * slope_ref[...].astype(F32)).astype(BF16)
    down_grad[...] = contract_rows(act_ref[...], grad[...]).astype(BF16).reshape(down_grad.shape)
    up_bias_grad[...] = jnp.sum(grad_pre.astype(F32), axis=0, keepdims=True)
    up_grad[...] = mm(normed_t[...], grad_pre).astype(BF16).reshape(up_grad.shape)
    part = contract_cols(grad_pre, up_ref[...])
    total[...] = jnp.where(step == 0, part, total[...] + part)

    @pl.when(step == last)
    def _():
        grad_hidden, gain_grad[...], shift_grad[...] = norm_backward(
            hidden_ref[...].astype(F32), total[...], gain_ref[...]
        )
        out_ref[...] = (grad[...].astype(F32) + grad_hidden).astype(BF16)


def ff_backward(incoming, mask, hidden, normed, act, slope, up, down, gain, guests, collective_id):
    rows, width = hidden.shape
    units, size = up.shape[1], width
    columns = pl.BlockSpec((rows, size), lambda i: (0, i))
    vector = jax.ShapeDtypeStruct((1, width), F32)
    in_specs = ([
            whole((rows, width)), whole((rows, 1)), whole((rows, width)), whole((rows, width)), columns, columns,
            pl.BlockSpec((width, size), lambda i: (0, i)), pl.BlockSpec((size, width), lambda i: (i, 0)),
            whole((1, width)),
        ])
    out_specs = ([
            pl.BlockSpec((16, width // 16, size), lambda i: (0, 0, i)),
            pl.BlockSpec((size * 32 // units, units // 32, width), lambda i: (i, 0, 0)),
            whole((rows, width)), whole((1, width)), whole((1, width)),
            pl.BlockSpec((1, size), lambda i: (0, i)), whole((1, width)),
        ])
    out_shape = ([
            jax.ShapeDtypeStruct((16, width // 16, units), BF16), jax.ShapeDtypeStruct((32, units // 32, width), BF16),
            jax.ShapeDtypeStruct((rows, width), BF16), vector, vector,
            jax.ShapeDtypeStruct((1, units), F32), vector,
        ])
    scratch = ([
            pltpu.VMEM((rows, width), BF16), pltpu.VMEM((width, rows), BF16), pltpu.VMEM((rows, width), F32),
        ])
    return hosted(
        ff_backward_body, units // size, list(zip((incoming, mask, hidden, normed, act, slope, up, down, gain), in_specs)), list(zip(out_shape, out_specs)), scratch,
        guests, collective_id, "ff_backward",
    )


def lane_ids(shape):
    return lax.broadcasted_iota(jnp.int32, shape, len(shape) - 1)


def three_parts(value):
    high = value.astype(BF16).astype(F32)
    rest = value - high
    middle = rest.astype(BF16).astype(F32)
    return high, middle, rest - middle


def extend_keys(keys_out, values_out, blocks, bias_ref, head):
    aux = HEAD_DIM * (1 - head)
    row = 0
    for key, value in blocks:
        rows = key.shape[0]
        span = slice(row, row + rows)
        lanes = lane_ids((rows, PAIR))
        inside = (lanes // HEAD_DIM) == head
        ones = jnp.where((lanes > aux) & (lanes <= aux + 3), 1.0, 0.0)
        extra = jnp.where(lanes == aux, bias_ref[span, :], ones)
        keys_out[span, :] = jnp.where(inside, key.astype(F32), extra).astype(BF16)
        ones = jnp.where((lanes >= aux) & (lanes < aux + 3), 1.0, 0.0)
        values_out[span, :] = jnp.where(inside, value.astype(F32), ones).astype(BF16)
        row += rows


def pair_forward(query_of, keys, values, rows, chunk, save):
    lanes = lane_ids((chunk, PAIR))
    units = [(start, head) for start in range(0, rows, chunk) for head in (0, 1)]

    def extended(start, head):
        aux = HEAD_DIM * (1 - head)
        inside = (lanes // HEAD_DIM) == head
        query = query_of(slice(start, start + chunk)).astype(F32)
        return jnp.where(inside, query, jnp.where(lanes == aux, 1.0, 0.0))

    def scores(start, head):
        return contract_cols(extended(start, head).astype(BF16), keys[head])

    ahead = [scores(*unit) for unit in units[:2]]
    for index, (start, head) in enumerate(units):
        now = ahead.pop(0)
        if index + 2 < len(units):
            ahead.append(scores(*units[index + 2]))
        aux = HEAD_DIM * (1 - head)
        top = jnp.max(now, axis=1, keepdims=True)
        summed = mm(jnp.exp(now - top).astype(BF16), values[head])
        total = summed[:, aux : aux + 1]
        query = extended(start, head)
        for lane, part in enumerate(three_parts(-(top + jnp.log(total))), aux + 1):
            query = jnp.where(lanes == lane, part, query)
        save(head, slice(start, start + chunk), query.astype(BF16), summed / total)


def attention_forward_body(
    spot, hidden_ref, mask_ref, gain_ref, shift_ref, weight_ref, bias_ref, key_bias_ref, out_bias_ref,
    normed_out, key_out, value_out, key_far_out, value_far_out, extended_out, attended_out, out_ref,
    normed, own, far, attended, keys, values, send, recv,
):
    step, last = pl.program_id(0), pl.num_programs(0) - 1
    rows, width = normed.shape
    pairs = width // PAIR

    def swaps():
        return [swap_with_mate(spot, own.at[j], far.at[j], send.at[j], recv.at[j]) for j in (0, 1)]

    @pl.when(step == 0)
    def _():
        unit, _ = norm_rows(hidden_ref[...].astype(F32))
        normed[...] = (unit * gain_ref[...] + shift_ref[...]).astype(BF16)
        normed_out[...] = normed[...]

    for j, scale in ((0, 1.0), (1, 1.0), (2, HEAD_DIM**-0.5)):
        @pl.when(step == j)
        def _(j=j, scale=scale):
            block = (mm(normed[...], weight_ref[...]) + bias_ref[...]).astype(BF16)
            if scale != 1.0:
                block = (block.astype(F32) * scale).astype(BF16)
            for p, part in enumerate(pairs_of(block)):
                own[j, p] = part
            if j < 2:
                swaps()[j].start()
            else:
                for copy in swaps():
                    copy.wait()

    @pl.when((step >= 3) & (step < 3 + pairs))
    def _():
        p = step - 3
        for head in (0, 1):
            extend_keys(
                keys.at[head], values.at[head], [(own[0, p], own[1, p]), (far[0, p], far[1, p])],
                key_bias_ref, head,
            )
        for j, out in enumerate((key_out, value_out)):
            out[0] = own[j, p]
        for j, out in enumerate((key_far_out, value_far_out)):
            out[0] = far[j, p]
        lanes = lane_ids((rows // 2, PAIR))
        firsts = {}

        def save(head, span, query, out):
            extended_out[head, span, :] = query
            if head == 0:
                firsts[span.start] = out
            else:
                both = jnp.where(lanes < HEAD_DIM, firsts[span.start], out)
                attended_out[0, span, :] = both
                attended[p, span, :] = both.astype(BF16)

        pair_forward(lambda span: own[2, p, span, :], keys, values, rows, rows // 2, save)

    @pl.when(step == last)
    def _():
        branch = contract_cols(joined(attended), weight_ref[...]) + out_bias_ref[...]
        out_ref[...] = (mask_ref[...] * (hidden_ref[...].astype(F32) + branch)).astype(BF16)


def attention_forward(
    hidden, mask, gain, shift, weight, bias, key_bias, out_bias, guests, collective_id
):
    rows, width = hidden.shape
    pairs = width // PAIR
    pair = lambda i: jnp.clip(i - 3, 0, pairs - 1)
    part = lambda i: jnp.where(i < 3, (i + 1) % 3, 3)
    block = pl.BlockSpec((1, rows, PAIR), lambda i: (pair(i), 0, 0))
    saved = jax.ShapeDtypeStruct((pairs, rows, PAIR), BF16)
    full = jax.ShapeDtypeStruct((rows, width), BF16)
    in_specs = ([
            whole((rows, width)), whole((rows, 1)), whole((1, width)), whole((1, width)),
            pl.BlockSpec((width, width), lambda i: (0, part(i))),
            pl.BlockSpec((1, width), lambda i: (0, jnp.minimum(part(i), 2))),
            whole((2 * rows, 1)), whole((1, width)),
        ])
    out_specs = ([whole((rows, width))] + [block] * 4
        + [pl.BlockSpec((2, rows, PAIR), lambda i: (pair(i), 0, 0)), block, whole((rows, width))])
    out_shape = ([full] + [saved] * 4 + [
            jax.ShapeDtypeStruct((2 * pairs, rows, PAIR), BF16),
            jax.ShapeDtypeStruct((pairs, rows, PAIR), F32), full,
        ])
    scratch = ([
            pltpu.VMEM((rows, width), BF16), pltpu.VMEM((3, pairs, rows, PAIR), BF16),
            pltpu.VMEM((2, pairs, rows, PAIR), BF16), pltpu.VMEM((pairs, rows, PAIR), BF16),
            pltpu.VMEM((2, 2 * rows, PAIR), BF16), pltpu.VMEM((2, 2 * rows, PAIR), BF16),
            pltpu.SemaphoreType.DMA((2,)), pltpu.SemaphoreType.DMA((2,)),
        ])
    return hosted(
        attention_forward_body, pairs + 4, list(zip((hidden, mask, gain, shift, weight, bias, key_bias, out_bias), in_specs)), list(zip(out_shape, out_specs)), scratch,
        guests, collective_id, "attention_forward",
    )


def pair_backward(query_of, grad_of, out_of, keys, values, key_sums, value_sums, rows, save):
    lanes = lane_ids((rows, PAIR))
    parts = []
    for head in (0, 1):
        aux = HEAD_DIM * (1 - head)
        inside = (lanes // HEAD_DIM) == head
        query = query_of(head)
        grad = jnp.where(inside, grad_of().astype(F32), 0.0)
        dots = jnp.sum(grad * out_of(), axis=1, keepdims=True)
        for lane, part in enumerate(three_parts(-dots), aux):
            grad = jnp.where(lanes == lane, part, grad)
        probs = jnp.exp(contract_cols(query, keys[head]))
        shifted = contract_cols(grad.astype(BF16), values[head])
        grad_scores = (probs * shifted).astype(BF16)
        parts.append(mm(grad_scores, keys[head]) * HEAD_DIM**-0.5)
        value_sums[head] = mm(grad.T.astype(BF16), probs.astype(BF16)).T
        key_sums[head] = mm(query.astype(F32).T.astype(BF16), grad_scores).T
    save(jnp.where(lanes < HEAD_DIM, parts[0], parts[1]).astype(BF16))


def attention_backward_body(
    spot, incoming_ref, mask_ref, hidden_ref, normed_ref, key_ref, value_ref, key_far_ref, value_far_ref,
    extended_ref, attended_ref, weight_ref, gain_ref, key_bias_ref,
    weight_grad, out_ref, gain_grad, shift_grad, query_bias_grad, value_bias_grad, out_bias_grad,
    grad, grad_out, attended, normed_t, total, grads, sent, arrived, keys, values, key_sums, value_sums,
    send, recv,
):
    step, last = pl.program_id(0), pl.num_programs(0) - 1
    rows, width = grad.shape
    pairs = width // PAIR

    def swap_of(p):
        return swap_with_mate(spot, sent.at[p], arrived.at[p], send.at[p], recv.at[p])

    @pl.when(step == 0)
    def _():
        grad_rows = mask_ref[...] * incoming_ref[...].astype(F32)
        grad[...] = grad_rows.astype(BF16)
        out_bias_grad[...] = jnp.sum(grad_rows, axis=0, keepdims=True)
        for p, part in enumerate(pairs_of(mm(grad[...], weight_ref[...]).astype(BF16))):
            grad_out[p] = part

    @pl.when(step < pairs)
    def _():
        p = step
        for head in (0, 1):
            extend_keys(
                keys.at[head], values.at[head],
                [(key_ref[0], value_ref[0]), (key_far_ref[0], value_far_ref[0])], key_bias_ref, head,
            )
        attended[p] = attended_ref[0].astype(BF16)

        def save(value):
            grads[0, p] = value

        pair_backward(
            lambda head: extended_ref[head], lambda: grad_out[p], lambda: attended_ref[0],
            keys, values, key_sums, value_sums, rows, save,
        )
        first = lane_ids((rows, PAIR)) < HEAD_DIM
        for j, sums in enumerate((key_sums, value_sums)):
            grads[1 + j, p] = jnp.where(first, sums[0, :rows, :], sums[1, :rows, :]).astype(BF16)
            sent[p, j] = jnp.where(first, sums[0, rows:, :], sums[1, rows:, :]).astype(BF16)
        swap_of(p).start()

    @pl.when(step == pairs)
    def _():
        normed_t[...] = normed_ref[...].astype(F32).T.astype(BF16)
        for p in range(pairs):
            swap_of(p).wait()
            for j in (0, 1):
                grads[1 + j, p] = (grads[1 + j, p].astype(F32) + arrived[p, j].astype(F32)).astype(BF16)

    @pl.when((step >= pairs) & (step < last))
    def _():
        j = step - pairs
        part = joined(grads, (j,))
        sums = jnp.sum(part.astype(F32), axis=0, keepdims=True)

        @pl.when(j == 0)
        def _():
            query_bias_grad[...] = sums

        @pl.when(j == 2)
        def _():
            value_bias_grad[...] = sums

        weight_grad[...] = mm(normed_t[...], part).astype(BF16).reshape(weight_grad.shape)
        product = contract_cols(part, weight_ref[...])
        total[...] = jnp.where(j == 0, product, total[...] + product)

    @pl.when(step == last)
    def _():
        weight_grad[...] = contract_rows(grad[...], joined(attended)).astype(BF16).reshape(weight_grad.shape)
        grad_hidden, gain_grad[...], shift_grad[...] = norm_backward(
            hidden_ref[...].astype(F32), total[...], gain_ref[...]
        )
        out_ref[...] = (grad[...].astype(F32) + grad_hidden).astype(BF16)


def attention_backward(
    incoming, mask, hidden, normed, key, value, key_far, value_far, extended, attended, weight, gain, key_bias,
    guests, collective_id,
):
    rows, width = hidden.shape
    pairs = width // PAIR
    pair = lambda i: jnp.minimum(i, pairs - 1)
    block = pl.BlockSpec((1, rows, PAIR), lambda i: (pair(i), 0, 0))
    vector = jax.ShapeDtypeStruct((1, width), F32)
    in_specs = ([whole((rows, width)), whole((rows, 1)), whole((rows, width)), whole((rows, width))]
        + [block] * 4
        + [
            pl.BlockSpec((2, rows, PAIR), lambda i: (pair(i), 0, 0)), block,
            pl.BlockSpec((width, width), lambda i: (0, jnp.where(i < pairs, 3, jnp.minimum(i - pairs, 2)))),
            whole((1, width)), whole((2 * rows, 1)),
        ])
    out_specs = ([
            pl.BlockSpec((16, width // 16, width), lambda i: (0, 0, jnp.maximum(i - pairs, 0))),
            whole((rows, width)),
        ] + [whole((1, width))] * 5)
    out_shape = ([
            jax.ShapeDtypeStruct((16, width // 16, 4 * width), BF16), jax.ShapeDtypeStruct((rows, width), BF16),
        ] + [vector] * 5)
    scratch = ([
            pltpu.VMEM((rows, width), BF16), pltpu.VMEM((pairs, rows, PAIR), BF16),
            pltpu.VMEM((pairs, rows, PAIR), BF16), pltpu.VMEM((width, rows), BF16),
            pltpu.VMEM((rows, width), F32), pltpu.VMEM((3, pairs, rows, PAIR), BF16),
            pltpu.VMEM((pairs, 2, rows, PAIR), BF16), pltpu.VMEM((pairs, 2, rows, PAIR), BF16),
            pltpu.VMEM((2, 2 * rows, PAIR), BF16), pltpu.VMEM((2, 2 * rows, PAIR), BF16),
            pltpu.VMEM((2, 2 * rows, PAIR), F32), pltpu.VMEM((2, 2 * rows, PAIR), F32),
            pltpu.SemaphoreType.DMA((pairs,)), pltpu.SemaphoreType.DMA((pairs,)),
        ])
    return hosted(
        attention_backward_body, pairs + 4, list(zip((incoming, mask, hidden, normed, key, value, key_far, value_far, extended, attended, weight, gain, key_bias), in_specs)), list(zip(out_shape, out_specs)), scratch,
        guests, collective_id, "attention_backward",
    )


def per_device(
    clip_inputs, out_grad, clip_class, w_front, w_back, norm_gain, norm_shift,
    bias_query_value, bias_attn_out, bias_up, bias_down,
):
    spot = Spot()
    sections = lax.axis_size("section")
    padded, width = clip_inputs.shape[1:]
    rows = -(-LONG // 32) * 16
    core, section = spot.core, spot.z

    owner, slot = section // 2, section % 2
    mine = jnp.stack([lax.dynamic_index_in_dim(a, slot, 0, False) for a in (clip_inputs, out_grad)])
    far = swap(lax.dynamic_slice_in_dim(mine, (1 - core) * rows, rows, 1), 1)
    near = lax.dynamic_slice_in_dim(mine, core * rows, rows, 1)
    clip_pair = jnp.where(core == owner, near, far)
    own_class = lax.dynamic_index_in_dim(clip_class, slot, 0, False).astype(F32)
    own_class = jnp.broadcast_to(own_class, (8, 128))
    clip_kind = jnp.where(core == owner, own_class, swap(own_class, 1))[0, 0]
    length = SHORT + (LONG - SHORT) * clip_kind
    positions = jnp.arange(rows, dtype=jnp.int32)
    own_rows = (positions + core * rows).astype(F32) < length
    far_rows = (positions + (1 - core) * rows).astype(F32) < length
    row_mask = own_rows.astype(F32)[:, None]
    key_bias = jnp.where(jnp.concatenate([own_rows, far_rows]), 0.0, MASKED)[:, None]

    norms = jnp.concatenate([norm_gain, norm_shift, jnp.zeros((6, width), F32)], axis=0)
    first_front, norm_all, owns = first_weights(w_front[0], w_back[0], norms)
    fronts, downs = [first_front.reshape(width, -1)] + [None] * (sections - 1), [None] * 2
    front_shape = first_front.shape
    down_shape = (32, w_back.shape[1] // 16, width)
    gains, shifts = norm_all[:, 0], norm_all[:, 1]

    hidden = (clip_pair[0].astype(F32) * row_mask).astype(BF16)
    row = lambda a: a.reshape(1, -1)
    acts_home = jnp.zeros((clip_inputs.shape[0], padded, width), BF16)
    grads_home = jnp.zeros((clip_inputs.shape[0], 2 * rows, width), BF16)
    saved, acts = [], []
    acts_beside = {
        ("f", 1): [(0, 0, 112)], ("f", 2): [(0, 112, 496), (1, 0, 128)], ("f", 3): [(1, 128, 320), (2, 0, 288)],
        ("b", 3): [(1, 448, 160), (2, 288, 320), (3, 0, 192)], ("b", 2): [(3, 192, 416)],
    }
    grads_beside = {("b", 1): [(3, 0, 400)], ("b", 0): [(3, 400, 208), (1, 0, rows), (2, 0, 192)]}

    def travel(where, held, plan, home):
        steps = 9 if where[1] % 2 == 0 else 3
        return deliver_guest([(held[s], s, start, size) for s, start, size in plan[where]], home, steps)

    for s in range(sections):
        layer = s // 2
        gain, shift = row(gains[s]), row(shifts[s])
        guests = []
        if s == 0:
            guests.append(plane_gather_guest([(owns["front", 1], 0, 0)], [front_shape], [(0, 5, 7)]))
            guests.append(spread_gather_guest(
                [(owns["back", 0], 0, (0, 4), (6, 9, 9), 0), (owns["back", 1], 1, (0,), (4, 8, 9), 16)], down_shape
            ))
        elif s == 2:
            parts = [(owns["front", 3], 0, 0), (owns["back", 2], 1, 0), (owns["back", 3], 1, 16)]
            guests.append(plane_gather_guest(parts, [front_shape, down_shape], [(0, 5, 8), (0, 7, 9), (0, 8, 9)]))
        elif s == 1:
            guests.append(plane_gather_guest([(owns["front", 2], 0, 0)], [front_shape], [(0, 3, 3)]))
        onward = {0: [("front", 2), ("front", 3), ("back", 2), ("back", 3)], 1: [("front", 3), ("back", 3)]}.get(s, [])
        if onward:
            hops = [(i, key[1], 2 + s, "both") for i, key in enumerate(onward)]
            if s == 0:
                hops.insert(0, (0, 2, 1, "up"))
            guests.append(spread_hop_guest([owns[key] for key in onward], hops))
        if s:
            guests.append(travel(("f", s), acts, acts_beside, acts_home))
        if s % 2 == 0:
            pair = bias_query_value[layer]
            bias = jnp.concatenate([pair[:width], jnp.zeros((width,), F32), pair[width:]])
            (*kept, leaving), carried = attention_forward(
                hidden, row_mask, gain, shift, fronts[s], row(bias), key_bias, row(bias_attn_out[layer]),
                guests, 2 + s,
            )
        else:
            (*kept, leaving), carried = ff_forward(
                hidden, row_mask, gain, shift, fronts[s], row(bias_up[layer]), downs[layer], row(bias_down[layer]),
                guests, 2 + s,
            )
        if s:
            (acts_home,) = carried[-1]
        if s == 0:
            fronts[1], downs[0] = carried[0][0].reshape(width, -1), carried[1][-1].reshape(-1, width)
        elif s == 2:
            fronts[3], downs[1] = carried[0][0].reshape(width, -1), carried[0][1].reshape(-1, width)
        elif s == 1:
            fronts[2] = carried[0][0].reshape(width, -1)
        if onward:
            owns.update(zip(onward, carried[2 - s]))
        saved.append((hidden, *kept))
        hidden = leaving
        acts.append(leaving)

    incoming = clip_pair[1]
    input_grads, grad_fronts, grad_downs = [None] * sections, [None] * sections, [None] * 2
    grad_gain, grad_shift = [None] * sections, [None] * sections
    query_sums, value_sums, out_sums, up_sums, down_sums = ([None] * 2 for _ in range(5))
    plane_stages = {
        2: ((0, 1, 4, 8), (0, 2, 6, 9), (0, 2, 7, 9)), 1: ((0, 1, 3, 3),), 0: ((0, 1, 4, 8), (0, 2, 6, 9), (0, 2, 7, 9)),
    }
    for s in reversed(range(sections)):
        layer, gain = s // 2, row(gains[s])
        guests = []
        if s < 3:
            jobs = [(grad_fronts[s + 1], 0)]
            if s % 2 == 0:
                jobs += [(grad_downs[layer], 0), (grad_downs[layer], 16)]
            guests.append(plane_sum_guest(jobs, plane_stages[s]))
        if s < 2:
            hops = {1: [(3, 0), (2, 0), (3, 0)], 0: [(3, 1), (2, 1), (3, 1), (2, 0)]}[s]
            guests.append(section_hop_guest([(part, target, done + 1) for part, (target, done) in zip(passing, hops)]))
        if ("b", s) in acts_beside:
            guests.append(travel(("b", s), acts, acts_beside, acts_home))
        else:
            guests.append(travel(("b", s), input_grads, grads_beside, grads_home))
        if s % 2 == 0:
            entered, normed, key, value, key_far, value_far, extended, attended = saved[s]
            (
                grad_fronts[s], incoming, grad_gain[s], grad_shift[s],
                query_sums[layer], value_sums[layer], out_sums[layer],
            ), carried = attention_backward(
                incoming, row_mask, entered, normed, key, value, key_far, value_far, extended, attended,
                fronts[s], gain, key_bias, guests, 6 + s,
            )
        else:
            entered, act, slope, normed = saved[s]
            (
                grad_fronts[s], grad_downs[layer], incoming, grad_gain[s], grad_shift[s],
                up_sums[layer], down_sums[layer],
            ), carried = ff_backward(
                incoming, row_mask, entered, normed, act, slope, fronts[s], downs[layer], gain, guests, 6 + s
            )
        input_grads[s] = incoming
        if ("b", s) in acts_beside:
            (acts_home,) = carried[-1]
        else:
            (grads_home,) = carried[-1]
        if s == 2:
            passing = carried[0]
        elif s == 1:
            passing = [*carried[1], *carried[0]]
        elif s == 0:
            (front_3, back_2, back_3, front_2), (front_1, back_0, back_1) = carried[1], carried[0]

    pair_sums = [jnp.concatenate([q, v], axis=1) for q, v in zip(query_sums, value_sums)]
    small = jnp.concatenate(
        [v.reshape(-1) for v in grad_gain + grad_shift + pair_sums + out_sums + up_sums + down_sums]
    )
    grads_home, front_out, back_out, small = collect(
        input_grads[0], input_grads[2], grads_home, grad_fronts[0],
        [front_3, back_3, front_2, back_2, front_1, back_0, back_1], small.reshape(-1, 128),
    )
    front_out = front_out.reshape(width, -1)
    back_out = back_out.reshape(-1, width)
    small = small.reshape(-1)
    for bit in spot.spare_bits:
        small = small + swap(small, bit)
        front_out, back_out = add(front_out, swap(front_out, bit)), add(back_out, swap(back_out, bit))
    grads_out = jnp.pad(grads_home.astype(F32), ((0, 0), (0, padded - 2 * rows), (0, 0)))
    parts, place_at = [], 0
    layers, hidden_units = bias_up.shape
    for count, size in (
        (sections, width), (sections, width), (layers, 2 * width), (layers, width),
        (layers, hidden_units), (layers, width),
    ):
        parts.append(small[place_at : place_at + count * size].reshape(count, size))
        place_at += count * size
    return (
        acts_home[None],
        grads_out[None],
        front_out.astype(F32)[None],
        back_out.astype(F32)[None],
        lax.dynamic_slice_in_dim(parts[0], section, 1, 0),
        lax.dynamic_slice_in_dim(parts[1], section, 1, 0),
        *parts[2:],
    )


def solution(mesh):
    placed = (
        P("dp", None, None), P("dp", None, None), P("dp"),
        P("section", None, None), P("section", None, None), P("section", None), P("section", None),
        P(), P(), P(), P(),
    )
    return jax.shard_map(
        per_device,
        mesh=mesh,
        in_specs=placed,
        out_specs=(
            P("section", "dp", None, None), P("section", "dp", None, None),
            P("section", None, None), P("section", None, None), P("section", None), P("section", None),
            P(), P(), P(), P(),
        ),
        check_vma=False,
    )
```

```python
import functools
import math

import jax
import jax.numpy as jnp
from jax import lax
from jax.experimental import pallas as pl
from jax.experimental.pallas import tpu as pltpu
from jax.sharding import PartitionSpec as P

HEADS = 12
LONG = 1214
SHORT = 514
EPS = 1e-06
HEAD_DIM = 64
PAIR = 2 * HEAD_DIM
MASKED = -1e30
F32 = jnp.float32
BF16 = jnp.bfloat16
KERNEL_VMEM = 56 * 2**20


def mm(left, right):
    return jnp.dot(left, right, preferred_element_type=F32)


def contract_rows(left, right):
    return lax.dot_general(left, right, (((0,), (0,)), ((), ())), preferred_element_type=F32)


def contract_cols(left, right):
    return lax.dot_general(left, right, (((1,), (1,)), ((), ())), preferred_element_type=F32)


def swap(block, bit):
    count = lax.axis_size("dp")
    return lax.ppermute(block, "dp", [(i, i ^ bit) for i in range(count)])


def add(a, b):
    return (a.astype(F32) + b.astype(F32)).astype(BF16)


class Spot:
    def __init__(self):
        self.z, self.sections = lax.axis_index("section"), lax.axis_size("section")
        self.d, self.count = lax.axis_index("dp"), lax.axis_size("dp")
        self.x_bit, self.y_bit = 2, 2 * math.isqrt(self.count // 2)
        self.core = self.d % 2
        self.xb, self.yb = (self.d // self.x_bit) % 2, (self.d // self.y_bit) % 2
        self.c, self.c_x = self.yb * 2 + self.xb, self.yb * 2 + 1 - self.xb
        self.c_y, self.c_d = (1 - self.yb) * 2 + self.xb, (1 - self.yb) * 2 + 1 - self.xb
        self.mate, self.x, self.y = (self.flipped(b) for b in (1, self.x_bit, self.y_bit))
        self.above, self.below = {"section": self.z + 1}, {"section": self.z - 1}
        self.spare_bits = [
            1 << i for i in range(self.count.bit_length() - 1) if 1 << i not in (1, self.x_bit, self.y_bit)
        ]

    def flipped(self, bit):
        return {"dp": self.d + bit * (1 - 2 * ((self.d // bit) % 2))}

    def greet_mate(self):
        barrier = pltpu.get_barrier_semaphore()
        pl.semaphore_signal(barrier, inc=1, device_id=self.mate, device_id_type=pl.DeviceIdType.MESH)
        pl.semaphore_wait(barrier, 1)

    def greet(self):
        barrier = pltpu.get_barrier_semaphore()
        devices = [self.x, self.y]
        for step in range(self.sections):
            for core in (0, 1):
                if step or core:
                    devices.append({
                        "section": (self.z + step) % self.sections,
                        "dp": self.d - self.core + (self.core + core) % 2,
                    })
        for device in devices:
            pl.semaphore_signal(barrier, inc=1, device_id=device, device_id_type=pl.DeviceIdType.MESH)
        pl.semaphore_wait(barrier, len(devices))


def remote(src, dst, send, recv, device):
    return pltpu.make_async_remote_copy(
        src_ref=src, dst_ref=dst, send_sem=send, recv_sem=recv,
        device_id=device, device_id_type=pl.DeviceIdType.MESH,
    )


class PlaneGather:
    SENDS, RECEIVES = 9, 9

    def __init__(self, spot, dst, send, recv):
        self.spot, self.dst, self.send, self.recv = spot, dst, send, recv

    def blocks(self, core, chip, half=None):
        at = core * 8 + chip * 2
        return pl.ds(at, 2) if half is None else pl.ds(at + half, 1)

    def copies(self, own=None):
        s, k = self.spot, self.spot.core
        plan = {
            "x": (self.blocks(k, s.c), s.x), "y": (self.blocks(k, s.c), s.y),
            "m": (self.blocks(k, s.c), s.mate),
            "xy": (self.blocks(k, s.c_x, 0), s.y), "yx": (self.blocks(k, s.c_y, 1), s.x),
            "mx": (self.blocks(k, s.c_x), s.mate), "my": (self.blocks(k, s.c_y), s.mate),
            "md0": (self.blocks(k, s.c_d, 0), s.mate), "md1": (self.blocks(k, s.c_d, 1), s.mate),
        }
        out = {}
        for index, (name, (rows, device)) in enumerate(plan.items()):
            src = own if own is not None and name in ("x", "y", "m") else self.dst.at[rows]
            out[name] = remote(src, self.dst.at[rows], self.send.at[index], self.recv.at[index], device)
        return out

    def arrivals(self):
        s, k = self.spot, self.spot.core
        plan = {
            "x": self.blocks(k, s.c_x), "y": self.blocks(k, s.c_y), "m": self.blocks(1 - k, s.c),
            "xy": self.blocks(k, s.c_d, 0), "yx": self.blocks(k, s.c_d, 1),
            "mx": self.blocks(1 - k, s.c_x), "my": self.blocks(1 - k, s.c_y),
            "md0": self.blocks(1 - k, s.c_d, 0), "md1": self.blocks(1 - k, s.c_d, 1),
        }
        return {
            name: remote(self.dst.at[rows], self.dst.at[rows], self.send.at[i], self.recv.at[i], s.mate)
            for i, (name, rows) in enumerate(plan.items())
        }

    def begin(self, own):
        copies = self.copies(own)
        for name in ("x", "y", "m"):
            copies[name].start()

    def second(self):
        copies, arrivals = self.copies(), self.arrivals()
        arrivals["x"].wait_recv()
        copies["xy"].start()
        copies["mx"].start()
        arrivals["y"].wait_recv()
        copies["yx"].start()
        copies["my"].start()

    def third(self):
        copies, arrivals = self.copies(), self.arrivals()
        for name, after in (("xy", "md0"), ("yx", "md1")):
            arrivals[name].wait_recv()
            copies[after].start()

    def finish(self):
        copies, arrivals = self.copies(), self.arrivals()
        for name in copies:
            copies[name].wait_send()
        for name in ("m", "mx", "my", "md0", "md1"):
            arrivals[name].wait_recv()


class Deliver:
    def __init__(self, spot, src, dst, target, send, recv, start=0, size=None):
        self.spot, self.src, self.dst, self.target, self.send, self.recv = spot, src, dst, target, send, recv
        self.rows, self.start_row = src.shape[0], start
        self.size = size or src.shape[0]
        self.owner, self.slot = spot.z // 2, spot.z % 2
        self.home = (spot.z == target) & (spot.core == self.owner)

    def place(self, slot, core):
        at = pl.multiple_of(core * self.rows + self.start_row, 16)
        return self.dst.at[slot, pl.ds(at, self.size)]

    def copies(self):
        s, spot = self, self.spot
        spot_at, src = s.place(s.slot, spot.core), s.src.at[pl.ds(s.start_row, s.size)]
        away = remote(
            src, spot_at, s.send.at[0], s.recv.at[s.slot * 2 + spot.core],
            {"section": s.target, "dp": spot.d - spot.core + s.owner},
        )
        return away, pltpu.make_async_copy(src, spot_at, s.send.at[1])

    def start(self):
        away, stay = self.copies()
        pl.when(self.home)(stay.start)
        pl.when(jnp.logical_not(self.home))(away.start)

    def finish(self):
        away, stay = self.copies()
        pl.when(self.home)(stay.wait)
        pl.when(jnp.logical_not(self.home))(away.wait_send)
        spot = self.spot
        for slot in (0, 1):
            for core in (0, 1):
                here = (spot.core * 2 + slot == spot.z) & (spot.core == core)
                block = self.place(slot, core)
                landing = remote(block, block, self.send.at[0], self.recv.at[slot * 2 + core], spot.mate)
                pl.when((spot.z == self.target) & jnp.logical_not(here))(landing.wait_recv)


class Guest:
    def __init__(self, inputs=(), outputs=(), scratch=(), aliases=(), plan=None):
        self.inputs, self.outputs, self.scratch = list(inputs), list(outputs), list(scratch)
        self.aliases, self.plan = list(aliases), plan


def hbm_spec():
    return pl.BlockSpec(memory_space=pl.ANY)


def vmem_spec():
    return pl.BlockSpec(memory_space=pltpu.VMEM)


def hosted(body, grid, operands, results, scratch, guests, collective_id, name, vmem=KERNEL_VMEM):
    guest_in = [pair for g in guests for pair in g.inputs]
    guest_out = [pair for g in guests for pair in g.outputs]
    guest_scratch = [s for g in guests for s in g.scratch]
    aliases, at_in, at_out = {}, len(operands), len(results)
    for g in guests:
        for i, o in g.aliases:
            aliases[at_in + i] = at_out + o
        at_in, at_out = at_in + len(g.inputs), at_out + len(g.outputs)

    def kernel(*refs):
        refs = list(refs)
        take = lambda n: [refs.pop(0) for _ in range(n)]
        ins, gins = take(len(operands)), take(len(guest_in))
        outs, gouts = take(len(results)), take(len(guest_out))
        held, gheld = take(len(scratch)), take(len(guest_scratch))
        spot, step = Spot(), pl.program_id(0)
        pl.when(step == 0)(spot.greet)
        hooks = {}
        for g in guests:
            parts = [[r.pop(0) for _ in range(n)] for r, n in (
                (gins, len(g.inputs)), (gouts, len(g.outputs)), (gheld, len(g.scratch))
            )]
            for at, actions in g.plan(spot, *parts).items():
                hooks.setdefault(at, []).extend(actions)

        def run(actions):
            for action in actions:
                action()

        for at in sorted(k for k in hooks if k != "end"):
            pl.when(step == at)(functools.partial(run, hooks[at]))
        body(spot, *ins, *outs, *held)
        if "end" in hooks:
            pl.when(step == grid - 1)(functools.partial(run, hooks["end"]))

    out = pl.pallas_call(
        kernel,
        grid=(grid,),
        in_specs=[s for _, s in operands + guest_in],
        out_specs=[s for _, s in results + guest_out],
        out_shape=[s for s, _ in results + guest_out],
        scratch_shapes=list(scratch) + guest_scratch,
        input_output_aliases=aliases,
        compiler_params=pltpu.CompilerParams(
            vmem_limit_bytes=vmem, collective_id=collective_id, has_side_effects=True
        ),
        name=name,
    )(*[a for a, _ in operands + guest_in])
    own, rest, per_guest = out[: len(results)], list(out[len(results) :]), []
    for g in guests:
        per_guest.append([rest.pop(0) for _ in g.outputs])
    return own, per_guest


def deliver_guest(pieces, home, steps):
    sems = pltpu.SemaphoreType.DMA
    count = len(pieces)

    def plan(spot, ins, outs, held):
        send, recv = held
        hooks = {}
        for i, (_, target, first, size) in enumerate(pieces):
            blocks = size // 16
            for step in range(steps):
                low, high = blocks * step // steps, blocks * (step + 1) // steps
                if high > low:
                    part = Deliver(
                        spot, ins[i], outs[0], target, send.at[i], recv.at[i], first + 16 * low, 16 * (high - low)
                    )
                    hooks.setdefault(step, []).append(part.start)
            every = Deliver(spot, ins[i], outs[0], target, send.at[i], recv.at[i], first, size)
            hooks.setdefault("end", []).append(every.finish)
        return hooks

    return Guest(
        [(piece[0], hbm_spec()) for piece in pieces] + [(home, hbm_spec())],
        [(jax.ShapeDtypeStruct(home.shape, home.dtype), hbm_spec())],
        [sems((count, 2)), sems((count, 4))],
        [(count, 0)], plan,
    )


def plane_sum_guest(jobs, stages):
    sems = pltpu.SemaphoreType.DMA
    shapes = [(a.shape[1], a.shape[2]) for a, _ in jobs]
    arrays = []
    for a, _ in jobs:
        if not any(a is b for b in arrays):
            arrays.append(a)
    index = [next(i for i, b in enumerate(arrays) if b is a) for a, _ in jobs]

    def plan(spot, ins, outs, held):
        send, recv = held[-2:]
        hooks = {}
        for i, (_, first) in enumerate(jobs):
            src = ins[index[i]].at[pl.ds(first, 16)]
            job = PlaneSum(spot, src, held[6 * i : 6 * i + 6], send.at[i], recv.at[i])
            actions = (job.start, job.first, job.second, functools.partial(job.third, outs[i]))
            for at, action in zip(stages[i], actions):
                hooks.setdefault(at, []).append(action)
            hooks.setdefault("end", []).append(job.finish)
        return hooks

    return Guest(
        [(a, hbm_spec()) for a in arrays],
        [(jax.ShapeDtypeStruct((2,) + s, BF16), vmem_spec()) for s in shapes],
        [b for s in shapes for b in PlaneSum.scratch(*s)] + [sems((len(jobs), 8)), sems((len(jobs), 8))],
        (), plan,
    )


def section_hop_guest(jobs, start=0):
    sems = pltpu.SemaphoreType.DMA

    def plan(spot, ins, outs, held):
        send, recv = held[-2:]
        hops = [
            SectionHop(spot, ins[i], outs[i], held[i], target, hop, send.at[i], recv.at[i])
            for i, (_, target, hop) in enumerate(jobs)
        ]
        return {start: [h.start for h in hops], "end": [h.finish for h in hops]}

    return Guest(
        [(a, vmem_spec()) for a, _, _ in jobs],
        [(jax.ShapeDtypeStruct(a.shape, BF16), vmem_spec()) for a, _, _ in jobs],
        [pltpu.VMEM((2 * a.shape[0],) + a.shape[1:], BF16) for a, _, _ in jobs]
        + [sems((len(jobs),)), sems((len(jobs), 2))],
        (), plan,
    )


def add_into(target, *others):
    def step(b, carry):
        total = target[b].astype(F32)
        for other in others:
            total = total + other[b].astype(F32)
        target[b] = total.astype(BF16)
        return carry

    lax.fori_loop(0, target.shape[0], step, 0)


class PlaneSum:
    def __init__(self, spot, src, bufs, send, recv):
        self.spot, self.src, self.send, self.recv = spot, src, send, recv
        self.half, self.from_mate, self.in_x, self.in_y, self.in_yx, self.in_xy = bufs

    @staticmethod
    def scratch(block_rows, columns):
        return [pltpu.VMEM((n, block_rows, columns), BF16) for n in (8, 8, 2, 2, 1, 1)]

    def mate_copies(self):
        s, spot = self, self.spot
        return (
            pltpu.make_async_copy(s.src.at[pl.ds(spot.core * 8, 8)], s.half, s.send.at[0]),
            remote(s.src.at[pl.ds((1 - spot.core) * 8, 8)], s.from_mate, s.send.at[1], s.recv.at[1], spot.mate),
        )

    def start(self):
        for copy in self.mate_copies():
            copy.start()

    def block(self, chip, half):
        return self.half.at[pl.ds(chip * 2 + half, 1)]

    def first_copies(self):
        s, spot = self, self.spot
        first, second = pl.ds(0, 1), pl.ds(1, 1)
        return (
            remote(s.block(spot.c_x, 0), s.in_x.at[first], s.send.at[2], s.recv.at[2], spot.x),
            remote(s.block(spot.c_d, 0), s.in_x.at[second], s.send.at[3], s.recv.at[3], spot.x),
            remote(s.block(spot.c_y, 1), s.in_y.at[first], s.send.at[4], s.recv.at[4], spot.y),
            remote(s.block(spot.c_d, 1), s.in_y.at[second], s.send.at[5], s.recv.at[5], spot.y),
        )

    def second_copies(self):
        s, spot = self, self.spot
        return (
            remote(s.block(spot.c_y, 0), s.in_xy, s.send.at[6], s.recv.at[6], spot.y),
            remote(s.block(spot.c_x, 1), s.in_yx, s.send.at[7], s.recv.at[7], spot.x),
        )

    def first(self):
        for copy in self.mate_copies():
            copy.wait()
        add_into(self.half, self.from_mate)
        for copy in self.first_copies():
            copy.start()

    def second(self):
        s, spot = self, self.spot
        for copy in self.first_copies():
            copy.wait_recv()
        first, other = pl.ds(0, 1), pl.ds(1, 1)
        add_into(s.block(spot.c_y, 0), s.in_x.at[other])
        add_into(s.block(spot.c_x, 1), s.in_y.at[other])
        for copy in self.second_copies():
            copy.start()

    def third(self, out):
        s, spot = self, self.spot
        for copy in self.second_copies():
            copy.wait_recv()
        first = pl.ds(0, 1)
        add_into(s.block(spot.c, 0), s.in_x.at[first], s.in_xy)
        add_into(s.block(spot.c, 1), s.in_y.at[first], s.in_yx)
        out[...] = s.half[pl.ds(spot.c * 2, 2)]

    def finish(self):
        for copy in self.first_copies() + self.second_copies():
            copy.wait_send()


class SectionHop:
    def __init__(self, spot, src, total, bufs, target, hop, send, recv):
        self.spot, self.src, self.total, self.bufs, self.send, self.recv = spot, src, total, bufs, send, recv
        last = spot.sections - 1
        self.below = hop - 1 if hop <= target else None
        self.above = last - hop + 1 if last - hop >= target else None

    def copies(self):
        s, spot, n = self, self.spot, self.src.shape[0]
        up = remote(s.src, s.bufs.at[pl.ds(n, n)], s.send, s.recv.at[1], spot.above)
        down = remote(s.src, s.bufs.at[pl.ds(0, n)], s.send, s.recv.at[0], spot.below)
        return up, down

    def start(self):
        up, down = self.copies()
        if self.below is not None:
            pl.when(self.spot.z == self.below)(up.start)
        if self.above is not None:
            pl.when(self.spot.z == self.above)(down.start)
        self.total[...] = self.src[...]

    def finish(self):
        up, down = self.copies()
        n = self.src.shape[0]
        if self.below is not None:
            pl.when(self.spot.z == self.below)(up.wait_send)

            @pl.when(self.spot.z == self.below + 1)
            def _():
                up.wait_recv()
                add_into(self.total, self.bufs.at[pl.ds(n, n)])
        if self.above is not None:
            pl.when(self.spot.z == self.above)(down.wait_send)

            @pl.when(self.spot.z == self.above - 1)
            def _():
                down.wait_recv()
                add_into(self.total, self.bufs.at[pl.ds(0, n)])


LEFT = (("front", 3, 2), ("back", 3, 2), ("front", 2, 1), ("back", 2, 2), ("front", 1, 0), ("back", 0, 0), ("back", 1, 0))


def collect_body(*refs):
    sections = lax.axis_size("section")
    refs_list = list(refs)
    take = lambda n: [refs_list.pop(0) for _ in range(n)]
    last, second, first_front = take(3)
    parts = take(len(LEFT))
    small, _ = take(2)
    home, front_out, back_out, small_out = take(4)
    plane_bufs, own, (sums, arriving) = take(6), take(1)[0], take(2)
    psend, precv, dsend, drecv, asend, arecv, ssend, srecv, stay_sem, zsend, zrecv = take(11)
    hop_refs = refs_list
    spot = Spot()
    spot.greet()
    delivers = [
        Deliver(spot, piece, home, target, dsend.at[target // 2], drecv.at[target // 2], *rows)
        for piece, target, rows in ((last, 0, ()), (second, 2, (192, second.shape[0] - 192)))
    ]
    plane = PlaneSum(spot, first_front, plane_bufs, psend, precv)
    count = 0

    def chain(src, target, done):
        nonlocal count
        hops = []
        for hop in range(done + 1, max(target, sections - 1 - target) + 1):
            total, bufs = hop_refs.pop(0), hop_refs.pop(0)
            hops.append(SectionHop(spot, src, total, bufs, target, hop, zsend.at[count], zrecv.at[count]))
            src, count = total, count + 1
        return hops, src

    chains = [chain(part, target, done) for part, (_, target, done) in zip(parts, LEFT)]
    first_chains = [chain(own.at[pl.ds(i, 1)], 0, 0) for i in (0, 1)]

    def turn(which, i):
        for hops, _ in which:
            if 0 < i <= len(hops):
                hops[i - 1].finish()
        for hops, _ in which:
            if i < len(hops):
                hops[i].start()

    plane.start()
    turn(chains, 0)
    sums[0] = small[...]
    partners = [spot.mate, spot.x, spot.y] + [
        {"section": spot.z + bit * (1 - 2 * ((spot.z // bit) % 2))}
        for bit in (1 << i for i in range((sections - 1).bit_length()))
    ]

    def small_step(i):
        copy = remote(sums.at[i], arriving.at[i], ssend.at[i], srecv.at[i], partners[i])
        copy.start()
        copy.wait()
        sums[i + 1] = sums[i] + arriving[i]

    small_step(0)
    plane.first()
    for deliver in delivers:
        deliver.start()
    turn(chains, 1)
    for i in range(1, len(partners)):
        small_step(i)
    small_out[...] = sums[len(partners)]
    plane.second()
    turn(chains, 2)
    plane.third(own)
    turn(first_chains[:1], 0)
    turn(first_chains[1:], 0)
    turn(chains, 3)
    gathers = [
        PlaneGather(spot, out, asend.at[i], arecv.at[i]) for i, out in enumerate((front_out, back_out))
    ]
    ends = {(kind, target): end for (kind, target, _), (_, end) in zip(LEFT, chains)}
    stays = []

    def begin(i, kind):
        gather = gathers[i]
        for z in range(sections):
            blocks = gather.blocks(spot.core, spot.c)
            if kind == "front" and z == 0:
                pieces = [
                    (end, gather.dst.at[gather.blocks(spot.core, spot.c, half)], stay_sem.at[half])
                    for half, (_, end) in enumerate(first_chains)
                ]
            else:
                pieces = [(ends[kind, z], gather.dst.at[blocks], stay_sem.at[2 + i])]
            copies = [pltpu.make_async_copy(*piece) for piece in pieces]

            @pl.when(spot.z == z)
            def _(gather=gather, copies=copies):
                for copy in copies:
                    copy.start()
                for copy in copies:
                    copy.wait()
                gather.begin(gather.dst.at[gather.blocks(spot.core, spot.c)])

    begin(1, "back")
    turn(first_chains[:1], 1)
    turn(first_chains[1:], 1)
    gathers[1].second()
    turn(first_chains[:1], 2)
    turn(first_chains[1:], 2)
    gathers[1].third()
    turn(first_chains[:1], 3)
    turn(first_chains[1:], 3)
    begin(0, "front")
    gathers[0].second()
    gathers[0].third()
    for gather in gathers:
        gather.finish()
    for deliver in delivers:
        deliver.finish()
    plane.finish()


def collect(last, second, home, first_front, parts, small):
    sections = lax.axis_size("section")
    hbm, vmem = hbm_spec(), vmem_spec()
    steps = 3 + (sections - 1).bit_length()
    sems = pltpu.SemaphoreType.DMA
    front_shape = first_front.shape
    back_shape = (16,) + parts[1].shape[1:]
    hop_scratch, hops = [], 0
    jobs = [(p.shape, target, done) for p, (_, target, done) in zip(parts, LEFT)]
    for shape, target, done in jobs + [((1,) + front_shape[1:], 0, 0)] * 2:
        for _ in range(done, max(target, sections - 1 - target)):
            hop_scratch += [pltpu.VMEM(shape, BF16), pltpu.VMEM((2 * shape[0],) + shape[1:], BF16)]
            hops += 1
    return pl.pallas_call(
        collect_body,
        in_specs=[hbm] * 3 + [vmem] * (len(parts) + 1) + [hbm],
        out_specs=[hbm] * 3 + [vmem],
        out_shape=[
            jax.ShapeDtypeStruct(home.shape, BF16), jax.ShapeDtypeStruct(front_shape, BF16),
            jax.ShapeDtypeStruct(back_shape, BF16), jax.ShapeDtypeStruct(small.shape, F32),
        ],
        scratch_shapes=PlaneSum.scratch(*front_shape[1:])
        + [
            pltpu.VMEM((2,) + front_shape[1:], BF16),
            pltpu.VMEM((steps + 1,) + small.shape, F32), pltpu.VMEM((steps,) + small.shape, F32),
            sems((8,)), sems((8,)), sems((2, 2)), sems((2, 4)),
            sems((2, 9)), sems((2, 9)), sems((steps,)), sems((steps,)), sems((4,)),
            sems((hops,)), sems((hops, 2)),
        ]
        + hop_scratch,
        input_output_aliases={4 + len(parts): 0},
        compiler_params=pltpu.CompilerParams(
            collective_id=1, has_side_effects=True, vmem_limit_bytes=KERNEL_VMEM
        ),
        name="collect",
    )(last, second, first_front, *parts, small, home)


def norm_rows(hidden):
    average = jnp.mean(hidden, axis=-1, keepdims=True)
    centred = hidden - average
    inverse = lax.rsqrt(jnp.mean(centred * centred, axis=-1, keepdims=True) + EPS)
    return centred * inverse, inverse


def norm_backward(hidden, grad_normed, gain):
    unit, inverse = norm_rows(hidden)
    scaled = grad_normed * gain
    first = jnp.mean(scaled, axis=-1, keepdims=True)
    second = jnp.mean(scaled * unit, axis=-1, keepdims=True)
    return (
        inverse * (scaled - first - unit * second),
        jnp.sum(grad_normed * unit, axis=0, keepdims=True),
        jnp.sum(grad_normed, axis=0, keepdims=True),
    )


def gelu_and_slope(pre):
    density = jnp.exp(-0.5 * pre * pre)
    t = 1.0 / (1.0 + (0.3275911 * 0.5**0.5) * jnp.abs(pre))
    series = t * (0.127414796 + t * (-0.142248368 + t * (0.7107068705 + t * (-0.7265760135 + t * 0.5307027145))))
    tail = series * density
    below = jnp.where(pre < 0, tail, 1.0 - tail)
    return pre * below, below + pre * density * (1.0 / math.sqrt(2.0 * math.pi))


def pairs_of(block):
    return [block[:, p * PAIR : (p + 1) * PAIR] for p in range(block.shape[1] // PAIR)]


def joined(ref, lead=()):
    return jnp.concatenate([ref[lead + (p,)] for p in range(ref.shape[len(lead)])], axis=1)


def whole(shape):
    return pl.BlockSpec(shape, lambda i: (0,) * len(shape))


def swap_with_mate(spot, src, dst, send, recv):
    return remote(src, dst, send, recv, spot.mate)


def transposed_norm(hidden_ref, norm_ref):
    unit, _ = norm_rows(hidden_ref[0].astype(F32))
    normed = (unit * norm_ref[0, 0:1, :] + norm_ref[0, 1:2, :]).astype(BF16)
    return normed.astype(F32).T.astype(BF16)


def ff_backward_body(
    spot, incoming_ref, mask_ref, hidden_ref, act_ref, slope_ref, up_ref, down_ref, norm_ref,
    up_grad, down_grad, out_ref, gain_grad, shift_grad, up_bias_grad, down_bias_grad,
    grad, normed_t, total,
):
    step, last = pl.program_id(0), pl.num_programs(0) - 1

    @pl.when(step == 0)
    def _():
        grad_rows = mask_ref[...] * incoming_ref[...].astype(F32)
        grad[...] = grad_rows.astype(BF16)
        down_bias_grad[...] = jnp.sum(grad_rows, axis=0, keepdims=True)
        normed_t[...] = transposed_norm(hidden_ref, norm_ref)

    width = grad.shape[1]
    up, down = up_ref[0].reshape(width, width), down_ref[0].reshape(width, width)
    grad_pre = (contract_cols(grad[...], down) * slope_ref[0].astype(F32)).astype(BF16)
    down_grad[...] = contract_rows(act_ref[0], grad[...]).astype(BF16).reshape(down_grad.shape)
    up_bias_grad[...] = jnp.sum(grad_pre.astype(F32), axis=0, keepdims=True)
    up_grad[...] = mm(normed_t[...], grad_pre).astype(BF16).reshape(up_grad.shape)
    part = contract_cols(grad_pre, up)
    total[...] = jnp.where(step == 0, part, total[...] + part)

    @pl.when(step == last)
    def _():
        grad_hidden, gain_grad[...], shift_grad[...] = norm_backward(
            hidden_ref[0].astype(F32), total[...], norm_ref[0, 0:1, :]
        )
        out_ref[...] = (grad[...].astype(F32) + grad_hidden).astype(BF16)


def ff_backward(incoming, mask, hidden, act, slope, fronts, downs, norms, s, guests, collective_id):
    rows, width = incoming.shape
    units, size, layer = fronts.shape[3], width, s // 2
    columns = pl.BlockSpec((1, rows, size), lambda i: (layer, 0, i))
    vector = jax.ShapeDtypeStruct((1, width), F32)
    in_specs = [
        whole((rows, width)), whole((rows, 1)), pl.BlockSpec((1, rows, width), lambda i: (s, 0, 0)), columns, columns,
        pl.BlockSpec((1, 16, width // 16, size), lambda i: (s, 0, 0, i)),
        pl.BlockSpec((1, size * 32 // units, units // 32, width), lambda i: (layer, i, 0, 0)),
        pl.BlockSpec((1,) + norms.shape[1:], lambda i: (s, 0, 0)),
    ]
    out_specs = ([
            pl.BlockSpec((16, width // 16, size), lambda i: (0, 0, i)),
            pl.BlockSpec((size * 32 // units, units // 32, width), lambda i: (i, 0, 0)),
            whole((rows, width)), whole((1, width)), whole((1, width)),
            pl.BlockSpec((1, size), lambda i: (0, i)), whole((1, width)),
        ])
    out_shape = ([
            jax.ShapeDtypeStruct((16, width // 16, units), BF16), jax.ShapeDtypeStruct((32, units // 32, width), BF16),
            jax.ShapeDtypeStruct((rows, width), BF16), vector, vector,
            jax.ShapeDtypeStruct((1, units), F32), vector,
        ])
    scratch = ([
            pltpu.VMEM((rows, width), BF16), pltpu.VMEM((width, rows), BF16), pltpu.VMEM((rows, width), F32),
        ])
    return hosted(
        ff_backward_body, units // size, list(zip((incoming, mask, hidden, act, slope, fronts, downs, norms), in_specs)), list(zip(out_shape, out_specs)), scratch,
        guests, collective_id, "ff_backward",
    )


def lane_ids(shape):
    return lax.broadcasted_iota(jnp.int32, shape, len(shape) - 1)


def three_parts(value):
    high = value.astype(BF16).astype(F32)
    rest = value - high
    middle = rest.astype(BF16).astype(F32)
    return high, middle, rest - middle


def extend_keys(keys_out, values_out, blocks, bias_ref, head):
    aux = HEAD_DIM * (1 - head)
    row = 0
    for key, value in blocks:
        rows = key.shape[0]
        span = slice(row, row + rows)
        lanes = lane_ids((rows, PAIR))
        inside = (lanes // HEAD_DIM) == head
        ones = jnp.where((lanes > aux) & (lanes <= aux + 3), 1.0, 0.0)
        extra = jnp.where(lanes == aux, bias_ref[span, :], ones)
        keys_out[span, :] = jnp.where(inside, key.astype(F32), extra).astype(BF16)
        ones = jnp.where((lanes >= aux) & (lanes < aux + 3), 1.0, 0.0)
        values_out[span, :] = jnp.where(inside, value.astype(F32), ones).astype(BF16)
        row += rows


def pair_forward(query_of, keys, values, rows, chunk, save):
    lanes = lane_ids((chunk, PAIR))
    units = [(start, head) for start in range(0, rows, chunk) for head in (0, 1)]

    def extended(start, head):
        aux = HEAD_DIM * (1 - head)
        inside = (lanes // HEAD_DIM) == head
        query = query_of(slice(start, start + chunk)).astype(F32)
        return jnp.where(inside, query, jnp.where(lanes == aux, 1.0, 0.0))

    def scores(start, head):
        return contract_cols(extended(start, head).astype(BF16), keys[head])

    ahead = [scores(*unit) for unit in units[:2]]
    for index, (start, head) in enumerate(units):
        now = ahead.pop(0)
        if index + 2 < len(units):
            ahead.append(scores(*units[index + 2]))
        aux = HEAD_DIM * (1 - head)
        top = jnp.max(now, axis=1, keepdims=True)
        summed = mm(jnp.exp(now - top).astype(BF16), values[head])
        total = summed[:, aux : aux + 1]
        query = extended(start, head)
        for lane, part in enumerate(three_parts(-(top + jnp.log(total))), aux + 1):
            query = jnp.where(lanes == lane, part, query)
        save(head, slice(start, start + chunk), query.astype(BF16), summed / total)


def pair_backward(query_of, grad_of, out_of, keys, values, key_sums, value_sums, rows, save):
    lanes = lane_ids((rows, PAIR))
    parts = []
    for head in (0, 1):
        aux = HEAD_DIM * (1 - head)
        inside = (lanes // HEAD_DIM) == head
        query = query_of(head)
        grad = jnp.where(inside, grad_of().astype(F32), 0.0)
        dots = jnp.sum(grad * out_of(), axis=1, keepdims=True)
        for lane, part in enumerate(three_parts(-dots), aux):
            grad = jnp.where(lanes == lane, part, grad)
        probs = jnp.exp(contract_cols(query, keys[head]))
        shifted = contract_cols(grad.astype(BF16), values[head])
        grad_scores = (probs * shifted).astype(BF16)
        parts.append(mm(grad_scores, keys[head]) * HEAD_DIM**-0.5)
        value_sums[head] = mm(grad.T.astype(BF16), probs.astype(BF16)).T
        key_sums[head] = mm(query.astype(F32).T.astype(BF16), grad_scores).T
    save(jnp.where(lanes < HEAD_DIM, parts[0], parts[1]).astype(BF16))


def attention_backward_body(
    spot, incoming_ref, mask_ref, hidden_ref, key_ref, value_ref, key_far_ref, value_far_ref,
    extended_ref, attended_ref, weight_ref, norm_ref, key_bias_ref,
    weight_grad, out_ref, gain_grad, shift_grad, query_bias_grad, value_bias_grad, out_bias_grad,
    grad, grad_out, attended, normed_t, total, grads, sent, arrived, keys, values, key_sums, value_sums,
    send, recv,
):
    step, last = pl.program_id(0), pl.num_programs(0) - 1
    rows, width = grad.shape
    pairs = width // PAIR

    def swap_of(p):
        return swap_with_mate(spot, sent.at[p], arrived.at[p], send.at[p], recv.at[p])

    @pl.when(step == 0)
    def _():
        grad_rows = mask_ref[...] * incoming_ref[...].astype(F32)
        grad[...] = grad_rows.astype(BF16)
        out_bias_grad[...] = jnp.sum(grad_rows, axis=0, keepdims=True)
        for p, part in enumerate(pairs_of(mm(grad[...], weight_ref[0].reshape(width, width)).astype(BF16))):
            grad_out[p] = part

    @pl.when(step < pairs)
    def _():
        p = step
        for head in (0, 1):
            extend_keys(
                keys.at[head], values.at[head],
                [(key_ref[0, 0], value_ref[0, 0]), (key_far_ref[0, 0], value_far_ref[0, 0])], key_bias_ref, head,
            )
        attended[p] = attended_ref[0, 0].astype(BF16)

        def save(value):
            grads[0, p] = value

        pair_backward(
            lambda head: extended_ref[0, head], lambda: grad_out[p], lambda: attended_ref[0, 0],
            keys, values, key_sums, value_sums, rows, save,
        )
        first = lane_ids((rows, PAIR)) < HEAD_DIM
        for j, sums in enumerate((key_sums, value_sums)):
            grads[1 + j, p] = jnp.where(first, sums[0, :rows, :], sums[1, :rows, :]).astype(BF16)
            sent[p, j] = jnp.where(first, sums[0, rows:, :], sums[1, rows:, :]).astype(BF16)
        swap_of(p).start()

    @pl.when(step == pairs)
    def _():
        normed_t[...] = transposed_norm(hidden_ref, norm_ref)
        for p in range(pairs):
            swap_of(p).wait()
            for j in (0, 1):
                grads[1 + j, p] = (grads[1 + j, p].astype(F32) + arrived[p, j].astype(F32)).astype(BF16)

    @pl.when((step >= pairs) & (step < last))
    def _():
        j = step - pairs
        part = joined(grads, (j,))
        sums = jnp.sum(part.astype(F32), axis=0, keepdims=True)

        @pl.when(j == 0)
        def _():
            query_bias_grad[...] = sums

        @pl.when(j == 2)
        def _():
            value_bias_grad[...] = sums

        weight_grad[...] = mm(normed_t[...], part).astype(BF16).reshape(weight_grad.shape)
        product = contract_cols(part, weight_ref[0].reshape(width, width))
        total[...] = jnp.where(j == 0, product, total[...] + product)

    @pl.when(step == last)
    def _():
        weight_grad[...] = contract_rows(grad[...], joined(attended)).astype(BF16).reshape(weight_grad.shape)
        grad_hidden, gain_grad[...], shift_grad[...] = norm_backward(
            hidden_ref[0].astype(F32), total[...], norm_ref[0, 0:1, :]
        )
        out_ref[...] = (grad[...].astype(F32) + grad_hidden).astype(BF16)


def attention_backward(
    incoming, mask, hidden, key, value, key_far, value_far, extended, attended, fronts, norms, key_bias, s,
    guests, collective_id,
):
    rows, width = incoming.shape
    layer = s // 2
    pairs = width // PAIR
    pair = lambda i: jnp.minimum(i, pairs - 1)
    block = pl.BlockSpec((1, 1, rows, PAIR), lambda i: (layer, pair(i), 0, 0))
    vector = jax.ShapeDtypeStruct((1, width), F32)
    part = lambda i: jnp.where(i < pairs, 3, jnp.minimum(i - pairs, 2))
    in_specs = [whole((rows, width)), whole((rows, 1)), pl.BlockSpec((1, rows, width), lambda i: (s, 0, 0))]
    in_specs += [block] * 4 + [
        pl.BlockSpec((1, 2, rows, PAIR), lambda i: (layer, pair(i), 0, 0)), block,
        pl.BlockSpec((1, 16, width // 16, width), lambda i: (s, 0, 0, part(i))),
        pl.BlockSpec((1,) + norms.shape[1:], lambda i: (s, 0, 0)), whole((2 * rows, 1)),
    ]
    out_specs = ([
            pl.BlockSpec((16, width // 16, width), lambda i: (0, 0, jnp.maximum(i - pairs, 0))),
            whole((rows, width)),
        ] + [whole((1, width))] * 5)
    out_shape = ([
            jax.ShapeDtypeStruct((16, width // 16, 4 * width), BF16), jax.ShapeDtypeStruct((rows, width), BF16),
        ] + [vector] * 5)
    scratch = ([
            pltpu.VMEM((rows, width), BF16), pltpu.VMEM((pairs, rows, PAIR), BF16),
            pltpu.VMEM((pairs, rows, PAIR), BF16), pltpu.VMEM((width, rows), BF16),
            pltpu.VMEM((rows, width), F32), pltpu.VMEM((3, pairs, rows, PAIR), BF16),
            pltpu.VMEM((pairs, 2, rows, PAIR), BF16), pltpu.VMEM((pairs, 2, rows, PAIR), BF16),
            pltpu.VMEM((2, 2 * rows, PAIR), BF16), pltpu.VMEM((2, 2 * rows, PAIR), BF16),
            pltpu.VMEM((2, 2 * rows, PAIR), F32), pltpu.VMEM((2, 2 * rows, PAIR), F32),
            pltpu.SemaphoreType.DMA((pairs,)), pltpu.SemaphoreType.DMA((pairs,)),
        ])
    return hosted(
        attention_backward_body, pairs + 4, list(zip((incoming, mask, hidden, key, value, key_far, value_far, extended, attended, fronts, norms, key_bias), in_specs)), list(zip(out_shape, out_specs)), scratch,
        guests, collective_id, "attention_backward",
    )


class Weight(PlaneGather):
    SENDS, RECEIVES = 13, 10

    def __init__(self, spot, src, dst, source, send, recv):
        super().__init__(spot, dst, send, recv)
        self.src, self.source = src, source
        self.own = self.blocks(spot.core, spot.c)

    def along(self, src):
        s = self.spot
        return (
            remote(src.at[self.own], self.dst.at[self.own], self.send.at[9], self.recv.at[9], s.above),
            remote(src.at[self.own], self.dst.at[self.own], self.send.at[10], self.recv.at[9], s.below),
        )

    def load(self):
        return pltpu.make_async_copy(self.src, self.dst, self.send.at[11])

    def open(self, up=True, down=True, load=True):
        rise, fall = self.along(self.src)

        @pl.when(self.spot.z == self.source)
        def _():
            if up and self.source + 1 < self.spot.sections:
                rise.start()
            if down and self.source:
                fall.start()
            if load:
                self.load().start()

    def pass_on(self, hop, begin=True):
        rise, fall = self.along(self.dst)
        last = self.spot.sections - 1
        for at, further, copy in ((self.source + hop, last, rise), (self.source - hop, 0, fall)):
            if not 0 <= at <= last:
                continue

            @pl.when(self.spot.z == at)
            def _(at=at, further=further, copy=copy):
                rise.wait_recv()
                if at != further:
                    copy.start()
                if begin:
                    self.begin(self.dst.at[self.own])

    def away(self, action):
        pl.when(self.spot.z != self.source)(action)

    def enter(self):
        self.away(lambda: self.begin(self.dst.at[self.own]))

    def middle(self):
        self.away(self.second)

    def late(self):
        self.away(self.third)

    def ready(self):
        rise, fall = self.along(self.src)
        last = self.spot.sections - 1
        if self.source < last:
            pl.when((self.spot.z >= self.source) & (self.spot.z < last))(rise.wait_send)
        if self.source:
            pl.when((self.spot.z <= self.source) & (self.spot.z > 0))(fall.wait_send)
        pl.when(self.spot.z == self.source)(self.load().wait)
        self.away(self.finish)


QKV_ORDER = (1, 2, 0, 3)
FORWARD_STEPS = 14


def forward_body(*refs):
    refs_list = list(refs)
    take = lambda n: [refs_list.pop(0) for _ in range(n)]
    clips, grads, front, back, norms, kind_in, bias_qv, bias_attn, bias_up, bias_down = take(10)
    key_out, value_out, key_far_out, value_far_out, extended_out, attended_out, act_out, slope_out = take(8)
    fronts_out, downs_out, hidden_out, grad_out, acts_home, mask_out, key_bias_out, norm_out = take(8)
    fronts, downs, hidden, own, far, attended, keys, values, normed, total, norm_all, kind, blank = take(13)
    wsend, wrecv, nsend, nrecv, csend, crecv, ksend, krecv, dsend, drecv, lsem = take(11)
    step = pl.program_id(0)
    layer, turn = step // FORWARD_STEPS, step % FORWARD_STEPS
    rows, width = normed.shape
    pairs = width // PAIR
    spot = Spot()
    owner, slot = spot.z // 2, spot.z % 2
    holds = spot.core == owner

    weights, count = {}, 0

    def weight(name, src, dst, source):
        nonlocal count
        weights[name] = Weight(spot, src, dst, source, wsend.at[count], wrecv.at[count])
        count += 1

    for j, block in enumerate(QKV_ORDER):
        at = pl.ds(block * width, width)
        weight(("first", j), front.at[:, :, at], fronts.at[0, :, :, at], 0)
    for s in range(1, 4):
        weight(("front", s), front, fronts.at[s], s)
    for s in range(4):
        weight(("back", s), back, downs.at[s // 2, pl.ds(16 * (s % 2), 16)], s)
    first = [weights["first", j] for j in range(4)]
    front_1, front_2, front_3 = (weights["front", s] for s in (1, 2, 3))
    back_0, back_1, back_2, back_3 = (weights["back", s] for s in range(4))

    norm_copies = [
        remote(norms, norm_all.at[spot.z], nsend.at[i], nrecv.at[i], {"section": (spot.z + i) % spot.sections})
        for i in range(1, spot.sections)
    ]

    def clip_copies():
        mine, other = (pl.ds(pl.multiple_of(c * rows, 16), rows) for c in (spot.core, 1 - spot.core))
        away = [
            remote(clips.at[slot, other], hidden.at[0], csend.at[0], crecv.at[0], spot.mate),
            remote(grads.at[slot, other], grad_out, csend.at[1], crecv.at[1], spot.mate),
            remote(kind_in, kind, csend.at[2], crecv.at[2], spot.mate),
        ]
        stay = [
            pltpu.make_async_copy(clips.at[slot, mine], hidden.at[0], csend.at[3]),
            pltpu.make_async_copy(grads.at[slot, mine], grad_out, csend.at[4]),
        ]
        return away, stay

    def pads():
        pad = acts_home.shape[1] - 2 * rows
        return [
            pltpu.make_async_copy(blank, acts_home.at[i, pl.ds(2 * rows, pad)], lsem.at[i]) for i in (0, 1)
        ]

    def enter():
        blank[...] = jnp.zeros_like(blank)
        spot.greet()
        for w in first:
            w.open()
        away, stay = clip_copies()

        @pl.when(holds)
        def _():
            for copy in (away[2], away[0], stay[0], away[1]):
                copy.start()
            kind[...] = kind_in[...]
        for copy in norm_copies:
            copy.start()
        norm_all[spot.z] = norms[...]
        for w in (front_1, back_1, front_2, back_2, front_3, back_3):
            w.open(up=False)
        back_2.open(down=False, load=False)
        for w in first:
            for hop in (1, 2, 3):
                w.pass_on(hop)
        for w in (front_1, back_1, front_2):
            w.open(down=False, load=False)
        back_0.open()

        @pl.when(holds)
        def _():
            stay[1].start()
            stay[0].wait()

        @pl.when(jnp.logical_not(holds))
        def _():
            away[0].wait_recv()
            away[2].wait_recv()
        for i, copy in enumerate(norm_copies, 1):
            block = norm_all.at[(spot.z + spot.sections - i) % spot.sections]
            remote(block, block, nsend.at[i], nrecv.at[i], spot.mate).wait_recv()
        norm_out[...] = norm_all[...]
        for copy in pads():
            copy.start()
        length = SHORT + (LONG - SHORT) * kind[0:1, 0:1]
        place = lax.broadcasted_iota(jnp.int32, (rows, 1), 0)
        near, there = ((place + c * rows).astype(F32) < length for c in (spot.core, 1 - spot.core))
        mask_out[...] = near.astype(F32)
        key_bias_out[:rows, :] = jnp.where(near, 0.0, MASKED)
        key_bias_out[rows:, :] = jnp.where(there, 0.0, MASKED)
        for w in first:
            w.middle()
        front_1.pass_on(1)
        back_1.pass_on(1)
        for w in first:
            w.late()
        front_1.pass_on(2)
        first[0].ready()

    plan = {
        0: [enter], 1: [first[1].ready, lambda: back_1.pass_on(2), lambda: back_0.pass_on(1)],
        2: [first[2].ready, lambda: back_0.pass_on(2), lambda: front_2.pass_on(1, False),
            lambda: back_2.pass_on(1, False)],
        3: [first[3].ready, lambda: back_0.pass_on(3), lambda: front_3.pass_on(1, False)],
        4: [front_1.middle, lambda: back_3.pass_on(1, False), lambda: front_2.pass_on(2, False)],
        5: [lambda: back_2.pass_on(2, False)],
        6: [back_1.middle, lambda: front_3.pass_on(2, False)],
        7: [back_0.middle, front_1.late, lambda: back_3.pass_on(2, False)],
        8: [front_2.enter],
        9: [back_1.late, lambda: front_3.pass_on(3, False)],
        10: [back_0.late, lambda: back_3.pass_on(3, False), front_1.ready, back_1.ready, back_0.ready],
        11: [front_3.enter],
        12: [front_2.middle],
        13: [front_2.late, back_2.enter, back_3.enter],
        14: [front_2.ready],
        16: [front_3.middle],
        18: [back_2.middle],
        19: [back_3.middle, front_3.late],
        21: [back_2.late],
        22: [back_3.late],
        24: [front_3.ready, back_2.ready, back_3.ready],
    }
    ends = []

    def keep(at, src, dst, index):
        copy = pltpu.make_async_copy(src, dst, lsem.at[2 + index])
        plan.setdefault(at, []).append(copy.start)
        ends.append(copy.wait)

    for s, at in ((0, 10), (1, 12), (2, 20), (3, 25)):
        keep(at, fronts.at[s], fronts_out.at[s], s)
    for layer_id, at in ((0, 15), (1, 26)):
        keep(at, downs.at[layer_id], downs_out.at[layer_id], 4 + layer_id)
    for s, at in ((0, 4), (1, 11), (2, 16), (3, 25)):
        keep(at, hidden.at[s], hidden_out.at[s], 6 + s)

    for n, (s, first_row, size, begin, stop) in enumerate(FORWARD_DELIVERIES):
        size = size or rows - first_row
        blocks = size // 16
        for i in range(stop - begin):
            low, high = blocks * i // (stop - begin), blocks * (i + 1) // (stop - begin)
            part = Deliver(
                spot, hidden.at[s + 1], acts_home, s, dsend.at[n], drecv.at[n], first_row + 16 * low, 16 * (high - low)
            )
            plan.setdefault(begin + i, []).append(part.start)
        ends.append(Deliver(spot, hidden.at[s + 1], acts_home, s, dsend.at[n], drecv.at[n], first_row, size).finish)

    for at, actions in sorted(plan.items()):
        @pl.when(step == at)
        def _(actions=actions):
            for action in actions:
                action()

    def norms_of(s):
        return norm_all[s, 0:1, :], norm_all[s, 1:2, :]

    def start_sub_layer(s):
        gain, shift = norms_of(s)
        unit, _ = norm_rows(hidden[s].astype(F32))
        normed[...] = (unit * gain + shift).astype(BF16)

    def front_block(s, block):
        return fronts[s, :, :, pl.ds(pl.multiple_of(block * width, width), width)].reshape(width, width)

    def swaps():
        return [
            remote(own.at[j], far.at[layer, j], ksend.at[layer, j], krecv.at[layer, j], spot.mate) for j in (0, 1)
        ]

    @pl.when(turn == 0)
    def _():
        start_sub_layer(2 * layer)

    for j, scale in ((0, 1.0), (1, 1.0), (2, HEAD_DIM**-0.5)):
        @pl.when(turn == j)
        def _(j=j, scale=scale):
            block = mm(normed[...], front_block(2 * layer, QKV_ORDER[j]))
            if j == 1:
                block = block + bias_qv[pl.ds(layer, 1), width:]
            elif j == 2:
                block = block + bias_qv[pl.ds(layer, 1), :width]
            block = block.astype(BF16)
            if scale != 1.0:
                block = (block.astype(F32) * scale).astype(BF16)
            for p, part in enumerate(pairs_of(block)):
                own[j, p] = part
            if j < 2:
                swaps()[j].start()
            else:
                for copy in swaps():
                    copy.wait()

    @pl.when((turn >= 3) & (turn < 3 + pairs))
    def _():
        p = turn - 3
        for head in (0, 1):
            extend_keys(
                keys.at[head], values.at[head], [(own[0, p], own[1, p]), (far[layer, 0, p], far[layer, 1, p])],
                key_bias_out, head,
            )
        for j, out in enumerate((key_out, value_out)):
            out[0, 0] = own[j, p]
        for j, out in enumerate((key_far_out, value_far_out)):
            out[0, 0] = far[layer, j, p]
        lanes = lane_ids((rows // 2, PAIR))
        firsts = {}

        def save(head, span, query, out):
            extended_out[0, head, span, :] = query
            if head == 0:
                firsts[span.start] = out
            else:
                both = jnp.where(lanes < HEAD_DIM, firsts[span.start], out)
                attended_out[0, 0, span, :] = both
                attended[p, span, :] = both.astype(BF16)

        pair_forward(lambda span: own[2, p, span, :], keys, values, rows, rows // 2, save)

    @pl.when(turn == 3 + pairs)
    def _():
        s = 2 * layer
        branch = contract_cols(joined(attended), front_block(s, 3)) + bias_attn[pl.ds(layer, 1), :]
        hidden[s + 1] = (mask_out[...] * (hidden[s].astype(F32) + branch)).astype(BF16)

    @pl.when(turn == 4 + pairs)
    def _():
        start_sub_layer(2 * layer + 1)

    @pl.when(turn >= 4 + pairs)
    def _():
        i = turn - 4 - pairs
        columns = pl.ds(pl.multiple_of(i * width, width), width)
        up = fronts[2 * layer + 1, :, :, columns].reshape(width, width)
        down_blocks = width * 32 // (width * 4)
        down = downs[layer, pl.ds(i * down_blocks, down_blocks)].reshape(width, width)
        bias = bias_up[pl.ds(layer, 1), columns]
        for span in (slice(0, rows // 2), slice(rows // 2, rows)):
            act, slope = gelu_and_slope(mm(normed[span, :], up) + bias)
            act_out[0, span, :] = act.astype(BF16)
            slope_out[0, span, :] = slope.astype(BF16)
            part = mm(act.astype(BF16), down)
            total[span, :] = jnp.where(i == 0, part, total[span, :] + part)

    @pl.when(turn == FORWARD_STEPS - 1)
    def _():
        s = 2 * layer + 1
        branch = total[...] + bias_down[pl.ds(layer, 1), :]
        hidden[s + 1] = (mask_out[...] * (hidden[s].astype(F32) + branch)).astype(BF16)

    @pl.when(step == 2 * FORWARD_STEPS - 1)
    def _():
        copy = pltpu.make_async_copy(hidden.at[4], hidden_out.at[4], lsem.at[12])
        copy.start()
        for end in ends:
            end()
        copy.wait()
        for pad in pads():
            pad.wait()
        for sent in norm_copies:
            sent.wait_send()
        away, stay = clip_copies()

        @pl.when(holds)
        def _():
            for sent in away:
                sent.wait_send()
            stay[1].wait()

        pl.when(jnp.logical_not(holds))(away[1].wait_recv)


FORWARD_DELIVERIES = ((0, 0, None, 10, 24), (1, 0, None, 14, 27), (2, 0, 160, 24, 27))


def forward(clips, grads, kind, front, back, norms, bias_qv, bias_attn, bias_up, bias_down, rows):
    sections = lax.axis_size("section")
    padded, width = clips.shape[1:]
    units, pairs = front.shape[1], width // PAIR
    front_b = front.reshape(16, width // 16, units)
    back_b = back.reshape(16, back.shape[0] // 16, width)
    layers = sections // 2
    layer = lambda i: i // FORWARD_STEPS
    pair = lambda i: jnp.clip(i % FORWARD_STEPS - 3, 0, pairs - 1)
    unit = lambda i: jnp.maximum(i % FORWARD_STEPS - 4 - pairs, 0)
    hbm, vmem = hbm_spec(), vmem_spec()
    per_pair = pl.BlockSpec((1, 1, rows, PAIR), lambda i: (layer(i), pair(i), 0, 0))
    per_unit = pl.BlockSpec((1, rows, width), lambda i: (layer(i), 0, unit(i)))
    shape = jax.ShapeDtypeStruct
    saved = shape((layers, pairs, rows, PAIR), BF16)
    sems = pltpu.SemaphoreType.DMA
    jobs = 4 + 3 + 4
    sent = len(FORWARD_DELIVERIES)
    return pl.pallas_call(
        forward_body,
        grid=(2 * FORWARD_STEPS,),
        in_specs=[hbm] * 4 + [vmem] * 6,
        out_specs=[per_pair] * 4
        + [pl.BlockSpec((1, 2, rows, PAIR), lambda i: (layer(i), pair(i), 0, 0)), per_pair, per_unit, per_unit]
        + [hbm] * 5 + [vmem] * 3,
        out_shape=[saved] * 4
        + [
            shape((layers, 2 * pairs, rows, PAIR), BF16), shape((layers, pairs, rows, PAIR), F32),
            shape((layers, rows, units), BF16), shape((layers, rows, units), BF16),
            shape((sections,) + front_b.shape, BF16), shape((layers, 32) + back_b.shape[1:], BF16),
            shape((sections + 1, rows, width), BF16), shape((rows, width), BF16),
            shape((clips.shape[0], padded, width), BF16),
            shape((rows, 1), F32), shape((2 * rows, 1), F32), shape((sections,) + norms.shape, F32),
        ],
        scratch_shapes=[
            pltpu.VMEM((sections,) + front_b.shape, BF16), pltpu.VMEM((layers, 32) + back_b.shape[1:], BF16),
            pltpu.VMEM((sections + 1, rows, width), BF16), pltpu.VMEM((3, pairs, rows, PAIR), BF16),
            pltpu.VMEM((layers, 2, pairs, rows, PAIR), BF16), pltpu.VMEM((pairs, rows, PAIR), BF16),
            pltpu.VMEM((2, 2 * rows, PAIR), BF16), pltpu.VMEM((2, 2 * rows, PAIR), BF16),
            pltpu.VMEM((rows, width), BF16), pltpu.VMEM((rows, width), F32),
            pltpu.VMEM((sections,) + norms.shape, F32), pltpu.VMEM(kind.shape, F32),
            pltpu.VMEM((padded - 2 * rows, width), BF16),
            sems((jobs, Weight.SENDS)), sems((jobs, Weight.RECEIVES)), sems((sections,)), sems((sections,)),
            sems((5,)), sems((3,)), sems((layers, 2)), sems((layers, 2)), sems((sent, 2)), sems((sent, 4)), sems((13,)),
        ],
        compiler_params=pltpu.CompilerParams(
            vmem_limit_bytes=63 * 2**20, collective_id=0, has_side_effects=True
        ),
        name="forward",
    )(clips, grads, front_b, back_b, norms, kind, bias_qv, bias_attn, bias_up, bias_down)


def per_device(
    clip_inputs, out_grad, clip_class, w_front, w_back, norm_gain, norm_shift,
    bias_query_value, bias_attn_out, bias_up, bias_down,
):
    spot = Spot()
    sections = lax.axis_size("section")
    padded, width = clip_inputs.shape[1:]
    rows = -(-LONG // 32) * 16
    section = spot.z

    kind = lax.dynamic_index_in_dim(clip_class, section % 2, 0, False).astype(F32)
    norms = jnp.concatenate([norm_gain, norm_shift, jnp.zeros((6, width), F32)], axis=0)
    (
        key, value, key_far, value_far, extended, attended, act, slope,
        fronts, downs, hidden, incoming, acts_home, row_mask, key_bias, norm_all,
    ) = forward(
        clip_inputs, out_grad, jnp.broadcast_to(kind, (8, 128)), w_front[0], w_back[0], norms,
        bias_query_value, bias_attn_out, bias_up, bias_down, rows,
    )
    acts = [hidden[s + 1] for s in range(sections)]
    grads_home = jnp.zeros((clip_inputs.shape[0], 2 * rows, width), BF16)
    acts_beside = {("b", 3): [(2, 160, 448), (3, 0, 192)], ("b", 2): [(3, 192, 416)]}
    grads_beside = {("b", 1): [(3, 0, 400)], ("b", 0): [(3, 400, 208), (1, 0, rows), (2, 0, 192)]}

    def travel(where, held, plan, home):
        steps = 9 if where[1] % 2 == 0 else 3
        return deliver_guest([(held[s], s, start, size) for s, start, size in plan[where]], home, steps)

    input_grads, grad_fronts, grad_downs = [None] * sections, [None] * sections, [None] * 2
    grad_gain, grad_shift = [None] * sections, [None] * sections
    query_sums, value_sums, out_sums, up_sums, down_sums = ([None] * 2 for _ in range(5))
    plane_stages = {
        2: ((0, 1, 4, 8), (0, 2, 6, 9), (0, 2, 7, 9)), 1: ((0, 1, 3, 3),), 0: ((0, 1, 4, 8), (0, 2, 6, 9), (0, 2, 7, 9)),
    }
    for s in reversed(range(sections)):
        layer = s // 2
        guests = []
        if s < 3:
            jobs = [(grad_fronts[s + 1], 0)]
            if s % 2 == 0:
                jobs += [(grad_downs[layer], 0), (grad_downs[layer], 16)]
            guests.append(plane_sum_guest(jobs, plane_stages[s]))
        if s < 2:
            hops = {1: [(3, 0), (2, 0), (3, 0)], 0: [(3, 1), (2, 1), (3, 1), (2, 0)]}[s]
            guests.append(section_hop_guest([(part, target, done + 1) for part, (target, done) in zip(passing, hops)]))
        if ("b", s) in acts_beside:
            guests.append(travel(("b", s), acts, acts_beside, acts_home))
        else:
            guests.append(travel(("b", s), input_grads, grads_beside, grads_home))
        if s % 2 == 0:
            (
                grad_fronts[s], incoming, grad_gain[s], grad_shift[s],
                query_sums[layer], value_sums[layer], out_sums[layer],
            ), carried = attention_backward(
                incoming, row_mask, hidden, key, value, key_far, value_far, extended, attended,
                fronts, norm_all, key_bias, s, guests, 6 + s,
            )
        else:
            (
                grad_fronts[s], grad_downs[layer], incoming, grad_gain[s], grad_shift[s],
                up_sums[layer], down_sums[layer],
            ), carried = ff_backward(
                incoming, row_mask, hidden, act, slope, fronts, downs, norm_all, s, guests, 6 + s
            )
        input_grads[s] = incoming
        if ("b", s) in acts_beside:
            (acts_home,) = carried[-1]
        else:
            (grads_home,) = carried[-1]
        if s == 2:
            passing = carried[0]
        elif s == 1:
            passing = [*carried[1], *carried[0]]
        elif s == 0:
            (front_3, back_2, back_3, front_2), (front_1, back_0, back_1) = carried[1], carried[0]

    pair_sums = [jnp.concatenate([q, v], axis=1) for q, v in zip(query_sums, value_sums)]
    small = jnp.concatenate(
        [v.reshape(-1) for v in grad_gain + grad_shift + pair_sums + out_sums + up_sums + down_sums]
    )
    grads_home, front_out, back_out, small = collect(
        input_grads[0], input_grads[2], grads_home, grad_fronts[0],
        [front_3, back_3, front_2, back_2, front_1, back_0, back_1], small.reshape(-1, 128),
    )
    front_out = front_out.reshape(width, -1)
    back_out = back_out.reshape(-1, width)
    small = small.reshape(-1)
    for bit in spot.spare_bits:
        small = small + swap(small, bit)
        front_out, back_out = add(front_out, swap(front_out, bit)), add(back_out, swap(back_out, bit))
    grads_out = jnp.pad(grads_home.astype(F32), ((0, 0), (0, padded - 2 * rows), (0, 0)))
    parts, place_at = [], 0
    layers, hidden_units = bias_up.shape
    for count, size in (
        (sections, width), (sections, width), (layers, 2 * width), (layers, width),
        (layers, hidden_units), (layers, width),
    ):
        parts.append(small[place_at : place_at + count * size].reshape(count, size))
        place_at += count * size
    return (
        acts_home[None],
        grads_out[None],
        front_out.astype(F32)[None],
        back_out.astype(F32)[None],
        lax.dynamic_slice_in_dim(parts[0], section, 1, 0),
        lax.dynamic_slice_in_dim(parts[1], section, 1, 0),
        *parts[2:],
    )


def solution(mesh):
    placed = (
        P("dp", None, None), P("dp", None, None), P("dp"),
        P("section", None, None), P("section", None, None), P("section", None), P("section", None),
        P(), P(), P(), P(),
    )
    return jax.shard_map(
        per_device,
        mesh=mesh,
        in_specs=placed,
        out_specs=(
            P("section", "dp", None, None), P("section", "dp", None, None),
            P("section", None, None), P("section", None, None), P("section", None), P("section", None),
            P(), P(), P(), P(),
        ),
        check_vma=False,
    )
```

```python
import functools
import math

import jax
import jax.numpy as jnp
from jax import lax
from jax.experimental import pallas as pl
from jax.experimental.pallas import tpu as pltpu
from jax.sharding import PartitionSpec as P

HEADS = 12
LONG = 1214
SHORT = 514
EPS = 1e-06
HEAD_DIM = 64
PAIR = 2 * HEAD_DIM
MASKED = -1e30
F32 = jnp.float32
BF16 = jnp.bfloat16
KERNEL_VMEM = 56 * 2**20


def mm(left, right):
    return jnp.dot(left, right, preferred_element_type=F32)


def contract_rows(left, right):
    return lax.dot_general(left, right, (((0,), (0,)), ((), ())), preferred_element_type=F32)


def contract_cols(left, right):
    return lax.dot_general(left, right, (((1,), (1,)), ((), ())), preferred_element_type=F32)


def swap(block, bit):
    count = lax.axis_size("dp")
    return lax.ppermute(block, "dp", [(i, i ^ bit) for i in range(count)])


def add(a, b):
    return (a.astype(F32) + b.astype(F32)).astype(BF16)


class Spot:
    def __init__(self):
        self.z, self.sections = lax.axis_index("section"), lax.axis_size("section")
        self.d, self.count = lax.axis_index("dp"), lax.axis_size("dp")
        self.x_bit, self.y_bit = 2, 2 * math.isqrt(self.count // 2)
        self.core = self.d % 2
        self.xb, self.yb = (self.d // self.x_bit) % 2, (self.d // self.y_bit) % 2
        self.c, self.c_x = self.yb * 2 + self.xb, self.yb * 2 + 1 - self.xb
        self.c_y, self.c_d = (1 - self.yb) * 2 + self.xb, (1 - self.yb) * 2 + 1 - self.xb
        self.mate, self.x, self.y = (self.flipped(b) for b in (1, self.x_bit, self.y_bit))
        self.above, self.below = {"section": self.z + 1}, {"section": self.z - 1}
        self.spare_bits = [
            1 << i for i in range(self.count.bit_length() - 1) if 1 << i not in (1, self.x_bit, self.y_bit)
        ]

    def flipped(self, bit):
        return {"dp": self.d + bit * (1 - 2 * ((self.d // bit) % 2))}

    def greet_mate(self):
        barrier = pltpu.get_barrier_semaphore()
        pl.semaphore_signal(barrier, inc=1, device_id=self.mate, device_id_type=pl.DeviceIdType.MESH)
        pl.semaphore_wait(barrier, 1)

    def greet(self):
        barrier = pltpu.get_barrier_semaphore()
        devices = [self.x, self.y]
        for step in range(self.sections):
            for core in (0, 1):
                if step or core:
                    devices.append({
                        "section": (self.z + step) % self.sections,
                        "dp": self.d - self.core + (self.core + core) % 2,
                    })
        for device in devices:
            pl.semaphore_signal(barrier, inc=1, device_id=device, device_id_type=pl.DeviceIdType.MESH)
        pl.semaphore_wait(barrier, len(devices))


def remote(src, dst, send, recv, device):
    return pltpu.make_async_remote_copy(
        src_ref=src, dst_ref=dst, send_sem=send, recv_sem=recv,
        device_id=device, device_id_type=pl.DeviceIdType.MESH,
    )


class PlaneGather:
    SENDS, RECEIVES = 9, 9

    def __init__(self, spot, dst, send, recv):
        self.spot, self.dst, self.send, self.recv = spot, dst, send, recv

    def blocks(self, core, chip, half=None):
        at = core * 8 + chip * 2
        return pl.ds(at, 2) if half is None else pl.ds(at + half, 1)

    def copies(self, own=None):
        s, k = self.spot, self.spot.core
        plan = {
            "x": (self.blocks(k, s.c), s.x), "y": (self.blocks(k, s.c), s.y),
            "m": (self.blocks(k, s.c), s.mate),
            "xy": (self.blocks(k, s.c_x, 0), s.y), "yx": (self.blocks(k, s.c_y, 1), s.x),
            "mx": (self.blocks(k, s.c_x), s.mate), "my": (self.blocks(k, s.c_y), s.mate),
            "md0": (self.blocks(k, s.c_d, 0), s.mate), "md1": (self.blocks(k, s.c_d, 1), s.mate),
        }
        out = {}
        for index, (name, (rows, device)) in enumerate(plan.items()):
            src = own if own is not None and name in ("x", "y", "m") else self.dst.at[rows]
            out[name] = remote(src, self.dst.at[rows], self.send.at[index], self.recv.at[index], device)
        return out

    def arrivals(self):
        s, k = self.spot, self.spot.core
        plan = {
            "x": self.blocks(k, s.c_x), "y": self.blocks(k, s.c_y), "m": self.blocks(1 - k, s.c),
            "xy": self.blocks(k, s.c_d, 0), "yx": self.blocks(k, s.c_d, 1),
            "mx": self.blocks(1 - k, s.c_x), "my": self.blocks(1 - k, s.c_y),
            "md0": self.blocks(1 - k, s.c_d, 0), "md1": self.blocks(1 - k, s.c_d, 1),
        }
        return {
            name: remote(self.dst.at[rows], self.dst.at[rows], self.send.at[i], self.recv.at[i], s.mate)
            for i, (name, rows) in enumerate(plan.items())
        }

    def begin(self, own):
        copies = self.copies(own)
        for name in ("x", "y", "m"):
            copies[name].start()

    def second(self):
        copies, arrivals = self.copies(), self.arrivals()
        arrivals["x"].wait_recv()
        copies["xy"].start()
        copies["mx"].start()
        arrivals["y"].wait_recv()
        copies["yx"].start()
        copies["my"].start()

    def third(self):
        copies, arrivals = self.copies(), self.arrivals()
        for name, after in (("xy", "md0"), ("yx", "md1")):
            arrivals[name].wait_recv()
            copies[after].start()

    def finish(self):
        copies, arrivals = self.copies(), self.arrivals()
        for name in copies:
            copies[name].wait_send()
        for name in ("m", "mx", "my", "md0", "md1"):
            arrivals[name].wait_recv()


class Deliver:
    def __init__(self, spot, src, dst, target, send, recv, start=0, size=None):
        self.spot, self.src, self.dst, self.target, self.send, self.recv = spot, src, dst, target, send, recv
        self.rows, self.start_row = src.shape[0], start
        self.size = size or src.shape[0]
        self.owner, self.slot = spot.z // 2, spot.z % 2
        self.home = (spot.z == target) & (spot.core == self.owner)

    def place(self, slot, core):
        at = pl.multiple_of(core * self.rows + self.start_row, 16)
        return self.dst.at[slot, pl.ds(at, self.size)]

    def copies(self):
        s, spot = self, self.spot
        spot_at, src = s.place(s.slot, spot.core), s.src.at[pl.ds(s.start_row, s.size)]
        away = remote(
            src, spot_at, s.send.at[0], s.recv.at[s.slot * 2 + spot.core],
            {"section": s.target, "dp": spot.d - spot.core + s.owner},
        )
        return away, pltpu.make_async_copy(src, spot_at, s.send.at[1])

    def start(self):
        away, stay = self.copies()
        pl.when(self.home)(stay.start)
        pl.when(jnp.logical_not(self.home))(away.start)

    def finish(self):
        away, stay = self.copies()
        pl.when(self.home)(stay.wait)
        pl.when(jnp.logical_not(self.home))(away.wait_send)
        spot = self.spot
        for slot in (0, 1):
            for core in (0, 1):
                here = (spot.core * 2 + slot == spot.z) & (spot.core == core)
                block = self.place(slot, core)
                landing = remote(block, block, self.send.at[0], self.recv.at[slot * 2 + core], spot.mate)
                pl.when((spot.z == self.target) & jnp.logical_not(here))(landing.wait_recv)


class Guest:
    def __init__(self, inputs=(), outputs=(), scratch=(), aliases=(), plan=None):
        self.inputs, self.outputs, self.scratch = list(inputs), list(outputs), list(scratch)
        self.aliases, self.plan = list(aliases), plan


def hbm_spec():
    return pl.BlockSpec(memory_space=pl.ANY)


def vmem_spec():
    return pl.BlockSpec(memory_space=pltpu.VMEM)


def hosted(body, grid, operands, results, scratch, guests, collective_id, name, vmem=KERNEL_VMEM):
    guest_in = [pair for g in guests for pair in g.inputs]
    guest_out = [pair for g in guests for pair in g.outputs]
    guest_scratch = [s for g in guests for s in g.scratch]
    aliases, at_in, at_out = {}, len(operands), len(results)
    for g in guests:
        for i, o in g.aliases:
            aliases[at_in + i] = at_out + o
        at_in, at_out = at_in + len(g.inputs), at_out + len(g.outputs)

    def kernel(*refs):
        refs = list(refs)
        take = lambda n: [refs.pop(0) for _ in range(n)]
        ins, gins = take(len(operands)), take(len(guest_in))
        outs, gouts = take(len(results)), take(len(guest_out))
        held, gheld = take(len(scratch)), take(len(guest_scratch))
        spot, step = Spot(), pl.program_id(0)
        pl.when(step == 0)(spot.greet)
        hooks = {}
        for g in guests:
            parts = [[r.pop(0) for _ in range(n)] for r, n in (
                (gins, len(g.inputs)), (gouts, len(g.outputs)), (gheld, len(g.scratch))
            )]
            for at, actions in g.plan(spot, *parts, held).items():
                hooks.setdefault(at, []).extend(actions)

        def run(actions):
            for action in actions:
                action()

        for at in sorted(k for k in hooks if k != "end"):
            pl.when(step == at)(functools.partial(run, hooks[at]))
        body(spot, *ins, *outs, *held)
        if "end" in hooks:
            pl.when(step == grid - 1)(functools.partial(run, hooks["end"]))

    out = pl.pallas_call(
        kernel,
        grid=(grid,),
        in_specs=[s for _, s in operands + guest_in],
        out_specs=[s for _, s in results + guest_out],
        out_shape=[s for s, _ in results + guest_out],
        scratch_shapes=list(scratch) + guest_scratch,
        input_output_aliases=aliases,
        compiler_params=pltpu.CompilerParams(
            vmem_limit_bytes=vmem, collective_id=collective_id, has_side_effects=True
        ),
        name=name,
    )(*[a for a, _ in operands + guest_in])
    own, rest, per_guest = out[: len(results)], list(out[len(results) :]), []
    for g in guests:
        per_guest.append([rest.pop(0) for _ in g.outputs])
    return own, per_guest


def deliver_guest(pieces, home):
    sems = pltpu.SemaphoreType.DMA
    count = len(pieces)
    arrays = [i for i, piece in enumerate(pieces) if not isinstance(piece[0], int)]

    def plan(spot, ins, outs, held, body):
        send, recv = held
        hooks = {}
        sources = [body[p[0]] if isinstance(p[0], int) else ins[arrays.index(i)] for i, p in enumerate(pieces)]
        for i, (_, target, first, size, steps) in enumerate(pieces):
            blocks = size // 16
            for turn, step in enumerate(steps):
                low, high = blocks * turn // len(steps), blocks * (turn + 1) // len(steps)
                if high > low:
                    part = Deliver(
                        spot, sources[i], outs[0], target, send.at[i], recv.at[i], first + 16 * low, 16 * (high - low)
                    )
                    hooks.setdefault(step, []).append(part.start)
            every = Deliver(spot, sources[i], outs[0], target, send.at[i], recv.at[i], first, size)
            hooks.setdefault("end", []).append(every.finish)
        return hooks

    return Guest(
        [(pieces[i][0], hbm_spec()) for i in arrays] + [(home, hbm_spec())],
        [(jax.ShapeDtypeStruct(home.shape, home.dtype), hbm_spec())],
        [sems((count, 2)), sems((count, 4))],
        [(len(arrays), 0)], plan,
    )


def add_into(target, *others):
    def step(b, carry):
        total = target[b].astype(F32)
        for other in others:
            total = total + other[b].astype(F32)
        target[b] = total.astype(BF16)
        return carry

    lax.fori_loop(0, target.shape[0], step, 0)


class PlaneSum:
    def __init__(self, spot, src, bufs, send, recv, in_place=False):
        self.spot, self.src, self.send, self.recv, self.in_place = spot, src, send, recv, in_place
        self.half, self.from_mate, self.in_x, self.in_y, self.in_yx, self.in_xy = bufs

    @staticmethod
    def scratch(block_rows, columns):
        return [pltpu.VMEM((n, block_rows, columns), BF16) for n in (8, 8, 2, 2, 1, 1)]

    def mate_copies(self):
        s, spot = self, self.spot
        away = remote(s.src.at[pl.ds((1 - spot.core) * 8, 8)], s.from_mate, s.send.at[1], s.recv.at[1], spot.mate)
        if s.in_place:
            return (away,)
        return (pltpu.make_async_copy(s.src.at[pl.ds(spot.core * 8, 8)], s.half, s.send.at[0]), away)

    def start(self):
        for copy in self.mate_copies():
            copy.start()

    def block(self, chip, half):
        return self.half.at[pl.ds(chip * 2 + half, 1)]

    def first_copies(self):
        s, spot = self, self.spot
        first, second = pl.ds(0, 1), pl.ds(1, 1)
        return (
            remote(s.block(spot.c_x, 0), s.in_x.at[first], s.send.at[2], s.recv.at[2], spot.x),
            remote(s.block(spot.c_d, 0), s.in_x.at[second], s.send.at[3], s.recv.at[3], spot.x),
            remote(s.block(spot.c_y, 1), s.in_y.at[first], s.send.at[4], s.recv.at[4], spot.y),
            remote(s.block(spot.c_d, 1), s.in_y.at[second], s.send.at[5], s.recv.at[5], spot.y),
        )

    def second_copies(self):
        s, spot = self, self.spot
        return (
            remote(s.block(spot.c_y, 0), s.in_xy, s.send.at[6], s.recv.at[6], spot.y),
            remote(s.block(spot.c_x, 1), s.in_yx, s.send.at[7], s.recv.at[7], spot.x),
        )

    def first(self):
        for copy in self.mate_copies():
            copy.wait()
        add_into(self.half, self.from_mate)
        for copy in self.first_copies():
            copy.start()

    def second(self):
        s, spot = self, self.spot
        for copy in self.first_copies():
            copy.wait_recv()
        first, other = pl.ds(0, 1), pl.ds(1, 1)
        add_into(s.block(spot.c_y, 0), s.in_x.at[other])
        add_into(s.block(spot.c_x, 1), s.in_y.at[other])
        for copy in self.second_copies():
            copy.start()

    def third(self, out):
        s, spot = self, self.spot
        for copy in self.second_copies():
            copy.wait_recv()
        first = pl.ds(0, 1)
        add_into(s.block(spot.c, 0), s.in_x.at[first], s.in_xy)
        add_into(s.block(spot.c, 1), s.in_y.at[first], s.in_yx)
        for half in (0, 1):
            out[half] = s.half[spot.c * 2 + half]

    def finish(self):
        for copy in self.first_copies() + self.second_copies():
            copy.wait_send()


LEFT = (
    ("front", 0, 3, 2), ("back", None, 2, 2), ("front", 1, 3, 2), ("back", None, 3, 2),
    ("front", 0, 1, 1), ("back", None, 0, 1), ("front", 1, 1, 1), ("back", None, 1, 1),
)


def collect_body(*refs):
    sections = lax.axis_size("section")
    refs_list = list(refs)
    take = lambda n: [refs_list.pop(0) for _ in range(n)]
    last, second, first_front, third_front = take(4)
    parts = take(len(LEFT))
    small, _ = take(2)
    home, front_out, back_out, small_out = take(4)
    plane_bufs, own, third_bufs, third_own, (sums, arriving) = take(6), take(1)[0], take(6), take(1)[0], take(2)
    totals = take(len(LEFT))
    psend, precv, tsend, trecv, dsend, drecv, asend, arecv, ssend, srecv, stay_sem, zsend, zrecv, lsem = take(14)
    spot = Spot()
    loads = [pltpu.make_async_copy(a, b, lsem.at[i]) for i, (a, b) in enumerate(zip(parts, totals))]
    for load in loads:
        load.start()
    spot.greet()
    plane = PlaneSum(spot, first_front, plane_bufs, psend, precv)
    third_plane = PlaneSum(spot, third_front, third_bufs, tsend, trecv)
    plane.start()
    third_plane.start()
    rows = last.shape[0]
    ahead = rows * 2 // 5 // 16 * 16
    early, late, every = (
        Deliver(spot, last, home, 0, dsend.at[0], drecv.at[0], *r) for r in ((0, ahead), (ahead, rows - ahead), ())
    )
    other = Deliver(spot, second, home, 2, dsend.at[1], drecv.at[1])

    sequences = []

    def sequence(total, target, done):
        n = len(sequences)
        chain = Chain(spot, total, take(len(sides(target))), target, zsend.at[n], zrecv.at[n])
        sequences.append((chain, range(done + 1, hops_of(target) + 1)))
        return sequences[-1]

    chains = [sequence(total, target, done) for total, (_, _, target, done) in zip(totals, LEFT)]
    first_chains = [sequence(own.at[pl.ds(i, 1)], 0, 0) for i in (0, 1)]
    third_chain = [sequence(third_own, 2, 0)]

    def advance(which, turn):
        for chain, hops in which:
            if 0 < turn <= len(hops):
                chain.take(hops[turn - 1])
            if turn < len(hops):
                chain.give(hops[turn])

    for load in loads:
        load.wait()
    advance(chains, 0)
    early.start()
    other.start()
    sums[0] = small[...]
    partners = [spot.mate, spot.x, spot.y] + [
        {"section": spot.z + bit * (1 - 2 * ((spot.z // bit) % 2))}
        for bit in (1 << i for i in range((sections - 1).bit_length()))
    ]
    steps = len(partners)

    def small_copy(i):
        return remote(sums.at[i], arriving.at[i], ssend.at[i], srecv.at[i], partners[i])

    def small_step(i):
        if 0 < i <= steps:
            small_copy(i - 1).wait()
            sums[i] = sums[i - 1] + arriving[i - 1]
        if i < steps:
            small_copy(i).start()

    small_step(0)
    plane.first()
    small_step(1)
    plane.second()
    third_plane.first()
    small_step(2)
    plane.third(own)
    advance(first_chains, 0)
    advance(chains, 1)
    third_plane.second()
    small_step(3)
    advance(first_chains, 1)
    advance(chains, 2)
    third_plane.third(third_own)
    advance(third_chain, 0)
    advance(first_chains, 2)
    late.start()
    small_step(4)
    gathers = [
        PlaneGather(spot, out, asend.at[i], arecv.at[i]) for i, out in enumerate((front_out, back_out))
    ]

    def begin(i, kind):
        gather = gathers[i]
        blocks = gather.blocks(spot.core, spot.c)
        for z in range(sections):
            if kind == "back":
                held = [t for t, (name, _, target, _) in zip(totals, LEFT) if name == kind and target == z]
                pieces = [(held[0], gather.dst.at[blocks])]
            elif z in (1, 3):
                held = [t for t, (name, _, target, _) in zip(totals, LEFT) if name == kind and target == z]
                size = held[0].shape[2]
                pieces = [(t, gather.dst.at[blocks, :, pl.ds(n * size, size)]) for n, t in enumerate(held)]
            else:
                pieces = [(own if z == 0 else third_own, gather.dst.at[blocks])]
            copies = [pltpu.make_async_copy(a, b, stay_sem.at[i, n]) for n, (a, b) in enumerate(pieces)]

            @pl.when(spot.z == z)
            def _(gather=gather, copies=copies, blocks=blocks):
                for copy in copies:
                    copy.start()
                for copy in copies:
                    copy.wait()
                gather.begin(gather.dst.at[blocks])

    begin(1, "back")
    advance(third_chain, 1)
    small_step(5)
    small_out[...] = sums[steps]
    gathers[1].second()
    advance(first_chains, 3)
    advance(third_chain, 2)
    begin(0, "front")
    gathers[1].third()
    gathers[0].second()
    gathers[0].third()
    for gather in gathers:
        gather.finish()
    for deliver in (every, other):
        deliver.finish()
    plane.finish()
    third_plane.finish()
    for chain, hops in sequences:
        for hop in hops:
            chain.leave(hop)


def collect(last, second, home, first_front, third_front, parts, small):
    sections = lax.axis_size("section")
    hbm, vmem = hbm_spec(), vmem_spec()
    steps = 3 + (sections - 1).bit_length()
    sems = pltpu.SemaphoreType.DMA
    front_shape = first_front.shape
    back_shape = (16,) + parts[1].shape[1:]
    buffers = []
    jobs = [(p.shape, left[2]) for p, left in zip(parts, LEFT)]
    jobs += [((1,) + front_shape[1:], 0)] * 2 + [((2,) + front_shape[1:], 2)]
    for shape, target in jobs:
        buffers += [pltpu.VMEM(shape, BF16)] * len(sides(target))
    return pl.pallas_call(
        collect_body,
        in_specs=[hbm] * (4 + len(parts)) + [vmem, hbm],
        out_specs=[hbm] * 3 + [vmem],
        out_shape=[
            jax.ShapeDtypeStruct(home.shape, BF16), jax.ShapeDtypeStruct(front_shape, BF16),
            jax.ShapeDtypeStruct(back_shape, BF16), jax.ShapeDtypeStruct(small.shape, F32),
        ],
        scratch_shapes=(PlaneSum.scratch(*front_shape[1:]) + [pltpu.VMEM((2,) + front_shape[1:], BF16)]) * 2
        + [pltpu.VMEM((steps + 1,) + small.shape, F32), pltpu.VMEM((steps,) + small.shape, F32)]
        + [pltpu.VMEM(p.shape, BF16) for p in parts]
        + [
            sems((8,)), sems((8,)), sems((8,)), sems((8,)), sems((2, 2)), sems((2, 4)),
            sems((2, 9)), sems((2, 9)), sems((steps,)), sems((steps,)), sems((2, 2)),
            sems((len(jobs),)), sems((len(jobs), 2)), sems((len(parts),)),
        ]
        + buffers,
        input_output_aliases={5 + len(parts): 0},
        compiler_params=pltpu.CompilerParams(
            collective_id=1, has_side_effects=True, vmem_limit_bytes=KERNEL_VMEM
        ),
        name="collect",
    )(last, second, first_front, third_front, *parts, small, home)


def norm_rows(hidden):
    average = jnp.mean(hidden, axis=-1, keepdims=True)
    centred = hidden - average
    inverse = lax.rsqrt(jnp.mean(centred * centred, axis=-1, keepdims=True) + EPS)
    return centred * inverse, inverse


def norm_backward(hidden, grad_normed, gain):
    unit, inverse = norm_rows(hidden)
    scaled = grad_normed * gain
    first = jnp.mean(scaled, axis=-1, keepdims=True)
    second = jnp.mean(scaled * unit, axis=-1, keepdims=True)
    return (
        inverse * (scaled - first - unit * second),
        jnp.sum(grad_normed * unit, axis=0, keepdims=True),
        jnp.sum(grad_normed, axis=0, keepdims=True),
    )


def gelu_and_slope(pre):
    density = jnp.exp(-0.5 * pre * pre)
    t = 1.0 / (1.0 + (0.3275911 * 0.5**0.5) * jnp.abs(pre))
    series = t * (0.127414796 + t * (-0.142248368 + t * (0.7107068705 + t * (-0.7265760135 + t * 0.5307027145))))
    tail = series * density
    below = jnp.where(pre < 0, tail, 1.0 - tail)
    return pre * below, below + pre * density * (1.0 / math.sqrt(2.0 * math.pi))


def pairs_of(block):
    return [block[:, p * PAIR : (p + 1) * PAIR] for p in range(block.shape[1] // PAIR)]


def joined(ref, lead=()):
    return jnp.concatenate([ref[lead + (p,)] for p in range(ref.shape[len(lead)])], axis=1)


def whole(shape):
    return pl.BlockSpec(shape, lambda i: (0,) * len(shape))


def swap_with_mate(spot, src, dst, send, recv):
    return remote(src, dst, send, recv, spot.mate)


def transposed_norm(hidden_ref, norm_ref):
    unit, _ = norm_rows(hidden_ref[0].astype(F32))
    normed = (unit * norm_ref[0, 0:1, :] + norm_ref[0, 1:2, :]).astype(BF16)
    return normed.astype(F32).T.astype(BF16)


def lane_ids(shape):
    return lax.broadcasted_iota(jnp.int32, shape, len(shape) - 1)


def three_parts(value):
    high = value.astype(BF16).astype(F32)
    rest = value - high
    middle = rest.astype(BF16).astype(F32)
    return high, middle, rest - middle


def extend_keys(keys_out, values_out, blocks, bias_ref, head):
    aux = HEAD_DIM * (1 - head)
    row = 0
    for key, value in blocks:
        rows = key.shape[0]
        span = slice(row, row + rows)
        lanes = lane_ids((rows, PAIR))
        inside = (lanes // HEAD_DIM) == head
        ones = jnp.where((lanes > aux) & (lanes <= aux + 3), 1.0, 0.0)
        extra = jnp.where(lanes == aux, bias_ref[span, :], ones)
        keys_out[span, :] = jnp.where(inside, key.astype(F32), extra).astype(BF16)
        ones = jnp.where((lanes >= aux) & (lanes < aux + 3), 1.0, 0.0)
        values_out[span, :] = jnp.where(inside, value.astype(F32), ones).astype(BF16)
        row += rows


def pair_forward(query_of, keys, values, rows, chunk, save):
    lanes = lane_ids((chunk, PAIR))
    units = [(start, head) for start in range(0, rows, chunk) for head in (0, 1)]

    def extended(start, head):
        aux = HEAD_DIM * (1 - head)
        inside = (lanes // HEAD_DIM) == head
        query = query_of(slice(start, start + chunk)).astype(F32)
        return jnp.where(inside, query, jnp.where(lanes == aux, 1.0, 0.0))

    def scores(start, head):
        return contract_cols(extended(start, head).astype(BF16), keys[head])

    ahead = [scores(*unit) for unit in units[:2]]
    for index, (start, head) in enumerate(units):
        now = ahead.pop(0)
        if index + 2 < len(units):
            ahead.append(scores(*units[index + 2]))
        aux = HEAD_DIM * (1 - head)
        top = jnp.max(now, axis=1, keepdims=True)
        summed = mm(jnp.exp(now - top).astype(BF16), values[head])
        total = summed[:, aux : aux + 1]
        query = extended(start, head)
        for lane, part in enumerate(three_parts(-(top + jnp.log(total))), aux + 1):
            query = jnp.where(lanes == lane, part, query)
        save(head, slice(start, start + chunk), query.astype(BF16), summed / total)


def pair_backward(query_of, grad_of, out_of, keys, values, key_sums, value_sums, rows, save):
    for start, size in ((0, 256), (256, rows - 256)):
        span = slice(start, start + size)
        lanes = lane_ids((size, PAIR))
        parts = []
        for head in (0, 1):
            aux = HEAD_DIM * (1 - head)
            inside = (lanes // HEAD_DIM) == head
            query = query_of(head, span)
            grad = jnp.where(inside, grad_of(span).astype(F32), 0.0)
            dots = jnp.sum(grad * out_of(span), axis=1, keepdims=True)
            for lane, part in enumerate(three_parts(-dots), aux):
                grad = jnp.where(lanes == lane, part, grad)
            probs = jnp.exp(contract_cols(query, keys[head]))
            shifted = contract_cols(grad.astype(BF16), values[head])
            grad_scores = (probs * shifted).astype(BF16)
            parts.append(mm(grad_scores, keys[head]) * HEAD_DIM**-0.5)
            to_values = mm(grad.T.astype(BF16), probs.astype(BF16)).T
            to_keys = mm(query.astype(F32).T.astype(BF16), grad_scores).T
            value_sums[head] = to_values if start == 0 else value_sums[head] + to_values
            key_sums[head] = to_keys if start == 0 else key_sums[head] + to_keys
        save(span, jnp.where(lanes < HEAD_DIM, parts[0], parts[1]).astype(BF16))


class Weight(PlaneGather):
    SENDS, RECEIVES = 13, 10

    def __init__(self, spot, src, dst, source, send, recv):
        super().__init__(spot, dst, send, recv)
        self.src, self.source = src, source
        self.own = self.blocks(spot.core, spot.c)

    def along(self, src):
        s = self.spot
        return (
            remote(src.at[self.own], self.dst.at[self.own], self.send.at[9], self.recv.at[9], s.above),
            remote(src.at[self.own], self.dst.at[self.own], self.send.at[10], self.recv.at[9], s.below),
        )

    def load(self):
        return pltpu.make_async_copy(self.src, self.dst, self.send.at[11])

    def open(self, up=True, down=True, load=True):
        rise, fall = self.along(self.src)

        @pl.when(self.spot.z == self.source)
        def _():
            if up and self.source + 1 < self.spot.sections:
                rise.start()
            if down and self.source:
                fall.start()
            if load:
                self.load().start()

    def pass_on(self, hop, begin=True):
        rise, fall = self.along(self.dst)
        last = self.spot.sections - 1
        for at, further, copy in ((self.source + hop, last, rise), (self.source - hop, 0, fall)):
            if not 0 <= at <= last:
                continue

            @pl.when(self.spot.z == at)
            def _(at=at, further=further, copy=copy):
                rise.wait_recv()
                if at != further:
                    copy.start()
                if begin:
                    self.begin(self.dst.at[self.own])

    def away(self, action):
        pl.when(self.spot.z != self.source)(action)

    def enter(self):
        self.away(lambda: self.begin(self.dst.at[self.own]))

    def middle(self):
        self.away(self.second)

    def late(self):
        self.away(self.third)

    def ready(self):
        rise, fall = self.along(self.src)
        last = self.spot.sections - 1
        if self.source < last:
            pl.when((self.spot.z >= self.source) & (self.spot.z < last))(rise.wait_send)
        if self.source:
            pl.when((self.spot.z <= self.source) & (self.spot.z > 0))(fall.wait_send)
        pl.when(self.spot.z == self.source)(self.load().wait)
        self.away(self.finish)


QKV_ORDER = (1, 2, 0, 3)
FORWARD_STEPS = 14


def forward_body(*refs):
    refs_list = list(refs)
    take = lambda n: [refs_list.pop(0) for _ in range(n)]
    clips, grads, front, back, norms, kind_in, bias_qv, bias_attn, bias_up, bias_down = take(10)
    key_out, value_out, key_far_out, value_far_out, extended_out, attended_out, act_out, slope_out = take(8)
    fronts_out, downs_out, hidden_out, grad_out, acts_home, mask_out, key_bias_out, norm_out = take(8)
    fronts, downs, hidden, own, far, attended, keys, values, normed, total, norm_all, kind, blank = take(13)
    wsend, wrecv, nsend, nrecv, csend, crecv, ksend, krecv, dsend, drecv, lsem = take(11)
    step = pl.program_id(0)
    layer, turn = step // FORWARD_STEPS, step % FORWARD_STEPS
    rows, width = normed.shape
    pairs = width // PAIR
    spot = Spot()
    owner, slot = spot.z // 2, spot.z % 2
    holds = spot.core == owner

    weights, count = {}, 0

    def weight(name, src, dst, source):
        nonlocal count
        weights[name] = Weight(spot, src, dst, source, wsend.at[count], wrecv.at[count])
        count += 1

    for j, block in enumerate(QKV_ORDER):
        at = pl.ds(block * width, width)
        weight(("first", j), front.at[:, :, at], fronts.at[0, :, :, at], 0)
    for s in range(1, 4):
        weight(("front", s), front, fronts.at[s], s)
    for s in range(4):
        weight(("back", s), back, downs.at[s // 2, pl.ds(16 * (s % 2), 16)], s)
    first = [weights["first", j] for j in range(4)]
    front_1, front_2, front_3 = (weights["front", s] for s in (1, 2, 3))
    back_0, back_1, back_2, back_3 = (weights["back", s] for s in range(4))

    norm_copies = [
        remote(norms, norm_all.at[spot.z], nsend.at[i], nrecv.at[i], {"section": (spot.z + i) % spot.sections})
        for i in range(1, spot.sections)
    ]

    def clip_copies():
        mine, other = (pl.ds(pl.multiple_of(c * rows, 16), rows) for c in (spot.core, 1 - spot.core))
        away = [
            remote(clips.at[slot, other], hidden.at[0], csend.at[0], crecv.at[0], spot.mate),
            remote(grads.at[slot, other], grad_out, csend.at[1], crecv.at[1], spot.mate),
            remote(kind_in, kind, csend.at[2], crecv.at[2], spot.mate),
        ]
        stay = [
            pltpu.make_async_copy(clips.at[slot, mine], hidden.at[0], csend.at[3]),
            pltpu.make_async_copy(grads.at[slot, mine], grad_out, csend.at[4]),
        ]
        return away, stay

    def pads():
        pad = acts_home.shape[1] - 2 * rows
        return [
            pltpu.make_async_copy(blank, acts_home.at[i, pl.ds(2 * rows, pad)], lsem.at[i]) for i in (0, 1)
        ]

    def enter():
        blank[...] = jnp.zeros_like(blank)
        spot.greet()
        for w in first:
            w.open()
        away, stay = clip_copies()

        @pl.when(holds)
        def _():
            for copy in (away[2], away[0], stay[0], away[1]):
                copy.start()
            kind[...] = kind_in[...]
        for copy in norm_copies:
            copy.start()
        norm_all[spot.z] = norms[...]
        for w in (front_1, back_1, front_2, back_2, front_3, back_3):
            w.open(up=False)
        back_2.open(down=False, load=False)
        for w in first:
            for hop in (1, 2, 3):
                w.pass_on(hop)
        for w in (front_1, back_1, front_2):
            w.open(down=False, load=False)
        back_0.open()

        @pl.when(holds)
        def _():
            stay[1].start()
            stay[0].wait()

        @pl.when(jnp.logical_not(holds))
        def _():
            away[0].wait_recv()
            away[2].wait_recv()
        for i, copy in enumerate(norm_copies, 1):
            block = norm_all.at[(spot.z + spot.sections - i) % spot.sections]
            remote(block, block, nsend.at[i], nrecv.at[i], spot.mate).wait_recv()
        norm_out[...] = norm_all[...]
        for copy in pads():
            copy.start()
        length = SHORT + (LONG - SHORT) * kind[0:1, 0:1]
        place = lax.broadcasted_iota(jnp.int32, (rows, 1), 0)
        near, there = ((place + c * rows).astype(F32) < length for c in (spot.core, 1 - spot.core))
        mask_out[...] = near.astype(F32)
        key_bias_out[:rows, :] = jnp.where(near, 0.0, MASKED)
        key_bias_out[rows:, :] = jnp.where(there, 0.0, MASKED)
        for w in first:
            w.middle()
        front_1.pass_on(1)
        back_1.pass_on(1)
        for w in first:
            w.late()
        front_1.pass_on(2)
        first[0].ready()

    plan = {
        0: [enter], 1: [first[1].ready, lambda: back_1.pass_on(2), lambda: back_0.pass_on(1)],
        2: [first[2].ready, lambda: back_0.pass_on(2), lambda: front_2.pass_on(1, False),
            lambda: back_2.pass_on(1, False)],
        3: [first[3].ready, lambda: back_0.pass_on(3), lambda: front_3.pass_on(1, False)],
        4: [front_1.middle, lambda: back_3.pass_on(1, False), lambda: front_2.pass_on(2, False)],
        5: [lambda: back_2.pass_on(2, False)],
        6: [back_1.middle, lambda: front_3.pass_on(2, False)],
        7: [back_0.middle, front_1.late, lambda: back_3.pass_on(2, False)],
        8: [front_2.enter],
        9: [back_1.late, lambda: front_3.pass_on(3, False)],
        10: [back_0.late, lambda: back_3.pass_on(3, False), front_1.ready, back_1.ready, back_0.ready],
        11: [front_3.enter],
        12: [front_2.middle],
        13: [front_2.late, back_2.enter, back_3.enter],
        14: [front_2.ready],
        16: [front_3.middle],
        18: [back_2.middle],
        19: [back_3.middle, front_3.late],
        21: [back_2.late],
        22: [back_3.late],
        24: [front_3.ready, back_2.ready, back_3.ready],
    }
    ends = []

    def keep(at, src, dst, index):
        copy = pltpu.make_async_copy(src, dst, lsem.at[2 + index])
        plan.setdefault(at, []).append(copy.start)
        ends.append(copy.wait)

    for s, at in ((0, 10), (1, 12), (2, 20), (3, 25)):
        keep(at, fronts.at[s], fronts_out.at[s], s)
    for layer_id, at in ((0, 15), (1, 26)):
        keep(at, downs.at[layer_id], downs_out.at[layer_id], 4 + layer_id)
    for s, at in ((0, 4), (1, 11), (2, 16), (3, 25)):
        keep(at, hidden.at[s], hidden_out.at[s], 6 + s)

    for n, (s, first_row, size, begin, stop) in enumerate(FORWARD_DELIVERIES):
        size = size or rows - first_row
        blocks = size // 16
        for i in range(stop - begin):
            low, high = blocks * i // (stop - begin), blocks * (i + 1) // (stop - begin)
            part = Deliver(
                spot, hidden.at[s + 1], acts_home, s, dsend.at[n], drecv.at[n], first_row + 16 * low, 16 * (high - low)
            )
            plan.setdefault(begin + i, []).append(part.start)
        ends.append(Deliver(spot, hidden.at[s + 1], acts_home, s, dsend.at[n], drecv.at[n], first_row, size).finish)

    for at, actions in sorted(plan.items()):
        @pl.when(step == at)
        def _(actions=actions):
            for action in actions:
                action()

    def norms_of(s):
        return norm_all[s, 0:1, :], norm_all[s, 1:2, :]

    def start_sub_layer(s):
        gain, shift = norms_of(s)
        unit, _ = norm_rows(hidden[s].astype(F32))
        normed[...] = (unit * gain + shift).astype(BF16)

    def front_block(s, block):
        return fronts[s, :, :, pl.ds(pl.multiple_of(block * width, width), width)].reshape(width, width)

    def swaps():
        return [
            remote(own.at[j], far.at[layer, j], ksend.at[layer, j], krecv.at[layer, j], spot.mate) for j in (0, 1)
        ]

    @pl.when(turn == 0)
    def _():
        start_sub_layer(2 * layer)

    for j, scale in ((0, 1.0), (1, 1.0), (2, HEAD_DIM**-0.5)):
        @pl.when(turn == j)
        def _(j=j, scale=scale):
            block = mm(normed[...], front_block(2 * layer, QKV_ORDER[j]))
            if j == 1:
                block = block + bias_qv[pl.ds(layer, 1), width:]
            elif j == 2:
                block = block + bias_qv[pl.ds(layer, 1), :width]
            block = block.astype(BF16)
            if scale != 1.0:
                block = (block.astype(F32) * scale).astype(BF16)
            for p, part in enumerate(pairs_of(block)):
                own[j, p] = part
            if j < 2:
                swaps()[j].start()
            else:
                for copy in swaps():
                    copy.wait()

    @pl.when((turn >= 3) & (turn < 3 + pairs))
    def _():
        p = turn - 3
        for head in (0, 1):
            extend_keys(
                keys.at[head], values.at[head], [(own[0, p], own[1, p]), (far[layer, 0, p], far[layer, 1, p])],
                key_bias_out, head,
            )
        for j, out in enumerate((key_out, value_out)):
            out[0, 0] = own[j, p]
        for j, out in enumerate((key_far_out, value_far_out)):
            out[0, 0] = far[layer, j, p]
        lanes = lane_ids((rows // 2, PAIR))
        firsts = {}

        def save(head, span, query, out):
            extended_out[0, head, span, :] = query
            if head == 0:
                firsts[span.start] = out
            else:
                both = jnp.where(lanes < HEAD_DIM, firsts[span.start], out)
                attended_out[0, 0, span, :] = both
                attended[p, span, :] = both.astype(BF16)

        pair_forward(lambda span: own[2, p, span, :], keys, values, rows, rows // 2, save)

    @pl.when(turn == 3 + pairs)
    def _():
        s = 2 * layer
        branch = contract_cols(joined(attended), front_block(s, 3)) + bias_attn[pl.ds(layer, 1), :]
        hidden[s + 1] = (mask_out[...] * (hidden[s].astype(F32) + branch)).astype(BF16)

    @pl.when(turn == 4 + pairs)
    def _():
        start_sub_layer(2 * layer + 1)

    @pl.when(turn >= 4 + pairs)
    def _():
        i = turn - 4 - pairs
        columns = pl.ds(pl.multiple_of(i * width, width), width)
        up = fronts[2 * layer + 1, :, :, columns].reshape(width, width)
        down_blocks = width * 32 // (width * 4)
        down = downs[layer, pl.ds(i * down_blocks, down_blocks)].reshape(width, width)
        bias = bias_up[pl.ds(layer, 1), columns]
        for span in (slice(0, rows // 2), slice(rows // 2, rows)):
            act, slope = gelu_and_slope(mm(normed[span, :], up) + bias)
            act_out[0, span, :] = act.astype(BF16)
            slope_out[0, span, :] = slope.astype(BF16)
            part = mm(act.astype(BF16), down)
            total[span, :] = jnp.where(i == 0, part, total[span, :] + part)

    @pl.when(turn == FORWARD_STEPS - 1)
    def _():
        s = 2 * layer + 1
        branch = total[...] + bias_down[pl.ds(layer, 1), :]
        hidden[s + 1] = (mask_out[...] * (hidden[s].astype(F32) + branch)).astype(BF16)

    @pl.when(step == 2 * FORWARD_STEPS - 1)
    def _():
        copy = pltpu.make_async_copy(hidden.at[4], hidden_out.at[4], lsem.at[12])
        copy.start()
        for end in ends:
            end()
        copy.wait()
        for pad in pads():
            pad.wait()
        for sent in norm_copies:
            sent.wait_send()
        away, stay = clip_copies()

        @pl.when(holds)
        def _():
            for sent in away:
                sent.wait_send()
            stay[1].wait()

        pl.when(jnp.logical_not(holds))(away[1].wait_recv)


FORWARD_DELIVERIES = ((0, 0, None, 10, 24), (1, 0, None, 14, 27), (2, 0, 160, 24, 27))


def forward(clips, grads, kind, front, back, norms, bias_qv, bias_attn, bias_up, bias_down, rows):
    sections = lax.axis_size("section")
    padded, width = clips.shape[1:]
    units, pairs = front.shape[1], width // PAIR
    front_b = front.reshape(16, width // 16, units)
    back_b = back.reshape(16, back.shape[0] // 16, width)
    layers = sections // 2
    layer = lambda i: i // FORWARD_STEPS
    pair = lambda i: jnp.clip(i % FORWARD_STEPS - 3, 0, pairs - 1)
    unit = lambda i: jnp.maximum(i % FORWARD_STEPS - 4 - pairs, 0)
    hbm, vmem = hbm_spec(), vmem_spec()
    per_pair = pl.BlockSpec((1, 1, rows, PAIR), lambda i: (layer(i), pair(i), 0, 0))
    per_unit = pl.BlockSpec((1, rows, width), lambda i: (layer(i), 0, unit(i)))
    shape = jax.ShapeDtypeStruct
    saved = shape((layers, pairs, rows, PAIR), BF16)
    sems = pltpu.SemaphoreType.DMA
    jobs = 4 + 3 + 4
    sent = len(FORWARD_DELIVERIES)
    return pl.pallas_call(
        forward_body,
        grid=(2 * FORWARD_STEPS,),
        in_specs=[hbm] * 4 + [vmem] * 6,
        out_specs=[per_pair] * 4
        + [pl.BlockSpec((1, 2, rows, PAIR), lambda i: (layer(i), pair(i), 0, 0)), per_pair, per_unit, per_unit]
        + [hbm] * 5 + [vmem] * 3,
        out_shape=[saved] * 4
        + [
            shape((layers, 2 * pairs, rows, PAIR), BF16), shape((layers, pairs, rows, PAIR), F32),
            shape((layers, rows, units), BF16), shape((layers, rows, units), BF16),
            shape((sections,) + front_b.shape, BF16), shape((layers, 32) + back_b.shape[1:], BF16),
            shape((sections + 1, rows, width), BF16), shape((rows, width), BF16),
            shape((clips.shape[0], padded, width), BF16),
            shape((rows, 1), F32), shape((2 * rows, 1), F32), shape((sections,) + norms.shape, F32),
        ],
        scratch_shapes=[
            pltpu.VMEM((sections,) + front_b.shape, BF16), pltpu.VMEM((layers, 32) + back_b.shape[1:], BF16),
            pltpu.VMEM((sections + 1, rows, width), BF16), pltpu.VMEM((3, pairs, rows, PAIR), BF16),
            pltpu.VMEM((layers, 2, pairs, rows, PAIR), BF16), pltpu.VMEM((pairs, rows, PAIR), BF16),
            pltpu.VMEM((2, 2 * rows, PAIR), BF16), pltpu.VMEM((2, 2 * rows, PAIR), BF16),
            pltpu.VMEM((rows, width), BF16), pltpu.VMEM((rows, width), F32),
            pltpu.VMEM((sections,) + norms.shape, F32), pltpu.VMEM(kind.shape, F32),
            pltpu.VMEM((padded - 2 * rows, width), BF16),
            sems((jobs, Weight.SENDS)), sems((jobs, Weight.RECEIVES)), sems((sections,)), sems((sections,)),
            sems((5,)), sems((3,)), sems((layers, 2)), sems((layers, 2)), sems((sent, 2)), sems((sent, 4)), sems((13,)),
        ],
        compiler_params=pltpu.CompilerParams(
            vmem_limit_bytes=63 * 2**20, collective_id=0, has_side_effects=True
        ),
        name="forward",
    )(clips, grads, front_b, back_b, norms, kind, bias_qv, bias_attn, bias_up, bias_down)


FF_STEPS = 4


def backward_body(
    spot, incoming_ref, mask_ref, hidden_ref, act_ref, slope_ref, front_ref, down_ref, norm_ref,
    key_ref, value_ref, key_far_ref, value_far_ref, extended_ref, attended_ref, key_bias_ref,
    weight_grad, mid_out, out_ref, ff_gain_grad, ff_shift_grad, up_bias_grad, down_bias_grad,
    gain_grad, shift_grad, query_bias_grad, value_bias_grad, out_bias_grad,
    mid, front_grad, down_grad, grad, normed_t, total, grad_out, attended, grads, sent, arrived,
    keys, values, key_sums, value_sums, send, recv,
):
    step, last = pl.program_id(0), pl.num_programs(0) - 1
    rows, width = grad.shape
    pairs = width // PAIR
    first_pair, first_part = FF_STEPS, FF_STEPS + pairs
    weight = front_ref[0].reshape(width, width)

    def swap_of(p):
        return remote(sent.at[p], arrived.at[p], send.at[p], recv.at[p], spot.mate)

    def start(source, bias_sums):
        grad_rows = mask_ref[...] * source.astype(F32)
        grad[...] = grad_rows.astype(BF16)
        bias_sums[...] = jnp.sum(grad_rows, axis=0, keepdims=True)

    def norm_grads(gain_sums, shift_sums):
        grad_hidden, gain_sums[...], shift_sums[...] = norm_backward(
            hidden_ref[0].astype(F32), total[...], norm_ref[0, 0:1, :]
        )
        return (grad[...].astype(F32) + grad_hidden).astype(BF16)

    @pl.when(step == 0)
    def _():
        start(incoming_ref[...], down_bias_grad)
        normed_t[...] = transposed_norm(hidden_ref, norm_ref)

    @pl.when(step < FF_STEPS)
    def _():
        down = down_ref[0].reshape(width, width)
        blocks = down_ref.shape[1]
        grad_pre = (contract_cols(grad[...], down) * slope_ref[0].astype(F32)).astype(BF16)
        down_part = contract_rows(act_ref[0], grad[...]).astype(BF16)
        down_grad[pl.ds(step * blocks, blocks)] = down_part.reshape(down_ref.shape[1:])
        up_bias_grad[...] = jnp.sum(grad_pre.astype(F32), axis=0, keepdims=True)
        up_part = mm(normed_t[...], grad_pre).astype(BF16)
        columns = pl.ds(pl.multiple_of(step * width, width), width)
        front_grad[:, :, columns] = up_part.reshape(16, width // 16, width)
        part = contract_cols(grad_pre, weight)
        total[...] = jnp.where(step == 0, part, total[...] + part)

    @pl.when(step == FF_STEPS - 1)
    def _():
        mid[...] = norm_grads(ff_gain_grad, ff_shift_grad)
        mid_out[...] = mid[...]

    @pl.when(step == first_pair)
    def _():
        start(mid[...], out_bias_grad)
        for p, part in enumerate(pairs_of(mm(grad[...], weight).astype(BF16))):
            grad_out[p] = part

    @pl.when((step >= first_pair) & (step < first_part))
    def _():
        p = step - first_pair
        for head in (0, 1):
            extend_keys(
                keys.at[head], values.at[head],
                [(key_ref[0, 0], value_ref[0, 0]), (key_far_ref[0, 0], value_far_ref[0, 0])], key_bias_ref, head,
            )
        attended[p] = attended_ref[0, 0].astype(BF16)

        def save(span, value):
            grads[0, p, span, :] = value

        pair_backward(
            lambda head, span: extended_ref[0, head, span, :], lambda span: grad_out[p, span, :],
            lambda span: attended_ref[0, 0, span, :], keys, values, key_sums, value_sums, rows, save,
        )
        first = lane_ids((rows, PAIR)) < HEAD_DIM
        for j, sums in enumerate((key_sums, value_sums)):
            grads[1 + j, p] = jnp.where(first, sums[0, :rows, :], sums[1, :rows, :]).astype(BF16)
            sent[p, j] = jnp.where(first, sums[0, rows:, :], sums[1, rows:, :]).astype(BF16)
        swap_of(p).start()

    @pl.when(step == first_part)
    def _():
        normed_t[...] = transposed_norm(hidden_ref, norm_ref)
        for p in range(pairs):
            swap_of(p).wait()
            for j in (0, 1):
                grads[1 + j, p] = (grads[1 + j, p].astype(F32) + arrived[p, j].astype(F32)).astype(BF16)

    @pl.when((step >= first_part) & (step < last))
    def _():
        j = step - first_part
        part = joined(grads, (j,))
        sums = jnp.sum(part.astype(F32), axis=0, keepdims=True)

        @pl.when(j == 0)
        def _():
            query_bias_grad[...] = sums

        @pl.when(j == 2)
        def _():
            value_bias_grad[...] = sums

        weight_grad[...] = mm(normed_t[...], part).astype(BF16).reshape(weight_grad.shape)
        product = contract_cols(part, weight)
        total[...] = jnp.where(j == 0, product, total[...] + product)

    @pl.when(step == last)
    def _():
        weight_grad[...] = contract_rows(grad[...], joined(attended)).astype(BF16).reshape(weight_grad.shape)
        out_ref[...] = norm_grads(gain_grad, shift_grad)


def backward(incoming, mask, hidden, act, slope, fronts, downs, norms, heads, key_bias, layer, guests, collective_id):
    rows, width = incoming.shape
    units, pairs = fronts.shape[3], width // PAIR
    first_part = FF_STEPS + pairs
    once = lambda shape: pl.BlockSpec(shape, lambda i: (0,) * len(shape), pipeline_mode=pl.Buffered(1))
    sub = lambda i: 2 * layer + jnp.where(i < FF_STEPS, 1, 0)
    unit = lambda i: jnp.minimum(i, FF_STEPS - 1)
    pair = lambda i: jnp.clip(i - FF_STEPS, 0, pairs - 1)
    column = lambda i: jnp.where(i < FF_STEPS, i, jnp.where(i < first_part, 3, jnp.minimum(i - first_part, 2)))
    per_unit = pl.BlockSpec((1, rows, width), lambda i: (layer, 0, unit(i)))
    per_pair = pl.BlockSpec((1, 1, rows, PAIR), lambda i: (layer, pair(i), 0, 0))
    down_blocks = 32 // FF_STEPS
    in_specs = [
        once((rows, width)), once((rows, 1)),
        pl.BlockSpec((1, rows, width), lambda i: (sub(i), 0, 0)), per_unit, per_unit,
        pl.BlockSpec((1, 16, width // 16, width), lambda i: (sub(i), 0, 0, column(i))),
        pl.BlockSpec((1, down_blocks) + downs.shape[2:], lambda i: (layer, unit(i), 0, 0)),
        pl.BlockSpec((1,) + norms.shape[1:], lambda i: (sub(i), 0, 0)),
        per_pair, per_pair, per_pair, per_pair,
        pl.BlockSpec((1, 2, rows, PAIR), lambda i: (layer, pair(i), 0, 0)), per_pair, once((2 * rows, 1)),
    ]
    full, vector = jax.ShapeDtypeStruct((rows, width), BF16), jax.ShapeDtypeStruct((1, width), F32)
    out_specs = [
        pl.BlockSpec((16, width // 16, width), lambda i: (0, 0, jnp.maximum(i - first_part, 0))),
        whole((rows, width)), whole((rows, width)), whole((1, width)), whole((1, width)),
        pl.BlockSpec((1, width), lambda i: (0, unit(i))),
    ] + [whole((1, width))] * 6
    out_shape = [
        jax.ShapeDtypeStruct((16, width // 16, units), BF16), full, full, vector, vector,
        jax.ShapeDtypeStruct((1, units), F32),
    ] + [vector] * 6
    vmem = pltpu.VMEM
    scratch = [
        vmem((rows, width), BF16), vmem((16, width // 16, units), BF16), vmem(downs.shape[1:], BF16),
        vmem((rows, width), BF16), vmem((width, rows), BF16), vmem((rows, width), F32),
        vmem((pairs, rows, PAIR), BF16), vmem((pairs, rows, PAIR), BF16), vmem((3, pairs, rows, PAIR), BF16),
        vmem((pairs, 2, rows, PAIR), BF16), vmem((pairs, 2, rows, PAIR), BF16),
        vmem((2, 2 * rows, PAIR), BF16), vmem((2, 2 * rows, PAIR), BF16),
        vmem((2, 2 * rows, PAIR), F32), vmem((2, 2 * rows, PAIR), F32),
        pltpu.SemaphoreType.DMA((pairs,)), pltpu.SemaphoreType.DMA((pairs,)),
    ]
    args = (incoming, mask, hidden, act, slope, fronts, downs, norms, *heads, key_bias)
    return hosted(
        backward_body, first_part + 4, list(zip(args, in_specs)), list(zip(out_shape, out_specs)), scratch,
        guests, collective_id, f"backward_{layer}", 63 * 2**20,
    )


def held_sum_guest(shapes, views, stages, targets, hop_steps):
    sems = pltpu.SemaphoreType.DMA
    sizes = [5 + len(sides(target)) for target in targets]

    def plan(spot, ins, outs, held, body):
        held = list(held)
        send, recv, csend, crecv = held[-4:]
        hooks = {}
        for i, (number, index) in enumerate(views):
            bufs, held = held[: sizes[i]], held[sizes[i] :]
            src = body[number].at[index]
            job = PlaneSum(
                spot, src, [src.at[pl.ds(spot.core * 8, 8)]] + bufs[:5], send.at[i], recv.at[i], in_place=True
            )
            chain = Chain(spot, outs[i], bufs[5:], targets[i], csend.at[i], crecv.at[i])
            actions = (job.start, job.first, job.second, functools.partial(job.third, outs[i]))
            for at, action in zip(stages[i], actions):
                hooks.setdefault(at, []).append(action)
            hooks.setdefault(hop_steps[i], []).append(functools.partial(chain.give, 1))
            hooks.setdefault("end", []).extend(
                [job.finish, functools.partial(chain.take, 1), functools.partial(chain.leave, 1)]
            )
        return hooks

    buffers = []
    for shape, target in zip(shapes, targets):
        buffers += PlaneSum.scratch(*shape)[1:] + [pltpu.VMEM((2,) + shape, BF16)] * len(sides(target))
    count = len(shapes)
    return Guest(
        (), [(jax.ShapeDtypeStruct((2,) + s, BF16), vmem_spec()) for s in shapes],
        buffers + [sems((count, 8)), sems((count, 8)), sems((count,)), sems((count, 2))], (), plan,
    )


def sides(target):
    return [name for name, any_there in (("below", target > 0), ("above", target < 3)) if any_there]


def hops_of(target):
    return max(target, 3 - target)


class Chain:
    def __init__(self, spot, total, bufs, target, send, recv):
        self.spot, self.total, self.target, self.send, self.recv = spot, total, target, send, recv
        self.from_below, self.from_above = bufs[0], bufs[-1]

    def ends(self, hop):
        last = self.spot.sections - 1
        return hop - 1 if hop <= self.target else None, last - hop + 1 if last - hop >= self.target else None

    def rise(self):
        return remote(self.total, self.from_below, self.send, self.recv.at[0], self.spot.above)

    def fall(self):
        return remote(self.total, self.from_above, self.send, self.recv.at[1], self.spot.below)

    def give(self, hop):
        below, above = self.ends(hop)
        if below is not None:
            pl.when(self.spot.z == below)(self.rise().start)
        if above is not None:
            pl.when(self.spot.z == above)(self.fall().start)

    def take(self, hop):
        below, above = self.ends(hop)
        if below is not None:
            @pl.when(self.spot.z == below + 1)
            def _():
                self.rise().wait_recv()
                add_into(self.total, self.from_below)
        if above is not None:
            @pl.when(self.spot.z == above - 1)
            def _():
                self.fall().wait_recv()
                add_into(self.total, self.from_above)

    def leave(self, hop):
        below, above = self.ends(hop)
        if below is not None:
            pl.when(self.spot.z == below)(self.rise().wait_send)
        if above is not None:
            pl.when(self.spot.z == above)(self.fall().wait_send)


def chain_guest(jobs, hop):
    sems = pltpu.SemaphoreType.DMA

    def plan(spot, ins, outs, held, body):
        held = list(held)
        send, recv, loads = held[-3:]
        begin, end = [], []
        for i, (_, target) in enumerate(jobs):
            bufs, held = held[: len(sides(target))], held[len(sides(target)) :]
            chain = Chain(spot, outs[i], bufs, target, send.at[i], recv.at[i])
            load = pltpu.make_async_copy(ins[i], outs[i], loads.at[i])
            begin.extend([load.start, load.wait, functools.partial(chain.give, hop)])
            end.extend([functools.partial(chain.take, hop), functools.partial(chain.leave, hop)])
        return {0: begin, "end": end}

    buffers = []
    for a, target in jobs:
        buffers += [pltpu.VMEM(a.shape, BF16)] * len(sides(target))
    return Guest(
        [(a, hbm_spec()) for a, _ in jobs], [(jax.ShapeDtypeStruct(a.shape, BF16), vmem_spec()) for a, _ in jobs],
        buffers + [sems((len(jobs),)), sems((len(jobs), 2)), sems((len(jobs),))], (), plan,
    )


def per_device(
    clip_inputs, out_grad, clip_class, w_front, w_back, norm_gain, norm_shift,
    bias_query_value, bias_attn_out, bias_up, bias_down,
):
    spot = Spot()
    sections = lax.axis_size("section")
    padded, width = clip_inputs.shape[1:]
    rows = -(-LONG // 32) * 16
    section = spot.z

    kind = lax.dynamic_index_in_dim(clip_class, section % 2, 0, False).astype(F32)
    norms = jnp.concatenate([norm_gain, norm_shift, jnp.zeros((6, width), F32)], axis=0)
    (
        key, value, key_far, value_far, extended, attended, act, slope,
        fronts, downs, hidden, incoming, acts_home, row_mask, key_bias, norm_all,
    ) = forward(
        clip_inputs, out_grad, jnp.broadcast_to(kind, (8, 128)), w_front[0], w_back[0], norms,
        bias_query_value, bias_attn_out, bias_up, bias_down, rows,
    )
    acts = [hidden[s + 1] for s in range(sections)]
    acts = [hidden[s + 1] for s in range(sections)]
    grads_home = jnp.zeros((clip_inputs.shape[0], 2 * rows, width), BF16)
    heads = (key, value, key_far, value_far, extended, attended)
    input_grads, grad_fronts = [None] * sections, [None] * sections
    grad_gain, grad_shift = [None] * sections, [None] * sections
    query_sums, value_sums, out_sums, up_sums, down_sums = ([None] * 2 for _ in range(5))
    units = fronts.shape[3] // 2
    halves = [pl.ds(0, units), pl.ds(units, units)]
    views = []
    for i in (0, 1):
        views += [(1, (slice(None), slice(None), halves[i])), (2, pl.ds(16 * i, 16))]
    shapes = [(width // 16, units), downs.shape[2:]] * 2
    stages = ((2, 3, 6, 8), (2, 3, 7, 9), (4, 5, 9, 11), (4, 5, 10, 12))
    hop_steps = (8, 9, 11, 12)
    early, late = range(0, 4), range(4, 8)
    for layer in (1, 0):
        targets = (2 * layer + 1, 2 * layer, 2 * layer + 1, 2 * layer + 1)
        guests = [held_sum_guest(shapes, views, stages, targets, hop_steps)]
        if layer == 1:
            guests.append(deliver_guest(
                [(acts[2], 2, 160, rows - 160, early), (acts[3], 3, 0, 528, early)], acts_home
            ))
        else:
            guests.append(chain_guest(list(zip(passing, (3, 2, 3, 3))), 2))
            guests.append(deliver_guest(
                [(input_grads[3], 3, 0, rows, early), (0, 1, 0, rows, late)], grads_home
            ))
            guests.append(deliver_guest([(acts[3], 3, 528, rows - 528, (0,))], acts_home))
        (
            grad_fronts[2 * layer], input_grads[2 * layer + 1], input_grads[2 * layer],
            grad_gain[2 * layer + 1], grad_shift[2 * layer + 1], up_sums[layer], down_sums[layer],
            grad_gain[2 * layer], grad_shift[2 * layer], query_sums[layer], value_sums[layer], out_sums[layer],
        ), carried = backward(
            incoming, row_mask, hidden, act, slope, fronts, downs, norm_all, heads, key_bias, layer, guests, 2 + layer
        )
        incoming = input_grads[2 * layer]
        if layer == 1:
            passing, (acts_home,) = carried
        else:
            later, earlier, (grads_home,), (acts_home,) = carried

    pair_sums = [jnp.concatenate([q, v], axis=1) for q, v in zip(query_sums, value_sums)]
    small = jnp.concatenate(
        [v.reshape(-1) for v in grad_gain + grad_shift + pair_sums + out_sums + up_sums + down_sums]
    )
    grads_home, front_out, back_out, small = collect(
        input_grads[0], input_grads[2], grads_home, grad_fronts[0],
        grad_fronts[2], [*earlier, *later], small.reshape(-1, 128),
    )
    front_out = front_out.reshape(width, -1)
    back_out = back_out.reshape(-1, width)
    small = small.reshape(-1)
    for bit in spot.spare_bits:
        small = small + swap(small, bit)
        front_out, back_out = add(front_out, swap(front_out, bit)), add(back_out, swap(back_out, bit))
    grads_out = jnp.pad(grads_home.astype(F32), ((0, 0), (0, padded - 2 * rows), (0, 0)))
    parts, place_at = [], 0
    layers, hidden_units = bias_up.shape
    for count, size in (
        (sections, width), (sections, width), (layers, 2 * width), (layers, width),
        (layers, hidden_units), (layers, width),
    ):
        parts.append(small[place_at : place_at + count * size].reshape(count, size))
        place_at += count * size
    return (
        acts_home[None],
        grads_out[None],
        front_out.astype(F32)[None],
        back_out.astype(F32)[None],
        lax.dynamic_slice_in_dim(parts[0], section, 1, 0),
        lax.dynamic_slice_in_dim(parts[1], section, 1, 0),
        *parts[2:],
    )


def solution(mesh):
    placed = (
        P("dp", None, None), P("dp", None, None), P("dp"),
        P("section", None, None), P("section", None, None), P("section", None), P("section", None),
        P(), P(), P(), P(),
    )
    return jax.shard_map(
        per_device,
        mesh=mesh,
        in_specs=placed,
        out_specs=(
            P("section", "dp", None, None), P("section", "dp", None, None),
            P("section", None, None), P("section", None, None), P("section", None), P("section", None),
            P(), P(), P(), P(),
        ),
        check_vma=False,
    )
```

```python
import functools
import math

import jax
import jax.numpy as jnp
from jax import lax
from jax.experimental import pallas as pl
from jax.experimental.pallas import tpu as pltpu
from jax.sharding import PartitionSpec as P

HEADS = 12
LONG = 1214
SHORT = 514
EPS = 1e-06
HEAD_DIM = 64
PAIR = 2 * HEAD_DIM
MASKED = -1e30
F32 = jnp.float32
BF16 = jnp.bfloat16
KERNEL_VMEM = 56 * 2**20


def mm(left, right):
    return jnp.dot(left, right, preferred_element_type=F32)


def contract_rows(left, right):
    return lax.dot_general(left, right, (((0,), (0,)), ((), ())), preferred_element_type=F32)


def contract_cols(left, right):
    return lax.dot_general(left, right, (((1,), (1,)), ((), ())), preferred_element_type=F32)


def swap(block, bit):
    count = lax.axis_size("dp")
    return lax.ppermute(block, "dp", [(i, i ^ bit) for i in range(count)])


def add(a, b):
    return (a.astype(F32) + b.astype(F32)).astype(BF16)


class Spot:
    def __init__(self):
        self.z, self.sections = lax.axis_index("section"), lax.axis_size("section")
        self.d, self.count = lax.axis_index("dp"), lax.axis_size("dp")
        self.x_bit, self.y_bit = 2, 2 * math.isqrt(self.count // 2)
        self.core = self.d % 2
        self.xb, self.yb = (self.d // self.x_bit) % 2, (self.d // self.y_bit) % 2
        self.c, self.c_x = self.yb * 2 + self.xb, self.yb * 2 + 1 - self.xb
        self.c_y, self.c_d = (1 - self.yb) * 2 + self.xb, (1 - self.yb) * 2 + 1 - self.xb
        self.mate, self.x, self.y = (self.flipped(b) for b in (1, self.x_bit, self.y_bit))
        self.above, self.below = {"section": self.z + 1}, {"section": self.z - 1}
        self.spare_bits = [
            1 << i for i in range(self.count.bit_length() - 1) if 1 << i not in (1, self.x_bit, self.y_bit)
        ]

    def flipped(self, bit):
        return {"dp": self.d + bit * (1 - 2 * ((self.d // bit) % 2))}

    def greet_mate(self):
        barrier = pltpu.get_barrier_semaphore()
        pl.semaphore_signal(barrier, inc=1, device_id=self.mate, device_id_type=pl.DeviceIdType.MESH)
        pl.semaphore_wait(barrier, 1)

    def greet(self):
        barrier = pltpu.get_barrier_semaphore()
        devices = [self.x, self.y]
        for step in range(self.sections):
            for core in (0, 1):
                if step or core:
                    devices.append({
                        "section": (self.z + step) % self.sections,
                        "dp": self.d - self.core + (self.core + core) % 2,
                    })
        for device in devices:
            pl.semaphore_signal(barrier, inc=1, device_id=device, device_id_type=pl.DeviceIdType.MESH)
        pl.semaphore_wait(barrier, len(devices))


def remote(src, dst, send, recv, device):
    return pltpu.make_async_remote_copy(
        src_ref=src, dst_ref=dst, send_sem=send, recv_sem=recv,
        device_id=device, device_id_type=pl.DeviceIdType.MESH,
    )


class PlaneGather:
    SENDS, RECEIVES = 9, 9

    def __init__(self, spot, dst, send, recv):
        self.spot, self.dst, self.send, self.recv = spot, dst, send, recv

    def blocks(self, core, chip, half=None):
        at = core * 8 + chip * 2
        return pl.ds(at, 2) if half is None else pl.ds(at + half, 1)

    def copies(self, own=None):
        s, k = self.spot, self.spot.core
        plan = {
            "x": (self.blocks(k, s.c), s.x), "y": (self.blocks(k, s.c), s.y),
            "m": (self.blocks(k, s.c), s.mate),
            "xy": (self.blocks(k, s.c_x, 0), s.y), "yx": (self.blocks(k, s.c_y, 1), s.x),
            "mx": (self.blocks(k, s.c_x), s.mate), "my": (self.blocks(k, s.c_y), s.mate),
            "md0": (self.blocks(k, s.c_d, 0), s.mate), "md1": (self.blocks(k, s.c_d, 1), s.mate),
        }
        out = {}
        for index, (name, (rows, device)) in enumerate(plan.items()):
            src = own if own is not None and name in ("x", "y", "m") else self.dst.at[rows]
            out[name] = remote(src, self.dst.at[rows], self.send.at[index], self.recv.at[index], device)
        return out

    def arrivals(self):
        s, k = self.spot, self.spot.core
        plan = {
            "x": self.blocks(k, s.c_x), "y": self.blocks(k, s.c_y), "m": self.blocks(1 - k, s.c),
            "xy": self.blocks(k, s.c_d, 0), "yx": self.blocks(k, s.c_d, 1),
            "mx": self.blocks(1 - k, s.c_x), "my": self.blocks(1 - k, s.c_y),
            "md0": self.blocks(1 - k, s.c_d, 0), "md1": self.blocks(1 - k, s.c_d, 1),
        }
        return {
            name: remote(self.dst.at[rows], self.dst.at[rows], self.send.at[i], self.recv.at[i], s.mate)
            for i, (name, rows) in enumerate(plan.items())
        }

    def begin(self, own):
        copies = self.copies(own)
        for name in ("x", "y", "m"):
            copies[name].start()

    def second(self):
        copies, arrivals = self.copies(), self.arrivals()
        arrivals["x"].wait_recv()
        copies["xy"].start()
        copies["mx"].start()
        arrivals["y"].wait_recv()
        copies["yx"].start()
        copies["my"].start()

    def third(self):
        copies, arrivals = self.copies(), self.arrivals()
        for name, after in (("xy", "md0"), ("yx", "md1")):
            arrivals[name].wait_recv()
            copies[after].start()

    def finish(self):
        copies, arrivals = self.copies(), self.arrivals()
        for name in copies:
            copies[name].wait_send()
        for name in ("m", "mx", "my", "md0", "md1"):
            arrivals[name].wait_recv()


class Deliver:
    def __init__(self, spot, src, dst, target, send, recv, start=0, size=None, sources=None):
        self.sources = range(spot.sections) if sources is None else sources
        self.spot, self.src, self.dst, self.target, self.send, self.recv = spot, src, dst, target, send, recv
        self.rows, self.start_row = src.shape[0], start
        self.size = size or src.shape[0]
        self.owner, self.slot = spot.z // 2, spot.z % 2
        self.home = (spot.z == target) & (spot.core == self.owner)

    def place(self, slot, core):
        at = pl.multiple_of(core * self.rows + self.start_row, 16)
        return self.dst.at[slot, pl.ds(at, self.size)]

    def copies(self):
        s, spot = self, self.spot
        spot_at, src = s.place(s.slot, spot.core), s.src.at[pl.ds(s.start_row, s.size)]
        away = remote(
            src, spot_at, s.send.at[0], s.recv.at[s.slot * 2 + spot.core],
            {"section": s.target, "dp": spot.d - spot.core + s.owner},
        )
        return away, pltpu.make_async_copy(src, spot_at, s.send.at[1])

    def start(self):
        away, stay = self.copies()
        chosen = self.chosen()
        pl.when(chosen & self.home)(stay.start)
        pl.when(chosen & jnp.logical_not(self.home))(away.start)

    def chosen(self):
        return (self.spot.z >= min(self.sources)) & (self.spot.z <= max(self.sources))

    def finish(self):
        away, stay = self.copies()
        chosen = self.chosen()
        pl.when(chosen & self.home)(stay.wait)
        pl.when(chosen & jnp.logical_not(self.home))(away.wait_send)
        spot = self.spot
        for slot in (0, 1):
            for core in (0, 1):
                source = spot.core * 2 + slot
                here = (source == spot.z) & (spot.core == core)
                sent = (source >= min(self.sources)) & (source <= max(self.sources))
                block = self.place(slot, core)
                landing = remote(block, block, self.send.at[0], self.recv.at[slot * 2 + core], spot.mate)
                pl.when((spot.z == self.target) & jnp.logical_not(here) & sent)(landing.wait_recv)


class Guest:
    def __init__(self, inputs=(), outputs=(), scratch=(), aliases=(), plan=None):
        self.inputs, self.outputs, self.scratch = list(inputs), list(outputs), list(scratch)
        self.aliases, self.plan = list(aliases), plan


def hbm_spec():
    return pl.BlockSpec(memory_space=pl.ANY)


def vmem_spec():
    return pl.BlockSpec(memory_space=pltpu.VMEM)


def hosted(body, grid, operands, results, scratch, guests, collective_id, name, vmem=KERNEL_VMEM):
    guest_in = [pair for g in guests for pair in g.inputs]
    guest_out = [pair for g in guests for pair in g.outputs]
    guest_scratch = [s for g in guests for s in g.scratch]
    aliases, at_in, at_out = {}, len(operands), len(results)
    for g in guests:
        for i, o in g.aliases:
            aliases[at_in + i] = at_out + o
        at_in, at_out = at_in + len(g.inputs), at_out + len(g.outputs)

    def kernel(*refs):
        refs = list(refs)
        take = lambda n: [refs.pop(0) for _ in range(n)]
        ins, gins = take(len(operands)), take(len(guest_in))
        outs, gouts = take(len(results)), take(len(guest_out))
        held, gheld = take(len(scratch)), take(len(guest_scratch))
        spot, step = Spot(), pl.program_id(0)
        pl.when(step == 0)(spot.greet)
        hooks = {}
        for g in guests:
            parts = [[r.pop(0) for _ in range(n)] for r, n in (
                (gins, len(g.inputs)), (gouts, len(g.outputs)), (gheld, len(g.scratch))
            )]
            for at, actions in g.plan(spot, *parts, held).items():
                hooks.setdefault(at, []).extend(actions)

        def run(actions):
            for action in actions:
                action()

        for at in sorted(k for k in hooks if k != "end"):
            pl.when(step == at)(functools.partial(run, hooks[at]))
        body(spot, *ins, *outs, *held)
        if "end" in hooks:
            pl.when(step == grid - 1)(functools.partial(run, hooks["end"]))

    out = pl.pallas_call(
        kernel,
        grid=(grid,),
        in_specs=[s for _, s in operands + guest_in],
        out_specs=[s for _, s in results + guest_out],
        out_shape=[s for s, _ in results + guest_out],
        scratch_shapes=list(scratch) + guest_scratch,
        input_output_aliases=aliases,
        compiler_params=pltpu.CompilerParams(
            vmem_limit_bytes=vmem, collective_id=collective_id, has_side_effects=True
        ),
        name=name,
    )(*[a for a, _ in operands + guest_in])
    own, rest, per_guest = out[: len(results)], list(out[len(results) :]), []
    for g in guests:
        per_guest.append([rest.pop(0) for _ in g.outputs])
    return own, per_guest


def deliver_guest(pieces, home):
    sems = pltpu.SemaphoreType.DMA
    count = len(pieces)
    arrays = [i for i, piece in enumerate(pieces) if not isinstance(piece[0], int)]

    def plan(spot, ins, outs, held, body):
        send, recv = held
        hooks = {}
        held_by = [body[p[0]] if isinstance(p[0], int) else ins[arrays.index(i)] for i, p in enumerate(pieces)]
        for i, (_, target, first, size, steps, *sources) in enumerate(pieces):
            blocks = size // 16
            for turn, step in enumerate(steps):
                low, high = blocks * turn // len(steps), blocks * (turn + 1) // len(steps)
                if high > low:
                    part = Deliver(
                        spot, held_by[i], outs[0], target, send.at[i], recv.at[i], first + 16 * low, 16 * (high - low),
                        *sources,
                    )
                    hooks.setdefault(step, []).append(part.start)
            every = Deliver(spot, held_by[i], outs[0], target, send.at[i], recv.at[i], first, size, *sources)
            hooks.setdefault("end", []).append(every.finish)
        return hooks

    return Guest(
        [(pieces[i][0], hbm_spec()) for i in arrays] + [(home, hbm_spec())],
        [(jax.ShapeDtypeStruct(home.shape, home.dtype), hbm_spec())],
        [sems((count, 2)), sems((count, 4))],
        [(len(arrays), 0)], plan,
    )


def add_into(target, *others):
    def step(b, carry):
        total = target[b].astype(F32)
        for other in others:
            total = total + other[b].astype(F32)
        target[b] = total.astype(BF16)
        return carry

    lax.fori_loop(0, target.shape[0], step, 0)


class PlaneSum:
    def __init__(self, spot, src, bufs, send, recv, in_place=False):
        self.spot, self.src, self.send, self.recv, self.in_place = spot, src, send, recv, in_place
        self.half, self.from_mate, self.in_x, self.in_y, self.in_yx, self.in_xy = bufs

    @staticmethod
    def scratch(block_rows, columns):
        return [pltpu.VMEM((n, block_rows, columns), BF16) for n in (8, 8, 2, 2, 1, 1)]

    def mate_copies(self):
        s, spot = self, self.spot
        away = remote(s.src.at[pl.ds((1 - spot.core) * 8, 8)], s.from_mate, s.send.at[1], s.recv.at[1], spot.mate)
        if s.in_place:
            return (away,)
        return (pltpu.make_async_copy(s.src.at[pl.ds(spot.core * 8, 8)], s.half, s.send.at[0]), away)

    def start(self):
        for copy in self.mate_copies():
            copy.start()

    def block(self, chip, half):
        return self.half.at[pl.ds(chip * 2 + half, 1)]

    def first_copies(self):
        s, spot = self, self.spot
        first, second = pl.ds(0, 1), pl.ds(1, 1)
        return (
            remote(s.block(spot.c_x, 0), s.in_x.at[first], s.send.at[2], s.recv.at[2], spot.x),
            remote(s.block(spot.c_d, 0), s.in_x.at[second], s.send.at[3], s.recv.at[3], spot.x),
            remote(s.block(spot.c_y, 1), s.in_y.at[first], s.send.at[4], s.recv.at[4], spot.y),
            remote(s.block(spot.c_d, 1), s.in_y.at[second], s.send.at[5], s.recv.at[5], spot.y),
        )

    def second_copies(self):
        s, spot = self, self.spot
        return (
            remote(s.block(spot.c_y, 0), s.in_xy, s.send.at[6], s.recv.at[6], spot.y),
            remote(s.block(spot.c_x, 1), s.in_yx, s.send.at[7], s.recv.at[7], spot.x),
        )

    def first(self):
        for copy in self.mate_copies():
            copy.wait()
        add_into(self.half, self.from_mate)
        for copy in self.first_copies():
            copy.start()

    def second(self):
        s, spot = self, self.spot
        for copy in self.first_copies():
            copy.wait_recv()
        first, other = pl.ds(0, 1), pl.ds(1, 1)
        add_into(s.block(spot.c_y, 0), s.in_x.at[other])
        add_into(s.block(spot.c_x, 1), s.in_y.at[other])
        for copy in self.second_copies():
            copy.start()

    def third(self, out):
        s, spot = self, self.spot
        for copy in self.second_copies():
            copy.wait_recv()
        first = pl.ds(0, 1)
        add_into(s.block(spot.c, 0), s.in_x.at[first], s.in_xy)
        add_into(s.block(spot.c, 1), s.in_y.at[first], s.in_yx)
        for half in (0, 1):
            out[half] = s.half[spot.c * 2 + half]

    def finish(self):
        for copy in self.first_copies() + self.second_copies():
            copy.wait_send()


LEFT = (
    ("front", 0, 3, 2), ("back", None, 2, 2), ("front", 1, 3, 2), ("back", None, 3, 2),
    ("front", 0, 1, 1), ("back", None, 0, 1), ("front", 1, 1, 1), ("back", None, 1, 0),
)


TAIL_CHUNKS = 4


def collect_body(*refs):
    sections = lax.axis_size("section")
    refs_list = list(refs)
    take = lambda n: [refs_list.pop(0) for _ in range(n)]
    last, second, third, first_front, third_front = take(5)
    parts = take(len(LEFT))
    vectors = take(2 * sections + 5 * (sections // 2))
    take(1)
    home, front_out, back_out, small_out = take(4)
    sums, arriving = take(2)
    totals = take(len(LEFT))
    psend, precv, dsend, drecv, asend, arecv, ssend, srecv, stay_sem, zsend, zrecv, lsem = take(12)
    spot = Spot()
    loads = [pltpu.make_async_copy(a, b, lsem.at[i]) for i, (a, b) in enumerate(zip(parts, totals))]
    for load in loads:
        load.start()
    spot.greet()
    size = first_front.shape[2] // TAIL_CHUNKS
    columns = [pl.ds(c * size, size) for c in range(TAIL_CHUNKS)]
    sequences = []

    def sequence(total, target, done):
        n = len(sequences)
        chain = Chain(spot, total, take(len(sides(target))), target, zsend.at[n], zrecv.at[n])
        sequences.append((chain, range(done + 1, hops_of(target) + 1)))
        return sequences[-1]

    def advance(which, turn):
        for chain, hops in which:
            if 0 < turn <= len(hops):
                chain.take(hops[turn - 1])
            if turn < len(hops):
                chain.give(hops[turn])

    chains = [sequence(total, target, done) for total, (_, _, target, done) in zip(totals, LEFT)]
    planes, owns, chunk_chains = {}, {}, {}
    for n, (z, grad) in enumerate(((0, first_front), (2, third_front))):
        for c in range(TAIL_CHUNKS):
            at = n * TAIL_CHUNKS + c
            planes[z, c] = PlaneSum(spot, grad.at[:, :, columns[c]], take(6), psend.at[at], precv.at[at])
            owns[z, c] = take(1)[0]
            chunk_chains[z, c] = sequence(owns[z, c], z, 0)
    every_chunk = range(TAIL_CHUNKS)
    for z in (0, 2):
        for c in every_chunk:
            planes[z, c].start()
    rows = last.shape[0]
    ahead = rows * 3 // 4 // 16 * 16
    early, late, every = (
        Deliver(spot, last, home, 0, dsend.at[0], drecv.at[0], *r) for r in ((0, ahead), (ahead, rows - ahead), ())
    )
    other = [
        Deliver(spot, second, home, 2, dsend.at[1], drecv.at[1], 0, rows, (0, 1)),
        Deliver(spot, third, home, 3, dsend.at[2], drecv.at[2], 400, rows - 400),
    ]
    at = 0
    for vector in vectors:
        for first in range(0, vector.shape[1], sums.shape[2]):
            sums[0, at : at + 1, :] = vector[:, first : first + sums.shape[2]]
            at += 1
    partners = [spot.mate, spot.x, spot.y] + [
        {"section": spot.z + bit * (1 - 2 * ((spot.z // bit) % 2))}
        for bit in (1 << i for i in range((sections - 1).bit_length()))
    ]
    steps = len(partners)

    def small_copy(i):
        return remote(sums.at[i], arriving.at[i], ssend.at[i], srecv.at[i], partners[i])

    def small_step(i):
        if 0 < i <= steps:
            small_copy(i - 1).wait()
            sums[i] = sums[i - 1] + arriving[i - 1]
        if i < steps:
            small_copy(i).start()

    small_step(0)
    for c in every_chunk:
        planes[0, c].first()
    for load in loads:
        load.wait()
    advance(chains, 0)
    early.start()
    for deliver in other:
        deliver.start()
    small_step(1)
    for c in every_chunk:
        planes[0, c].second()
        if c:
            planes[0, c - 1].third(owns[0, c - 1])
            advance([chunk_chains[0, c - 1]], 0)
        planes[2, c].first()
    planes[0, TAIL_CHUNKS - 1].third(owns[0, TAIL_CHUNKS - 1])
    advance([chunk_chains[0, TAIL_CHUNKS - 1]], 0)
    small_step(2)
    late.start()
    for c in every_chunk:
        advance([chunk_chains[0, c]], 1)
    advance(chains, 1)
    small_step(3)
    for c in every_chunk:
        advance([chunk_chains[0, c]], 2)
        planes[2, c].second()
        if c:
            planes[2, c - 1].third(owns[2, c - 1])
            advance([chunk_chains[2, c - 1]], 0)
    planes[2, TAIL_CHUNKS - 1].third(owns[2, TAIL_CHUNKS - 1])
    advance([chunk_chains[2, TAIL_CHUNKS - 1]], 0)
    small_step(4)
    advance(chains, 2)
    fronts = [PlaneGather(spot, front_out.at[:, :, columns[c]], asend.at[c], arecv.at[c]) for c in every_chunk]
    back = PlaneGather(spot, back_out, asend.at[TAIL_CHUNKS], arecv.at[TAIL_CHUNKS])

    def held(kind, z, c):
        if kind == "front" and z in (0, 2):
            return owns[z, c]
        found = [t for t, (name, _, target, _) in zip(totals, LEFT) if name == kind and target == z]
        if kind == "back":
            return found[0]
        half, at = divmod(c * size, found[0].shape[2])
        return found[half].at[:, :, pl.ds(at, size)]

    def begin(gather, kind, sections_now, c=0):
        for z in sections_now:
            stay = pltpu.make_async_copy(
                held(kind, z, c), gather.dst.at[gather.blocks(spot.core, spot.c)],
                stay_sem.at[TAIL_CHUNKS if kind == "back" else c],
            )

            @pl.when(spot.z == z)
            def _(z=z, stay=stay):
                stay.start()
                gather.begin(held(kind, z, c))

    def stayed():
        for c in range(TAIL_CHUNKS + 1):
            kind, gather = ("front", fronts[c]) if c < TAIL_CHUNKS else ("back", back)
            pltpu.make_async_copy(
                held(kind, 1, 0 if kind == "back" else c), gather.dst.at[gather.blocks(spot.core, spot.c)],
                stay_sem.at[c],
            ).wait()

    for c in every_chunk:
        begin(fronts[c], "front", (1, 3), c)
    for c in every_chunk:
        advance([chunk_chains[0, c]], 3)
        begin(fronts[c], "front", (0,), c)
    for c in every_chunk:
        advance([chunk_chains[2, c]], 1)
    small_step(5)
    small_out[...] = sums[steps]
    for c in every_chunk:
        advance([chunk_chains[2, c]], 2)
        begin(fronts[c], "front", (2,), c)
    begin(back, "back", range(sections))
    for gather in fronts:
        gather.second()
    back.second()
    for gather in (*fronts, back):
        gather.third()
    for gather in (*fronts, back):
        gather.finish()
    stayed()
    for deliver in (every, *other):
        deliver.finish()
    for plane in planes.values():
        plane.finish()
    for chain, hops in sequences:
        for hop in hops:
            chain.leave(hop)


def collect(last, second, third, home, first_front, third_front, parts, vectors):
    sections = lax.axis_size("section")
    width = last.shape[1]
    small = jax.ShapeDtypeStruct((sum(v.shape[1] // width for v in vectors), width), F32)
    hbm, vmem = hbm_spec(), vmem_spec()
    steps = 3 + (sections - 1).bit_length()
    sems = pltpu.SemaphoreType.DMA
    front_shape = first_front.shape
    chunk = (front_shape[1], front_shape[2] // TAIL_CHUNKS)
    back_shape = (16,) + parts[1].shape[1:]
    buffers = []
    for part, left in zip(parts, LEFT):
        buffers += [pltpu.VMEM(part.shape, BF16)] * len(sides(left[2]))
    for target in (0, 2):
        for _ in range(TAIL_CHUNKS):
            buffers += PlaneSum.scratch(*chunk) + [pltpu.VMEM((2,) + chunk, BF16)] * (1 + len(sides(target)))
    jobs = len(parts) + 2 * TAIL_CHUNKS
    return pl.pallas_call(
        collect_body,
        in_specs=[hbm] * (5 + len(parts)) + [vmem] * len(vectors) + [hbm],
        out_specs=[hbm] * 3 + [vmem],
        out_shape=[
            jax.ShapeDtypeStruct(home.shape, BF16), jax.ShapeDtypeStruct(front_shape, BF16),
            jax.ShapeDtypeStruct(back_shape, BF16), jax.ShapeDtypeStruct(small.shape, F32),
        ],
        scratch_shapes=[pltpu.VMEM((steps + 1,) + small.shape, F32), pltpu.VMEM((steps,) + small.shape, F32)]
        + [pltpu.VMEM(p.shape, BF16) for p in parts]
        + [
            sems((2 * TAIL_CHUNKS, 8)), sems((2 * TAIL_CHUNKS, 8)), sems((3, 2)), sems((3, 4)),
            sems((TAIL_CHUNKS + 1, 9)), sems((TAIL_CHUNKS + 1, 9)), sems((steps,)), sems((steps,)),
            sems((TAIL_CHUNKS + 1,)), sems((jobs,)), sems((jobs, 2)), sems((len(parts),)),
        ]
        + buffers,
        input_output_aliases={5 + len(parts) + len(vectors): 0},
        compiler_params=pltpu.CompilerParams(
            collective_id=1, has_side_effects=True, vmem_limit_bytes=KERNEL_VMEM
        ),
        name="collect",
    )(last, second, third, first_front, third_front, *parts, *vectors, home)


def norm_rows(hidden):
    average = jnp.mean(hidden, axis=-1, keepdims=True)
    centred = hidden - average
    inverse = lax.rsqrt(jnp.mean(centred * centred, axis=-1, keepdims=True) + EPS)
    return centred * inverse, inverse


def norm_backward(hidden, grad_normed, gain):
    unit, inverse = norm_rows(hidden)
    scaled = grad_normed * gain
    first = jnp.mean(scaled, axis=-1, keepdims=True)
    second = jnp.mean(scaled * unit, axis=-1, keepdims=True)
    return (
        inverse * (scaled - first - unit * second),
        jnp.sum(grad_normed * unit, axis=0, keepdims=True),
        jnp.sum(grad_normed, axis=0, keepdims=True),
    )


def gelu_and_slope(pre):
    density = jnp.exp(-0.5 * pre * pre)
    t = 1.0 / (1.0 + (0.3275911 * 0.5**0.5) * jnp.abs(pre))
    series = t * (0.127414796 + t * (-0.142248368 + t * (0.7107068705 + t * (-0.7265760135 + t * 0.5307027145))))
    tail = series * density
    below = jnp.where(pre < 0, tail, 1.0 - tail)
    return pre * below, below + pre * density * (1.0 / math.sqrt(2.0 * math.pi))


def pairs_of(block):
    return [block[:, p * PAIR : (p + 1) * PAIR] for p in range(block.shape[1] // PAIR)]


def joined(ref, lead=()):
    return jnp.concatenate([ref[lead + (p,)] for p in range(ref.shape[len(lead)])], axis=1)


def whole(shape):
    return pl.BlockSpec(shape, lambda i: (0,) * len(shape))


def swap_with_mate(spot, src, dst, send, recv):
    return remote(src, dst, send, recv, spot.mate)


def transposed_norm(hidden_ref, norm_ref):
    unit, _ = norm_rows(hidden_ref[0].astype(F32))
    normed = (unit * norm_ref[0, 0:1, :] + norm_ref[0, 1:2, :]).astype(BF16)
    return normed.astype(F32).T.astype(BF16)


def lane_ids(shape):
    return lax.broadcasted_iota(jnp.int32, shape, len(shape) - 1)


def three_parts(value):
    high = value.astype(BF16).astype(F32)
    rest = value - high
    middle = rest.astype(BF16).astype(F32)
    return high, middle, rest - middle


def extend_keys(keys_out, values_out, blocks, bias_ref, head):
    aux = HEAD_DIM * (1 - head)
    row = 0
    for key, value in blocks:
        rows = key.shape[0]
        span = slice(row, row + rows)
        lanes = lane_ids((rows, PAIR))
        inside = (lanes // HEAD_DIM) == head
        ones = jnp.where((lanes > aux) & (lanes <= aux + 3), 1.0, 0.0)
        extra = jnp.where(lanes == aux, bias_ref[span, :], ones)
        keys_out[span, :] = jnp.where(inside, key.astype(F32), extra).astype(BF16)
        ones = jnp.where((lanes >= aux) & (lanes < aux + 3), 1.0, 0.0)
        values_out[span, :] = jnp.where(inside, value.astype(F32), ones).astype(BF16)
        row += rows


def pair_forward(query_of, keys, values, rows, chunk, save):
    lanes = lane_ids((chunk, PAIR))
    units = [(start, head) for start in range(0, rows, chunk) for head in (0, 1)]

    def extended(start, head):
        aux = HEAD_DIM * (1 - head)
        inside = (lanes // HEAD_DIM) == head
        query = query_of(slice(start, start + chunk)).astype(F32)
        return jnp.where(inside, query, jnp.where(lanes == aux, 1.0, 0.0))

    def scores(start, head):
        return contract_cols(extended(start, head).astype(BF16), keys[head])

    ahead = [scores(*unit) for unit in units[:2]]
    for index, (start, head) in enumerate(units):
        now = ahead.pop(0)
        if index + 2 < len(units):
            ahead.append(scores(*units[index + 2]))
        aux = HEAD_DIM * (1 - head)
        top = jnp.max(now, axis=1, keepdims=True)
        summed = mm(jnp.exp(now - top).astype(BF16), values[head])
        total = summed[:, aux : aux + 1]
        query = extended(start, head)
        for lane, part in enumerate(three_parts(-(top + jnp.log(total))), aux + 1):
            query = jnp.where(lanes == lane, part, query)
        save(head, slice(start, start + chunk), query.astype(BF16), summed / total)


def pair_backward(query_of, grad_of, out_of, keys, values, key_sums, value_sums, rows, save):
    for start, size in ((0, 256), (256, rows - 256)):
        span = slice(start, start + size)
        lanes = lane_ids((size, PAIR))
        parts = []
        for head in (0, 1):
            aux = HEAD_DIM * (1 - head)
            inside = (lanes // HEAD_DIM) == head
            query = query_of(head, span)
            grad = jnp.where(inside, grad_of(span).astype(F32), 0.0)
            dots = jnp.sum(grad * out_of(span), axis=1, keepdims=True)
            for lane, part in enumerate(three_parts(-dots), aux):
                grad = jnp.where(lanes == lane, part, grad)
            probs = jnp.exp(contract_cols(query, keys[head]))
            shifted = contract_cols(grad.astype(BF16), values[head])
            grad_scores = (probs * shifted).astype(BF16)
            parts.append(mm(grad_scores, keys[head]) * HEAD_DIM**-0.5)
            to_values = mm(grad.T.astype(BF16), probs.astype(BF16)).T
            to_keys = mm(query.astype(F32).T.astype(BF16), grad_scores).T
            value_sums[head] = to_values if start == 0 else value_sums[head] + to_values
            key_sums[head] = to_keys if start == 0 else key_sums[head] + to_keys
        save(span, jnp.where(lanes < HEAD_DIM, parts[0], parts[1]).astype(BF16))


class Weight(PlaneGather):
    SENDS, RECEIVES = 13, 10

    def __init__(self, spot, src, dst, source, send, recv):
        super().__init__(spot, dst, send, recv)
        self.src, self.source = src, source
        self.own = self.blocks(spot.core, spot.c)

    def along(self, src):
        s = self.spot
        return (
            remote(src.at[self.own], self.dst.at[self.own], self.send.at[9], self.recv.at[9], s.above),
            remote(src.at[self.own], self.dst.at[self.own], self.send.at[10], self.recv.at[9], s.below),
        )

    def load(self):
        return pltpu.make_async_copy(self.src, self.dst, self.send.at[11])

    def open(self, up=True, down=True, load=True):
        rise, fall = self.along(self.src)

        @pl.when(self.spot.z == self.source)
        def _():
            if up and self.source + 1 < self.spot.sections:
                rise.start()
            if down and self.source:
                fall.start()
            if load:
                self.load().start()

    def pass_on(self, hop, begin=True):
        rise, fall = self.along(self.dst)
        last = self.spot.sections - 1
        for at, further, copy in ((self.source + hop, last, rise), (self.source - hop, 0, fall)):
            if not 0 <= at <= last:
                continue

            @pl.when(self.spot.z == at)
            def _(at=at, further=further, copy=copy):
                rise.wait_recv()
                if at != further:
                    copy.start()
                if begin:
                    self.begin(self.dst.at[self.own])

    def away(self, action):
        pl.when(self.spot.z != self.source)(action)

    def enter(self):
        self.away(lambda: self.begin(self.dst.at[self.own]))

    def middle(self):
        self.away(self.second)

    def late(self):
        self.away(self.third)

    def ready(self):
        rise, fall = self.along(self.src)
        last = self.spot.sections - 1
        if self.source < last:
            pl.when((self.spot.z >= self.source) & (self.spot.z < last))(rise.wait_send)
        if self.source:
            pl.when((self.spot.z <= self.source) & (self.spot.z > 0))(fall.wait_send)
        pl.when(self.spot.z == self.source)(self.load().wait)
        self.away(self.finish)


QKV_ORDER = (1, 2, 0, 3)
FORWARD_STEPS = 14


def forward_body(*refs):
    refs_list = list(refs)
    take = lambda n: [refs_list.pop(0) for _ in range(n)]
    clips, grads, front, back, norms, kind_in, bias_qv, bias_attn, bias_up, bias_down = take(10)
    key_out, value_out, key_far_out, value_far_out, extended_out, attended_out, act_out, slope_out = take(8)
    fronts_out, downs_out, hidden_out, grad_out, acts_home, mask_out, key_bias_out, norm_out = take(8)
    fronts, downs, hidden, own, far, attended, keys, values, normed, total, norm_all, kind, blank = take(13)
    wsend, wrecv, nsend, nrecv, csend, crecv, ksend, krecv, dsend, drecv, lsem = take(11)
    step = pl.program_id(0)
    layer, turn = step // FORWARD_STEPS, step % FORWARD_STEPS
    rows, width = normed.shape
    pairs = width // PAIR
    spot = Spot()
    owner, slot = spot.z // 2, spot.z % 2
    holds = spot.core == owner

    weights, count = {}, 0

    def weight(name, src, dst, source):
        nonlocal count
        weights[name] = Weight(spot, src, dst, source, wsend.at[count], wrecv.at[count])
        count += 1

    for j, block in enumerate(QKV_ORDER):
        at = pl.ds(block * width, width)
        weight(("first", j), front.at[:, :, at], fronts.at[0, :, :, at], 0)
    for s in range(1, 4):
        for n in range(1 + s % 2):
            size = fronts.shape[3] // (1 + s % 2)
            at = pl.ds(n * size, size)
            weight(("front", s, n), front.at[:, :, at], fronts.at[s, :, :, at], s)
    for s in range(4):
        weight(("back", s), back, downs.at[s // 2, pl.ds(16 * (s % 2), 16)], s)
    first = [weights["first", j] for j in range(4)]
    front_1, front_2, front_3 = ([weights["front", s, n] for n in range(1 + s % 2)] for s in (1, 2, 3))
    (front_2,) = front_2
    back_0, back_1, back_2, back_3 = (weights["back", s] for s in range(4))

    norm_copies = [
        remote(norms, norm_all.at[spot.z], nsend.at[i], nrecv.at[i], {"section": (spot.z + i) % spot.sections})
        for i in range(1, spot.sections)
    ]

    def clip_copies():
        mine, other = (pl.ds(pl.multiple_of(c * rows, 16), rows) for c in (spot.core, 1 - spot.core))
        away = [
            remote(clips.at[slot, other], hidden.at[0], csend.at[0], crecv.at[0], spot.mate),
            remote(grads.at[slot, other], grad_out, csend.at[1], crecv.at[1], spot.mate),
            remote(kind_in, kind, csend.at[2], crecv.at[2], spot.mate),
        ]
        stay = [
            pltpu.make_async_copy(clips.at[slot, mine], hidden.at[0], csend.at[3]),
            pltpu.make_async_copy(grads.at[slot, mine], grad_out, csend.at[4]),
        ]
        return away, stay

    def pads():
        pad = acts_home.shape[1] - 2 * rows
        return [
            pltpu.make_async_copy(blank, acts_home.at[i, pl.ds(2 * rows, pad)], lsem.at[i]) for i in (0, 1)
        ]

    def enter():
        blank[...] = jnp.zeros_like(blank)
        spot.greet()
        for w in first:
            w.open()
        away, stay = clip_copies()

        @pl.when(holds)
        def _():
            for copy in (away[2], away[0], stay[0], away[1]):
                copy.start()
            kind[...] = kind_in[...]
        for copy in norm_copies:
            copy.start()
        norm_all[spot.z] = norms[...]
        for w in (*front_1, back_1, front_2, back_2, *front_3, back_3):
            w.open(up=False)
        back_2.open(down=False, load=False)
        for w in first:
            for hop in (1, 2, 3):
                w.pass_on(hop)
        for w in (front_1[0], front_1[1], back_1, front_2):
            w.open(down=False, load=False)
        back_0.open()

        @pl.when(holds)
        def _():
            stay[1].start()
            stay[0].wait()

        @pl.when(jnp.logical_not(holds))
        def _():
            away[0].wait_recv()
            away[2].wait_recv()
        for i, copy in enumerate(norm_copies, 1):
            block = norm_all.at[(spot.z + spot.sections - i) % spot.sections]
            remote(block, block, nsend.at[i], nrecv.at[i], spot.mate).wait_recv()
        norm_out[...] = norm_all[...]
        for copy in pads():
            copy.start()
        length = SHORT + (LONG - SHORT) * kind[0:1, 0:1]
        place = lax.broadcasted_iota(jnp.int32, (rows, 1), 0)
        near, there = ((place + c * rows).astype(F32) < length for c in (spot.core, 1 - spot.core))
        mask_out[...] = near.astype(F32)
        key_bias_out[:rows, :] = jnp.where(near, 0.0, MASKED)
        key_bias_out[rows:, :] = jnp.where(there, 0.0, MASKED)
        for w in first:
            w.middle()
        for w in front_1:
            w.pass_on(1)
        back_1.pass_on(1)
        for w in first:
            w.late()
        for w in front_1:
            w.pass_on(2)
        first[0].ready()

    early, late = functools.partial, False
    plan = {
        0: [enter],
        1: [first[1].ready, early(back_1.pass_on, 2), early(back_0.pass_on, 1)],
        2: [first[2].ready, early(back_0.pass_on, 2), early(front_2.pass_on, 1, late), early(back_2.pass_on, 1, late)],
        3: [first[3].ready, early(back_0.pass_on, 3), *(early(w.pass_on, 1, late) for w in front_3)],
        4: [front_1[0].middle, early(back_3.pass_on, 1, late), early(front_2.pass_on, 2, late)],
        5: [front_1[1].middle, early(back_2.pass_on, 2, late)],
        6: [back_1.middle, *(early(w.pass_on, 2, late) for w in front_3), front_1[0].late],
        7: [back_0.middle, front_1[1].late, early(back_3.pass_on, 2, late)],
        8: [front_2.enter],
        9: [back_1.late, *(early(w.pass_on, 3, late) for w in front_3)],
        10: [back_0.late, early(back_3.pass_on, 3, late), front_1[0].ready, back_0.ready],
        11: [front_3[0].enter, back_2.enter],
        12: [front_1[1].ready, back_1.ready, front_2.middle],
        13: [front_2.late, front_3[1].enter, back_3.enter],
        14: [front_2.ready],
        15: [front_3[0].middle],
        17: [back_2.middle, front_3[0].late],
        18: [front_3[1].middle],
        19: [back_3.middle, back_2.late],
        20: [front_3[1].late],
        22: [back_3.late],
        24: [front_3[0].ready, back_2.ready],
        26: [front_3[1].ready, back_3.ready],
    }
    ends = []

    def keep(at, src, dst, index):
        copy = pltpu.make_async_copy(src, dst, lsem.at[2 + index])
        plan.setdefault(at, []).append(copy.start)
        ends.append(copy.wait)

    for s, at in ((0, 10), (1, 13), (2, 20), (3, 27)):
        keep(at, fronts.at[s], fronts_out.at[s], s)
    for layer_id, at in ((0, 15), (1, 27)):
        keep(at, downs.at[layer_id], downs_out.at[layer_id], 4 + layer_id)
    for s, at in ((0, 4), (1, 11), (2, 16), (3, 25)):
        keep(at, hidden.at[s], hidden_out.at[s], 6 + s)

    for n, (s, first_row, size, begin, stop) in enumerate(FORWARD_DELIVERIES):
        size = size or rows - first_row
        blocks = size // 16
        for i in range(stop - begin):
            low, high = blocks * i // (stop - begin), blocks * (i + 1) // (stop - begin)
            part = Deliver(
                spot, hidden.at[s + 1], acts_home, s, dsend.at[n], drecv.at[n], first_row + 16 * low, 16 * (high - low)
            )
            plan.setdefault(begin + i, []).append(part.start)
        ends.append(Deliver(spot, hidden.at[s + 1], acts_home, s, dsend.at[n], drecv.at[n], first_row, size).finish)

    for at, actions in sorted(plan.items()):
        @pl.when(step == at)
        def _(actions=actions):
            for action in actions:
                action()

    def norms_of(s):
        return norm_all[s, 0:1, :], norm_all[s, 1:2, :]

    def start_sub_layer(s):
        gain, shift = norms_of(s)
        unit, _ = norm_rows(hidden[s].astype(F32))
        normed[...] = (unit * gain + shift).astype(BF16)

    def front_block(s, block):
        return fronts[s, :, :, pl.ds(pl.multiple_of(block * width, width), width)].reshape(width, width)

    def swaps():
        return [
            remote(own.at[j], far.at[layer, j], ksend.at[layer, j], krecv.at[layer, j], spot.mate) for j in (0, 1)
        ]

    @pl.when(turn == 0)
    def _():
        start_sub_layer(2 * layer)

    for j, scale in ((0, 1.0), (1, 1.0), (2, HEAD_DIM**-0.5)):
        @pl.when(turn == j)
        def _(j=j, scale=scale):
            block = mm(normed[...], front_block(2 * layer, QKV_ORDER[j]))
            if j == 1:
                block = block + bias_qv[pl.ds(layer, 1), width:]
            elif j == 2:
                block = block + bias_qv[pl.ds(layer, 1), :width]
            block = block.astype(BF16)
            if scale != 1.0:
                block = (block.astype(F32) * scale).astype(BF16)
            for p, part in enumerate(pairs_of(block)):
                own[j, p] = part
            if j < 2:
                swaps()[j].start()
            else:
                for copy in swaps():
                    copy.wait()

    @pl.when((turn >= 3) & (turn < 3 + pairs))
    def _():
        p = turn - 3
        for head in (0, 1):
            extend_keys(
                keys.at[head], values.at[head], [(own[0, p], own[1, p]), (far[layer, 0, p], far[layer, 1, p])],
                key_bias_out, head,
            )
        for j, out in enumerate((key_out, value_out)):
            out[0, 0] = own[j, p]
        for j, out in enumerate((key_far_out, value_far_out)):
            out[0, 0] = far[layer, j, p]
        lanes = lane_ids((rows // 2, PAIR))
        firsts = {}

        def save(head, span, query, out):
            extended_out[0, head, span, :] = query
            if head == 0:
                firsts[span.start] = out
            else:
                both = jnp.where(lanes < HEAD_DIM, firsts[span.start], out)
                attended_out[0, 0, span, :] = both
                attended[p, span, :] = both.astype(BF16)

        pair_forward(lambda span: own[2, p, span, :], keys, values, rows, rows // 2, save)

    @pl.when(turn == 3 + pairs)
    def _():
        s = 2 * layer
        branch = contract_cols(joined(attended), front_block(s, 3)) + bias_attn[pl.ds(layer, 1), :]
        hidden[s + 1] = (mask_out[...] * (hidden[s].astype(F32) + branch)).astype(BF16)

    @pl.when(turn == 4 + pairs)
    def _():
        start_sub_layer(2 * layer + 1)

    @pl.when(turn >= 4 + pairs)
    def _():
        i = turn - 4 - pairs
        columns = pl.ds(pl.multiple_of(i * width, width), width)
        up = fronts[2 * layer + 1, :, :, columns].reshape(width, width)
        down_blocks = width * 32 // (width * 4)
        down = downs[layer, pl.ds(i * down_blocks, down_blocks)].reshape(width, width)
        bias = bias_up[pl.ds(layer, 1), columns]
        for span in (slice(0, rows // 2), slice(rows // 2, rows)):
            act, slope = gelu_and_slope(mm(normed[span, :], up) + bias)
            act_out[0, span, :] = act.astype(BF16)
            slope_out[0, span, :] = slope.astype(BF16)
            part = mm(act.astype(BF16), down)
            total[span, :] = jnp.where(i == 0, part, total[span, :] + part)

    @pl.when(turn == FORWARD_STEPS - 1)
    def _():
        s = 2 * layer + 1
        branch = total[...] + bias_down[pl.ds(layer, 1), :]
        hidden[s + 1] = (mask_out[...] * (hidden[s].astype(F32) + branch)).astype(BF16)

    @pl.when(step == 2 * FORWARD_STEPS - 1)
    def _():
        copy = pltpu.make_async_copy(hidden.at[4], hidden_out.at[4], lsem.at[12])
        copy.start()
        for end in ends:
            end()
        copy.wait()
        for pad in pads():
            pad.wait()
        for sent in norm_copies:
            sent.wait_send()
        away, stay = clip_copies()

        @pl.when(holds)
        def _():
            for sent in away:
                sent.wait_send()
            stay[1].wait()

        pl.when(jnp.logical_not(holds))(away[1].wait_recv)


FORWARD_DELIVERIES = ((0, 0, None, 10, 18), (1, 0, None, 14, 20))


def forward(clips, grads, kind, front, back, norms, bias_qv, bias_attn, bias_up, bias_down, rows):
    sections = lax.axis_size("section")
    padded, width = clips.shape[1:]
    units, pairs = front.shape[1], width // PAIR
    front_b = front.reshape(16, width // 16, units)
    back_b = back.reshape(16, back.shape[0] // 16, width)
    layers = sections // 2
    layer = lambda i: i // FORWARD_STEPS
    pair = lambda i: jnp.clip(i % FORWARD_STEPS - 3, 0, pairs - 1)
    unit = lambda i: jnp.maximum(i % FORWARD_STEPS - 4 - pairs, 0)
    hbm, vmem = hbm_spec(), vmem_spec()
    per_pair = pl.BlockSpec((1, 1, rows, PAIR), lambda i: (layer(i), pair(i), 0, 0))
    per_unit = pl.BlockSpec((1, rows, width), lambda i: (layer(i), 0, unit(i)))
    shape = jax.ShapeDtypeStruct
    saved = shape((layers, pairs, rows, PAIR), BF16)
    sems = pltpu.SemaphoreType.DMA
    jobs = 4 + 5 + 4
    sent = len(FORWARD_DELIVERIES)
    return pl.pallas_call(
        forward_body,
        grid=(2 * FORWARD_STEPS,),
        in_specs=[hbm] * 4 + [vmem] * 6,
        out_specs=[per_pair] * 4
        + [pl.BlockSpec((1, 2, rows, PAIR), lambda i: (layer(i), pair(i), 0, 0)), per_pair, per_unit, per_unit]
        + [hbm] * 5 + [vmem] * 3,
        out_shape=[saved] * 4
        + [
            shape((layers, 2 * pairs, rows, PAIR), BF16), shape((layers, pairs, rows, PAIR), F32),
            shape((layers, rows, units), BF16), shape((layers, rows, units), BF16),
            shape((sections,) + front_b.shape, BF16), shape((layers, 32) + back_b.shape[1:], BF16),
            shape((sections + 1, rows, width), BF16), shape((rows, width), BF16),
            shape((clips.shape[0], padded, width), BF16),
            shape((rows, 1), F32), shape((2 * rows, 1), F32), shape((sections,) + norms.shape, F32),
        ],
        scratch_shapes=[
            pltpu.VMEM((sections,) + front_b.shape, BF16), pltpu.VMEM((layers, 32) + back_b.shape[1:], BF16),
            pltpu.VMEM((sections + 1, rows, width), BF16), pltpu.VMEM((3, pairs, rows, PAIR), BF16),
            pltpu.VMEM((layers, 2, pairs, rows, PAIR), BF16), pltpu.VMEM((pairs, rows, PAIR), BF16),
            pltpu.VMEM((2, 2 * rows, PAIR), BF16), pltpu.VMEM((2, 2 * rows, PAIR), BF16),
            pltpu.VMEM((rows, width), BF16), pltpu.VMEM((rows, width), F32),
            pltpu.VMEM((sections,) + norms.shape, F32), pltpu.VMEM(kind.shape, F32),
            pltpu.VMEM((padded - 2 * rows, width), BF16),
            sems((jobs, Weight.SENDS)), sems((jobs, Weight.RECEIVES)), sems((sections,)), sems((sections,)),
            sems((5,)), sems((3,)), sems((layers, 2)), sems((layers, 2)), sems((sent, 2)), sems((sent, 4)), sems((13,)),
        ],
        compiler_params=pltpu.CompilerParams(
            vmem_limit_bytes=63 * 2**20, collective_id=0, has_side_effects=True
        ),
        name="forward",
    )(clips, grads, front_b, back_b, norms, kind, bias_qv, bias_attn, bias_up, bias_down)


FF_STEPS = 4


def backward_body(
    spot, incoming_ref, mask_ref, hidden_ref, act_ref, slope_ref, front_ref, down_ref, norm_ref,
    key_ref, value_ref, key_far_ref, value_far_ref, extended_ref, attended_ref, key_bias_ref,
    weight_grad, mid_out, out_ref, ff_gain_grad, ff_shift_grad, up_bias_grad, down_bias_grad,
    gain_grad, shift_grad, query_bias_grad, value_bias_grad, out_bias_grad,
    mid, front_grad, down_grad, grad, normed_t, total, grad_out, attended, grads, sent, arrived,
    keys, values, key_sums, value_sums, send, recv,
):
    step, last = pl.program_id(0), pl.num_programs(0) - 1
    rows, width = grad.shape
    pairs = width // PAIR
    first_pair, first_part = FF_STEPS, FF_STEPS + pairs
    weight = front_ref[0].reshape(width, width)

    def swap_of(p):
        return remote(sent.at[p], arrived.at[p], send.at[p], recv.at[p], spot.mate)

    def start(source, bias_sums):
        grad_rows = mask_ref[...] * source.astype(F32)
        grad[...] = grad_rows.astype(BF16)
        bias_sums[...] = jnp.sum(grad_rows, axis=0, keepdims=True)

    def norm_grads(gain_sums, shift_sums):
        grad_hidden, gain_sums[...], shift_sums[...] = norm_backward(
            hidden_ref[0].astype(F32), total[...], norm_ref[0, 0:1, :]
        )
        return (grad[...].astype(F32) + grad_hidden).astype(BF16)

    @pl.when(step == 0)
    def _():
        start(incoming_ref[...], down_bias_grad)
        normed_t[...] = transposed_norm(hidden_ref, norm_ref)

    @pl.when(step < FF_STEPS)
    def _():
        down = down_ref[0].reshape(width, width)
        blocks = down_ref.shape[1]
        grad_pre = (contract_cols(grad[...], down) * slope_ref[0].astype(F32)).astype(BF16)
        down_part = contract_rows(act_ref[0], grad[...]).astype(BF16)
        down_grad[pl.ds(step * blocks, blocks)] = down_part.reshape(down_ref.shape[1:])
        up_bias_grad[...] = jnp.sum(grad_pre.astype(F32), axis=0, keepdims=True)
        up_part = mm(normed_t[...], grad_pre).astype(BF16)
        columns = pl.ds(pl.multiple_of(step * width, width), width)
        front_grad[:, :, columns] = up_part.reshape(16, width // 16, width)
        part = contract_cols(grad_pre, weight)
        total[...] = jnp.where(step == 0, part, total[...] + part)

    @pl.when(step == FF_STEPS - 1)
    def _():
        mid[...] = norm_grads(ff_gain_grad, ff_shift_grad)
        mid_out[...] = mid[...]

    @pl.when(step == first_pair)
    def _():
        start(mid[...], out_bias_grad)
        for p, part in enumerate(pairs_of(mm(grad[...], weight).astype(BF16))):
            grad_out[p] = part

    @pl.when((step >= first_pair) & (step < first_part))
    def _():
        p = step - first_pair
        for head in (0, 1):
            extend_keys(
                keys.at[head], values.at[head],
                [(key_ref[0, 0], value_ref[0, 0]), (key_far_ref[0, 0], value_far_ref[0, 0])], key_bias_ref, head,
            )
        attended[p] = attended_ref[0, 0].astype(BF16)

        def save(span, value):
            grads[0, p, span, :] = value

        pair_backward(
            lambda head, span: extended_ref[0, head, span, :], lambda span: grad_out[p, span, :],
            lambda span: attended_ref[0, 0, span, :], keys, values, key_sums, value_sums, rows, save,
        )
        first = lane_ids((rows, PAIR)) < HEAD_DIM
        for j, sums in enumerate((key_sums, value_sums)):
            grads[1 + j, p] = jnp.where(first, sums[0, :rows, :], sums[1, :rows, :]).astype(BF16)
            sent[p, j] = jnp.where(first, sums[0, rows:, :], sums[1, rows:, :]).astype(BF16)
        swap_of(p).start()

    @pl.when(step == first_part)
    def _():
        normed_t[...] = transposed_norm(hidden_ref, norm_ref)
        for p in range(pairs):
            swap_of(p).wait()
            for j in (0, 1):
                grads[1 + j, p] = (grads[1 + j, p].astype(F32) + arrived[p, j].astype(F32)).astype(BF16)

    @pl.when((step >= first_part) & (step < last))
    def _():
        j = step - first_part
        part = joined(grads, (j,))
        sums = jnp.sum(part.astype(F32), axis=0, keepdims=True)

        @pl.when(j == 0)
        def _():
            query_bias_grad[...] = sums

        @pl.when(j == 2)
        def _():
            value_bias_grad[...] = sums

        weight_grad[...] = mm(normed_t[...], part).astype(BF16).reshape(weight_grad.shape)
        product = contract_cols(part, weight)
        total[...] = jnp.where(j == 0, product, total[...] + product)

    @pl.when(step == last)
    def _():
        weight_grad[...] = contract_rows(grad[...], joined(attended)).astype(BF16).reshape(weight_grad.shape)
        out_ref[...] = norm_grads(gain_grad, shift_grad)


def backward(incoming, mask, hidden, act, slope, fronts, downs, norms, heads, key_bias, layer, guests, collective_id):
    rows, width = incoming.shape
    units, pairs = fronts.shape[3], width // PAIR
    first_part = FF_STEPS + pairs
    once = lambda shape: pl.BlockSpec(shape, lambda i: (0,) * len(shape), pipeline_mode=pl.Buffered(1))
    sub = lambda i: 2 * layer + jnp.where(i < FF_STEPS, 1, 0)
    unit = lambda i: jnp.minimum(i, FF_STEPS - 1)
    pair = lambda i: jnp.clip(i - FF_STEPS, 0, pairs - 1)
    column = lambda i: jnp.where(i < FF_STEPS, i, jnp.where(i < first_part, 3, jnp.minimum(i - first_part, 2)))
    per_unit = pl.BlockSpec((1, rows, width), lambda i: (layer, 0, unit(i)))
    per_pair = pl.BlockSpec((1, 1, rows, PAIR), lambda i: (layer, pair(i), 0, 0))
    down_blocks = 32 // FF_STEPS
    in_specs = [
        once((rows, width)), once((rows, 1)),
        pl.BlockSpec((1, rows, width), lambda i: (sub(i), 0, 0)), per_unit, per_unit,
        pl.BlockSpec((1, 16, width // 16, width), lambda i: (sub(i), 0, 0, column(i))),
        pl.BlockSpec((1, down_blocks) + downs.shape[2:], lambda i: (layer, unit(i), 0, 0)),
        pl.BlockSpec((1,) + norms.shape[1:], lambda i: (sub(i), 0, 0)),
        per_pair, per_pair, per_pair, per_pair,
        pl.BlockSpec((1, 2, rows, PAIR), lambda i: (layer, pair(i), 0, 0)), per_pair, once((2 * rows, 1)),
    ]
    full, vector = jax.ShapeDtypeStruct((rows, width), BF16), jax.ShapeDtypeStruct((1, width), F32)
    out_specs = [
        pl.BlockSpec((16, width // 16, width), lambda i: (0, 0, jnp.maximum(i - first_part, 0))),
        whole((rows, width)), whole((rows, width)), whole((1, width)), whole((1, width)),
        pl.BlockSpec((1, width), lambda i: (0, unit(i))),
    ] + [whole((1, width))] * 6
    out_shape = [
        jax.ShapeDtypeStruct((16, width // 16, units), BF16), full, full, vector, vector,
        jax.ShapeDtypeStruct((1, units), F32),
    ] + [vector] * 6
    vmem = pltpu.VMEM
    scratch = [
        vmem((rows, width), BF16), vmem((16, width // 16, units), BF16), vmem(downs.shape[1:], BF16),
        vmem((rows, width), BF16), vmem((width, rows), BF16), vmem((rows, width), F32),
        vmem((pairs, rows, PAIR), BF16), vmem((pairs, rows, PAIR), BF16), vmem((3, pairs, rows, PAIR), BF16),
        vmem((pairs, 2, rows, PAIR), BF16), vmem((pairs, 2, rows, PAIR), BF16),
        vmem((2, 2 * rows, PAIR), BF16), vmem((2, 2 * rows, PAIR), BF16),
        vmem((2, 2 * rows, PAIR), F32), vmem((2, 2 * rows, PAIR), F32),
        pltpu.SemaphoreType.DMA((pairs,)), pltpu.SemaphoreType.DMA((pairs,)),
    ]
    args = (incoming, mask, hidden, act, slope, fronts, downs, norms, *heads, key_bias)
    return hosted(
        backward_body, first_part + 4, list(zip(args, in_specs)), list(zip(out_shape, out_specs)), scratch,
        guests, collective_id, f"backward_{layer}", 63 * 2**20,
    )


def held_sum_guest(shapes, views, stages, targets, hop_steps):
    sems = pltpu.SemaphoreType.DMA
    hopping = [sides(target) if at is not None else [] for target, at in zip(targets, hop_steps)]
    sizes = [5 + len(names) for names in hopping]

    def plan(spot, ins, outs, held, body):
        held = list(held)
        send, recv, csend, crecv = held[-4:]
        hooks = {}
        for i, (number, index) in enumerate(views):
            bufs, held = held[: sizes[i]], held[sizes[i] :]
            src = body[number].at[index]
            job = PlaneSum(
                spot, src, [src.at[pl.ds(spot.core * 8, 8)]] + bufs[:5], send.at[i], recv.at[i], in_place=True
            )
            actions = (job.start, job.first, job.second, functools.partial(job.third, outs[i]))
            for at, action in zip(stages[i], actions):
                hooks.setdefault(at, []).append(action)
            hooks.setdefault("end", []).append(job.finish)
            if hop_steps[i] is not None:
                chain = Chain(spot, outs[i], bufs[5:], targets[i], csend.at[i], crecv.at[i])
                hooks.setdefault(hop_steps[i], []).append(functools.partial(chain.give, 1))
                hooks["end"].extend([functools.partial(chain.take, 1), functools.partial(chain.leave, 1)])
        return hooks

    buffers = []
    for shape, names in zip(shapes, hopping):
        buffers += PlaneSum.scratch(*shape)[1:] + [pltpu.VMEM((2,) + shape, BF16)] * len(names)
    count = len(shapes)
    return Guest(
        (), [(jax.ShapeDtypeStruct((2,) + s, BF16), vmem_spec()) for s in shapes],
        buffers + [sems((count, 8)), sems((count, 8)), sems((count,)), sems((count, 2))], (), plan,
    )


def sides(target):
    return [name for name, any_there in (("below", target > 0), ("above", target < 3)) if any_there]


def hops_of(target):
    return max(target, 3 - target)


class Chain:
    def __init__(self, spot, total, bufs, target, send, recv):
        self.spot, self.total, self.target, self.send, self.recv = spot, total, target, send, recv
        self.from_below, self.from_above = bufs[0], bufs[-1]

    def ends(self, hop):
        last = self.spot.sections - 1
        return hop - 1 if hop <= self.target else None, last - hop + 1 if last - hop >= self.target else None

    def rise(self):
        return remote(self.total, self.from_below, self.send, self.recv.at[0], self.spot.above)

    def fall(self):
        return remote(self.total, self.from_above, self.send, self.recv.at[1], self.spot.below)

    def give(self, hop):
        below, above = self.ends(hop)
        if below is not None:
            pl.when(self.spot.z == below)(self.rise().start)
        if above is not None:
            pl.when(self.spot.z == above)(self.fall().start)

    def take(self, hop):
        below, above = self.ends(hop)
        if below is not None:
            @pl.when(self.spot.z == below + 1)
            def _():
                self.rise().wait_recv()
                add_into(self.total, self.from_below)
        if above is not None:
            @pl.when(self.spot.z == above - 1)
            def _():
                self.fall().wait_recv()
                add_into(self.total, self.from_above)

    def leave(self, hop):
        below, above = self.ends(hop)
        if below is not None:
            pl.when(self.spot.z == below)(self.rise().wait_send)
        if above is not None:
            pl.when(self.spot.z == above)(self.fall().wait_send)


def chain_guest(jobs):
    sems = pltpu.SemaphoreType.DMA

    def plan(spot, ins, outs, held, body):
        held = list(held)
        send, recv, loads = held[-3:]
        hooks, ends = {}, []
        for i, (_, target, first, steps) in enumerate(jobs):
            bufs, held = held[: len(sides(target))], held[len(sides(target)) :]
            chain = Chain(spot, outs[i], bufs, target, send.at[i], recv.at[i])
            load = pltpu.make_async_copy(ins[i], outs[i], loads.at[i])
            hooks.setdefault(0, []).extend([load.start, load.wait])
            for n, at in enumerate(steps):
                hop = first + n
                if n:
                    hooks.setdefault(at, []).append(functools.partial(chain.take, hop - 1))
                hooks.setdefault(at, []).append(functools.partial(chain.give, hop))
                ends.append(functools.partial(chain.leave, hop))
            ends.append(functools.partial(chain.take, first + len(steps) - 1))
        hooks["end"] = ends
        return hooks

    buffers = []
    for a, target, _, _ in jobs:
        buffers += [pltpu.VMEM(a.shape, BF16)] * len(sides(target))
    return Guest(
        [(job[0], hbm_spec()) for job in jobs],
        [(jax.ShapeDtypeStruct(job[0].shape, BF16), vmem_spec()) for job in jobs],
        buffers + [sems((len(jobs),)), sems((len(jobs), 2)), sems((len(jobs),))], (), plan,
    )


def per_device(
    clip_inputs, out_grad, clip_class, w_front, w_back, norm_gain, norm_shift,
    bias_query_value, bias_attn_out, bias_up, bias_down,
):
    spot = Spot()
    sections = lax.axis_size("section")
    padded, width = clip_inputs.shape[1:]
    rows = -(-LONG // 32) * 16
    section = spot.z

    kind = lax.dynamic_index_in_dim(clip_class, section % 2, 0, False).astype(F32)
    norms = jnp.concatenate([norm_gain, norm_shift, jnp.zeros((6, width), F32)], axis=0)
    (
        key, value, key_far, value_far, extended, attended, act, slope,
        fronts, downs, hidden, incoming, acts_home, row_mask, key_bias, norm_all,
    ) = forward(
        clip_inputs, out_grad, jnp.broadcast_to(kind, (8, 128)), w_front[0], w_back[0], norms,
        bias_query_value, bias_attn_out, bias_up, bias_down, rows,
    )
    acts = [hidden[s + 1] for s in range(sections)]
    acts = [hidden[s + 1] for s in range(sections)]
    grads_home = jnp.zeros((clip_inputs.shape[0], 2 * rows, width), BF16)
    heads = (key, value, key_far, value_far, extended, attended)
    input_grads, grad_fronts = [None] * sections, [None] * sections
    grad_gain, grad_shift = [None] * sections, [None] * sections
    query_sums, value_sums, out_sums, up_sums, down_sums = ([None] * 2 for _ in range(5))
    units = fronts.shape[3] // 2
    halves = [pl.ds(0, units), pl.ds(units, units)]
    views = []
    for i in (0, 1):
        views += [(1, (slice(None), slice(None), halves[i])), (2, pl.ds(16 * i, 16))]
    shapes = [(width // 16, units), downs.shape[2:]] * 2
    stages = ((2, 3, 6, 8), (2, 3, 7, 9), (4, 5, 9, 12), (4, 5, 11, "end"))
    hop_steps = {1: (8, 9, None, None), 0: (8, 9, 12, None)}
    early, late = range(0, 4), range(4, 8)
    for layer in (1, 0):
        targets = (2 * layer + 1, 2 * layer, 2 * layer + 1, 2 * layer + 1)
        guests = [held_sum_guest(shapes, views, stages, targets, hop_steps[layer])]
        if layer == 1:
            guests.append(deliver_guest(
                [(acts[2], 2, 0, rows, early), (acts[3], 3, 0, 400, early)], acts_home
            ))
        else:
            done = ((3, 2, (1,)), (2, 2, (1,)), (3, 1, (0, 5)), (3, 1, (0, 5)))
            guests.append(chain_guest([(part, *hops) for part, hops in zip(passing, done)]))
            guests.append(deliver_guest(
                [(input_grads[3], 3, 0, 400, early), (0, 1, 0, rows, late), (input_grads[2], 2, 0, rows, early, (2, 3))],
                grads_home
            ))
            guests.append(deliver_guest([(acts[3], 3, 400, rows - 400, early)], acts_home))
        (
            grad_fronts[2 * layer], input_grads[2 * layer + 1], input_grads[2 * layer],
            grad_gain[2 * layer + 1], grad_shift[2 * layer + 1], up_sums[layer], down_sums[layer],
            grad_gain[2 * layer], grad_shift[2 * layer], query_sums[layer], value_sums[layer], out_sums[layer],
        ), carried = backward(
            incoming, row_mask, hidden, act, slope, fronts, downs, norm_all, heads, key_bias, layer, guests, 2 + layer
        )
        incoming = input_grads[2 * layer]
        if layer == 1:
            passing, (acts_home,) = carried
        else:
            later, earlier, (grads_home,), (acts_home,) = carried

    pair_sums = [v for both in zip(query_sums, value_sums) for v in both]
    vectors = grad_gain + grad_shift + pair_sums + out_sums + up_sums + down_sums
    grads_home, front_out, back_out, small = collect(
        input_grads[0], input_grads[2], input_grads[3], grads_home, grad_fronts[0],
        grad_fronts[2], [*earlier, *later], vectors,
    )
    front_out = front_out.reshape(width, -1)
    back_out = back_out.reshape(-1, width)
    for bit in spot.spare_bits:
        small = small + swap(small, bit)
        front_out, back_out = add(front_out, swap(front_out, bit)), add(back_out, swap(back_out, bit))
    grads_out = jnp.pad(grads_home.astype(F32), ((0, 0), (0, padded - 2 * rows), (0, 0)))
    parts, place_at = [], 0
    layers, hidden_units = bias_up.shape
    for count, size in (
        (sections, width), (sections, width), (layers, 2 * width), (layers, width),
        (layers, hidden_units), (layers, width),
    ):
        taken = count * size // width
        parts.append(small[place_at : place_at + taken].reshape(count, size))
        place_at += taken
    return (
        acts_home[None],
        grads_out[None],
        front_out.astype(F32)[None],
        back_out.astype(F32)[None],
        lax.dynamic_slice_in_dim(parts[0], section, 1, 0),
        lax.dynamic_slice_in_dim(parts[1], section, 1, 0),
        *parts[2:],
    )


def solution(mesh):
    placed = (
        P("dp", None, None), P("dp", None, None), P("dp"),
        P("section", None, None), P("section", None, None), P("section", None), P("section", None),
        P(), P(), P(), P(),
    )
    return jax.shard_map(
        per_device,
        mesh=mesh,
        in_specs=placed,
        out_specs=(
            P("section", "dp", None, None), P("section", "dp", None, None),
            P("section", None, None), P("section", None, None), P("section", None), P("section", None),
            P(), P(), P(), P(),
        ),
        check_vma=False,
    )
```

```python
import functools
import math

import jax
import jax.numpy as jnp
from jax import lax
from jax.experimental import pallas as pl
from jax.experimental.pallas import tpu as pltpu
from jax.sharding import PartitionSpec as P

HEADS = 12
LONG = 1214
SHORT = 514
EPS = 1e-06
HEAD_DIM = 64
PAIR = 2 * HEAD_DIM
MASKED = -1e30
F32 = jnp.float32
BF16 = jnp.bfloat16
KERNEL_VMEM = 56 * 2**20


def mm(left, right):
    return jnp.dot(left, right, preferred_element_type=F32)


def contract_rows(left, right):
    return lax.dot_general(left, right, (((0,), (0,)), ((), ())), preferred_element_type=F32)


def contract_cols(left, right):
    return lax.dot_general(left, right, (((1,), (1,)), ((), ())), preferred_element_type=F32)


def swap(block, bit):
    count = lax.axis_size("dp")
    return lax.ppermute(block, "dp", [(i, i ^ bit) for i in range(count)])


def add(a, b):
    return (a.astype(F32) + b.astype(F32)).astype(BF16)


class Spot:
    def __init__(self):
        self.z, self.sections = lax.axis_index("section"), lax.axis_size("section")
        self.d, self.count = lax.axis_index("dp"), lax.axis_size("dp")
        self.x_bit, self.y_bit = 2, 2 * math.isqrt(self.count // 2)
        self.core = self.d % 2
        self.xb, self.yb = (self.d // self.x_bit) % 2, (self.d // self.y_bit) % 2
        self.c, self.c_x = self.yb * 2 + self.xb, self.yb * 2 + 1 - self.xb
        self.c_y, self.c_d = (1 - self.yb) * 2 + self.xb, (1 - self.yb) * 2 + 1 - self.xb
        self.mate, self.x, self.y = (self.flipped(b) for b in (1, self.x_bit, self.y_bit))
        self.above, self.below = {"section": self.z + 1}, {"section": self.z - 1}
        self.spare_bits = [
            1 << i for i in range(self.count.bit_length() - 1) if 1 << i not in (1, self.x_bit, self.y_bit)
        ]

    def flipped(self, bit):
        return {"dp": self.d + bit * (1 - 2 * ((self.d // bit) % 2))}

    def greet_mate(self):
        barrier = pltpu.get_barrier_semaphore()
        pl.semaphore_signal(barrier, inc=1, device_id=self.mate, device_id_type=pl.DeviceIdType.MESH)
        pl.semaphore_wait(barrier, 1)

    def greet(self):
        barrier = pltpu.get_barrier_semaphore()
        devices = [self.x, self.y]
        for step in range(self.sections):
            for core in (0, 1):
                if step or core:
                    devices.append({
                        "section": (self.z + step) % self.sections,
                        "dp": self.d - self.core + (self.core + core) % 2,
                    })
        for device in devices:
            pl.semaphore_signal(barrier, inc=1, device_id=device, device_id_type=pl.DeviceIdType.MESH)
        pl.semaphore_wait(barrier, len(devices))


def remote(src, dst, send, recv, device):
    return pltpu.make_async_remote_copy(
        src_ref=src, dst_ref=dst, send_sem=send, recv_sem=recv,
        device_id=device, device_id_type=pl.DeviceIdType.MESH,
    )


class PlaneGather:
    SENDS, RECEIVES = 9, 9

    def __init__(self, spot, dst, send, recv):
        self.spot, self.dst, self.send, self.recv = spot, dst, send, recv

    def blocks(self, core, chip, half=None):
        at = core * 8 + chip * 2
        return pl.ds(at, 2) if half is None else pl.ds(at + half, 1)

    def copies(self, own=None):
        s, k = self.spot, self.spot.core
        plan = {
            "x": (self.blocks(k, s.c), s.x), "y": (self.blocks(k, s.c), s.y),
            "m": (self.blocks(k, s.c), s.mate),
            "xy": (self.blocks(k, s.c_x, 0), s.y), "yx": (self.blocks(k, s.c_y, 1), s.x),
            "mx": (self.blocks(k, s.c_x), s.mate), "my": (self.blocks(k, s.c_y), s.mate),
            "md0": (self.blocks(k, s.c_d, 0), s.mate), "md1": (self.blocks(k, s.c_d, 1), s.mate),
        }
        out = {}
        for index, (name, (rows, device)) in enumerate(plan.items()):
            src = own if own is not None and name in ("x", "y", "m") else self.dst.at[rows]
            out[name] = remote(src, self.dst.at[rows], self.send.at[index], self.recv.at[index], device)
        return out

    def arrivals(self):
        s, k = self.spot, self.spot.core
        plan = {
            "x": self.blocks(k, s.c_x), "y": self.blocks(k, s.c_y), "m": self.blocks(1 - k, s.c),
            "xy": self.blocks(k, s.c_d, 0), "yx": self.blocks(k, s.c_d, 1),
            "mx": self.blocks(1 - k, s.c_x), "my": self.blocks(1 - k, s.c_y),
            "md0": self.blocks(1 - k, s.c_d, 0), "md1": self.blocks(1 - k, s.c_d, 1),
        }
        return {
            name: remote(self.dst.at[rows], self.dst.at[rows], self.send.at[i], self.recv.at[i], s.mate)
            for i, (name, rows) in enumerate(plan.items())
        }

    def begin(self, own):
        copies = self.copies(own)
        for name in ("x", "y", "m"):
            copies[name].start()

    def second(self):
        copies, arrivals = self.copies(), self.arrivals()
        arrivals["x"].wait_recv()
        copies["xy"].start()
        copies["mx"].start()
        arrivals["y"].wait_recv()
        copies["yx"].start()
        copies["my"].start()

    def third(self):
        copies, arrivals = self.copies(), self.arrivals()
        for name, after in (("xy", "md0"), ("yx", "md1")):
            arrivals[name].wait_recv()
            copies[after].start()

    def finish(self):
        copies, arrivals = self.copies(), self.arrivals()
        for name in copies:
            copies[name].wait_send()
        for name in ("m", "mx", "my", "md0", "md1"):
            arrivals[name].wait_recv()


class Deliver:
    def __init__(self, spot, src, dst, target, send, recv, start=0, size=None, sources=None):
        self.sources = range(spot.sections) if sources is None else sources
        self.spot, self.src, self.dst, self.target, self.send, self.recv = spot, src, dst, target, send, recv
        self.rows, self.start_row = src.shape[0], start
        self.size = size or src.shape[0]
        self.owner, self.slot = spot.z // 2, spot.z % 2
        self.home = (spot.z == target) & (spot.core == self.owner)

    def place(self, slot, core):
        at = pl.multiple_of(core * self.rows + self.start_row, 16)
        return self.dst.at[slot, pl.ds(at, self.size)]

    def copies(self):
        s, spot = self, self.spot
        spot_at, src = s.place(s.slot, spot.core), s.src.at[pl.ds(s.start_row, s.size)]
        away = remote(
            src, spot_at, s.send.at[0], s.recv.at[s.slot * 2 + spot.core],
            {"section": s.target, "dp": spot.d - spot.core + s.owner},
        )
        return away, pltpu.make_async_copy(src, spot_at, s.send.at[1])

    def start(self):
        away, stay = self.copies()
        chosen = self.chosen()
        pl.when(chosen & self.home)(stay.start)
        pl.when(chosen & jnp.logical_not(self.home))(away.start)

    def chosen(self):
        return (self.spot.z >= min(self.sources)) & (self.spot.z <= max(self.sources))

    def finish(self):
        away, stay = self.copies()
        chosen = self.chosen()
        pl.when(chosen & self.home)(stay.wait)
        pl.when(chosen & jnp.logical_not(self.home))(away.wait_send)
        spot = self.spot
        for slot in (0, 1):
            for core in (0, 1):
                source = spot.core * 2 + slot
                here = (source == spot.z) & (spot.core == core)
                sent = (source >= min(self.sources)) & (source <= max(self.sources))
                block = self.place(slot, core)
                landing = remote(block, block, self.send.at[0], self.recv.at[slot * 2 + core], spot.mate)
                pl.when((spot.z == self.target) & jnp.logical_not(here) & sent)(landing.wait_recv)


class Guest:
    def __init__(self, inputs=(), outputs=(), scratch=(), aliases=(), plan=None):
        self.inputs, self.outputs, self.scratch = list(inputs), list(outputs), list(scratch)
        self.aliases, self.plan = list(aliases), plan


def hbm_spec():
    return pl.BlockSpec(memory_space=pl.ANY)


def vmem_spec():
    return pl.BlockSpec(memory_space=pltpu.VMEM)


def hosted(body, grid, operands, results, scratch, guests, collective_id, name, vmem=KERNEL_VMEM):
    guest_in = [pair for g in guests for pair in g.inputs]
    guest_out = [pair for g in guests for pair in g.outputs]
    guest_scratch = [s for g in guests for s in g.scratch]
    aliases, at_in, at_out = {}, len(operands), len(results)
    for g in guests:
        for i, o in g.aliases:
            aliases[at_in + i] = at_out + o
        at_in, at_out = at_in + len(g.inputs), at_out + len(g.outputs)

    def kernel(*refs):
        refs = list(refs)
        take = lambda n: [refs.pop(0) for _ in range(n)]
        ins, gins = take(len(operands)), take(len(guest_in))
        outs, gouts = take(len(results)), take(len(guest_out))
        held, gheld = take(len(scratch)), take(len(guest_scratch))
        spot, step = Spot(), pl.program_id(0)
        pl.when(step == 0)(spot.greet)
        hooks = {}
        for g in guests:
            parts = [[r.pop(0) for _ in range(n)] for r, n in (
                (gins, len(g.inputs)), (gouts, len(g.outputs)), (gheld, len(g.scratch))
            )]
            for at, actions in g.plan(spot, *parts, held).items():
                hooks.setdefault(at, []).extend(actions)

        def run(actions):
            for action in actions:
                action()

        for at in sorted(k for k in hooks if k != "end"):
            pl.when(step == at)(functools.partial(run, hooks[at]))
        body(spot, *ins, *outs, *held)
        if "end" in hooks:
            pl.when(step == grid - 1)(functools.partial(run, hooks["end"]))

    out = pl.pallas_call(
        kernel,
        grid=(grid,),
        in_specs=[s for _, s in operands + guest_in],
        out_specs=[s for _, s in results + guest_out],
        out_shape=[s for s, _ in results + guest_out],
        scratch_shapes=list(scratch) + guest_scratch,
        input_output_aliases=aliases,
        compiler_params=pltpu.CompilerParams(
            vmem_limit_bytes=vmem, collective_id=collective_id, has_side_effects=True
        ),
        name=name,
    )(*[a for a, _ in operands + guest_in])
    own, rest, per_guest = out[: len(results)], list(out[len(results) :]), []
    for g in guests:
        per_guest.append([rest.pop(0) for _ in g.outputs])
    return own, per_guest


def deliver_guest(pieces, home):
    sems = pltpu.SemaphoreType.DMA
    count = len(pieces)
    fresh = isinstance(home, jax.ShapeDtypeStruct)
    arrays = [i for i, piece in enumerate(pieces) if not isinstance(piece[0], int)]

    def plan(spot, ins, outs, held, body):
        send, recv = held
        hooks = {}
        held_by = []
        for i, piece in enumerate(pieces):
            if isinstance(piece[0], int):
                held_by.append(body[piece[0]])
            elif isinstance(piece[0], tuple):
                held_by.append(ins[arrays.index(i)].at[piece[0][1]])
            else:
                held_by.append(ins[arrays.index(i)])
        for i, (_, target, first, size, steps, *sources) in enumerate(pieces):
            blocks = size // 16
            for turn, step in enumerate(steps):
                low, high = blocks * turn // len(steps), blocks * (turn + 1) // len(steps)
                if high > low:
                    part = Deliver(
                        spot, held_by[i], outs[0], target, send.at[i], recv.at[i], first + 16 * low, 16 * (high - low),
                        *sources,
                    )
                    hooks.setdefault(step, []).append(part.start)
            every = Deliver(spot, held_by[i], outs[0], target, send.at[i], recv.at[i], first, size, *sources)
            hooks.setdefault("end", []).append(every.finish)
        return hooks

    return Guest(
        [(pieces[i][0][0] if isinstance(pieces[i][0], tuple) else pieces[i][0], hbm_spec()) for i in arrays]
        + ([] if fresh else [(home, hbm_spec())]),
        [(jax.ShapeDtypeStruct(home.shape, home.dtype), hbm_spec())],
        [sems((count, 2)), sems((count, 4))],
        [] if fresh else [(len(arrays), 0)], plan,
    )


def add_into(target, *others):
    def step(b, carry):
        total = target[b].astype(F32)
        for other in others:
            total = total + other[b].astype(F32)
        target[b] = total.astype(BF16)
        return carry

    lax.fori_loop(0, target.shape[0], step, 0)


class PlaneSum:
    def __init__(self, spot, src, bufs, send, recv, in_place=False):
        self.spot, self.src, self.send, self.recv, self.in_place = spot, src, send, recv, in_place
        self.half, self.from_mate, self.in_x, self.in_y, self.in_yx, self.in_xy = bufs

    @staticmethod
    def scratch(block_rows, columns):
        return [pltpu.VMEM((n, block_rows, columns), BF16) for n in (8, 8, 2, 2, 1, 1)]

    def mate_copies(self):
        s, spot = self, self.spot
        away = remote(s.src.at[pl.ds((1 - spot.core) * 8, 8)], s.from_mate, s.send.at[1], s.recv.at[1], spot.mate)
        if s.in_place:
            return (away,)
        return (pltpu.make_async_copy(s.src.at[pl.ds(spot.core * 8, 8)], s.half, s.send.at[0]), away)

    def start(self):
        for copy in self.mate_copies():
            copy.start()

    def block(self, chip, half):
        return self.half.at[pl.ds(chip * 2 + half, 1)]

    def first_copies(self):
        s, spot = self, self.spot
        first, second = pl.ds(0, 1), pl.ds(1, 1)
        return (
            remote(s.block(spot.c_x, 0), s.in_x.at[first], s.send.at[2], s.recv.at[2], spot.x),
            remote(s.block(spot.c_d, 0), s.in_x.at[second], s.send.at[3], s.recv.at[3], spot.x),
            remote(s.block(spot.c_y, 1), s.in_y.at[first], s.send.at[4], s.recv.at[4], spot.y),
            remote(s.block(spot.c_d, 1), s.in_y.at[second], s.send.at[5], s.recv.at[5], spot.y),
        )

    def second_copies(self):
        s, spot = self, self.spot
        return (
            remote(s.block(spot.c_y, 0), s.in_xy, s.send.at[6], s.recv.at[6], spot.y),
            remote(s.block(spot.c_x, 1), s.in_yx, s.send.at[7], s.recv.at[7], spot.x),
        )

    def first(self):
        for copy in self.mate_copies():
            copy.wait()
        add_into(self.half, self.from_mate)
        for copy in self.first_copies():
            copy.start()

    def second(self):
        s, spot = self, self.spot
        for copy in self.first_copies():
            copy.wait_recv()
        first, other = pl.ds(0, 1), pl.ds(1, 1)
        add_into(s.block(spot.c_y, 0), s.in_x.at[other])
        add_into(s.block(spot.c_x, 1), s.in_y.at[other])
        for copy in self.second_copies():
            copy.start()

    def third(self, out):
        s, spot = self, self.spot
        for copy in self.second_copies():
            copy.wait_recv()
        first = pl.ds(0, 1)
        add_into(s.block(spot.c, 0), s.in_x.at[first], s.in_xy)
        add_into(s.block(spot.c, 1), s.in_y.at[first], s.in_yx)
        for half in (0, 1):
            out[half] = s.half[spot.c * 2 + half]

    def finish(self):
        for copy in self.first_copies() + self.second_copies():
            copy.wait_send()


LEFT = (
    ("front", 0, 3, 2), ("back", None, 2, 2), ("front", 1, 3, 2), ("back", None, 3, 2),
    ("front", 0, 1, 1), ("back", None, 0, 1), ("front", 1, 1, 1), ("back", None, 1, 0),
)


TAIL_CHUNKS = 4


def collect_body(*refs):
    sections = lax.axis_size("section")
    refs_list = list(refs)
    take = lambda n: [refs_list.pop(0) for _ in range(n)]
    last, second, third, first_front, third_front = take(5)
    parts = take(len(LEFT))
    vectors = take(2 * sections + 5 * (sections // 2))
    take(1)
    home, front_out, back_out, small_out = take(4)
    sums, arriving = take(2)
    totals = take(len(LEFT))
    psend, precv, dsend, drecv, asend, arecv, ssend, srecv, stay_sem, zsend, zrecv, lsem = take(12)
    spot = Spot()
    loads = [pltpu.make_async_copy(a, b, lsem.at[i]) for i, (a, b) in enumerate(zip(parts, totals))]
    for load in loads:
        load.start()
    spot.greet()
    size = first_front.shape[2] // TAIL_CHUNKS
    columns = [pl.ds(c * size, size) for c in range(TAIL_CHUNKS)]
    sequences = []

    def sequence(total, target, done):
        n = len(sequences)
        chain = Chain(spot, total, take(len(sides(target))), target, zsend.at[n], zrecv.at[n])
        sequences.append((chain, range(done + 1, hops_of(target) + 1)))
        return sequences[-1]

    def advance(which, turn):
        for chain, hops in which:
            if 0 < turn <= len(hops):
                chain.take(hops[turn - 1])
            if turn < len(hops):
                chain.give(hops[turn])

    chains = [sequence(total, target, done) for total, (_, _, target, done) in zip(totals, LEFT)]
    planes, owns, chunk_chains = {}, {}, {}
    for n, (z, grad) in enumerate(((0, first_front), (2, third_front))):
        for c in range(TAIL_CHUNKS):
            at = n * TAIL_CHUNKS + c
            planes[z, c] = PlaneSum(spot, grad.at[:, :, columns[c]], take(6), psend.at[at], precv.at[at])
            owns[z, c] = take(1)[0]
            chunk_chains[z, c] = sequence(owns[z, c], z, 0)
    every_chunk = range(TAIL_CHUNKS)
    for z in (0, 2):
        for c in every_chunk:
            planes[z, c].start()
    rows = last.shape[0]
    ahead = rows * 3 // 4 // 16 * 16
    early, late, every = (
        Deliver(spot, last, home, 0, dsend.at[0], drecv.at[0], *r) for r in ((0, ahead), (ahead, rows - ahead), ())
    )
    other = [
        Deliver(spot, second, home, 2, dsend.at[1], drecv.at[1], 0, rows, (0, 1)),
        Deliver(spot, third, home, 3, dsend.at[2], drecv.at[2], 400, rows - 400),
    ]
    at = 0
    for vector in vectors:
        for first in range(0, vector.shape[1], sums.shape[2]):
            sums[0, at : at + 1, :] = vector[:, first : first + sums.shape[2]]
            at += 1
    partners = [spot.mate, spot.x, spot.y] + [
        {"section": spot.z + bit * (1 - 2 * ((spot.z // bit) % 2))}
        for bit in (1 << i for i in range((sections - 1).bit_length()))
    ]
    steps = len(partners)

    def small_copy(i):
        return remote(sums.at[i], arriving.at[i], ssend.at[i], srecv.at[i], partners[i])

    def small_step(i):
        if 0 < i <= steps:
            small_copy(i - 1).wait()
            sums[i] = sums[i - 1] + arriving[i - 1]
        if i < steps:
            small_copy(i).start()

    small_step(0)
    for c in every_chunk:
        planes[0, c].first()
    for load in loads:
        load.wait()
    advance(chains, 0)
    early.start()
    for deliver in other:
        deliver.start()
    small_step(1)
    for c in every_chunk:
        planes[0, c].second()
        if c:
            planes[0, c - 1].third(owns[0, c - 1])
            advance([chunk_chains[0, c - 1]], 0)
        planes[2, c].first()
    planes[0, TAIL_CHUNKS - 1].third(owns[0, TAIL_CHUNKS - 1])
    advance([chunk_chains[0, TAIL_CHUNKS - 1]], 0)
    fronts = [PlaneGather(spot, front_out.at[:, :, columns[c]], asend.at[c], arecv.at[c]) for c in every_chunk]
    back = PlaneGather(spot, back_out, asend.at[TAIL_CHUNKS], arecv.at[TAIL_CHUNKS])

    def held(kind, z, c):
        if kind == "front" and z in (0, 2):
            return owns[z, c]
        found = [t for t, (name, _, target, _) in zip(totals, LEFT) if name == kind and target == z]
        if kind == "back":
            return found[0]
        half, at = divmod(c * size, found[0].shape[2])
        return found[half].at[:, :, pl.ds(at, size)]

    def begin(gather, kind, sections_now, c=0):
        for z in sections_now:
            stay = pltpu.make_async_copy(
                held(kind, z, c), gather.dst.at[gather.blocks(spot.core, spot.c)],
                stay_sem.at[TAIL_CHUNKS if kind == "back" else c],
            )

            @pl.when(spot.z == z)
            def _(z=z, stay=stay):
                stay.start()
                gather.begin(held(kind, z, c))

    def stayed():
        for c in range(TAIL_CHUNKS + 1):
            kind, gather = ("front", fronts[c]) if c < TAIL_CHUNKS else ("back", back)
            pltpu.make_async_copy(
                held(kind, 1, 0 if kind == "back" else c), gather.dst.at[gather.blocks(spot.core, spot.c)],
                stay_sem.at[c],
            ).wait()

    small_step(2)
    late.start()
    for c in every_chunk:
        advance([chunk_chains[0, c]], 1)
    advance(chains, 1)
    small_step(3)
    for c in every_chunk:
        advance([chunk_chains[0, c]], 2)
        planes[2, c].second()
        if c:
            planes[2, c - 1].third(owns[2, c - 1])
            advance([chunk_chains[2, c - 1]], 0)
    planes[2, TAIL_CHUNKS - 1].third(owns[2, TAIL_CHUNKS - 1])
    advance([chunk_chains[2, TAIL_CHUNKS - 1]], 0)
    for c in every_chunk:
        begin(fronts[c], "front", (1, 3), c)
    begin(back, "back", (2, 3))
    small_step(4)
    advance(chains, 2)
    begin(back, "back", (0, 1))
    for c in every_chunk:
        advance([chunk_chains[0, c]], 3)
        begin(fronts[c], "front", (0,), c)
    for c in every_chunk:
        advance([chunk_chains[2, c]], 1)
    small_step(5)
    small_out[...] = sums[steps]
    for c in every_chunk:
        advance([chunk_chains[2, c]], 2)
        begin(fronts[c], "front", (2,), c)
    for gather in fronts:
        gather.second()
    back.second()
    for gather in (*fronts, back):
        gather.third()
    for gather in (*fronts, back):
        gather.finish()
    stayed()
    for deliver in (every, *other):
        deliver.finish()
    for plane in planes.values():
        plane.finish()
    for chain, hops in sequences:
        for hop in hops:
            chain.leave(hop)


def collect(last, second, third, home, first_front, third_front, parts, vectors):
    sections = lax.axis_size("section")
    width = last.shape[1]
    small = jax.ShapeDtypeStruct((sum(v.shape[1] // width for v in vectors), width), F32)
    hbm, vmem = hbm_spec(), vmem_spec()
    steps = 3 + (sections - 1).bit_length()
    sems = pltpu.SemaphoreType.DMA
    front_shape = first_front.shape
    chunk = (front_shape[1], front_shape[2] // TAIL_CHUNKS)
    back_shape = (16,) + parts[1].shape[1:]
    buffers = []
    for part, left in zip(parts, LEFT):
        buffers += [pltpu.VMEM(part.shape, BF16)] * len(sides(left[2]))
    for target in (0, 2):
        for _ in range(TAIL_CHUNKS):
            buffers += PlaneSum.scratch(*chunk) + [pltpu.VMEM((2,) + chunk, BF16)] * (1 + len(sides(target)))
    jobs = len(parts) + 2 * TAIL_CHUNKS
    return pl.pallas_call(
        collect_body,
        in_specs=[hbm] * (5 + len(parts)) + [vmem] * len(vectors) + [hbm],
        out_specs=[hbm] * 3 + [vmem],
        out_shape=[
            jax.ShapeDtypeStruct(home.shape, BF16), jax.ShapeDtypeStruct(front_shape, BF16),
            jax.ShapeDtypeStruct(back_shape, BF16), jax.ShapeDtypeStruct(small.shape, F32),
        ],
        scratch_shapes=[pltpu.VMEM((steps + 1,) + small.shape, F32), pltpu.VMEM((steps,) + small.shape, F32)]
        + [pltpu.VMEM(p.shape, BF16) for p in parts]
        + [
            sems((2 * TAIL_CHUNKS, 8)), sems((2 * TAIL_CHUNKS, 8)), sems((3, 2)), sems((3, 4)),
            sems((TAIL_CHUNKS + 1, 9)), sems((TAIL_CHUNKS + 1, 9)), sems((steps,)), sems((steps,)),
            sems((TAIL_CHUNKS + 1,)), sems((jobs,)), sems((jobs, 2)), sems((len(parts),)),
        ]
        + buffers,
        input_output_aliases={5 + len(parts) + len(vectors): 0},
        compiler_params=pltpu.CompilerParams(
            collective_id=1, has_side_effects=True, vmem_limit_bytes=KERNEL_VMEM
        ),
        name="collect",
    )(last, second, third, first_front, third_front, *parts, *vectors, home)


def norm_rows(hidden):
    average = jnp.mean(hidden, axis=-1, keepdims=True)
    centred = hidden - average
    inverse = lax.rsqrt(jnp.mean(centred * centred, axis=-1, keepdims=True) + EPS)
    return centred * inverse, inverse


def norm_backward(hidden, grad_normed, gain):
    unit, inverse = norm_rows(hidden)
    scaled = grad_normed * gain
    first = jnp.mean(scaled, axis=-1, keepdims=True)
    second = jnp.mean(scaled * unit, axis=-1, keepdims=True)
    return (
        inverse * (scaled - first - unit * second),
        jnp.sum(grad_normed * unit, axis=0, keepdims=True),
        jnp.sum(grad_normed, axis=0, keepdims=True),
    )


def gelu_and_slope(pre):
    density = jnp.exp(-0.5 * pre * pre)
    t = 1.0 / (1.0 + (0.3275911 * 0.5**0.5) * jnp.abs(pre))
    series = t * (0.127414796 + t * (-0.142248368 + t * (0.7107068705 + t * (-0.7265760135 + t * 0.5307027145))))
    tail = series * density
    below = jnp.where(pre < 0, tail, 1.0 - tail)
    return pre * below, below + pre * density * (1.0 / math.sqrt(2.0 * math.pi))


def pairs_of(block):
    return [block[:, p * PAIR : (p + 1) * PAIR] for p in range(block.shape[1] // PAIR)]


def joined(ref, lead=()):
    return jnp.concatenate([ref[lead + (p,)] for p in range(ref.shape[len(lead)])], axis=1)


def whole(shape):
    return pl.BlockSpec(shape, lambda i: (0,) * len(shape))


def swap_with_mate(spot, src, dst, send, recv):
    return remote(src, dst, send, recv, spot.mate)


def transposed_norm(hidden_ref, norm_ref):
    unit, _ = norm_rows(hidden_ref[0].astype(F32))
    normed = (unit * norm_ref[0, 0:1, :] + norm_ref[0, 1:2, :]).astype(BF16)
    return normed.astype(F32).T.astype(BF16)


def lane_ids(shape):
    return lax.broadcasted_iota(jnp.int32, shape, len(shape) - 1)


def three_parts(value):
    high = value.astype(BF16).astype(F32)
    rest = value - high
    middle = rest.astype(BF16).astype(F32)
    return high, middle, rest - middle


def extend_keys(keys_out, values_out, blocks, bias_ref, head):
    aux = HEAD_DIM * (1 - head)
    row = 0
    for key, value in blocks:
        rows = key.shape[0]
        span = slice(row, row + rows)
        lanes = lane_ids((rows, PAIR))
        inside = (lanes // HEAD_DIM) == head
        ones = jnp.where((lanes > aux) & (lanes <= aux + 3), 1.0, 0.0)
        extra = jnp.where(lanes == aux, bias_ref[span, :], ones)
        keys_out[span, :] = jnp.where(inside, key.astype(F32), extra).astype(BF16)
        ones = jnp.where((lanes >= aux) & (lanes < aux + 3), 1.0, 0.0)
        values_out[span, :] = jnp.where(inside, value.astype(F32), ones).astype(BF16)
        row += rows


def pair_forward(query_of, keys, values, rows, chunk, save):
    lanes = lane_ids((chunk, PAIR))
    units = [(start, head) for start in range(0, rows, chunk) for head in (0, 1)]

    def extended(start, head):
        aux = HEAD_DIM * (1 - head)
        inside = (lanes // HEAD_DIM) == head
        query = query_of(slice(start, start + chunk)).astype(F32)
        return jnp.where(inside, query, jnp.where(lanes == aux, 1.0, 0.0))

    def scores(start, head):
        return contract_cols(extended(start, head).astype(BF16), keys[head])

    ahead = [scores(*unit) for unit in units[:2]]
    for index, (start, head) in enumerate(units):
        now = ahead.pop(0)
        if index + 2 < len(units):
            ahead.append(scores(*units[index + 2]))
        aux = HEAD_DIM * (1 - head)
        top = jnp.max(now, axis=1, keepdims=True)
        summed = mm(jnp.exp(now - top).astype(BF16), values[head])
        total = summed[:, aux : aux + 1]
        query = extended(start, head)
        for lane, part in enumerate(three_parts(-(top + jnp.log(total))), aux + 1):
            query = jnp.where(lanes == lane, part, query)
        save(head, slice(start, start + chunk), query.astype(BF16), summed / total)


def pair_backward(query_of, grad_of, out_of, keys, values, key_sums, value_sums, rows, save):
    for start, size in ((0, 256), (256, rows - 256)):
        span = slice(start, start + size)
        lanes = lane_ids((size, PAIR))
        parts = []
        for head in (0, 1):
            aux = HEAD_DIM * (1 - head)
            inside = (lanes // HEAD_DIM) == head
            query = query_of(head, span)
            grad = jnp.where(inside, grad_of(span).astype(F32), 0.0)
            dots = jnp.sum(grad * out_of(span), axis=1, keepdims=True)
            for lane, part in enumerate(three_parts(-dots), aux):
                grad = jnp.where(lanes == lane, part, grad)
            probs = jnp.exp(contract_cols(query, keys[head]))
            shifted = contract_cols(grad.astype(BF16), values[head])
            grad_scores = (probs * shifted).astype(BF16)
            parts.append(mm(grad_scores, keys[head]) * HEAD_DIM**-0.5)
            to_values = mm(grad.T.astype(BF16), probs.astype(BF16)).T
            to_keys = mm(query.astype(F32).T.astype(BF16), grad_scores).T
            value_sums[head] = to_values if start == 0 else value_sums[head] + to_values
            key_sums[head] = to_keys if start == 0 else key_sums[head] + to_keys
        save(span, jnp.where(lanes < HEAD_DIM, parts[0], parts[1]).astype(BF16))


class Weight(PlaneGather):
    SENDS, RECEIVES = 13, 10

    def __init__(self, spot, src, dst, source, send, recv):
        super().__init__(spot, dst, send, recv)
        self.src, self.source = src, source
        self.own = self.blocks(spot.core, spot.c)

    def along(self, src):
        s = self.spot
        return (
            remote(src.at[self.own], self.dst.at[self.own], self.send.at[9], self.recv.at[9], s.above),
            remote(src.at[self.own], self.dst.at[self.own], self.send.at[10], self.recv.at[9], s.below),
        )

    def load(self):
        return pltpu.make_async_copy(self.src, self.dst, self.send.at[11])

    def open(self, up=True, down=True, load=True):
        rise, fall = self.along(self.src)

        @pl.when(self.spot.z == self.source)
        def _():
            if up and self.source + 1 < self.spot.sections:
                rise.start()
            if down and self.source:
                fall.start()
            if load:
                self.load().start()

    def pass_on(self, hop, begin=True):
        rise, fall = self.along(self.dst)
        last = self.spot.sections - 1
        for at, further, copy in ((self.source + hop, last, rise), (self.source - hop, 0, fall)):
            if not 0 <= at <= last:
                continue

            @pl.when(self.spot.z == at)
            def _(at=at, further=further, copy=copy):
                rise.wait_recv()
                if at != further:
                    copy.start()
                if begin:
                    self.begin(self.dst.at[self.own])

    def away(self, action):
        pl.when(self.spot.z != self.source)(action)

    def enter(self):
        self.away(lambda: self.begin(self.dst.at[self.own]))

    def middle(self):
        self.away(self.second)

    def late(self):
        self.away(self.third)

    def ready(self):
        rise, fall = self.along(self.src)
        last = self.spot.sections - 1
        if self.source < last:
            pl.when((self.spot.z >= self.source) & (self.spot.z < last))(rise.wait_send)
        if self.source:
            pl.when((self.spot.z <= self.source) & (self.spot.z > 0))(fall.wait_send)
        pl.when(self.spot.z == self.source)(self.load().wait)
        self.away(self.finish)


QKV_ORDER = (1, 2, 0, 3)
FORWARD_STEPS = 14


def forward_body(*refs):
    refs_list = list(refs)
    take = lambda n: [refs_list.pop(0) for _ in range(n)]
    clips, grads, front, back, norms, kind_in, bias_qv, bias_attn, bias_up, bias_down = take(10)
    key_out, value_out, key_far_out, value_far_out, extended_out, attended_out, act_out, slope_out = take(8)
    fronts_out, downs_out, hidden_out, grad_out, acts_home, mask_out, key_bias_out, norm_out = take(8)
    fronts, downs, hidden, own, far, attended, keys, values, normed, total, norm_all, kind, blank = take(13)
    wsend, wrecv, nsend, nrecv, csend, crecv, ksend, krecv, dsend, drecv, lsem = take(11)
    step = pl.program_id(0)
    layer, turn = step // FORWARD_STEPS, step % FORWARD_STEPS
    rows, width = normed.shape
    pairs = width // PAIR
    spot = Spot()
    owner, slot = spot.z // 2, spot.z % 2
    holds = spot.core == owner

    weights, count = {}, 0

    def weight(name, src, dst, source):
        nonlocal count
        weights[name] = Weight(spot, src, dst, source, wsend.at[count], wrecv.at[count])
        count += 1

    for j, block in enumerate(QKV_ORDER):
        at = pl.ds(block * width, width)
        weight(("first", j), front.at[:, :, at], fronts.at[0, :, :, at], 0)
    for s in range(1, 4):
        for n in range(1 + s % 2):
            size = fronts.shape[3] // (1 + s % 2)
            at = pl.ds(n * size, size)
            weight(("front", s, n), front.at[:, :, at], fronts.at[s, :, :, at], s)
    for s in range(4):
        weight(("back", s), back, downs.at[s // 2, pl.ds(16 * (s % 2), 16)], s)
    first = [weights["first", j] for j in range(4)]
    front_1, front_2, front_3 = ([weights["front", s, n] for n in range(1 + s % 2)] for s in (1, 2, 3))
    (front_2,) = front_2
    back_0, back_1, back_2, back_3 = (weights["back", s] for s in range(4))

    norm_copies = [
        remote(norms, norm_all.at[spot.z], nsend.at[i], nrecv.at[i], {"section": (spot.z + i) % spot.sections})
        for i in range(1, spot.sections)
    ]

    def clip_copies():
        mine, other = (pl.ds(pl.multiple_of(c * rows, 16), rows) for c in (spot.core, 1 - spot.core))
        away = [
            remote(clips.at[slot, other], hidden.at[0], csend.at[0], crecv.at[0], spot.mate),
            remote(grads.at[slot, other], grad_out, csend.at[1], crecv.at[1], spot.mate),
            remote(kind_in, kind, csend.at[2], crecv.at[2], spot.mate),
        ]
        stay = [
            pltpu.make_async_copy(clips.at[slot, mine], hidden.at[0], csend.at[3]),
            pltpu.make_async_copy(grads.at[slot, mine], grad_out, csend.at[4]),
        ]
        return away, stay

    def pads():
        pad = acts_home.shape[1] - 2 * rows
        return [
            pltpu.make_async_copy(blank, acts_home.at[i, pl.ds(2 * rows, pad)], lsem.at[i]) for i in (0, 1)
        ]

    def enter():
        blank[...] = jnp.zeros_like(blank)
        spot.greet()
        for w in first:
            w.open()
        away, stay = clip_copies()

        @pl.when(holds)
        def _():
            for copy in (away[2], away[0], stay[0], away[1]):
                copy.start()
            kind[...] = kind_in[...]
        for copy in norm_copies:
            copy.start()
        norm_all[spot.z] = norms[...]
        for w in (*front_1, back_1, front_2, back_2, *front_3, back_3):
            w.open(up=False)
        back_2.open(down=False, load=False)
        for w in first:
            for hop in (1, 2, 3):
                w.pass_on(hop)
        for w in (front_1[0], front_1[1], back_1, front_2):
            w.open(down=False, load=False)
        back_0.open()

        @pl.when(holds)
        def _():
            stay[1].start()
            stay[0].wait()

        @pl.when(jnp.logical_not(holds))
        def _():
            away[0].wait_recv()
            away[2].wait_recv()
        for i, copy in enumerate(norm_copies, 1):
            block = norm_all.at[(spot.z + spot.sections - i) % spot.sections]
            remote(block, block, nsend.at[i], nrecv.at[i], spot.mate).wait_recv()
        norm_out[...] = norm_all[...]
        for copy in pads():
            copy.start()
        length = SHORT + (LONG - SHORT) * kind[0:1, 0:1]
        place = lax.broadcasted_iota(jnp.int32, (rows, 1), 0)
        near, there = ((place + c * rows).astype(F32) < length for c in (spot.core, 1 - spot.core))
        mask_out[...] = near.astype(F32)
        key_bias_out[:rows, :] = jnp.where(near, 0.0, MASKED)
        key_bias_out[rows:, :] = jnp.where(there, 0.0, MASKED)
        for w in first:
            w.middle()
        for w in front_1:
            w.pass_on(1)
        back_1.pass_on(1)
        for w in first:
            w.late()
        for w in front_1:
            w.pass_on(2)
        first[0].ready()

    early, late = functools.partial, False
    plan = {
        0: [enter],
        1: [first[1].ready, early(back_1.pass_on, 2), early(back_0.pass_on, 1)],
        2: [first[2].ready, early(back_0.pass_on, 2), early(front_2.pass_on, 1, late), early(back_2.pass_on, 1, late)],
        3: [first[3].ready, early(back_0.pass_on, 3), *(early(w.pass_on, 1, late) for w in front_3)],
        4: [front_1[0].middle, early(back_3.pass_on, 1, late), early(front_2.pass_on, 2, late)],
        5: [front_1[1].middle, early(back_2.pass_on, 2, late)],
        6: [back_1.middle, *(early(w.pass_on, 2, late) for w in front_3), front_1[0].late],
        7: [back_0.middle, front_1[1].late, early(back_3.pass_on, 2, late)],
        8: [front_2.enter],
        9: [back_1.late, *(early(w.pass_on, 3, late) for w in front_3)],
        10: [back_0.late, early(back_3.pass_on, 3, late), front_1[0].ready, back_0.ready],
        11: [front_3[0].enter, back_2.enter],
        12: [front_1[1].ready, back_1.ready, front_2.middle],
        13: [front_2.late, front_3[1].enter, back_3.enter],
        14: [front_2.ready],
        15: [front_3[0].middle],
        17: [back_2.middle, front_3[0].late],
        18: [front_3[1].middle],
        19: [back_3.middle, back_2.late],
        20: [front_3[1].late],
        22: [back_3.late],
        24: [front_3[0].ready, back_2.ready],
        26: [front_3[1].ready, back_3.ready],
    }
    ends = []

    def keep(at, src, dst, index):
        copy = pltpu.make_async_copy(src, dst, lsem.at[2 + index])
        plan.setdefault(at, []).append(copy.start)
        ends.append(copy.wait)

    for s, at in ((0, 10), (1, 13), (2, 20), (3, 27)):
        keep(at, fronts.at[s], fronts_out.at[s], s)
    for layer_id, at in ((0, 15), (1, 27)):
        keep(at, downs.at[layer_id], downs_out.at[layer_id], 4 + layer_id)
    for s, at in ((0, 4), (1, 11), (2, 16), (3, 25)):
        keep(at, hidden.at[s], hidden_out.at[s], 6 + s)

    for n, (s, first_row, size, begin, stop) in enumerate(FORWARD_DELIVERIES):
        size = size or rows - first_row
        blocks = size // 16
        for i in range(stop - begin):
            low, high = blocks * i // (stop - begin), blocks * (i + 1) // (stop - begin)
            part = Deliver(
                spot, hidden.at[s + 1], acts_home, s, dsend.at[n], drecv.at[n], first_row + 16 * low, 16 * (high - low)
            )
            plan.setdefault(begin + i, []).append(part.start)
        ends.append(Deliver(spot, hidden.at[s + 1], acts_home, s, dsend.at[n], drecv.at[n], first_row, size).finish)

    for at, actions in sorted(plan.items()):
        @pl.when(step == at)
        def _(actions=actions):
            for action in actions:
                action()

    def norms_of(s):
        return norm_all[s, 0:1, :], norm_all[s, 1:2, :]

    def start_sub_layer(s):
        gain, shift = norms_of(s)
        unit, _ = norm_rows(hidden[s].astype(F32))
        normed[...] = (unit * gain + shift).astype(BF16)

    def front_block(s, block):
        return fronts[s, :, :, pl.ds(pl.multiple_of(block * width, width), width)].reshape(width, width)

    def swaps():
        return [
            remote(own.at[j], far.at[layer, j], ksend.at[layer, j], krecv.at[layer, j], spot.mate) for j in (0, 1)
        ]

    @pl.when(turn == 0)
    def _():
        start_sub_layer(2 * layer)

    for j, scale in ((0, 1.0), (1, 1.0), (2, HEAD_DIM**-0.5)):
        @pl.when(turn == j)
        def _(j=j, scale=scale):
            block = mm(normed[...], front_block(2 * layer, QKV_ORDER[j]))
            if j == 1:
                block = block + bias_qv[pl.ds(layer, 1), width:]
            elif j == 2:
                block = block + bias_qv[pl.ds(layer, 1), :width]
            block = block.astype(BF16)
            if scale != 1.0:
                block = (block.astype(F32) * scale).astype(BF16)
            for p, part in enumerate(pairs_of(block)):
                own[j, p] = part
            if j < 2:
                swaps()[j].start()
            else:
                for copy in swaps():
                    copy.wait()

    @pl.when((turn >= 3) & (turn < 3 + pairs))
    def _():
        p = turn - 3
        for head in (0, 1):
            extend_keys(
                keys.at[head], values.at[head], [(own[0, p], own[1, p]), (far[layer, 0, p], far[layer, 1, p])],
                key_bias_out, head,
            )
        for j, out in enumerate((key_out, value_out)):
            out[0, 0] = own[j, p]
        for j, out in enumerate((key_far_out, value_far_out)):
            out[0, 0] = far[layer, j, p]
        lanes = lane_ids((rows // 2, PAIR))
        firsts = {}

        def save(head, span, query, out):
            extended_out[0, head, span, :] = query
            if head == 0:
                firsts[span.start] = out
            else:
                both = jnp.where(lanes < HEAD_DIM, firsts[span.start], out)
                attended_out[0, 0, span, :] = both
                attended[p, span, :] = both.astype(BF16)

        pair_forward(lambda span: own[2, p, span, :], keys, values, rows, rows // 2, save)

    @pl.when(turn == 3 + pairs)
    def _():
        s = 2 * layer
        branch = contract_cols(joined(attended), front_block(s, 3)) + bias_attn[pl.ds(layer, 1), :]
        hidden[s + 1] = (mask_out[...] * (hidden[s].astype(F32) + branch)).astype(BF16)

    @pl.when(turn == 4 + pairs)
    def _():
        start_sub_layer(2 * layer + 1)

    @pl.when(turn >= 4 + pairs)
    def _():
        i = turn - 4 - pairs
        columns = pl.ds(pl.multiple_of(i * width, width), width)
        up = fronts[2 * layer + 1, :, :, columns].reshape(width, width)
        down_blocks = width * 32 // (width * 4)
        down = downs[layer, pl.ds(i * down_blocks, down_blocks)].reshape(width, width)
        bias = bias_up[pl.ds(layer, 1), columns]
        for span in (slice(0, rows // 2), slice(rows // 2, rows)):
            act, slope = gelu_and_slope(mm(normed[span, :], up) + bias)
            act_out[0, span, :] = act.astype(BF16)
            slope_out[0, span, :] = slope.astype(BF16)
            part = mm(act.astype(BF16), down)
            total[span, :] = jnp.where(i == 0, part, total[span, :] + part)

    @pl.when(turn == FORWARD_STEPS - 1)
    def _():
        s = 2 * layer + 1
        branch = total[...] + bias_down[pl.ds(layer, 1), :]
        hidden[s + 1] = (mask_out[...] * (hidden[s].astype(F32) + branch)).astype(BF16)

    @pl.when(step == 2 * FORWARD_STEPS - 1)
    def _():
        copy = pltpu.make_async_copy(hidden.at[4], hidden_out.at[4], lsem.at[12])
        copy.start()
        for end in ends:
            end()
        copy.wait()
        for pad in pads():
            pad.wait()
        for sent in norm_copies:
            sent.wait_send()
        away, stay = clip_copies()

        @pl.when(holds)
        def _():
            for sent in away:
                sent.wait_send()
            stay[1].wait()

        pl.when(jnp.logical_not(holds))(away[1].wait_recv)


FORWARD_DELIVERIES = ((0, 0, None, 10, 18), (1, 0, None, 14, 20))


def forward(clips, grads, kind, front, back, norms, bias_qv, bias_attn, bias_up, bias_down, rows):
    sections = lax.axis_size("section")
    padded, width = clips.shape[1:]
    units, pairs = front.shape[1], width // PAIR
    front_b = front.reshape(16, width // 16, units)
    back_b = back.reshape(16, back.shape[0] // 16, width)
    layers = sections // 2
    layer = lambda i: i // FORWARD_STEPS
    pair = lambda i: jnp.clip(i % FORWARD_STEPS - 3, 0, pairs - 1)
    unit = lambda i: jnp.maximum(i % FORWARD_STEPS - 4 - pairs, 0)
    hbm, vmem = hbm_spec(), vmem_spec()
    per_pair = pl.BlockSpec((1, 1, rows, PAIR), lambda i: (layer(i), pair(i), 0, 0))
    per_unit = pl.BlockSpec((1, rows, width), lambda i: (layer(i), 0, unit(i)))
    shape = jax.ShapeDtypeStruct
    saved = shape((layers, pairs, rows, PAIR), BF16)
    sems = pltpu.SemaphoreType.DMA
    jobs = 4 + 5 + 4
    sent = len(FORWARD_DELIVERIES)
    return pl.pallas_call(
        forward_body,
        grid=(2 * FORWARD_STEPS,),
        in_specs=[hbm] * 4 + [vmem] * 6,
        out_specs=[per_pair] * 4
        + [pl.BlockSpec((1, 2, rows, PAIR), lambda i: (layer(i), pair(i), 0, 0)), per_pair, per_unit, per_unit]
        + [hbm] * 5 + [vmem] * 3,
        out_shape=[saved] * 4
        + [
            shape((layers, 2 * pairs, rows, PAIR), BF16), shape((layers, pairs, rows, PAIR), F32),
            shape((layers, rows, units), BF16), shape((layers, rows, units), BF16),
            shape((sections,) + front_b.shape, BF16), shape((layers, 32) + back_b.shape[1:], BF16),
            shape((sections + 1, rows, width), BF16), shape((rows, width), BF16),
            shape((clips.shape[0], padded, width), BF16),
            shape((rows, 1), F32), shape((2 * rows, 1), F32), shape((sections,) + norms.shape, F32),
        ],
        scratch_shapes=[
            pltpu.VMEM((sections,) + front_b.shape, BF16), pltpu.VMEM((layers, 32) + back_b.shape[1:], BF16),
            pltpu.VMEM((sections + 1, rows, width), BF16), pltpu.VMEM((3, pairs, rows, PAIR), BF16),
            pltpu.VMEM((layers, 2, pairs, rows, PAIR), BF16), pltpu.VMEM((pairs, rows, PAIR), BF16),
            pltpu.VMEM((2, 2 * rows, PAIR), BF16), pltpu.VMEM((2, 2 * rows, PAIR), BF16),
            pltpu.VMEM((rows, width), BF16), pltpu.VMEM((rows, width), F32),
            pltpu.VMEM((sections,) + norms.shape, F32), pltpu.VMEM(kind.shape, F32),
            pltpu.VMEM((padded - 2 * rows, width), BF16),
            sems((jobs, Weight.SENDS)), sems((jobs, Weight.RECEIVES)), sems((sections,)), sems((sections,)),
            sems((5,)), sems((3,)), sems((layers, 2)), sems((layers, 2)), sems((sent, 2)), sems((sent, 4)), sems((13,)),
        ],
        compiler_params=pltpu.CompilerParams(
            vmem_limit_bytes=63 * 2**20, collective_id=0, has_side_effects=True
        ),
        name="forward",
    )(clips, grads, front_b, back_b, norms, kind, bias_qv, bias_attn, bias_up, bias_down)


FF_STEPS = 4


def backward_body(
    spot, incoming_ref, mask_ref, hidden_ref, act_ref, slope_ref, front_ref, down_ref, norm_ref,
    key_ref, value_ref, key_far_ref, value_far_ref, extended_ref, attended_ref, key_bias_ref,
    weight_grad, mid_out, out_ref, ff_gain_grad, ff_shift_grad, up_bias_grad, down_bias_grad,
    gain_grad, shift_grad, query_bias_grad, value_bias_grad, out_bias_grad,
    mid, front_grad, down_grad, grad, normed_t, total, grad_out, attended, grads, sent, arrived,
    keys, values, key_sums, value_sums, send, recv,
):
    step, last = pl.program_id(0), pl.num_programs(0) - 1
    rows, width = grad.shape
    pairs = width // PAIR
    first_pair, first_part = FF_STEPS, FF_STEPS + pairs
    weight = front_ref[0].reshape(width, width)

    def swap_of(p):
        return remote(sent.at[p], arrived.at[p], send.at[p], recv.at[p], spot.mate)

    def start(source, bias_sums):
        grad_rows = mask_ref[...] * source.astype(F32)
        grad[...] = grad_rows.astype(BF16)
        bias_sums[...] = jnp.sum(grad_rows, axis=0, keepdims=True)

    def norm_grads(gain_sums, shift_sums):
        grad_hidden, gain_sums[...], shift_sums[...] = norm_backward(
            hidden_ref[0].astype(F32), total[...], norm_ref[0, 0:1, :]
        )
        return (grad[...].astype(F32) + grad_hidden).astype(BF16)

    @pl.when(step == 0)
    def _():
        start(incoming_ref[...], down_bias_grad)
        normed_t[...] = transposed_norm(hidden_ref, norm_ref)

    @pl.when(step < FF_STEPS)
    def _():
        down = down_ref[0].reshape(width, width)
        blocks = down_ref.shape[1]
        grad_pre = (contract_cols(grad[...], down) * slope_ref[0].astype(F32)).astype(BF16)
        down_part = contract_rows(act_ref[0], grad[...]).astype(BF16)
        down_grad[pl.ds(step * blocks, blocks)] = down_part.reshape(down_ref.shape[1:])
        up_bias_grad[...] = jnp.sum(grad_pre.astype(F32), axis=0, keepdims=True)
        up_part = mm(normed_t[...], grad_pre).astype(BF16)
        columns = pl.ds(pl.multiple_of(step * width, width), width)
        front_grad[:, :, columns] = up_part.reshape(16, width // 16, width)
        part = contract_cols(grad_pre, weight)
        total[...] = jnp.where(step == 0, part, total[...] + part)

    @pl.when(step == FF_STEPS - 1)
    def _():
        mid[...] = norm_grads(ff_gain_grad, ff_shift_grad)
        mid_out[...] = mid[...]

    @pl.when(step == first_pair)
    def _():
        start(mid[...], out_bias_grad)
        for p, part in enumerate(pairs_of(mm(grad[...], weight).astype(BF16))):
            grad_out[p] = part

    @pl.when((step >= first_pair) & (step < first_part))
    def _():
        p = step - first_pair
        for head in (0, 1):
            extend_keys(
                keys.at[head], values.at[head],
                [(key_ref[0, 0], value_ref[0, 0]), (key_far_ref[0, 0], value_far_ref[0, 0])], key_bias_ref, head,
            )
        attended[p] = attended_ref[0, 0].astype(BF16)

        def save(span, value):
            grads[0, p, span, :] = value

        pair_backward(
            lambda head, span: extended_ref[0, head, span, :], lambda span: grad_out[p, span, :],
            lambda span: attended_ref[0, 0, span, :], keys, values, key_sums, value_sums, rows, save,
        )
        first = lane_ids((rows, PAIR)) < HEAD_DIM
        for j, sums in enumerate((key_sums, value_sums)):
            grads[1 + j, p] = jnp.where(first, sums[0, :rows, :], sums[1, :rows, :]).astype(BF16)
            sent[p, j] = jnp.where(first, sums[0, rows:, :], sums[1, rows:, :]).astype(BF16)
        swap_of(p).start()

    @pl.when(step == first_part)
    def _():
        normed_t[...] = transposed_norm(hidden_ref, norm_ref)
        for p in range(pairs):
            swap_of(p).wait()
            for j in (0, 1):
                grads[1 + j, p] = (grads[1 + j, p].astype(F32) + arrived[p, j].astype(F32)).astype(BF16)

    @pl.when((step >= first_part) & (step < last))
    def _():
        j = step - first_part
        part = joined(grads, (j,))
        sums = jnp.sum(part.astype(F32), axis=0, keepdims=True)

        @pl.when(j == 0)
        def _():
            query_bias_grad[...] = sums

        @pl.when(j == 2)
        def _():
            value_bias_grad[...] = sums

        weight_grad[...] = mm(normed_t[...], part).astype(BF16).reshape(weight_grad.shape)
        product = contract_cols(part, weight)
        total[...] = jnp.where(j == 0, product, total[...] + product)

    @pl.when(step == last)
    def _():
        weight_grad[...] = contract_rows(grad[...], joined(attended)).astype(BF16).reshape(weight_grad.shape)
        out_ref[...] = norm_grads(gain_grad, shift_grad)


def backward(incoming, mask, hidden, act, slope, fronts, downs, norms, heads, key_bias, layer, guests, collective_id):
    rows, width = incoming.shape
    units, pairs = fronts.shape[3], width // PAIR
    first_part = FF_STEPS + pairs
    once = lambda shape: pl.BlockSpec(shape, lambda i: (0,) * len(shape), pipeline_mode=pl.Buffered(1))
    sub = lambda i: 2 * layer + jnp.where(i < FF_STEPS, 1, 0)
    unit = lambda i: jnp.minimum(i, FF_STEPS - 1)
    pair = lambda i: jnp.clip(i - FF_STEPS, 0, pairs - 1)
    column = lambda i: jnp.where(i < FF_STEPS, i, jnp.where(i < first_part, 3, jnp.minimum(i - first_part, 2)))
    per_unit = pl.BlockSpec((1, rows, width), lambda i: (layer, 0, unit(i)))
    per_pair = pl.BlockSpec((1, 1, rows, PAIR), lambda i: (layer, pair(i), 0, 0))
    down_blocks = 32 // FF_STEPS
    in_specs = [
        once((rows, width)), once((rows, 1)),
        pl.BlockSpec((1, rows, width), lambda i: (sub(i), 0, 0)), per_unit, per_unit,
        pl.BlockSpec((1, 16, width // 16, width), lambda i: (sub(i), 0, 0, column(i))),
        pl.BlockSpec((1, down_blocks) + downs.shape[2:], lambda i: (layer, unit(i), 0, 0)),
        pl.BlockSpec((1,) + norms.shape[1:], lambda i: (sub(i), 0, 0)),
        per_pair, per_pair, per_pair, per_pair,
        pl.BlockSpec((1, 2, rows, PAIR), lambda i: (layer, pair(i), 0, 0)), per_pair, once((2 * rows, 1)),
    ]
    full, vector = jax.ShapeDtypeStruct((rows, width), BF16), jax.ShapeDtypeStruct((1, width), F32)
    out_specs = [
        pl.BlockSpec((16, width // 16, width), lambda i: (0, 0, jnp.maximum(i - first_part, 0))),
        whole((rows, width)), whole((rows, width)), whole((1, width)), whole((1, width)),
        pl.BlockSpec((1, width), lambda i: (0, unit(i))),
    ] + [whole((1, width))] * 6
    out_shape = [
        jax.ShapeDtypeStruct((16, width // 16, units), BF16), full, full, vector, vector,
        jax.ShapeDtypeStruct((1, units), F32),
    ] + [vector] * 6
    vmem = pltpu.VMEM
    scratch = [
        vmem((rows, width), BF16), vmem((16, width // 16, units), BF16), vmem(downs.shape[1:], BF16),
        vmem((rows, width), BF16), vmem((width, rows), BF16), vmem((rows, width), F32),
        vmem((pairs, rows, PAIR), BF16), vmem((pairs, rows, PAIR), BF16), vmem((3, pairs, rows, PAIR), BF16),
        vmem((pairs, 2, rows, PAIR), BF16), vmem((pairs, 2, rows, PAIR), BF16),
        vmem((2, 2 * rows, PAIR), BF16), vmem((2, 2 * rows, PAIR), BF16),
        vmem((2, 2 * rows, PAIR), F32), vmem((2, 2 * rows, PAIR), F32),
        pltpu.SemaphoreType.DMA((pairs,)), pltpu.SemaphoreType.DMA((pairs,)),
    ]
    args = (incoming, mask, hidden, act, slope, fronts, downs, norms, *heads, key_bias)
    return hosted(
        backward_body, first_part + 4, list(zip(args, in_specs)), list(zip(out_shape, out_specs)), scratch,
        guests, collective_id, f"backward_{layer}", 63 * 2**20,
    )


def held_sum_guest(shapes, views, stages, targets, hop_steps):
    sems = pltpu.SemaphoreType.DMA
    hopping = [sides(target) if at is not None else [] for target, at in zip(targets, hop_steps)]
    sizes = [5 + len(names) for names in hopping]

    def plan(spot, ins, outs, held, body):
        held = list(held)
        send, recv, csend, crecv = held[-4:]
        hooks = {}
        for i, (number, index) in enumerate(views):
            bufs, held = held[: sizes[i]], held[sizes[i] :]
            src = body[number].at[index]
            job = PlaneSum(
                spot, src, [src.at[pl.ds(spot.core * 8, 8)]] + bufs[:5], send.at[i], recv.at[i], in_place=True
            )
            actions = (job.start, job.first, job.second, functools.partial(job.third, outs[i]))
            for at, action in zip(stages[i], actions):
                hooks.setdefault(at, []).append(action)
            hooks.setdefault("end", []).append(job.finish)
            if hop_steps[i] is not None:
                chain = Chain(spot, outs[i], bufs[5:], targets[i], csend.at[i], crecv.at[i])
                hooks.setdefault(hop_steps[i], []).append(functools.partial(chain.give, 1))
                hooks["end"].extend([functools.partial(chain.take, 1), functools.partial(chain.leave, 1)])
        return hooks

    buffers = []
    for shape, names in zip(shapes, hopping):
        buffers += PlaneSum.scratch(*shape)[1:] + [pltpu.VMEM((2,) + shape, BF16)] * len(names)
    count = len(shapes)
    return Guest(
        (), [(jax.ShapeDtypeStruct((2,) + s, BF16), vmem_spec()) for s in shapes],
        buffers + [sems((count, 8)), sems((count, 8)), sems((count,)), sems((count, 2))], (), plan,
    )


def sides(target):
    return [name for name, any_there in (("below", target > 0), ("above", target < 3)) if any_there]


def hops_of(target):
    return max(target, 3 - target)


class Chain:
    def __init__(self, spot, total, bufs, target, send, recv):
        self.spot, self.total, self.target, self.send, self.recv = spot, total, target, send, recv
        self.from_below, self.from_above = bufs[0], bufs[-1]

    def ends(self, hop):
        last = self.spot.sections - 1
        return hop - 1 if hop <= self.target else None, last - hop + 1 if last - hop >= self.target else None

    def rise(self):
        return remote(self.total, self.from_below, self.send, self.recv.at[0], self.spot.above)

    def fall(self):
        return remote(self.total, self.from_above, self.send, self.recv.at[1], self.spot.below)

    def give(self, hop):
        below, above = self.ends(hop)
        if below is not None:
            pl.when(self.spot.z == below)(self.rise().start)
        if above is not None:
            pl.when(self.spot.z == above)(self.fall().start)

    def take(self, hop):
        below, above = self.ends(hop)
        if below is not None:
            @pl.when(self.spot.z == below + 1)
            def _():
                self.rise().wait_recv()
                add_into(self.total, self.from_below)
        if above is not None:
            @pl.when(self.spot.z == above - 1)
            def _():
                self.fall().wait_recv()
                add_into(self.total, self.from_above)

    def leave(self, hop):
        below, above = self.ends(hop)
        if below is not None:
            pl.when(self.spot.z == below)(self.rise().wait_send)
        if above is not None:
            pl.when(self.spot.z == above)(self.fall().wait_send)


def chain_guest(jobs):
    sems = pltpu.SemaphoreType.DMA

    def plan(spot, ins, outs, held, body):
        held = list(held)
        send, recv, loads = held[-3:]
        hooks, ends = {}, []
        for i, (_, target, first, steps) in enumerate(jobs):
            bufs, held = held[: len(sides(target))], held[len(sides(target)) :]
            chain = Chain(spot, outs[i], bufs, target, send.at[i], recv.at[i])
            load = pltpu.make_async_copy(ins[i], outs[i], loads.at[i])
            hooks.setdefault(0, []).extend([load.start, load.wait])
            for n, at in enumerate(steps):
                hop = first + n
                if n:
                    hooks.setdefault(at, []).append(functools.partial(chain.take, hop - 1))
                hooks.setdefault(at, []).append(functools.partial(chain.give, hop))
                ends.append(functools.partial(chain.leave, hop))
            ends.append(functools.partial(chain.take, first + len(steps) - 1))
        hooks["end"] = ends
        return hooks

    buffers = []
    for a, target, _, _ in jobs:
        buffers += [pltpu.VMEM(a.shape, BF16)] * len(sides(target))
    return Guest(
        [(job[0], hbm_spec()) for job in jobs],
        [(jax.ShapeDtypeStruct(job[0].shape, BF16), vmem_spec()) for job in jobs],
        buffers + [sems((len(jobs),)), sems((len(jobs), 2)), sems((len(jobs),))], (), plan,
    )


def per_device(
    clip_inputs, out_grad, clip_class, w_front, w_back, norm_gain, norm_shift,
    bias_query_value, bias_attn_out, bias_up, bias_down,
):
    spot = Spot()
    sections = lax.axis_size("section")
    padded, width = clip_inputs.shape[1:]
    rows = -(-LONG // 32) * 16
    section = spot.z

    kind = lax.dynamic_index_in_dim(clip_class, section % 2, 0, False).astype(F32)
    norms = jnp.concatenate([norm_gain, norm_shift, jnp.zeros((6, width), F32)], axis=0)
    (
        key, value, key_far, value_far, extended, attended, act, slope,
        fronts, downs, hidden, incoming, acts_home, row_mask, key_bias, norm_all,
    ) = forward(
        clip_inputs, out_grad, jnp.broadcast_to(kind, (8, 128)), w_front[0], w_back[0], norms,
        bias_query_value, bias_attn_out, bias_up, bias_down, rows,
    )
    acts = [(hidden, s + 1) for s in range(sections)]
    grads_home = jax.ShapeDtypeStruct((clip_inputs.shape[0], 2 * rows, width), BF16)
    heads = (key, value, key_far, value_far, extended, attended)
    input_grads, grad_fronts = [None] * sections, [None] * sections
    grad_gain, grad_shift = [None] * sections, [None] * sections
    query_sums, value_sums, out_sums, up_sums, down_sums = ([None] * 2 for _ in range(5))
    units = fronts.shape[3] // 2
    halves = [pl.ds(0, units), pl.ds(units, units)]
    views = []
    for i in (0, 1):
        views += [(1, (slice(None), slice(None), halves[i])), (2, pl.ds(16 * i, 16))]
    shapes = [(width // 16, units), downs.shape[2:]] * 2
    stages = ((2, 3, 6, 8), (2, 3, 7, 9), (4, 5, 9, 12), (4, 5, 11, "end"))
    hop_steps = {1: (8, 9, None, None), 0: (8, 9, 12, None)}
    early, late = range(0, 4), range(4, 8)
    for layer in (1, 0):
        targets = (2 * layer + 1, 2 * layer, 2 * layer + 1, 2 * layer + 1)
        guests = [held_sum_guest(shapes, views, stages, targets, hop_steps[layer])]
        if layer == 1:
            guests.append(deliver_guest(
                [(acts[2], 2, 0, rows, early), (acts[3], 3, 0, 400, early)], acts_home
            ))
        else:
            done = ((3, 2, (1,)), (2, 2, (1,)), (3, 1, (0, 5)), (3, 1, (0, 5)))
            guests.append(chain_guest([(part, *hops) for part, hops in zip(passing, done)]))
            guests.append(deliver_guest(
                [(input_grads[3], 3, 0, 400, early), (0, 1, 0, rows, late), (input_grads[2], 2, 0, rows, early, (2, 3))],
                grads_home
            ))
            guests.append(deliver_guest([(acts[3], 3, 400, rows - 400, early)], acts_home))
        (
            grad_fronts[2 * layer], input_grads[2 * layer + 1], input_grads[2 * layer],
            grad_gain[2 * layer + 1], grad_shift[2 * layer + 1], up_sums[layer], down_sums[layer],
            grad_gain[2 * layer], grad_shift[2 * layer], query_sums[layer], value_sums[layer], out_sums[layer],
        ), carried = backward(
            incoming, row_mask, hidden, act, slope, fronts, downs, norm_all, heads, key_bias, layer, guests, 2 + layer
        )
        incoming = input_grads[2 * layer]
        if layer == 1:
            passing, (acts_home,) = carried
        else:
            later, earlier, (grads_home,), (acts_home,) = carried

    pair_sums = [v for both in zip(query_sums, value_sums) for v in both]
    vectors = grad_gain + grad_shift + pair_sums + out_sums + up_sums + down_sums
    grads_home, front_out, back_out, small = collect(
        input_grads[0], input_grads[2], input_grads[3], grads_home, grad_fronts[0],
        grad_fronts[2], [*earlier, *later], vectors,
    )
    front_out = front_out.reshape(width, -1)
    back_out = back_out.reshape(-1, width)
    for bit in spot.spare_bits:
        small = small + swap(small, bit)
        front_out, back_out = add(front_out, swap(front_out, bit)), add(back_out, swap(back_out, bit))
    grads_out = jnp.pad(grads_home.astype(F32), ((0, 0), (0, padded - 2 * rows), (0, 0)))
    parts, place_at = [], 0
    layers, hidden_units = bias_up.shape
    for count, size in (
        (sections, width), (sections, width), (layers, 2 * width), (layers, width),
        (layers, hidden_units), (layers, width),
    ):
        taken = count * size // width
        parts.append(small[place_at : place_at + taken].reshape(count, size))
        place_at += taken
    return (
        acts_home[None],
        grads_out[None],
        front_out.astype(F32)[None],
        back_out.astype(F32)[None],
        lax.dynamic_slice_in_dim(parts[0], section, 1, 0),
        lax.dynamic_slice_in_dim(parts[1], section, 1, 0),
        *parts[2:],
    )


def solution(mesh):
    placed = (
        P("dp", None, None), P("dp", None, None), P("dp"),
        P("section", None, None), P("section", None, None), P("section", None), P("section", None),
        P(), P(), P(), P(),
    )
    return jax.shard_map(
        per_device,
        mesh=mesh,
        in_specs=placed,
        out_specs=(
            P("section", "dp", None, None), P("section", "dp", None, None),
            P("section", None, None), P("section", None, None), P("section", None), P("section", None),
            P(), P(), P(), P(),
        ),
        check_vma=False,
    )
```

```python
import functools
import math

import jax
import jax.numpy as jnp
from jax import lax
from jax.experimental import pallas as pl
from jax.experimental.pallas import tpu as pltpu
from jax.sharding import PartitionSpec as P

HEADS = 12
LONG = 1214
SHORT = 514
EPS = 1e-06
HEAD_DIM = 64
PAIR = 2 * HEAD_DIM
MASKED = -1e30
F32 = jnp.float32
BF16 = jnp.bfloat16
KERNEL_VMEM = 56 * 2**20


def mm(left, right):
    return jnp.dot(left, right, preferred_element_type=F32)


def contract_rows(left, right):
    return lax.dot_general(left, right, (((0,), (0,)), ((), ())), preferred_element_type=F32)


def contract_cols(left, right):
    return lax.dot_general(left, right, (((1,), (1,)), ((), ())), preferred_element_type=F32)


def swap(block, bit):
    count = lax.axis_size("dp")
    return lax.ppermute(block, "dp", [(i, i ^ bit) for i in range(count)])


def add(a, b):
    return (a.astype(F32) + b.astype(F32)).astype(BF16)


class Spot:
    def __init__(self):
        self.z, self.sections = lax.axis_index("section"), lax.axis_size("section")
        self.d, self.count = lax.axis_index("dp"), lax.axis_size("dp")
        self.x_bit, self.y_bit = 2, 2 * math.isqrt(self.count // 2)
        self.core = self.d % 2
        self.xb, self.yb = (self.d // self.x_bit) % 2, (self.d // self.y_bit) % 2
        self.c, self.c_x = self.yb * 2 + self.xb, self.yb * 2 + 1 - self.xb
        self.c_y, self.c_d = (1 - self.yb) * 2 + self.xb, (1 - self.yb) * 2 + 1 - self.xb
        self.mate, self.x, self.y = (self.flipped(b) for b in (1, self.x_bit, self.y_bit))
        self.above, self.below = {"section": self.z + 1}, {"section": self.z - 1}
        self.spare_bits = [
            1 << i for i in range(self.count.bit_length() - 1) if 1 << i not in (1, self.x_bit, self.y_bit)
        ]

    def flipped(self, bit):
        return {"dp": self.d + bit * (1 - 2 * ((self.d // bit) % 2))}

    def greet_mate(self):
        barrier = pltpu.get_barrier_semaphore()
        pl.semaphore_signal(barrier, inc=1, device_id=self.mate, device_id_type=pl.DeviceIdType.MESH)
        pl.semaphore_wait(barrier, 1)

    def greet(self):
        barrier = pltpu.get_barrier_semaphore()
        devices = [self.x, self.y]
        for step in range(self.sections):
            for core in (0, 1):
                if step or core:
                    devices.append({
                        "section": (self.z + step) % self.sections,
                        "dp": self.d - self.core + (self.core + core) % 2,
                    })
        for device in devices:
            pl.semaphore_signal(barrier, inc=1, device_id=device, device_id_type=pl.DeviceIdType.MESH)
        pl.semaphore_wait(barrier, len(devices))


def remote(src, dst, send, recv, device):
    return pltpu.make_async_remote_copy(
        src_ref=src, dst_ref=dst, send_sem=send, recv_sem=recv,
        device_id=device, device_id_type=pl.DeviceIdType.MESH,
    )


class PlaneGather:
    SENDS, RECEIVES = 9, 9

    def __init__(self, spot, dst, send, recv):
        self.spot, self.dst, self.send, self.recv = spot, dst, send, recv

    def blocks(self, core, chip, half=None):
        at = core * 8 + chip * 2
        return pl.ds(at, 2) if half is None else pl.ds(at + half, 1)

    def copies(self, own=None):
        s, k = self.spot, self.spot.core
        plan = {
            "x": (self.blocks(k, s.c), s.x), "y": (self.blocks(k, s.c), s.y),
            "m": (self.blocks(k, s.c), s.mate),
            "xy": (self.blocks(k, s.c_x, 0), s.y), "yx": (self.blocks(k, s.c_y, 1), s.x),
            "mx": (self.blocks(k, s.c_x), s.mate), "my": (self.blocks(k, s.c_y), s.mate),
            "md0": (self.blocks(k, s.c_d, 0), s.mate), "md1": (self.blocks(k, s.c_d, 1), s.mate),
        }
        out = {}
        for index, (name, (rows, device)) in enumerate(plan.items()):
            src = own if own is not None and name in ("x", "y", "m") else self.dst.at[rows]
            out[name] = remote(src, self.dst.at[rows], self.send.at[index], self.recv.at[index], device)
        return out

    def arrivals(self):
        s, k = self.spot, self.spot.core
        plan = {
            "x": self.blocks(k, s.c_x), "y": self.blocks(k, s.c_y), "m": self.blocks(1 - k, s.c),
            "xy": self.blocks(k, s.c_d, 0), "yx": self.blocks(k, s.c_d, 1),
            "mx": self.blocks(1 - k, s.c_x), "my": self.blocks(1 - k, s.c_y),
            "md0": self.blocks(1 - k, s.c_d, 0), "md1": self.blocks(1 - k, s.c_d, 1),
        }
        return {
            name: remote(self.dst.at[rows], self.dst.at[rows], self.send.at[i], self.recv.at[i], s.mate)
            for i, (name, rows) in enumerate(plan.items())
        }

    def begin(self, own):
        copies = self.copies(own)
        for name in ("x", "y", "m"):
            copies[name].start()

    def second(self):
        copies, arrivals = self.copies(), self.arrivals()
        arrivals["x"].wait_recv()
        copies["xy"].start()
        copies["mx"].start()
        arrivals["y"].wait_recv()
        copies["yx"].start()
        copies["my"].start()

    def third(self):
        copies, arrivals = self.copies(), self.arrivals()
        for name, after in (("xy", "md0"), ("yx", "md1")):
            arrivals[name].wait_recv()
            copies[after].start()

    def finish(self):
        copies, arrivals = self.copies(), self.arrivals()
        for name in copies:
            copies[name].wait_send()
        for name in ("m", "mx", "my", "md0", "md1"):
            arrivals[name].wait_recv()


class Deliver:
    def __init__(self, spot, src, dst, target, send, recv, start=0, size=None, sources=None):
        self.sources = range(spot.sections) if sources is None else sources
        self.spot, self.src, self.dst, self.target, self.send, self.recv = spot, src, dst, target, send, recv
        self.rows, self.start_row = src.shape[0], start
        self.size = size or src.shape[0]
        self.owner, self.slot = spot.z // 2, spot.z % 2
        self.home = (spot.z == target) & (spot.core == self.owner)

    def place(self, slot, core):
        at = pl.multiple_of(core * self.rows + self.start_row, 16)
        return self.dst.at[slot, pl.ds(at, self.size)]

    def copies(self):
        s, spot = self, self.spot
        spot_at, src = s.place(s.slot, spot.core), s.src.at[pl.ds(s.start_row, s.size)]
        away = remote(
            src, spot_at, s.send.at[0], s.recv.at[s.slot * 2 + spot.core],
            {"section": s.target, "dp": spot.d - spot.core + s.owner},
        )
        return away, pltpu.make_async_copy(src, spot_at, s.send.at[1])

    def start(self):
        away, stay = self.copies()
        chosen = self.chosen()
        pl.when(chosen & self.home)(stay.start)
        pl.when(chosen & jnp.logical_not(self.home))(away.start)

    def chosen(self):
        return (self.spot.z >= min(self.sources)) & (self.spot.z <= max(self.sources))

    def finish(self):
        away, stay = self.copies()
        chosen = self.chosen()
        pl.when(chosen & self.home)(stay.wait)
        pl.when(chosen & jnp.logical_not(self.home))(away.wait_send)
        spot = self.spot
        for slot in (0, 1):
            for core in (0, 1):
                source = spot.core * 2 + slot
                here = (source == spot.z) & (spot.core == core)
                sent = (source >= min(self.sources)) & (source <= max(self.sources))
                block = self.place(slot, core)
                landing = remote(block, block, self.send.at[0], self.recv.at[slot * 2 + core], spot.mate)
                pl.when((spot.z == self.target) & jnp.logical_not(here) & sent)(landing.wait_recv)


class Guest:
    def __init__(self, inputs=(), outputs=(), scratch=(), aliases=(), plan=None):
        self.inputs, self.outputs, self.scratch = list(inputs), list(outputs), list(scratch)
        self.aliases, self.plan = list(aliases), plan


def hbm_spec():
    return pl.BlockSpec(memory_space=pl.ANY)


def vmem_spec():
    return pl.BlockSpec(memory_space=pltpu.VMEM)


def hosted(body, grid, operands, results, scratch, guests, collective_id, name, vmem=KERNEL_VMEM):
    guest_in = [pair for g in guests for pair in g.inputs]
    guest_out = [pair for g in guests for pair in g.outputs]
    guest_scratch = [s for g in guests for s in g.scratch]
    aliases, at_in, at_out = {}, len(operands), len(results)
    for g in guests:
        for i, o in g.aliases:
            aliases[at_in + i] = at_out + o
        at_in, at_out = at_in + len(g.inputs), at_out + len(g.outputs)

    def kernel(*refs):
        refs = list(refs)
        take = lambda n: [refs.pop(0) for _ in range(n)]
        ins, gins = take(len(operands)), take(len(guest_in))
        outs, gouts = take(len(results)), take(len(guest_out))
        held, gheld = take(len(scratch)), take(len(guest_scratch))
        spot, step = Spot(), pl.program_id(0)
        pl.when(step == 0)(spot.greet)
        hooks = {}
        for g in guests:
            parts = [[r.pop(0) for _ in range(n)] for r, n in (
                (gins, len(g.inputs)), (gouts, len(g.outputs)), (gheld, len(g.scratch))
            )]
            for at, actions in g.plan(spot, *parts, held).items():
                hooks.setdefault(at, []).extend(actions)

        def run(actions):
            for action in actions:
                action()

        for at in sorted(k for k in hooks if k != "end"):
            pl.when(step == at)(functools.partial(run, hooks[at]))
        body(spot, *ins, *outs, *held)
        if "end" in hooks:
            pl.when(step == grid - 1)(functools.partial(run, hooks["end"]))

    out = pl.pallas_call(
        kernel,
        grid=(grid,),
        in_specs=[s for _, s in operands + guest_in],
        out_specs=[s for _, s in results + guest_out],
        out_shape=[s for s, _ in results + guest_out],
        scratch_shapes=list(scratch) + guest_scratch,
        input_output_aliases=aliases,
        compiler_params=pltpu.CompilerParams(
            vmem_limit_bytes=vmem, collective_id=collective_id, has_side_effects=True
        ),
        name=name,
    )(*[a for a, _ in operands + guest_in])
    own, rest, per_guest = out[: len(results)], list(out[len(results) :]), []
    for g in guests:
        per_guest.append([rest.pop(0) for _ in g.outputs])
    return own, per_guest


def deliver_guest(pieces, home):
    sems = pltpu.SemaphoreType.DMA
    count = len(pieces)
    fresh = isinstance(home, jax.ShapeDtypeStruct)
    arrays = [i for i, piece in enumerate(pieces) if not isinstance(piece[0], int)]

    def plan(spot, ins, outs, held, body):
        send, recv = held
        hooks = {}
        held_by = []
        for i, piece in enumerate(pieces):
            if isinstance(piece[0], int):
                held_by.append(body[piece[0]])
            elif isinstance(piece[0], tuple):
                held_by.append(ins[arrays.index(i)].at[piece[0][1]])
            else:
                held_by.append(ins[arrays.index(i)])
        for i, (_, target, first, size, steps, *sources) in enumerate(pieces):
            blocks = size // 16
            for turn, step in enumerate(steps):
                low, high = blocks * turn // len(steps), blocks * (turn + 1) // len(steps)
                if high > low:
                    part = Deliver(
                        spot, held_by[i], outs[0], target, send.at[i], recv.at[i], first + 16 * low, 16 * (high - low),
                        *sources,
                    )
                    hooks.setdefault(step, []).append(part.start)
            every = Deliver(spot, held_by[i], outs[0], target, send.at[i], recv.at[i], first, size, *sources)
            hooks.setdefault("end", []).append(every.finish)
        return hooks

    return Guest(
        [(pieces[i][0][0] if isinstance(pieces[i][0], tuple) else pieces[i][0], hbm_spec()) for i in arrays]
        + ([] if fresh else [(home, hbm_spec())]),
        [(jax.ShapeDtypeStruct(home.shape, home.dtype), hbm_spec())],
        [sems((count, 2)), sems((count, 4))],
        [] if fresh else [(len(arrays), 0)], plan,
    )


def add_into(target, *others):
    def step(b, carry):
        total = target[b].astype(F32)
        for other in others:
            total = total + other[b].astype(F32)
        target[b] = total.astype(BF16)
        return carry

    lax.fori_loop(0, target.shape[0], step, 0)


class PlaneSum:
    def __init__(self, spot, src, bufs, send, recv, in_place=False):
        self.spot, self.src, self.send, self.recv, self.in_place = spot, src, send, recv, in_place
        self.half, self.from_mate, self.in_x, self.in_y, self.in_yx, self.in_xy = bufs

    @staticmethod
    def scratch(block_rows, columns):
        return [pltpu.VMEM((n, block_rows, columns), BF16) for n in (8, 8, 2, 2, 1, 1)]

    def mate_copies(self):
        s, spot = self, self.spot
        away = remote(s.src.at[pl.ds((1 - spot.core) * 8, 8)], s.from_mate, s.send.at[1], s.recv.at[1], spot.mate)
        if s.in_place:
            return (away,)
        return (pltpu.make_async_copy(s.src.at[pl.ds(spot.core * 8, 8)], s.half, s.send.at[0]), away)

    def start(self):
        for copy in self.mate_copies():
            copy.start()

    def block(self, chip, half):
        return self.half.at[pl.ds(chip * 2 + half, 1)]

    def first_copies(self):
        s, spot = self, self.spot
        first, second = pl.ds(0, 1), pl.ds(1, 1)
        return (
            remote(s.block(spot.c_x, 0), s.in_x.at[first], s.send.at[2], s.recv.at[2], spot.x),
            remote(s.block(spot.c_d, 0), s.in_x.at[second], s.send.at[3], s.recv.at[3], spot.x),
            remote(s.block(spot.c_y, 1), s.in_y.at[first], s.send.at[4], s.recv.at[4], spot.y),
            remote(s.block(spot.c_d, 1), s.in_y.at[second], s.send.at[5], s.recv.at[5], spot.y),
        )

    def second_copies(self):
        s, spot = self, self.spot
        return (
            remote(s.block(spot.c_y, 0), s.in_xy, s.send.at[6], s.recv.at[6], spot.y),
            remote(s.block(spot.c_x, 1), s.in_yx, s.send.at[7], s.recv.at[7], spot.x),
        )

    def first(self):
        for copy in self.mate_copies():
            copy.wait()
        add_into(self.half, self.from_mate)
        for copy in self.first_copies():
            copy.start()

    def second(self):
        s, spot = self, self.spot
        for copy in self.first_copies():
            copy.wait_recv()
        first, other = pl.ds(0, 1), pl.ds(1, 1)
        add_into(s.block(spot.c_y, 0), s.in_x.at[other])
        add_into(s.block(spot.c_x, 1), s.in_y.at[other])
        for copy in self.second_copies():
            copy.start()

    def third(self, out):
        s, spot = self, self.spot
        for copy in self.second_copies():
            copy.wait_recv()
        first = pl.ds(0, 1)
        add_into(s.block(spot.c, 0), s.in_x.at[first], s.in_xy)
        add_into(s.block(spot.c, 1), s.in_y.at[first], s.in_yx)
        for half in (0, 1):
            out[half] = s.half[spot.c * 2 + half]

    def finish(self):
        for copy in self.first_copies() + self.second_copies():
            copy.wait_send()


LEFT = (
    ("front", 0, 3, 2), ("back", None, 2, 2), ("front", 1, 3, 2), ("back", None, 3, 2),
    ("front", 0, 1, 1), ("back", None, 0, 1), ("front", 1, 1, 1), ("back", None, 1, 0),
)


TAIL_CHUNKS = 4


def collect_body(*refs):
    sections = lax.axis_size("section")
    refs_list = list(refs)
    take = lambda n: [refs_list.pop(0) for _ in range(n)]
    last, second, third, first_front, third_front = take(5)
    parts = take(len(LEFT))
    vectors = take(2 * sections + 5 * (sections // 2))
    take(1)
    home, front_out, back_out, small_out = take(4)
    sums, arriving = take(2)
    totals = take(len(LEFT))
    psend, precv, dsend, drecv, asend, arecv, ssend, srecv, stay_sem, zsend, zrecv, lsem = take(12)
    spot = Spot()
    loads = [pltpu.make_async_copy(a, b, lsem.at[i]) for i, (a, b) in enumerate(zip(parts, totals))]
    for load in loads:
        load.start()
    spot.greet()
    size = first_front.shape[2] // TAIL_CHUNKS
    columns = [pl.ds(c * size, size) for c in range(TAIL_CHUNKS)]
    sequences = []

    def sequence(total, target, done):
        n = len(sequences)
        chain = Chain(spot, total, take(len(sides(target))), target, zsend.at[n], zrecv.at[n])
        sequences.append((chain, range(done + 1, hops_of(target) + 1)))
        return sequences[-1]

    def advance(which, turn):
        for chain, hops in which:
            if 0 < turn <= len(hops):
                chain.take(hops[turn - 1])
            if turn < len(hops):
                chain.give(hops[turn])

    chains = [sequence(total, target, done) for total, (_, _, target, done) in zip(totals, LEFT)]
    planes, owns, chunk_chains = {}, {}, {}
    for n, (z, grad) in enumerate(((0, first_front), (2, third_front))):
        for c in range(TAIL_CHUNKS):
            at = n * TAIL_CHUNKS + c
            planes[z, c] = PlaneSum(spot, grad.at[:, :, columns[c]], take(6), psend.at[at], precv.at[at])
            owns[z, c] = take(1)[0]
            chunk_chains[z, c] = sequence(owns[z, c], z, 0)
    every_chunk = range(TAIL_CHUNKS)
    for z in (0, 2):
        for c in every_chunk:
            planes[z, c].start()
    rows = last.shape[0]
    ahead = rows * 3 // 4 // 16 * 16
    early, late, every = (
        Deliver(spot, last, home, 0, dsend.at[0], drecv.at[0], *r) for r in ((0, ahead), (ahead, rows - ahead), ())
    )
    other = [
        Deliver(spot, second, home, 2, dsend.at[1], drecv.at[1], 0, rows, (0, 1)),
        Deliver(spot, third, home, 3, dsend.at[2], drecv.at[2], 400, rows - 400),
    ]
    at = 0
    for vector in vectors:
        for first in range(0, vector.shape[1], sums.shape[2]):
            sums[0, at : at + 1, :] = vector[:, first : first + sums.shape[2]]
            at += 1
    partners = [spot.mate, spot.x, spot.y] + [
        {"section": spot.z + bit * (1 - 2 * ((spot.z // bit) % 2))}
        for bit in (1 << i for i in range((sections - 1).bit_length()))
    ]
    steps = len(partners)

    def small_copy(i):
        return remote(sums.at[i], arriving.at[i], ssend.at[i], srecv.at[i], partners[i])

    def small_step(i):
        if 0 < i <= steps:
            small_copy(i - 1).wait()
            sums[i] = sums[i - 1] + arriving[i - 1]
        if i < steps:
            small_copy(i).start()

    small_step(0)
    for c in every_chunk:
        planes[0, c].first()
    for load in loads:
        load.wait()
    advance(chains, 0)
    early.start()
    for deliver in other:
        deliver.start()
    small_step(1)
    for c in every_chunk:
        planes[0, c].second()
        if c:
            planes[0, c - 1].third(owns[0, c - 1])
            advance([chunk_chains[0, c - 1]], 0)
        planes[2, c].first()
    planes[0, TAIL_CHUNKS - 1].third(owns[0, TAIL_CHUNKS - 1])
    advance([chunk_chains[0, TAIL_CHUNKS - 1]], 0)
    fronts = [PlaneGather(spot, front_out.at[:, :, columns[c]], asend.at[c], arecv.at[c]) for c in every_chunk]
    back = PlaneGather(spot, back_out, asend.at[TAIL_CHUNKS], arecv.at[TAIL_CHUNKS])

    def held(kind, z, c):
        if kind == "front" and z in (0, 2):
            return owns[z, c]
        found = [t for t, (name, _, target, _) in zip(totals, LEFT) if name == kind and target == z]
        if kind == "back":
            return found[0]
        half, at = divmod(c * size, found[0].shape[2])
        return found[half].at[:, :, pl.ds(at, size)]

    def begin(gather, kind, sections_now, c=0):
        for z in sections_now:
            stay = pltpu.make_async_copy(
                held(kind, z, c), gather.dst.at[gather.blocks(spot.core, spot.c)],
                stay_sem.at[TAIL_CHUNKS if kind == "back" else c],
            )

            @pl.when(spot.z == z)
            def _(z=z, stay=stay):
                stay.start()
                gather.begin(held(kind, z, c))

    def stayed():
        for c in range(TAIL_CHUNKS + 1):
            kind, gather = ("front", fronts[c]) if c < TAIL_CHUNKS else ("back", back)
            pltpu.make_async_copy(
                held(kind, 1, 0 if kind == "back" else c), gather.dst.at[gather.blocks(spot.core, spot.c)],
                stay_sem.at[c],
            ).wait()

    small_step(2)
    late.start()
    for c in every_chunk:
        advance([chunk_chains[0, c]], 1)
    advance(chains, 1)
    small_step(3)
    for c in every_chunk:
        advance([chunk_chains[0, c]], 2)
        planes[2, c].second()
        if c:
            planes[2, c - 1].third(owns[2, c - 1])
            advance([chunk_chains[2, c - 1]], 0)
    planes[2, TAIL_CHUNKS - 1].third(owns[2, TAIL_CHUNKS - 1])
    advance([chunk_chains[2, TAIL_CHUNKS - 1]], 0)
    for c in every_chunk:
        begin(fronts[c], "front", (1, 3), c)
    begin(back, "back", (2, 3))
    small_step(4)
    advance(chains, 2)
    begin(back, "back", (0, 1))
    for c in every_chunk:
        advance([chunk_chains[0, c]], 3)
        begin(fronts[c], "front", (0,), c)
    for c in every_chunk:
        advance([chunk_chains[2, c]], 1)
    small_step(5)
    small_out[...] = sums[steps]
    for c in every_chunk:
        advance([chunk_chains[2, c]], 2)
        begin(fronts[c], "front", (2,), c)
    for gather in fronts:
        gather.second()
    back.second()
    for gather in (*fronts, back):
        gather.third()
    for gather in (*fronts, back):
        gather.finish()
    stayed()
    for deliver in (every, *other):
        deliver.finish()
    for plane in planes.values():
        plane.finish()
    for chain, hops in sequences:
        for hop in hops:
            chain.leave(hop)


def collect(last, second, third, home, first_front, third_front, parts, vectors):
    sections = lax.axis_size("section")
    width = last.shape[1]
    small = jax.ShapeDtypeStruct((sum(v.shape[1] // width for v in vectors), width), F32)
    hbm, vmem = hbm_spec(), vmem_spec()
    steps = 3 + (sections - 1).bit_length()
    sems = pltpu.SemaphoreType.DMA
    front_shape = first_front.shape
    chunk = (front_shape[1], front_shape[2] // TAIL_CHUNKS)
    back_shape = (16,) + parts[1].shape[1:]
    buffers = []
    for part, left in zip(parts, LEFT):
        buffers += [pltpu.VMEM(part.shape, BF16)] * len(sides(left[2]))
    for target in (0, 2):
        for _ in range(TAIL_CHUNKS):
            buffers += PlaneSum.scratch(*chunk) + [pltpu.VMEM((2,) + chunk, BF16)] * (1 + len(sides(target)))
    jobs = len(parts) + 2 * TAIL_CHUNKS
    return pl.pallas_call(
        collect_body,
        in_specs=[hbm] * (5 + len(parts)) + [vmem] * len(vectors) + [hbm],
        out_specs=[hbm] * 3 + [vmem],
        out_shape=[
            jax.ShapeDtypeStruct(home.shape, BF16), jax.ShapeDtypeStruct(front_shape, BF16),
            jax.ShapeDtypeStruct(back_shape, BF16), jax.ShapeDtypeStruct(small.shape, F32),
        ],
        scratch_shapes=[pltpu.VMEM((steps + 1,) + small.shape, F32), pltpu.VMEM((steps,) + small.shape, F32)]
        + [pltpu.VMEM(p.shape, BF16) for p in parts]
        + [
            sems((2 * TAIL_CHUNKS, 8)), sems((2 * TAIL_CHUNKS, 8)), sems((3, 2)), sems((3, 4)),
            sems((TAIL_CHUNKS + 1, 9)), sems((TAIL_CHUNKS + 1, 9)), sems((steps,)), sems((steps,)),
            sems((TAIL_CHUNKS + 1,)), sems((jobs,)), sems((jobs, 2)), sems((len(parts),)),
        ]
        + buffers,
        input_output_aliases={5 + len(parts) + len(vectors): 0},
        compiler_params=pltpu.CompilerParams(
            collective_id=1, has_side_effects=True, vmem_limit_bytes=KERNEL_VMEM
        ),
        name="collect",
    )(last, second, third, first_front, third_front, *parts, *vectors, home)


def norm_rows(hidden):
    average = jnp.mean(hidden, axis=-1, keepdims=True)
    centred = hidden - average
    inverse = lax.rsqrt(jnp.mean(centred * centred, axis=-1, keepdims=True) + EPS)
    return centred * inverse, inverse


def norm_backward(hidden, grad_normed, gain):
    unit, inverse = norm_rows(hidden)
    scaled = grad_normed * gain
    first = jnp.mean(scaled, axis=-1, keepdims=True)
    second = jnp.mean(scaled * unit, axis=-1, keepdims=True)
    return (
        inverse * (scaled - first - unit * second),
        jnp.sum(grad_normed * unit, axis=0, keepdims=True),
        jnp.sum(grad_normed, axis=0, keepdims=True),
    )


def gelu_and_slope(pre):
    density = jnp.exp(-0.5 * pre * pre)
    t = 1.0 / (1.0 + (0.3275911 * 0.5**0.5) * jnp.abs(pre))
    series = t * (0.127414796 + t * (-0.142248368 + t * (0.7107068705 + t * (-0.7265760135 + t * 0.5307027145))))
    tail = series * density
    below = jnp.where(pre < 0, tail, 1.0 - tail)
    return pre * below, below + pre * density * (1.0 / math.sqrt(2.0 * math.pi))


def pairs_of(block):
    return [block[:, p * PAIR : (p + 1) * PAIR] for p in range(block.shape[1] // PAIR)]


def joined(ref, lead=()):
    return jnp.concatenate([ref[lead + (p,)] for p in range(ref.shape[len(lead)])], axis=1)


def whole(shape):
    return pl.BlockSpec(shape, lambda i: (0,) * len(shape))


def swap_with_mate(spot, src, dst, send, recv):
    return remote(src, dst, send, recv, spot.mate)


def transposed_norm(hidden_ref, norm_ref):
    unit, _ = norm_rows(hidden_ref[0].astype(F32))
    normed = (unit * norm_ref[0, 0:1, :] + norm_ref[0, 1:2, :]).astype(BF16)
    return normed.astype(F32).T.astype(BF16)


def lane_ids(shape):
    return lax.broadcasted_iota(jnp.int32, shape, len(shape) - 1)


def three_parts(value):
    high = value.astype(BF16).astype(F32)
    rest = value - high
    middle = rest.astype(BF16).astype(F32)
    return high, middle, rest - middle


def extend_keys(keys_out, values_out, blocks, bias_ref, head):
    aux = HEAD_DIM * (1 - head)
    row = 0
    for key, value in blocks:
        rows = key.shape[0]
        span = slice(row, row + rows)
        lanes = lane_ids((rows, PAIR))
        inside = (lanes // HEAD_DIM) == head
        ones = jnp.where((lanes > aux) & (lanes <= aux + 3), 1.0, 0.0)
        extra = jnp.where(lanes == aux, bias_ref[span, :], ones)
        keys_out[span, :] = jnp.where(inside, key.astype(F32), extra).astype(BF16)
        ones = jnp.where((lanes >= aux) & (lanes < aux + 3), 1.0, 0.0)
        values_out[span, :] = jnp.where(inside, value.astype(F32), ones).astype(BF16)
        row += rows


def pair_forward(query_of, keys, values, rows, chunk, save):
    lanes = lane_ids((chunk, PAIR))
    units = [(start, head) for start in range(0, rows, chunk) for head in (0, 1)]

    def extended(start, head):
        aux = HEAD_DIM * (1 - head)
        inside = (lanes // HEAD_DIM) == head
        query = query_of(slice(start, start + chunk)).astype(F32)
        return jnp.where(inside, query, jnp.where(lanes == aux, 1.0, 0.0))

    def scores(start, head):
        return contract_cols(extended(start, head).astype(BF16), keys[head])

    ahead = [scores(*unit) for unit in units[:2]]
    for index, (start, head) in enumerate(units):
        now = ahead.pop(0)
        if index + 2 < len(units):
            ahead.append(scores(*units[index + 2]))
        aux = HEAD_DIM * (1 - head)
        top = jnp.max(now, axis=1, keepdims=True)
        summed = mm(jnp.exp(now - top).astype(BF16), values[head])
        total = summed[:, aux : aux + 1]
        query = extended(start, head)
        for lane, part in enumerate(three_parts(-(top + jnp.log(total))), aux + 1):
            query = jnp.where(lanes == lane, part, query)
        save(head, slice(start, start + chunk), query.astype(BF16), summed / total)


def pair_backward(query_of, grad_of, out_of, keys, values, key_sums, value_sums, rows, save):
    for start, size in ((0, 256), (256, rows - 256)):
        span = slice(start, start + size)
        lanes = lane_ids((size, PAIR))
        parts = []
        for head in (0, 1):
            aux = HEAD_DIM * (1 - head)
            inside = (lanes // HEAD_DIM) == head
            query = query_of(head, span)
            grad = jnp.where(inside, grad_of(span).astype(F32), 0.0)
            dots = jnp.sum(grad * out_of(span), axis=1, keepdims=True)
            for lane, part in enumerate(three_parts(-dots), aux):
                grad = jnp.where(lanes == lane, part, grad)
            probs = jnp.exp(contract_cols(query, keys[head]))
            shifted = contract_cols(grad.astype(BF16), values[head])
            grad_scores = (probs * shifted).astype(BF16)
            parts.append(mm(grad_scores, keys[head]) * HEAD_DIM**-0.5)
            to_values = mm(grad.T.astype(BF16), probs.astype(BF16)).T
            to_keys = mm(query.astype(F32).T.astype(BF16), grad_scores).T
            value_sums[head] = to_values if start == 0 else value_sums[head] + to_values
            key_sums[head] = to_keys if start == 0 else key_sums[head] + to_keys
        save(span, jnp.where(lanes < HEAD_DIM, parts[0], parts[1]).astype(BF16))


class Weight(PlaneGather):
    SENDS, RECEIVES = 13, 10

    def __init__(self, spot, src, dst, source, send, recv):
        super().__init__(spot, dst, send, recv)
        self.src, self.source = src, source
        self.own = self.blocks(spot.core, spot.c)

    def along(self, src):
        s = self.spot
        return (
            remote(src.at[self.own], self.dst.at[self.own], self.send.at[9], self.recv.at[9], s.above),
            remote(src.at[self.own], self.dst.at[self.own], self.send.at[10], self.recv.at[9], s.below),
        )

    def load(self):
        return pltpu.make_async_copy(self.src, self.dst, self.send.at[11])

    def open(self, up=True, down=True, load=True):
        rise, fall = self.along(self.src)

        @pl.when(self.spot.z == self.source)
        def _():
            if up and self.source + 1 < self.spot.sections:
                rise.start()
            if down and self.source:
                fall.start()
            if load:
                self.load().start()

    def pass_on(self, hop, begin=True):
        rise, fall = self.along(self.dst)
        last = self.spot.sections - 1
        for at, further, copy in ((self.source + hop, last, rise), (self.source - hop, 0, fall)):
            if not 0 <= at <= last:
                continue

            @pl.when(self.spot.z == at)
            def _(at=at, further=further, copy=copy):
                rise.wait_recv()
                if at != further:
                    copy.start()
                if begin:
                    self.begin(self.dst.at[self.own])

    def away(self, action):
        pl.when(self.spot.z != self.source)(action)

    def enter(self):
        self.away(lambda: self.begin(self.dst.at[self.own]))

    def middle(self):
        self.away(self.second)

    def late(self):
        self.away(self.third)

    def ready(self):
        rise, fall = self.along(self.src)
        last = self.spot.sections - 1
        if self.source < last:
            pl.when((self.spot.z >= self.source) & (self.spot.z < last))(rise.wait_send)
        if self.source:
            pl.when((self.spot.z <= self.source) & (self.spot.z > 0))(fall.wait_send)
        pl.when(self.spot.z == self.source)(self.load().wait)
        self.away(self.finish)


QKV_ORDER = (1, 2, 0, 3)
FORWARD_STEPS = 14


def forward_body(*refs):
    refs_list = list(refs)
    take = lambda n: [refs_list.pop(0) for _ in range(n)]
    clips, grads, front, back, norms, kind_in, bias_qv, bias_attn, bias_up, bias_down = take(10)
    key_out, value_out, key_far_out, value_far_out, extended_out, attended_out, act_out, slope_out = take(8)
    fronts_out, downs_out, hidden_out, grad_out, acts_home, mask_out, key_bias_out, norm_out = take(8)
    fronts, downs, hidden, own, far, attended, keys, values, normed, total, norm_all, kind, blank = take(13)
    wsend, wrecv, nsend, nrecv, csend, crecv, ksend, krecv, dsend, drecv, lsem = take(11)
    step = pl.program_id(0)
    layer, turn = step // FORWARD_STEPS, step % FORWARD_STEPS
    rows, width = normed.shape
    pairs = width // PAIR
    spot = Spot()
    owner, slot = spot.z // 2, spot.z % 2
    holds = spot.core == owner

    weights, count = {}, 0

    def weight(name, src, dst, source):
        nonlocal count
        weights[name] = Weight(spot, src, dst, source, wsend.at[count], wrecv.at[count])
        count += 1

    for j, block in enumerate(QKV_ORDER):
        at = pl.ds(block * width, width)
        weight(("first", j), front.at[:, :, at], fronts.at[0, :, :, at], 0)
    for s in range(1, 4):
        for n in range(1 + s % 2):
            size = fronts.shape[3] // (1 + s % 2)
            at = pl.ds(n * size, size)
            weight(("front", s, n), front.at[:, :, at], fronts.at[s, :, :, at], s)
    for s in range(4):
        weight(("back", s), back, downs.at[s // 2, pl.ds(16 * (s % 2), 16)], s)
    first = [weights["first", j] for j in range(4)]
    front_1, front_2, front_3 = ([weights["front", s, n] for n in range(1 + s % 2)] for s in (1, 2, 3))
    (front_2,) = front_2
    back_0, back_1, back_2, back_3 = (weights["back", s] for s in range(4))

    norm_copies = [
        remote(norms, norm_all.at[spot.z], nsend.at[i], nrecv.at[i], {"section": (spot.z + i) % spot.sections})
        for i in range(1, spot.sections)
    ]

    def clip_copies():
        mine, other = (pl.ds(pl.multiple_of(c * rows, 16), rows) for c in (spot.core, 1 - spot.core))
        away = [
            remote(clips.at[slot, other], hidden.at[0], csend.at[0], crecv.at[0], spot.mate),
            remote(grads.at[slot, other], grad_out, csend.at[1], crecv.at[1], spot.mate),
            remote(kind_in, kind, csend.at[2], crecv.at[2], spot.mate),
        ]
        stay = [
            pltpu.make_async_copy(clips.at[slot, mine], hidden.at[0], csend.at[3]),
            pltpu.make_async_copy(grads.at[slot, mine], grad_out, csend.at[4]),
        ]
        return away, stay

    def pads():
        pad = acts_home.shape[1] - 2 * rows
        return [
            pltpu.make_async_copy(blank, acts_home.at[i, pl.ds(2 * rows, pad)], lsem.at[i]) for i in (0, 1)
        ]

    def enter():
        blank[...] = jnp.zeros_like(blank)
        spot.greet()
        for w in first:
            w.open()
        away, stay = clip_copies()

        @pl.when(holds)
        def _():
            for copy in (away[2], away[0], stay[0], away[1]):
                copy.start()
            kind[...] = kind_in[...]
        for copy in norm_copies:
            copy.start()
        norm_all[spot.z] = norms[...]
        for w in (*front_1, back_1, front_2, back_2, *front_3, back_3):
            w.open(up=False)
        back_2.open(down=False, load=False)
        for w in first:
            for hop in (1, 2, 3):
                w.pass_on(hop)
        for w in (front_1[0], front_1[1], back_1, front_2):
            w.open(down=False, load=False)
        back_0.open()

        @pl.when(holds)
        def _():
            stay[1].start()
            stay[0].wait()

        @pl.when(jnp.logical_not(holds))
        def _():
            away[0].wait_recv()
            away[2].wait_recv()
        for i, copy in enumerate(norm_copies, 1):
            block = norm_all.at[(spot.z + spot.sections - i) % spot.sections]
            remote(block, block, nsend.at[i], nrecv.at[i], spot.mate).wait_recv()
        norm_out[...] = norm_all[...]
        for copy in pads():
            copy.start()
        length = SHORT + (LONG - SHORT) * kind[0:1, 0:1]
        place = lax.broadcasted_iota(jnp.int32, (rows, 1), 0)
        near, there = ((place + c * rows).astype(F32) < length for c in (spot.core, 1 - spot.core))
        mask_out[...] = near.astype(F32)
        key_bias_out[:rows, :] = jnp.where(near, 0.0, MASKED)
        key_bias_out[rows:, :] = jnp.where(there, 0.0, MASKED)
        for w in first:
            w.middle()
        for w in front_1:
            w.pass_on(1)
        back_1.pass_on(1)
        for w in first:
            w.late()
        for w in front_1:
            w.pass_on(2)
        first[0].ready()

    early, late = functools.partial, False
    plan = {
        0: [enter],
        1: [first[1].ready, early(back_1.pass_on, 2), early(back_0.pass_on, 1)],
        2: [first[2].ready, early(back_0.pass_on, 2), early(front_2.pass_on, 1, late), early(back_2.pass_on, 1, late)],
        3: [first[3].ready, early(back_0.pass_on, 3), *(early(w.pass_on, 1, late) for w in front_3)],
        4: [front_1[0].middle, early(back_3.pass_on, 1, late), early(front_2.pass_on, 2, late)],
        5: [front_1[1].middle, early(back_2.pass_on, 2, late)],
        6: [back_1.middle, *(early(w.pass_on, 2, late) for w in front_3), front_1[0].late],
        7: [back_0.middle, front_1[1].late, early(back_3.pass_on, 2, late)],
        8: [front_2.enter],
        9: [back_1.late, *(early(w.pass_on, 3, late) for w in front_3)],
        10: [back_0.late, early(back_3.pass_on, 3, late), front_3[0].enter, back_2.enter, front_1[0].ready, back_0.ready],
        12: [front_1[1].ready, back_1.ready, front_2.middle],
        13: [front_2.late, front_3[1].enter, back_3.enter],
        14: [front_2.ready],
        15: [front_3[0].middle],
        17: [back_2.middle, front_3[0].late],
        18: [front_3[1].middle],
        19: [back_3.middle, back_2.late],
        20: [front_3[1].late],
        22: [back_3.late],
        24: [front_3[0].ready, back_2.ready],
        26: [front_3[1].ready, back_3.ready],
    }
    ends = []

    def keep(at, src, dst, index):
        copy = pltpu.make_async_copy(src, dst, lsem.at[2 + index])
        plan.setdefault(at, []).append(copy.start)
        ends.append(copy.wait)

    for s, at in ((0, 10), (1, 13), (2, 20)):
        keep(at, fronts.at[s], fronts_out.at[s], s)
    keep(15, downs.at[0], downs_out.at[0], 4)
    half = fronts.shape[3] // 2
    for n, at in ((0, 24), (1, 26)):
        columns, blocks = pl.ds(n * half, half), pl.ds(16 * n, 16)
        keep(at, fronts.at[3, :, :, columns], fronts_out.at[3, :, :, columns], (3, 11)[n])
        keep(at, downs.at[1, blocks], downs_out.at[1, blocks], (5, 12)[n])
    for s, at in ((0, 4), (1, 11), (2, 16), (3, 25)):
        keep(at, hidden.at[s], hidden_out.at[s], 6 + s)

    for n, (s, first_row, size, begin, stop) in enumerate(FORWARD_DELIVERIES):
        size = size or rows - first_row
        blocks = size // 16
        for i in range(stop - begin):
            low, high = blocks * i // (stop - begin), blocks * (i + 1) // (stop - begin)
            part = Deliver(
                spot, hidden.at[s + 1], acts_home, s, dsend.at[n], drecv.at[n], first_row + 16 * low, 16 * (high - low)
            )
            plan.setdefault(begin + i, []).append(part.start)
        ends.append(Deliver(spot, hidden.at[s + 1], acts_home, s, dsend.at[n], drecv.at[n], first_row, size).finish)

    for at, actions in sorted(plan.items()):
        @pl.when(step == at)
        def _(actions=actions):
            for action in actions:
                action()

    def norms_of(s):
        return norm_all[s, 0:1, :], norm_all[s, 1:2, :]

    def start_sub_layer(s):
        gain, shift = norms_of(s)
        unit, _ = norm_rows(hidden[s].astype(F32))
        normed[...] = (unit * gain + shift).astype(BF16)

    def front_block(s, block):
        return fronts[s, :, :, pl.ds(pl.multiple_of(block * width, width), width)].reshape(width, width)

    def swaps():
        return [
            remote(own.at[j], far.at[layer, j], ksend.at[layer, j], krecv.at[layer, j], spot.mate) for j in (0, 1)
        ]

    @pl.when(turn == 0)
    def _():
        start_sub_layer(2 * layer)

    for j, scale in ((0, 1.0), (1, 1.0), (2, HEAD_DIM**-0.5)):
        @pl.when(turn == j)
        def _(j=j, scale=scale):
            block = mm(normed[...], front_block(2 * layer, QKV_ORDER[j]))
            if j == 1:
                block = block + bias_qv[pl.ds(layer, 1), width:]
            elif j == 2:
                block = block + bias_qv[pl.ds(layer, 1), :width]
            block = block.astype(BF16)
            if scale != 1.0:
                block = (block.astype(F32) * scale).astype(BF16)
            for p, part in enumerate(pairs_of(block)):
                own[j, p] = part
            if j < 2:
                swaps()[j].start()
            else:
                for copy in swaps():
                    copy.wait()

    @pl.when((turn >= 3) & (turn < 3 + pairs))
    def _():
        p = turn - 3
        for head in (0, 1):
            extend_keys(
                keys.at[head], values.at[head], [(own[0, p], own[1, p]), (far[layer, 0, p], far[layer, 1, p])],
                key_bias_out, head,
            )
        for j, out in enumerate((key_out, value_out)):
            out[0, 0] = own[j, p]
        for j, out in enumerate((key_far_out, value_far_out)):
            out[0, 0] = far[layer, j, p]
        lanes = lane_ids((rows // 2, PAIR))
        firsts = {}

        def save(head, span, query, out):
            extended_out[0, head, span, :] = query
            if head == 0:
                firsts[span.start] = out
            else:
                both = jnp.where(lanes < HEAD_DIM, firsts[span.start], out)
                attended_out[0, 0, span, :] = both
                attended[p, span, :] = both.astype(BF16)

        pair_forward(lambda span: own[2, p, span, :], keys, values, rows, rows // 2, save)

    @pl.when(turn == 3 + pairs)
    def _():
        s = 2 * layer
        branch = contract_cols(joined(attended), front_block(s, 3)) + bias_attn[pl.ds(layer, 1), :]
        hidden[s + 1] = (mask_out[...] * (hidden[s].astype(F32) + branch)).astype(BF16)

    @pl.when(turn == 4 + pairs)
    def _():
        start_sub_layer(2 * layer + 1)

    @pl.when(turn >= 4 + pairs)
    def _():
        i = turn - 4 - pairs
        columns = pl.ds(pl.multiple_of(i * width, width), width)
        up = fronts[2 * layer + 1, :, :, columns].reshape(width, width)
        down_blocks = width * 32 // (width * 4)
        down = downs[layer, pl.ds(i * down_blocks, down_blocks)].reshape(width, width)
        bias = bias_up[pl.ds(layer, 1), columns]
        for span in (slice(0, rows // 2), slice(rows // 2, rows)):
            act, slope = gelu_and_slope(mm(normed[span, :], up) + bias)
            act_out[0, span, :] = act.astype(BF16)
            slope_out[0, span, :] = slope.astype(BF16)
            part = mm(act.astype(BF16), down)
            total[span, :] = jnp.where(i == 0, part, total[span, :] + part)

    @pl.when(turn == FORWARD_STEPS - 1)
    def _():
        s = 2 * layer + 1
        branch = total[...] + bias_down[pl.ds(layer, 1), :]
        hidden[s + 1] = (mask_out[...] * (hidden[s].astype(F32) + branch)).astype(BF16)

    @pl.when(step == 2 * FORWARD_STEPS - 1)
    def _():
        copy = pltpu.make_async_copy(hidden.at[4], hidden_out.at[4], lsem.at[12])
        copy.start()
        for end in ends:
            end()
        copy.wait()
        for pad in pads():
            pad.wait()
        for sent in norm_copies:
            sent.wait_send()
        away, stay = clip_copies()

        @pl.when(holds)
        def _():
            for sent in away:
                sent.wait_send()
            stay[1].wait()

        pl.when(jnp.logical_not(holds))(away[1].wait_recv)


FORWARD_DELIVERIES = ((0, 0, None, 10, 18), (1, 0, None, 14, 20))


def forward(clips, grads, kind, front, back, norms, bias_qv, bias_attn, bias_up, bias_down, rows):
    sections = lax.axis_size("section")
    padded, width = clips.shape[1:]
    units, pairs = front.shape[1], width // PAIR
    front_b = front.reshape(16, width // 16, units)
    back_b = back.reshape(16, back.shape[0] // 16, width)
    layers = sections // 2
    layer = lambda i: i // FORWARD_STEPS
    pair = lambda i: jnp.clip(i % FORWARD_STEPS - 3, 0, pairs - 1)
    unit = lambda i: jnp.maximum(i % FORWARD_STEPS - 4 - pairs, 0)
    hbm, vmem = hbm_spec(), vmem_spec()
    per_pair = pl.BlockSpec((1, 1, rows, PAIR), lambda i: (layer(i), pair(i), 0, 0))
    per_unit = pl.BlockSpec((1, rows, width), lambda i: (layer(i), 0, unit(i)))
    shape = jax.ShapeDtypeStruct
    saved = shape((layers, pairs, rows, PAIR), BF16)
    sems = pltpu.SemaphoreType.DMA
    jobs = 4 + 5 + 4
    sent = len(FORWARD_DELIVERIES)
    return pl.pallas_call(
        forward_body,
        grid=(2 * FORWARD_STEPS,),
        in_specs=[hbm] * 4 + [vmem] * 6,
        out_specs=[per_pair] * 4
        + [pl.BlockSpec((1, 2, rows, PAIR), lambda i: (layer(i), pair(i), 0, 0)), per_pair, per_unit, per_unit]
        + [hbm] * 5 + [vmem] * 3,
        out_shape=[saved] * 4
        + [
            shape((layers, 2 * pairs, rows, PAIR), BF16), shape((layers, pairs, rows, PAIR), F32),
            shape((layers, rows, units), BF16), shape((layers, rows, units), BF16),
            shape((sections,) + front_b.shape, BF16), shape((layers, 32) + back_b.shape[1:], BF16),
            shape((sections + 1, rows, width), BF16), shape((rows, width), BF16),
            shape((clips.shape[0], padded, width), BF16),
            shape((rows, 1), F32), shape((2 * rows, 1), F32), shape((sections,) + norms.shape, F32),
        ],
        scratch_shapes=[
            pltpu.VMEM((sections,) + front_b.shape, BF16), pltpu.VMEM((layers, 32) + back_b.shape[1:], BF16),
            pltpu.VMEM((sections + 1, rows, width), BF16), pltpu.VMEM((3, pairs, rows, PAIR), BF16),
            pltpu.VMEM((layers, 2, pairs, rows, PAIR), BF16), pltpu.VMEM((pairs, rows, PAIR), BF16),
            pltpu.VMEM((2, 2 * rows, PAIR), BF16), pltpu.VMEM((2, 2 * rows, PAIR), BF16),
            pltpu.VMEM((rows, width), BF16), pltpu.VMEM((rows, width), F32),
            pltpu.VMEM((sections,) + norms.shape, F32), pltpu.VMEM(kind.shape, F32),
            pltpu.VMEM((padded - 2 * rows, width), BF16),
            sems((jobs, Weight.SENDS)), sems((jobs, Weight.RECEIVES)), sems((sections,)), sems((sections,)),
            sems((5,)), sems((3,)), sems((layers, 2)), sems((layers, 2)), sems((sent, 2)), sems((sent, 4)), sems((15,)),
        ],
        compiler_params=pltpu.CompilerParams(
            vmem_limit_bytes=63 * 2**20, collective_id=0, has_side_effects=True
        ),
        name="forward",
    )(clips, grads, front_b, back_b, norms, kind, bias_qv, bias_attn, bias_up, bias_down)


FF_STEPS = 4


def backward_body(
    spot, incoming_ref, mask_ref, hidden_ref, act_ref, slope_ref, front_ref, down_ref, norm_ref,
    key_ref, value_ref, key_far_ref, value_far_ref, extended_ref, attended_ref, key_bias_ref,
    weight_grad, mid_out, out_ref, ff_gain_grad, ff_shift_grad, up_bias_grad, down_bias_grad,
    gain_grad, shift_grad, query_bias_grad, value_bias_grad, out_bias_grad,
    mid, front_grad, down_grad, grad, normed_t, total, grad_out, attended, grads, sent, arrived,
    keys, values, key_sums, value_sums, send, recv,
):
    step, last = pl.program_id(0), pl.num_programs(0) - 1
    rows, width = grad.shape
    pairs = width // PAIR
    first_pair, first_part = FF_STEPS, FF_STEPS + pairs
    weight = front_ref[0].reshape(width, width)

    def swap_of(p):
        return remote(sent.at[p], arrived.at[p], send.at[p], recv.at[p], spot.mate)

    def start(source, bias_sums):
        grad_rows = mask_ref[...] * source.astype(F32)
        grad[...] = grad_rows.astype(BF16)
        bias_sums[...] = jnp.sum(grad_rows, axis=0, keepdims=True)

    def norm_grads(gain_sums, shift_sums):
        grad_hidden, gain_sums[...], shift_sums[...] = norm_backward(
            hidden_ref[0].astype(F32), total[...], norm_ref[0, 0:1, :]
        )
        return (grad[...].astype(F32) + grad_hidden).astype(BF16)

    @pl.when(step == 0)
    def _():
        start(incoming_ref[...], down_bias_grad)
        normed_t[...] = transposed_norm(hidden_ref, norm_ref)

    @pl.when(step < FF_STEPS)
    def _():
        down = down_ref[0].reshape(width, width)
        blocks = down_ref.shape[1]
        grad_pre = (contract_cols(grad[...], down) * slope_ref[0].astype(F32)).astype(BF16)
        down_part = contract_rows(act_ref[0], grad[...]).astype(BF16)
        down_grad[pl.ds(step * blocks, blocks)] = down_part.reshape(down_ref.shape[1:])
        up_bias_grad[...] = jnp.sum(grad_pre.astype(F32), axis=0, keepdims=True)
        up_part = mm(normed_t[...], grad_pre).astype(BF16)
        columns = pl.ds(pl.multiple_of(step * width, width), width)
        front_grad[:, :, columns] = up_part.reshape(16, width // 16, width)
        part = contract_cols(grad_pre, weight)
        total[...] = jnp.where(step == 0, part, total[...] + part)

    @pl.when(step == FF_STEPS - 1)
    def _():
        mid[...] = norm_grads(ff_gain_grad, ff_shift_grad)
        mid_out[...] = mid[...]

    @pl.when(step == first_pair)
    def _():
        start(mid[...], out_bias_grad)
        for p, part in enumerate(pairs_of(mm(grad[...], weight).astype(BF16))):
            grad_out[p] = part

    @pl.when((step >= first_pair) & (step < first_part))
    def _():
        p = step - first_pair
        for head in (0, 1):
            extend_keys(
                keys.at[head], values.at[head],
                [(key_ref[0, 0], value_ref[0, 0]), (key_far_ref[0, 0], value_far_ref[0, 0])], key_bias_ref, head,
            )
        attended[p] = attended_ref[0, 0].astype(BF16)

        def save(span, value):
            grads[0, p, span, :] = value

        pair_backward(
            lambda head, span: extended_ref[0, head, span, :], lambda span: grad_out[p, span, :],
            lambda span: attended_ref[0, 0, span, :], keys, values, key_sums, value_sums, rows, save,
        )
        first = lane_ids((rows, PAIR)) < HEAD_DIM
        for j, sums in enumerate((key_sums, value_sums)):
            grads[1 + j, p] = jnp.where(first, sums[0, :rows, :], sums[1, :rows, :]).astype(BF16)
            sent[p, j] = jnp.where(first, sums[0, rows:, :], sums[1, rows:, :]).astype(BF16)
        swap_of(p).start()

    @pl.when(step == first_part)
    def _():
        normed_t[...] = transposed_norm(hidden_ref, norm_ref)
        for p in range(pairs):
            swap_of(p).wait()
            for j in (0, 1):
                grads[1 + j, p] = (grads[1 + j, p].astype(F32) + arrived[p, j].astype(F32)).astype(BF16)

    @pl.when((step >= first_part) & (step < last))
    def _():
        j = step - first_part
        part = joined(grads, (j,))
        sums = jnp.sum(part.astype(F32), axis=0, keepdims=True)

        @pl.when(j == 0)
        def _():
            query_bias_grad[...] = sums

        @pl.when(j == 2)
        def _():
            value_bias_grad[...] = sums

        weight_grad[...] = mm(normed_t[...], part).astype(BF16).reshape(weight_grad.shape)
        product = contract_cols(part, weight)
        total[...] = jnp.where(j == 0, product, total[...] + product)

    @pl.when(step == last)
    def _():
        weight_grad[...] = contract_rows(grad[...], joined(attended)).astype(BF16).reshape(weight_grad.shape)
        out_ref[...] = norm_grads(gain_grad, shift_grad)


def backward(incoming, mask, hidden, act, slope, fronts, downs, norms, heads, key_bias, layer, guests, collective_id):
    rows, width = incoming.shape
    units, pairs = fronts.shape[3], width // PAIR
    first_part = FF_STEPS + pairs
    once = lambda shape: pl.BlockSpec(shape, lambda i: (0,) * len(shape), pipeline_mode=pl.Buffered(1))
    sub = lambda i: 2 * layer + jnp.where(i < FF_STEPS, 1, 0)
    unit = lambda i: jnp.minimum(i, FF_STEPS - 1)
    pair = lambda i: jnp.clip(i - FF_STEPS, 0, pairs - 1)
    column = lambda i: jnp.where(i < FF_STEPS, i, jnp.where(i < first_part, 3, jnp.minimum(i - first_part, 2)))
    per_unit = pl.BlockSpec((1, rows, width), lambda i: (layer, 0, unit(i)))
    per_pair = pl.BlockSpec((1, 1, rows, PAIR), lambda i: (layer, pair(i), 0, 0))
    down_blocks = 32 // FF_STEPS
    in_specs = [
        once((rows, width)), once((rows, 1)),
        pl.BlockSpec((1, rows, width), lambda i: (sub(i), 0, 0)), per_unit, per_unit,
        pl.BlockSpec((1, 16, width // 16, width), lambda i: (sub(i), 0, 0, column(i))),
        pl.BlockSpec((1, down_blocks) + downs.shape[2:], lambda i: (layer, unit(i), 0, 0)),
        pl.BlockSpec((1,) + norms.shape[1:], lambda i: (sub(i), 0, 0)),
        per_pair, per_pair, per_pair, per_pair,
        pl.BlockSpec((1, 2, rows, PAIR), lambda i: (layer, pair(i), 0, 0)), per_pair, once((2 * rows, 1)),
    ]
    full, vector = jax.ShapeDtypeStruct((rows, width), BF16), jax.ShapeDtypeStruct((1, width), F32)
    out_specs = [
        pl.BlockSpec((16, width // 16, width), lambda i: (0, 0, jnp.maximum(i - first_part, 0))),
        whole((rows, width)), whole((rows, width)), whole((1, width)), whole((1, width)),
        pl.BlockSpec((1, width), lambda i: (0, unit(i))),
    ] + [whole((1, width))] * 6
    out_shape = [
        jax.ShapeDtypeStruct((16, width // 16, units), BF16), full, full, vector, vector,
        jax.ShapeDtypeStruct((1, units), F32),
    ] + [vector] * 6
    vmem = pltpu.VMEM
    scratch = [
        vmem((rows, width), BF16), vmem((16, width // 16, units), BF16), vmem(downs.shape[1:], BF16),
        vmem((rows, width), BF16), vmem((width, rows), BF16), vmem((rows, width), F32),
        vmem((pairs, rows, PAIR), BF16), vmem((pairs, rows, PAIR), BF16), vmem((3, pairs, rows, PAIR), BF16),
        vmem((pairs, 2, rows, PAIR), BF16), vmem((pairs, 2, rows, PAIR), BF16),
        vmem((2, 2 * rows, PAIR), BF16), vmem((2, 2 * rows, PAIR), BF16),
        vmem((2, 2 * rows, PAIR), F32), vmem((2, 2 * rows, PAIR), F32),
        pltpu.SemaphoreType.DMA((pairs,)), pltpu.SemaphoreType.DMA((pairs,)),
    ]
    args = (incoming, mask, hidden, act, slope, fronts, downs, norms, *heads, key_bias)
    return hosted(
        backward_body, first_part + 4, list(zip(args, in_specs)), list(zip(out_shape, out_specs)), scratch,
        guests, collective_id, f"backward_{layer}", 63 * 2**20,
    )


def held_sum_guest(shapes, views, stages, targets, hop_steps):
    sems = pltpu.SemaphoreType.DMA
    hopping = [sides(target) if at is not None else [] for target, at in zip(targets, hop_steps)]
    sizes = [5 + len(names) for names in hopping]

    def plan(spot, ins, outs, held, body):
        held = list(held)
        send, recv, csend, crecv = held[-4:]
        hooks = {}
        for i, (number, index) in enumerate(views):
            bufs, held = held[: sizes[i]], held[sizes[i] :]
            src = body[number].at[index]
            job = PlaneSum(
                spot, src, [src.at[pl.ds(spot.core * 8, 8)]] + bufs[:5], send.at[i], recv.at[i], in_place=True
            )
            actions = (job.start, job.first, job.second, functools.partial(job.third, outs[i]))
            for at, action in zip(stages[i], actions):
                hooks.setdefault(at, []).append(action)
            hooks.setdefault("end", []).append(job.finish)
            if hop_steps[i] is not None:
                chain = Chain(spot, outs[i], bufs[5:], targets[i], csend.at[i], crecv.at[i])
                hooks.setdefault(hop_steps[i], []).append(functools.partial(chain.give, 1))
                hooks["end"].extend([functools.partial(chain.take, 1), functools.partial(chain.leave, 1)])
        return hooks

    buffers = []
    for shape, names in zip(shapes, hopping):
        buffers += PlaneSum.scratch(*shape)[1:] + [pltpu.VMEM((2,) + shape, BF16)] * len(names)
    count = len(shapes)
    return Guest(
        (), [(jax.ShapeDtypeStruct((2,) + s, BF16), vmem_spec()) for s in shapes],
        buffers + [sems((count, 8)), sems((count, 8)), sems((count,)), sems((count, 2))], (), plan,
    )


def sides(target):
    return [name for name, any_there in (("below", target > 0), ("above", target < 3)) if any_there]


def hops_of(target):
    return max(target, 3 - target)


class Chain:
    def __init__(self, spot, total, bufs, target, send, recv):
        self.spot, self.total, self.target, self.send, self.recv = spot, total, target, send, recv
        self.from_below, self.from_above = bufs[0], bufs[-1]

    def ends(self, hop):
        last = self.spot.sections - 1
        return hop - 1 if hop <= self.target else None, last - hop + 1 if last - hop >= self.target else None

    def rise(self):
        return remote(self.total, self.from_below, self.send, self.recv.at[0], self.spot.above)

    def fall(self):
        return remote(self.total, self.from_above, self.send, self.recv.at[1], self.spot.below)

    def give(self, hop):
        below, above = self.ends(hop)
        if below is not None:
            pl.when(self.spot.z == below)(self.rise().start)
        if above is not None:
            pl.when(self.spot.z == above)(self.fall().start)

    def take(self, hop):
        below, above = self.ends(hop)
        if below is not None:
            @pl.when(self.spot.z == below + 1)
            def _():
                self.rise().wait_recv()
                add_into(self.total, self.from_below)
        if above is not None:
            @pl.when(self.spot.z == above - 1)
            def _():
                self.fall().wait_recv()
                add_into(self.total, self.from_above)

    def leave(self, hop):
        below, above = self.ends(hop)
        if below is not None:
            pl.when(self.spot.z == below)(self.rise().wait_send)
        if above is not None:
            pl.when(self.spot.z == above)(self.fall().wait_send)


def chain_guest(jobs):
    sems = pltpu.SemaphoreType.DMA

    def plan(spot, ins, outs, held, body):
        held = list(held)
        send, recv, loads = held[-3:]
        hooks, ends = {}, []
        for i, (_, target, first, steps) in enumerate(jobs):
            bufs, held = held[: len(sides(target))], held[len(sides(target)) :]
            chain = Chain(spot, outs[i], bufs, target, send.at[i], recv.at[i])
            load = pltpu.make_async_copy(ins[i], outs[i], loads.at[i])
            hooks.setdefault(0, []).extend([load.start, load.wait])
            for n, at in enumerate(steps):
                hop = first + n
                if n:
                    hooks.setdefault(at, []).append(functools.partial(chain.take, hop - 1))
                hooks.setdefault(at, []).append(functools.partial(chain.give, hop))
                ends.append(functools.partial(chain.leave, hop))
            ends.append(functools.partial(chain.take, first + len(steps) - 1))
        hooks["end"] = ends
        return hooks

    buffers = []
    for a, target, _, _ in jobs:
        buffers += [pltpu.VMEM(a.shape, BF16)] * len(sides(target))
    return Guest(
        [(job[0], hbm_spec()) for job in jobs],
        [(jax.ShapeDtypeStruct(job[0].shape, BF16), vmem_spec()) for job in jobs],
        buffers + [sems((len(jobs),)), sems((len(jobs), 2)), sems((len(jobs),))], (), plan,
    )


def per_device(
    clip_inputs, out_grad, clip_class, w_front, w_back, norm_gain, norm_shift,
    bias_query_value, bias_attn_out, bias_up, bias_down,
):
    spot = Spot()
    sections = lax.axis_size("section")
    padded, width = clip_inputs.shape[1:]
    rows = -(-LONG // 32) * 16
    section = spot.z

    kind = lax.dynamic_index_in_dim(clip_class, section % 2, 0, False).astype(F32)
    norms = jnp.concatenate([norm_gain, norm_shift, jnp.zeros((6, width), F32)], axis=0)
    (
        key, value, key_far, value_far, extended, attended, act, slope,
        fronts, downs, hidden, incoming, acts_home, row_mask, key_bias, norm_all,
    ) = forward(
        clip_inputs, out_grad, jnp.broadcast_to(kind, (8, 128)), w_front[0], w_back[0], norms,
        bias_query_value, bias_attn_out, bias_up, bias_down, rows,
    )
    acts = [(hidden, s + 1) for s in range(sections)]
    grads_home = jax.ShapeDtypeStruct((clip_inputs.shape[0], 2 * rows, width), BF16)
    heads = (key, value, key_far, value_far, extended, attended)
    input_grads, grad_fronts = [None] * sections, [None] * sections
    grad_gain, grad_shift = [None] * sections, [None] * sections
    query_sums, value_sums, out_sums, up_sums, down_sums = ([None] * 2 for _ in range(5))
    units = fronts.shape[3] // 2
    halves = [pl.ds(0, units), pl.ds(units, units)]
    views = []
    for i in (0, 1):
        views += [(1, (slice(None), slice(None), halves[i])), (2, pl.ds(16 * i, 16))]
    shapes = [(width // 16, units), downs.shape[2:]] * 2
    stages = ((2, 3, 6, 8), (2, 3, 7, 9), (4, 5, 9, 12), (4, 5, 11, "end"))
    hop_steps = {1: (8, 9, None, None), 0: (8, 9, 12, None)}
    early, late = range(0, 4), range(4, 8)
    for layer in (1, 0):
        targets = (2 * layer + 1, 2 * layer, 2 * layer + 1, 2 * layer + 1)
        guests = [held_sum_guest(shapes, views, stages, targets, hop_steps[layer])]
        if layer == 1:
            guests.append(deliver_guest(
                [(acts[2], 2, 0, rows, early), (acts[3], 3, 0, 400, early)], acts_home
            ))
        else:
            done = ((3, 2, (1,)), (2, 2, (1,)), (3, 1, (0, 5)), (3, 1, (0, 5)))
            guests.append(chain_guest([(part, *hops) for part, hops in zip(passing, done)]))
            guests.append(deliver_guest(
                [(input_grads[3], 3, 0, 400, early), (0, 1, 0, rows, late), (input_grads[2], 2, 0, rows, early, (2, 3))],
                grads_home
            ))
            guests.append(deliver_guest([(acts[3], 3, 400, rows - 400, early)], acts_home))
        (
            grad_fronts[2 * layer], input_grads[2 * layer + 1], input_grads[2 * layer],
            grad_gain[2 * layer + 1], grad_shift[2 * layer + 1], up_sums[layer], down_sums[layer],
            grad_gain[2 * layer], grad_shift[2 * layer], query_sums[layer], value_sums[layer], out_sums[layer],
        ), carried = backward(
            incoming, row_mask, hidden, act, slope, fronts, downs, norm_all, heads, key_bias, layer, guests, 2 + layer
        )
        incoming = input_grads[2 * layer]
        if layer == 1:
            passing, (acts_home,) = carried
        else:
            later, earlier, (grads_home,), (acts_home,) = carried

    pair_sums = [v for both in zip(query_sums, value_sums) for v in both]
    vectors = grad_gain + grad_shift + pair_sums + out_sums + up_sums + down_sums
    grads_home, front_out, back_out, small = collect(
        input_grads[0], input_grads[2], input_grads[3], grads_home, grad_fronts[0],
        grad_fronts[2], [*earlier, *later], vectors,
    )
    front_out = front_out.reshape(width, -1)
    back_out = back_out.reshape(-1, width)
    for bit in spot.spare_bits:
        small = small + swap(small, bit)
        front_out, back_out = add(front_out, swap(front_out, bit)), add(back_out, swap(back_out, bit))
    grads_out = jnp.pad(grads_home.astype(F32), ((0, 0), (0, padded - 2 * rows), (0, 0)))
    parts, place_at = [], 0
    layers, hidden_units = bias_up.shape
    for count, size in (
        (sections, width), (sections, width), (layers, 2 * width), (layers, width),
        (layers, hidden_units), (layers, width),
    ):
        taken = count * size // width
        parts.append(small[place_at : place_at + taken].reshape(count, size))
        place_at += taken
    return (
        acts_home[None],
        grads_out[None],
        front_out.astype(F32)[None],
        back_out.astype(F32)[None],
        lax.dynamic_slice_in_dim(parts[0], section, 1, 0),
        lax.dynamic_slice_in_dim(parts[1], section, 1, 0),
        *parts[2:],
    )


def solution(mesh):
    placed = (
        P("dp", None, None), P("dp", None, None), P("dp"),
        P("section", None, None), P("section", None, None), P("section", None), P("section", None),
        P(), P(), P(), P(),
    )
    return jax.shard_map(
        per_device,
        mesh=mesh,
        in_specs=placed,
        out_specs=(
            P("section", "dp", None, None), P("section", "dp", None, None),
            P("section", None, None), P("section", None, None), P("section", None), P("section", None),
            P(), P(), P(), P(),
        ),
        check_vma=False,
    )
```
